32 devices in a mesh: dp: 8 (over z, x), vocab: 4 (over y, core).
Axes of the slice: x: 2, y: 2, z: 4, core: 2. Of those that a mesh axis runs over, the one named last changes fastest.
Arguments:
- ids: int32 [8, 728], P('dp'), may hold values from 0 to 15359
- docs: int32 [8, 728], P('dp'), may hold values from 0 to 5, never falling along the last dimension, each value on 1 to 364 neighbouring positions
- resets: int32 [8, 1], P('dp'), may hold values 0 or 1
- mlm_pos: int32 [8, 112], P('dp'), may hold values from 0 to 727
- mlm_label: int32 [8, 112], P('dp'), may hold values from 0 to 15359
- step: int32 [1], replicated, may hold values from 2 to 20
- qkv_master: float32 [1, 768, 2304], P(None, 'dp'), may hold values from -0.21875 to 0.21875
- qkv_first: float32 [1, 768, 2304], P(None, 'dp'), may hold values from -7.6293945e-06 to 7.6293945e-06
- qkv_second: float32 [1, 768, 2304], P(None, 'dp'), may hold values from 2.0838335e-14 to 8.335334e-14
- out_master: float32 [1, 768, 768], P(None, 'dp'), may hold values from -0.625 to 0.625
- out_first: float32 [1, 768, 768], P(None, 'dp'), may hold values from -7.6293945e-06 to 7.6293945e-06
- out_second: float32 [1, 768, 768], P(None, 'dp'), may hold values from 2.0838335e-14 to 8.335334e-14
- up_master: float32 [1, 768, 3072], P(None, 'dp'), may hold values from -0.21875 to 0.21875
- up_first: float32 [1, 768, 3072], P(None, 'dp'), may hold values from -7.6293945e-06 to 7.6293945e-06
- up_second: float32 [1, 768, 3072], P(None, 'dp'), may hold values from 2.0838335e-14 to 8.335334e-14
- down_master: float32 [1, 3072, 768], P(None, 'dp'), may hold values from -0.109375 to 0.109375
- down_first: float32 [1, 3072, 768], P(None, 'dp'), may hold values from -7.6293945e-06 to 7.6293945e-06
- down_second: float32 [1, 3072, 768], P(None, 'dp'), may hold values from 2.0838335e-14 to 8.335334e-14
- embed_master: float32 [15360, 768], P(('dp', 'vocab')), may hold values from -0.42 to 0.42
- embed_first: float32 [15360, 768], P(('dp', 'vocab')), may hold values from -3.8146973e-06 to 3.8146973e-06
- embed_second: float32 [15360, 768], P(('dp', 'vocab')), may hold values from 5.209584e-15 to 2.0838335e-14
- vectors_master: float32 [1, 9216], replicated, may hold values from -1 to 1.2
- vectors_first: float32 [1, 9216], replicated, may hold values from -3.0517578e-05 to 3.0517578e-05
- vectors_second: float32 [1, 9216], replicated, may hold values from 3.3341336e-13 to 1.3336535e-12
- extras_master: float32 [406, 768], replicated, may hold values from -4 to 4
- extras_first: float32 [406, 768], replicated, may hold values from -1.5258789e-05 to 1.5258789e-05
- extras_second: float32 [406, 768], replicated, may hold values from 8.335334e-14 to 3.3341336e-13
Outputs:
- loss: float32 [], replicated
- grad_norm: float32 [], replicated
- qkv_new: float32 [1, 768, 2304], P(None, 'dp')
- qkv_first_new: float32 [1, 768, 2304], P(None, 'dp')
- qkv_second_new: float32 [1, 768, 2304], P(None, 'dp')
- out_new: float32 [1, 768, 768], P(None, 'dp')
- out_first_new: float32 [1, 768, 768], P(None, 'dp')
- out_second_new: float32 [1, 768, 768], P(None, 'dp')
- up_new: float32 [1, 768, 3072], P(None, 'dp')
- up_first_new: float32 [1, 768, 3072], P(None, 'dp')
- up_second_new: float32 [1, 768, 3072], P(None, 'dp')
- down_new: float32 [1, 3072, 768], P(None, 'dp')
- down_first_new: float32 [1, 3072, 768], P(None, 'dp')
- down_second_new: float32 [1, 3072, 768], P(None, 'dp')
- embed_new: float32 [15360, 768], P(('dp', 'vocab'))
- embed_first_new: float32 [15360, 768], P(('dp', 'vocab'))
- embed_second_new: float32 [15360, 768], P(('dp', 'vocab'))
- vectors_new: float32 [1, 9216], replicated
- vectors_first_new: float32 [1, 9216], replicated
- vectors_second_new: float32 [1, 9216], replicated
- extras_new: float32 [406, 768], replicated
- extras_first_new: float32 [406, 768], replicated
- extras_second_new: float32 [406, 768], replicated
The draws below stay inside these ranges and needn't reach their ends.
All inputs are finite; a program needn't handle non-finite values. No bound on the sum of `resets` on one device may be relied on, other than what follows from the above.
Results may differ from the reference program's by a relative error of at most 0.006.
Values may be sent and summed in bfloat16 or wider, within the bound.
A program may use at most 256 MiB of HBM per device.

```python
import math
import jax
import jax.numpy as jnp
import numpy as np
from jax import lax

D = 768
HEADS = 12
HD = 64
FF = 3072
MEM = 10
SEG = 364
SEGS = 2
LAYERS = 1
MLM = 112
DOCS = 6
ROWS = 384
ITEMS = 8
VOCAB = 15360
VEC = 9216
EXROWS = 406
NPARAM = 19195392
CNT = 896


def draw_vectors_master(key, part):
    key = jax.random.fold_in(key, 3)
    cols = jnp.arange(VEC)
    gains = (cols >= 3 * D) & (cols < 4 * D) | (cols >= 6 * D + FF) & (cols < 7 * D + FF)
    first_key, second_key = jax.random.split(key)
    spread = jax.random.uniform(first_key, (LAYERS, VEC), jnp.float32, 0.8, 1.2)
    noise = jnp.clip(0.2 * jax.random.normal(second_key, (LAYERS, VEC), jnp.float32), -1.0, 1.0)
    return jnp.where(gains[None, :], spread, noise)


def draw_extras_master(key, part):
    key = jax.random.fold_in(key, 7)
    rows = jnp.arange(EXROWS)[:, None]
    first_key, second_key = jax.random.split(key)
    noise = jax.random.normal(first_key, (EXROWS, D), jnp.float32)
    spread = jax.random.uniform(second_key, (EXROWS, D), jnp.float32, 0.8, 1.2)
    scale = jnp.where(rows < ROWS, 0.07, jnp.where(rows < ROWS + 2 * MEM, 1.0, 0.1))
    values = jnp.clip(noise * scale, -4.0, 4.0)
    return jnp.where(rows == ROWS + 2 * MEM, spread, values)


def set_ends(drawn, own_key, least, top_value):
    place = [jax.random.randint(jax.random.fold_in(own_key, axis), (), 0, length) for axis, length in enumerate(drawn.shape)]
    longest = drawn.shape.index(max(drawn.shape))
    next_to = place[:longest] + [(place[longest] + 1) % drawn.shape[longest]] + place[longest + 1:]
    return drawn.at[tuple(place)].set(least).at[tuple(next_to)].set(top_value)


def levels(key, extent, cuts, low, largest):
    loudness, own = 1.0, jax.random.fold_in(key, 6)
    for axis_at, blocks in cuts:
        draws = jnp.exp(jax.random.uniform(jax.random.fold_in(own, axis_at), (blocks,), jnp.float32, low / len(cuts), largest / len(cuts)))
        loudness = loudness * jnp.repeat(draws, extent[axis_at] // blocks).reshape([-1 if axis == axis_at else 1 for axis in range(len(extent))])
    return loudness


def rank_bounds(amount, slope):
    weights = [(1 << 20) // math.isqrt(grade ** slope) + 1 for grade in range(1, amount + 1)]
    scale = 1 + sum(weights) // (1 << 30)
    return np.cumsum(np.array([max(1, weight // scale) for weight in weights]))


def ranked_ids(stream_key, extent, number_of, skew):
    listing = rank_bounds(number_of, skew)
    pick = jax.random.randint(jax.random.fold_in(stream_key, 1), extent, 0, int(listing[number_of - 1]))
    standing = jnp.searchsorted(jnp.asarray(listing, jnp.int32), pick, side="right")
    return jax.random.permutation(jax.random.fold_in(stream_key, 2), number_of)[standing].astype(jnp.int32)


def length_profile(number_of, total, most, slope):
    weights = [(1 << 20) // math.isqrt(grade ** slope) + 1 for grade in range(2, number_of + 1)]
    rest, holding = total - most - (number_of - 1), [1] * (number_of - 1)
    while rest > 0:
        movable = [i for i in range(number_of - 1) if holding[i] < most]
        pool, budget = sum([weights[i] for i in movable]), rest
        for i in movable:
            more = min(most - holding[i], max(1, budget * weights[i] // pool), rest)
            holding[i] = holding[i] + more
            rest = rest - more
    return np.array([most] + holding)


def uneven(rng, number_of, total, bound, skew):
    if number_of == 2:
        one = jax.random.randint(rng, (), max(1, total - bound), min(bound, total - 1) + 1)
        return jnp.stack([one, total - one])
    tallies = jnp.asarray(length_profile(number_of, total, bound, skew), jnp.int32)
    pairs = (number_of - 1) // 2
    donor, taker = tallies[1:1 + 2 * pairs:2], tallies[2:2 + 2 * pairs:2]
    slack = jnp.minimum(donor - 1, bound - taker)
    shifted = jax.random.randint(jax.random.fold_in(rng, 1), (pairs,), 0, 1 << 20) % (slack + 1)
    tallies = tallies.at[1:1 + 2 * pairs:2].set(donor - shifted).at[2:2 + 2 * pairs:2].set(taker + shifted)
    return tallies[jax.random.permutation(jax.random.fold_in(rng, 2), number_of)]


def normal_values(rng, shape, scale, most, cuts=(), kind=jnp.bfloat16):
    level = levels(rng, shape, cuts, -0.22, 0.18) if cuts else 1.0
    entries = jax.random.normal(rng, shape, jnp.float32) * scale * level
    return jnp.minimum(jnp.maximum(entries, -most), most).astype(kind)


def setup_inputs(seed: int = 0) -> dict:
    arg_keys = jax.random.split(jax.random.key(seed), 28)
    return {
        "ids": set_ends(ranked_ids(arg_keys[0], (ITEMS, SEGS * SEG), VOCAB, 0), jax.random.fold_in(arg_keys[0], 3), 0, VOCAB - 1).astype(jnp.int32),
        "docs": jax.vmap(lambda own: jnp.searchsorted(jnp.cumsum(uneven(own, DOCS, SEGS * SEG, SEGS * SEG // 2, 1)), jnp.arange(SEGS * SEG), side="right"))(jax.random.split(arg_keys[1], ITEMS)).reshape((ITEMS, SEGS * SEG)).astype(jnp.int32),
        "resets": set_ends((jax.random.randint(arg_keys[2], (ITEMS, SEGS - 1), 0, 2) < 1).astype(jnp.int32), jax.random.fold_in(arg_keys[2], 1), 0, 1),
        "mlm_pos": set_ends(jax.random.randint(arg_keys[3], (ITEMS, MLM), 0, SEGS * SEG), jax.random.fold_in(arg_keys[3], 1), 0, (SEGS * SEG) - 1).astype(jnp.int32),
        "mlm_label": set_ends(ranked_ids(arg_keys[4], (ITEMS, MLM), VOCAB, 0), jax.random.fold_in(arg_keys[4], 3), 0, VOCAB - 1).astype(jnp.int32),
        "step": jax.random.randint(arg_keys[5], (1,), 2, 21).astype(jnp.int32),
        "qkv_master": normal_values(arg_keys[6], (LAYERS, D, 3 * D), D ** -0.5, 0.21875, ((1, 8),), jnp.float32),
        "qkv_first": normal_values(arg_keys[7], (LAYERS, D, 3 * D), (0.0022 / NPARAM ** 0.5), 7.62939453125e-06, ((1, 8),), jnp.float32),
        "qkv_second": jnp.clip(jnp.exp(math.log(8.335334104794118e-14) - 1.3862944 * jax.random.uniform(arg_keys[8], (LAYERS, D, 3 * D), jnp.float32) ** levels(arg_keys[8], (LAYERS, D, 3 * D), ((1, 8),), -0.2, 0.2)), 2.0838335261985294e-14, 8.335334104794118e-14),
        "out_master": normal_values(arg_keys[9], (LAYERS, D, D), (D // 8) ** -0.5, 0.625, ((1, 8),), jnp.float32),
        "out_first": normal_values(arg_keys[10], (LAYERS, D, D), (0.0022 / NPARAM ** 0.5), 7.62939453125e-06, ((1, 8),), jnp.float32),
        "out_second": jnp.clip(jnp.exp(math.log(8.335334104794118e-14) - 1.3862944 * jax.random.uniform(arg_keys[11], (LAYERS, D, D), jnp.float32) ** levels(arg_keys[11], (LAYERS, D, D), ((1, 8),), -0.2, 0.2)), 2.0838335261985294e-14, 8.335334104794118e-14),
        "up_master": normal_values(arg_keys[12], (LAYERS, D, FF), D ** -0.5, 0.21875, ((1, 8),), jnp.float32),
        "up_first": normal_values(arg_keys[13], (LAYERS, D, FF), (0.0022 / NPARAM ** 0.5), 7.62939453125e-06, ((1, 8),), jnp.float32),
        "up_second": jnp.clip(jnp.exp(math.log(8.335334104794118e-14) - 1.3862944 * jax.random.uniform(arg_keys[14], (LAYERS, D, FF), jnp.float32) ** levels(arg_keys[14], (LAYERS, D, FF), ((1, 8),), -0.2, 0.2)), 2.0838335261985294e-14, 8.335334104794118e-14),
        "down_master": normal_values(arg_keys[15], (LAYERS, FF, D), FF ** -0.5, 0.109375, ((1, 8),), jnp.float32),
        "down_first": normal_values(arg_keys[16], (LAYERS, FF, D), (0.0022 / NPARAM ** 0.5), 7.62939453125e-06, ((1, 8),), jnp.float32),
        "down_second": jnp.clip(jnp.exp(math.log(8.335334104794118e-14) - 1.3862944 * jax.random.uniform(arg_keys[17], (LAYERS, FF, D), jnp.float32) ** levels(arg_keys[17], (LAYERS, FF, D), ((1, 8),), -0.2, 0.2)), 2.0838335261985294e-14, 8.335334104794118e-14),
        "embed_master": normal_values(arg_keys[18], (VOCAB, D), 0.07, 0.42, ((0, 32),), jnp.float32),
        "embed_first": normal_values(arg_keys[19], (VOCAB, D), (0.0011 / NPARAM ** 0.5), 3.814697265625e-06, ((0, 32),), jnp.float32),
        "embed_second": jnp.clip(jnp.exp(math.log(2.0838335261985294e-14) - 1.3862944 * jax.random.uniform(arg_keys[20], (VOCAB, D), jnp.float32) ** levels(arg_keys[20], (VOCAB, D), ((0, 32),), -0.2, 0.2)), 5.2095838154963235e-15, 2.0838335261985294e-14),
        "vectors_master": draw_vectors_master(jax.random.fold_in(arg_keys[27], 71), 0),
        "vectors_first": normal_values(arg_keys[22], (LAYERS, VEC), (0.0089 / NPARAM ** 0.5), 3.0517578125e-05, (), jnp.float32),
        "vectors_second": jnp.clip(jnp.exp(jax.random.uniform(arg_keys[23], (LAYERS, VEC), jnp.float32, math.log(3.334133641917647e-13), math.log(1.3336534567670588e-12))), 3.334133641917647e-13, 1.3336534567670588e-12),
        "extras_master": draw_extras_master(jax.random.fold_in(arg_keys[27], 71), 0),
        "extras_first": normal_values(arg_keys[25], (EXROWS, D), (0.0044 / NPARAM ** 0.5), 1.52587890625e-05, (), jnp.float32),
        "extras_second": jnp.clip(jnp.exp(jax.random.uniform(arg_keys[26], (EXROWS, D), jnp.float32, math.log(8.335334104794118e-14), math.log(3.334133641917647e-13))), 8.335334104794118e-14, 3.334133641917647e-13),
    }


BETA_ONE = 0.9
BETA_TWO = 0.999
ADAM_EPS = 1e-08
DECAY = 0.01
LN_EPS = 1e-06
CLIP = 0.02
LR_BIG = 0.04
LR_SMALL = 0.5
MASKED = -1000000000.0
HIGH = lax.Precision.HIGHEST

@jax.custom_vjp
def low(v):
    return lax.optimization_barrier(v.astype(jnp.bfloat16)).astype(jnp.float32)

@jax.custom_vjp
def low_back(v):
    return v

def low_keep(v):
    return (low(v), None)

def low_pass(kept, grad):
    return (grad,)

def back_keep(v):
    return (v, None)

def back_low(kept, grad):
    return (low(grad),)
low.defvjp(low_keep, low_pass)
low_back.defvjp(back_keep, back_low)

def layer_norm(values, gain, shift):
    mean = lax.optimization_barrier(jnp.mean(values, axis=-1, keepdims=True))
    centered = values - mean
    var = lax.optimization_barrier(jnp.mean(centered * centered, axis=-1, keepdims=True))
    return centered * lax.rsqrt(var + LN_EPS) * gain + shift

def split_vec(vec):
    widths = [D, D, D, D, D, FF, D, D, D]
    parts = []
    start = 0
    for width in widths:
        parts.append(vec[start:start + width])
        start += width
    return parts

def mask_of(doc_row):
    marks = jnp.full((MEM,), -1, jnp.int32)
    full = jnp.concatenate([marks, doc_row.astype(jnp.int32), marks])
    memory = full < 0
    return (full[:, None] == full[None, :]) | memory[:, None] | memory[None, :]

def ref_layer(hidden, w_qkv, w_out, w_up, w_down, vec, allowed):
    b_q, b_v, b_o, g_one, b_one, b_up, b_down, g_two, b_two = split_vec(vec)
    rows = hidden.shape[0]
    bias = jnp.concatenate([b_q, jnp.zeros_like(b_q), b_v])
    proj = jnp.dot(low(hidden), w_qkv, precision=HIGH) + bias
    proj = low(low_back(proj))
    query = proj[:, :D].reshape(rows, HEADS, HD)
    keyed = proj[:, D:2 * D].reshape(rows, HEADS, HD)
    values = proj[:, 2 * D:].reshape(rows, HEADS, HD)
    scores = jnp.einsum('qhd,khd->hqk', query, keyed, precision=HIGH) * HD ** (-0.5)
    scores = jnp.where(allowed[None], low_back(scores), MASKED)
    probs = low(jax.nn.softmax(scores, axis=-1))
    context = jnp.einsum('hqk,khd->qhd', probs, values, precision=HIGH).reshape(rows, D)
    context = low_back(low(context))
    attended = low_back(jnp.dot(context, w_out, precision=HIGH) + b_o)
    mid = layer_norm(hidden + attended, g_one, b_one)
    upped = low_back(jnp.dot(low(mid), w_up, precision=HIGH) + b_up)
    act = jax.nn.gelu(upped, approximate=False)
    downed = low_back(jnp.dot(low(act), w_down, precision=HIGH) + b_down)
    return layer_norm(mid + downed, g_two, b_two)

def item_loss(params, ids_row, doc_row, reset_row, positions, labels):
    qkv_w, out_w, up_w, down_w, embed_w, vectors, extras = params
    table = low(embed_w)
    pos_rows = extras[:ROWS]
    first_mem = extras[ROWS:ROWS + MEM]
    write_mem = extras[ROWS + MEM:ROWS + 2 * MEM]
    gain_e = extras[ROWS + 2 * MEM]
    bias_e = extras[ROWS + 2 * MEM + 1]
    tokens = low_back(table[ids_row])
    w_qkv, w_out, w_up, w_down = (low(qkv_w), low(out_w), low(up_w), low(down_w))
    memory = first_mem
    finals = []
    for seg in range(SEGS):
        if seg > 0:
            memory = jnp.where(reset_row[seg - 1] > 0, first_mem, memory)
        allowed = mask_of(doc_row[seg * SEG:(seg + 1) * SEG])
        start_x = jnp.concatenate([memory, tokens[seg * SEG:(seg + 1) * SEG], write_mem]) + pos_rows
        hidden = layer_norm(start_x, gain_e, bias_e)
        for lay in range(LAYERS):
            hidden = ref_layer(hidden, w_qkv[lay], w_out[lay], w_up[lay], w_down[lay], vectors[lay], allowed)
        memory = hidden[MEM + SEG:]
        finals.append(hidden[MEM:MEM + SEG])
    chosen = jnp.concatenate(finals)[positions]
    logits = low_back(jnp.dot(low(chosen), table.T, precision=HIGH))
    top = lax.optimization_barrier(jnp.max(logits, axis=-1, keepdims=True))
    lse = top[:, 0] + jnp.log(lax.optimization_barrier(jnp.sum(jnp.exp(logits - top), axis=-1)))
    target = jnp.take_along_axis(logits, labels[:, None].astype(jnp.int32), axis=1)[:, 0]
    return jnp.sum(lse - target) / CNT

def adam(master, first, second, grad, coef, count, rate):
    clipped = grad * coef
    first_new = BETA_ONE * first + (1.0 - BETA_ONE) * clipped
    second_new = BETA_TWO * second + (1.0 - BETA_TWO) * clipped * clipped
    first_hat = first_new / (1.0 - BETA_ONE ** count)
    second_hat = second_new / (1.0 - BETA_TWO ** count)
    master_new = master - rate * (first_hat / (jnp.sqrt(second_hat) + ADAM_EPS) + DECAY * master)
    return (master_new, first_new, second_new)

def reference(ids, docs, resets, mlm_pos, mlm_label, step, qkv_master, qkv_first, qkv_second, out_master, out_first, out_second, up_master, up_first, up_second, down_master, down_first, down_second, embed_master, embed_first, embed_second, vectors_master, vectors_first, vectors_second, extras_master, extras_first, extras_second):
    masters = (qkv_master, out_master, up_master, down_master, embed_master, vectors_master, extras_master)

    def one_item(carry, item):
        total, grads = carry
        loss_item, back = jax.vjp(lambda params: item_loss(params, *item), masters)
        delta = back(jnp.ones_like(loss_item))[0]
        return ((total + loss_item, jax.tree.map(jnp.add, grads, delta)), None)
    zero = jax.tree.map(jnp.zeros_like, masters)
    start = (jnp.zeros((), qkv_master.dtype), zero)
    (loss, grads), _ = lax.scan(one_item, start, (ids, docs, resets, mlm_pos, mlm_label))
    total_sq = jnp.zeros((), qkv_master.dtype)
    for grad in grads:
        total_sq = total_sq + jnp.sum(grad * grad)
    norm = jnp.sqrt(total_sq)
    coef = jnp.minimum(1.0, CLIP / (norm + 1e-06))
    count = step[0].astype(jnp.float32)
    q_new = adam(qkv_master, qkv_first, qkv_second, grads[0], coef, count, LR_BIG)
    o_new = adam(out_master, out_first, out_second, grads[1], coef, count, LR_BIG)
    u_new = adam(up_master, up_first, up_second, grads[2], coef, count, LR_BIG)
    d_new = adam(down_master, down_first, down_second, grads[3], coef, count, LR_BIG)
    e_new = adam(embed_master, embed_first, embed_second, grads[4], coef, count, LR_BIG)
    v_new = adam(vectors_master, vectors_first, vectors_second, grads[5], coef, count, LR_SMALL)
    x_new = adam(extras_master, extras_first, extras_second, grads[6], coef, count, LR_SMALL)
    return (loss, norm, q_new[0], q_new[1], q_new[2], o_new[0], o_new[1], o_new[2], u_new[0], u_new[1], u_new[2], d_new[0], d_new[1], d_new[2], e_new[0], e_new[1], e_new[2], v_new[0], v_new[1], v_new[2], x_new[0], x_new[1], x_new[2])
```

```python
import functools

import jax
import jax.numpy as jnp
from jax import lax
from jax.experimental import pallas as pl
from jax.experimental.pallas import tpu as pltpu
from jax.sharding import PartitionSpec as P

D = 768
HEADS = 12
HD = 64
FF = 3072
MEM = 10
SEG = 364
SEGS = 2
LAYERS = 1
MLM = 112
ROWS = 384


BETA_ONE = 0.9
BETA_TWO = 0.999
ADAM_EPS = 1e-08
DECAY = 0.01
LN_EPS = 1e-06
CLIP = 0.02
LR_BIG = 0.04
LR_SMALL = 0.5
MASKED = -1000000000.0


def squares(arrays):
    total = jnp.zeros((), jnp.float32)
    for values in arrays:
        total = total + jnp.sum(values * values)
    return total


def adam(master, first, second, grad, coef, count, rate):
    clipped = grad * coef
    first_new = BETA_ONE * first + (1.0 - BETA_ONE) * clipped
    second_new = BETA_TWO * second + (1.0 - BETA_TWO) * clipped * clipped
    first_hat = first_new / (1.0 - BETA_ONE**count)
    second_hat = second_new / (1.0 - BETA_TWO**count)
    master_new = master - rate * (first_hat / (jnp.sqrt(second_hat) + ADAM_EPS) + DECAY * master)
    return (master_new, first_new, second_new)


MESH = pl.DeviceIdType.MESH
MLM_PAD = 128
EXT = ROWS + 2 * MEM + 2


class Place:
    def __init__(self, n_dp, n_v):
        self.A, self.Y = n_dp // 2, n_v // 2
        self.d, self.v = lax.axis_index("dp"), lax.axis_index("vocab")
        self.a, self.x = self.d // 2, self.d % 2
        self.y, self.c = self.v // 2, self.v % 2
        self.me = (self.d, self.v)
        self.xp = (self.d + 1 - 2 * self.x, self.v)
        self.cp = (self.d, self.v + 1 - 2 * self.c)

    def from_a(self, k):
        return lax.rem(self.a + self.A - k, self.A)

    def to_a(self, k):
        return lax.rem(self.a + k, self.A)

    def from_y(self, k):
        return lax.rem(self.y + self.Y - k, self.Y)

    def zp(self, k):
        return (self.to_a(k) * 2 + self.x, self.v)

    def yp(self, k):
        return (self.d, lax.rem(self.y + k, self.Y) * 2 + self.c)

    def barrier(self, extra=()):
        sem = pltpu.get_barrier_semaphore()
        partners = [self.zp(k) for k in range(1, self.A)] + [self.xp]
        partners += [self.yp(k) for k in range(1, self.Y)] + [self.cp] + list(extra)
        for partner in partners:
            pl.semaphore_signal(sem, 1, device_id=partner, device_id_type=MESH)
        pl.semaphore_wait(sem, len(partners))


class Copies:
    def __init__(self, me, send_sem, recv_sem):
        self.me, self.send_sem, self.recv_sem, self.started = me, send_sem, recv_sem, []

    def send(self, number, src, dst, partner):
        copy = pltpu.make_async_remote_copy(
            src, dst, self.send_sem.at[number], self.recv_sem.at[number], partner, MESH
        )
        copy.start()
        self.started.append(copy)

    def arrived(self, number, dst):
        pltpu.make_async_remote_copy(
            dst, dst, self.send_sem.at[number], self.recv_sem.at[number], self.me, MESH
        ).wait_recv()

    def finish(self):
        for copy in self.started:
            copy.wait_send()


class Gather:
    def __init__(self, place, copies, base, ref, own=None):
        self.p, self.q, self.base, self.ref, self.own = place, copies, base, ref, own
        A, Y = place.A, place.Y
        self.x0 = base + A - 1
        self.y0 = self.x0 + A
        self.c0 = self.y0 + 2 * A * (Y - 1)
        self.end = self.c0 + 2 * A * Y

    @staticmethod
    def count(n_dp, n_v):
        A, Y = n_dp // 2, n_v // 2
        return A - 1 + A + 2 * A * (Y - 1) + 2 * A * Y

    def at(self, slot, j=0, c=None):
        p = self.p
        k = slot % p.A
        x = p.x if slot < p.A else 1 - p.x
        c = p.c if c is None else c
        return self.ref(p.from_a(k) * 2 + x, p.from_y(j) * 2 + c)

    def spread(self, slot):
        p = self.p
        src = self.at(slot) if (slot or self.own is None) else self.own
        if slot < p.A:
            self.q.send(self.x0 + slot, src, self.at(slot), p.xp)
        for k in range(1, p.Y):
            self.q.send(self.y0 + slot * (p.Y - 1) + k - 1, src, self.at(slot), p.yp(k))
        self.q.send(self.c0 + slot * p.Y, src, self.at(slot), p.cp)

    def start(self):
        p = self.p
        src = self.at(0) if self.own is None else self.own
        for k in range(1, p.A):
            self.q.send(self.base + k - 1, src, self.at(0), p.zp(k))
        self.spread(0)

    def step_a(self):
        for k in range(1, self.p.A):
            self.q.arrived(self.base + k - 1, self.at(k))
            self.spread(k)

    def step_x(self):
        A = self.p.A
        for k in range(A):
            self.q.arrived(self.x0 + k, self.at(A + k))
            self.spread(A + k)

    def step_y(self):
        p = self.p
        for slot in range(2 * p.A):
            for j in range(1, p.Y):
                self.q.arrived(self.y0 + slot * (p.Y - 1) + j - 1, self.at(slot, j))
                self.q.send(self.c0 + slot * p.Y + j, self.at(slot, j), self.at(slot, j), p.cp)

    def step_c(self):
        p = self.p
        for slot in range(2 * p.A):
            for j in range(p.Y):
                self.q.arrived(self.c0 + slot * p.Y + j, self.at(slot, j, 1 - p.c))


def weights_kernel(n_dp, n_v, w_ref, tok_ref, out_ref, tok_out, ss, rs, ls):
    p = Place(n_dp, n_v)
    others = []
    for k in range(1, p.A):
        others.append((p.to_a(k) * 2 + 1 - p.x, p.v))
    p.barrier(others)
    q = Copies(p.me, ss, rs)
    groups = w_ref.shape[0] // n_v
    local = pltpu.make_async_copy(tok_ref.at[p.d], tok_out.at[p.d, p.v], ls.at[0])
    local.start()
    locals_ = [local]
    gathers = []
    base = 0
    for g in range(groups):
        own = pltpu.make_async_copy(
            w_ref.at[g * n_v + p.v], out_ref.at[p.d, g * n_v + p.v], ls.at[1 + g]
        )
        own.start()
        locals_.append(own)
        gather = Gather(
            p,
            q,
            base,
            lambda d, v, g=g: out_ref.at[d, g * n_v + v],
            own=w_ref.at[g * n_v + p.v],
        )
        base = gather.end
        gathers.append(gather)
    for k in range(1, n_dp):
        to = lax.rem(p.d + k, n_dp)
        q.send(base + k - 1, tok_ref.at[to], tok_out.at[p.d, p.v], (to, p.v))
    for gather in gathers:
        gather.start()
    local.wait()
    first = base
    base = base + n_dp - 1

    def relay(slot, src_d):
        for k in range(1, p.Y):
            number = base + slot * (p.Y - 1) + k - 1
            q.send(number, tok_out.at[src_d, p.v], tok_out.at[src_d, p.v], p.yp(k))
        number = base + n_dp * (p.Y - 1) + slot * p.Y
        q.send(number, tok_out.at[src_d, p.v], tok_out.at[src_d, p.v], p.cp)

    relay(0, p.d)
    for k in range(1, n_dp):
        src_d = lax.rem(p.d + n_dp - k, n_dp)
        q.arrived(first + k - 1, tok_out.at[src_d, p.v])
        relay(k, src_d)
    for gather in gathers:
        gather.step_a()
    for gather in gathers:
        gather.step_x()
    for slot in range(n_dp):
        src_d = lax.rem(p.d + n_dp - slot, n_dp)
        for j in range(1, p.Y):
            v = p.from_y(j) * 2 + p.c
            q.arrived(base + slot * (p.Y - 1) + j - 1, tok_out.at[src_d, v])
            number = base + n_dp * (p.Y - 1) + slot * p.Y + j
            q.send(number, tok_out.at[src_d, v], tok_out.at[src_d, v], p.cp)
    for gather in gathers:
        gather.step_y()
    for slot in range(n_dp):
        src_d = lax.rem(p.d + n_dp - slot, n_dp)
        for j in range(p.Y):
            v = p.from_y(j) * 2 + 1 - p.c
            q.arrived(base + n_dp * (p.Y - 1) + slot * p.Y + j, tok_out.at[src_d, v])
    for gather in gathers:
        gather.step_c()
    q.finish()
    for copy in locals_[1:]:
        copy.wait()


def gather_weights(blocks, packed, n_dp, n_v):
    groups = blocks.shape[0] // n_v
    count = groups * Gather.count(n_dp, n_v) + (n_dp - 1) + n_dp * (n_v // 2 - 1) + n_dp * (n_v // 2)
    return pl.pallas_call(
        functools.partial(weights_kernel, n_dp, n_v),
        out_shape=(
            jax.ShapeDtypeStruct((n_dp,) + blocks.shape, blocks.dtype),
            jax.ShapeDtypeStruct((n_dp, n_v) + packed.shape[1:], packed.dtype),
        ),
        in_specs=[pl.BlockSpec(memory_space=pl.ANY)] * 2,
        out_specs=(pl.BlockSpec(memory_space=pl.ANY),) * 2,
        scratch_shapes=[
            pltpu.SemaphoreType.DMA((count,)),
            pltpu.SemaphoreType.DMA((count,)),
            pltpu.SemaphoreType.DMA((1 + groups,)),
        ],
        compiler_params=pltpu.CompilerParams(collective_id=0, has_side_effects=True),
    )(blocks, packed)


def chosen_kernel(n_dp, n_v, in_ref, out_ref, ss, rs):
    p = Place(n_dp, n_v)
    p.barrier()
    q = Copies(p.me, ss, rs)
    gather = Gather(p, q, 0, lambda d, v: out_ref.at[d, v])
    out_ref[p.d, p.v] = in_ref[p.v]
    gather.start()
    gather.step_a()
    gather.step_x()
    gather.step_y()
    gather.step_c()
    q.finish()


def gather_chosen(chosen, n_dp, n_v):
    count = Gather.count(n_dp, n_v)
    return pl.pallas_call(
        functools.partial(chosen_kernel, n_dp, n_v),
        out_shape=jax.ShapeDtypeStruct((n_dp,) + chosen.shape, chosen.dtype),
        in_specs=[pl.BlockSpec(memory_space=pltpu.VMEM)],
        out_specs=pl.BlockSpec(memory_space=pltpu.VMEM),
        scratch_shapes=[pltpu.SemaphoreType.DMA((count,)), pltpu.SemaphoreType.DMA((count,))],
        compiler_params=pltpu.CompilerParams(collective_id=1, has_side_effects=True),
    )(chosen)


def d_chosen_kernel(n_dp, n_v, in_ref, out_ref, bc, by, bx, bz, pc, py, px, ss, rs):
    f32, bf = jnp.float32, jnp.bfloat16
    p = Place(n_dp, n_v)
    p.barrier()
    q = Copies(p.me, ss, rs)
    A, Y = p.A, p.Y
    q.send(0, in_ref.at[:, :, :, 1 - p.c], bc, p.cp)
    q.arrived(0, bc)
    pc[...] = (in_ref[:, :, :, p.c].astype(f32) + bc[...].astype(f32)).astype(bf)
    n = 1
    for k in range(1, Y):
        q.send(n + k - 1, pc.at[:, :, lax.rem(p.y + k, Y)], by.at[k - 1], p.yp(k))
    total = pc[:, :, p.y].astype(f32)
    for k in range(1, Y):
        q.arrived(n + k - 1, by.at[k - 1])
        total = total + by[k - 1].astype(f32)
    py[...] = total.astype(bf)
    n = n + Y - 1
    q.send(n, py.at[:, 1 - p.x], bx, p.xp)
    q.arrived(n, bx)
    n = n + 1
    px[...] = (py[:, p.x].astype(f32) + bx[...].astype(f32)).astype(bf)
    for k in range(1, A):
        q.send(n + k - 1, px.at[p.to_a(k)], bz.at[k - 1], p.zp(k))
    total = px[p.a].astype(f32)
    for k in range(1, A):
        q.arrived(n + k - 1, bz.at[k - 1])
        total = total + bz[k - 1].astype(f32)
    n = n + A - 1
    out_ref[p.v] = total.astype(bf)
    for k in range(1, Y):
        q.send(n + k - 1, out_ref.at[p.v], out_ref.at[p.v], p.yp(k))
    q.send(n + Y - 1, out_ref.at[p.v], out_ref.at[p.v], p.cp)
    for j in range(1, Y):
        v = p.from_y(j) * 2 + p.c
        q.arrived(n + j - 1, out_ref.at[v])
        q.send(n + Y - 1 + j, out_ref.at[v], out_ref.at[v], p.cp)
    for j in range(Y):
        v = p.from_y(j) * 2 + 1 - p.c
        q.arrived(n + Y - 1 + j, out_ref.at[v])
    q.finish()


def reduce_d_chosen(partial, n_dp, n_v):
    A, _, Y, _, rows, width = partial.shape
    count = 1 + (Y - 1) + 1 + (A - 1) + (Y - 1) + Y
    kind = partial.dtype
    return pl.pallas_call(
        functools.partial(d_chosen_kernel, n_dp, n_v),
        out_shape=jax.ShapeDtypeStruct((n_v, rows, width), kind),
        in_specs=[pl.BlockSpec(memory_space=pltpu.VMEM)],
        out_specs=pl.BlockSpec(memory_space=pltpu.VMEM),
        scratch_shapes=[
            pltpu.VMEM((A, 2, Y, rows, width), kind),
            pltpu.VMEM((Y - 1, A, 2, rows, width), kind),
            pltpu.VMEM((A, rows, width), kind),
            pltpu.VMEM((A - 1, rows, width), kind),
            pltpu.VMEM((A, 2, Y, rows, width), kind),
            pltpu.VMEM((A, 2, rows, width), kind),
            pltpu.VMEM((A, rows, width), kind),
            pltpu.SemaphoreType.DMA((count,)),
            pltpu.SemaphoreType.DMA((count,)),
        ],
        compiler_params=pltpu.CompilerParams(
            collective_id=2, has_side_effects=True, vmem_limit_bytes=56 << 20
        ),
    )(partial)


def grads_kernel(n_dp, n_v, g_ref, e_ref, t_ref, g_out, e_out, t_out, bx, px, bz, ebx, epx, ebz, ss, rs, ls):
    f32, bf = jnp.float32, jnp.bfloat16
    p = Place(n_dp, n_v)
    A, Y = p.A, p.Y
    p.barrier([(p.to_a(k) * 2 + 1 - p.x, p.v) for k in range(1, A)])
    q = Copies(p.me, ss, rs)
    groups = g_ref.shape[0]
    n = 0
    for g in range(groups):
        q.send(n + g, g_ref.at[g, :, 1 - p.x], bx.at[g], p.xp)
    x0 = n
    n = n + groups
    q.send(n, e_ref.at[:, 1 - p.x], ebx, p.xp)
    ex0 = n
    n = n + 1
    t0 = n
    for k in range(1, n_dp):
        to = lax.rem(p.d + k, n_dp)
        q.send(t0 + k - 1, t_ref.at[to], t_out.at[p.d], (to, p.v))
    n = n + n_dp - 1
    local = pltpu.make_async_copy(t_ref.at[p.d], t_out.at[p.d], ls)
    local.start()
    z0 = n
    n = n + groups * (A - 1)
    ez0 = n
    n = n + A - 1
    for g in range(groups):
        q.arrived(x0 + g, bx.at[g])
        for k in range(1, A + 1):
            to = p.to_a(k)
            px[g, to] = (g_ref[g, to, p.x].astype(f32) + bx[g, to].astype(f32)).astype(bf)
            if k < A:
                q.send(z0 + g * (A - 1) + k - 1, px.at[g, to], bz.at[g, k - 1], p.zp(k))
    q.arrived(ex0, ebx)
    epx[...] = (e_ref[:, p.x].astype(f32) + ebx[...].astype(f32)).astype(bf)
    for k in range(1, A):
        q.send(ez0 + k - 1, epx.at[p.to_a(k)], ebz.at[k - 1], p.zp(k))
    total = epx[p.a].astype(f32)
    for k in range(1, A):
        q.arrived(ez0 + k - 1, ebz.at[k - 1])
        total = total + ebz[k - 1].astype(f32)
    e_out[p.d, p.v] = total.astype(bf)
    small = Gather(p, q, n, lambda d, v: e_out.at[d, v])
    n = small.end
    small.start()
    y0 = n
    n = n + groups * (Y - 1)
    c0 = n
    for g in range(groups):
        total = px[g, p.a].astype(f32)
        for k in range(1, A):
            q.arrived(z0 + g * (A - 1) + k - 1, bz.at[g, k - 1])
            total = total + bz[g, k - 1].astype(f32)
        mine = g_out.at[g * n_v + p.v]
        g_out[g * n_v + p.v] = total.astype(bf)
        for k in range(1, Y):
            q.send(y0 + g * (Y - 1) + k - 1, mine, mine, p.yp(k))
        q.send(c0 + g * Y, mine, mine, p.cp)
    small.step_a()
    small.step_x()
    for g in range(groups):
        for j in range(1, Y):
            piece = g_out.at[g * n_v + p.from_y(j) * 2 + p.c]
            q.arrived(y0 + g * (Y - 1) + j - 1, piece)
            q.send(c0 + g * Y + j, piece, piece, p.cp)
    small.step_y()
    for g in range(groups):
        for j in range(Y):
            q.arrived(c0 + g * Y + j, g_out.at[g * n_v + p.from_y(j) * 2 + 1 - p.c])
    small.step_c()
    for k in range(1, n_dp):
        q.arrived(t0 + k - 1, t_out.at[lax.rem(p.d + n_dp - k, n_dp)])
    q.finish()
    local.wait()


def reduce_grads(grads, extras, tokens, n_dp, n_v):
    A, Y = n_dp // 2, n_v // 2
    groups, _, _, rows, width = grads.shape
    e_rows, e_width = extras.shape[2:]
    kind = grads.dtype
    count = groups * (1 + A - 1 + Y - 1 + Y) + 1 + (n_dp - 1) + (A - 1) + Gather.count(n_dp, n_v)
    vmem = pl.BlockSpec(memory_space=pltpu.VMEM)
    return pl.pallas_call(
        functools.partial(grads_kernel, n_dp, n_v),
        out_shape=(
            jax.ShapeDtypeStruct((groups * n_v, rows, width), kind),
            jax.ShapeDtypeStruct((n_dp, n_v, e_rows, e_width), kind),
            jax.ShapeDtypeStruct(tokens.shape, tokens.dtype),
        ),
        in_specs=[vmem, vmem, vmem],
        out_specs=(vmem, vmem, vmem),
        scratch_shapes=[
            pltpu.VMEM((groups, A, rows, width), kind),
            pltpu.VMEM((groups, A, rows, width), kind),
            pltpu.VMEM((groups, A - 1, rows, width), kind),
            pltpu.VMEM((A, e_rows, e_width), kind),
            pltpu.VMEM((A, e_rows, e_width), kind),
            pltpu.VMEM((A - 1, e_rows, e_width), kind),
            pltpu.SemaphoreType.DMA((count,)),
            pltpu.SemaphoreType.DMA((count,)),
            pltpu.SemaphoreType.DMA,
        ],
        compiler_params=pltpu.CompilerParams(
            collective_id=3, has_side_effects=True, vmem_limit_bytes=56 << 20
        ),
    )(grads, extras, tokens)


def lane_mean(values):
    return jnp.sum(values, axis=-1, keepdims=True) * (1.0 / D)


def norm_parts(values):
    centered = values - lane_mean(values)
    rate = lax.rsqrt(lane_mean(centered * centered) + LN_EPS)
    return centered * rate, rate


def norm_back(values, grad, gain):
    unit, rate = norm_parts(values)
    scaled = grad * gain
    d_values = rate * (scaled - lane_mean(scaled) - unit * lane_mean(scaled * unit))
    return (
        d_values,
        jnp.sum(grad * unit, axis=0, keepdims=True),
        jnp.sum(grad, axis=0, keepdims=True),
    )


def dot(left, right, dims=((1,), (0,))):
    return lax.dot_general(left, right, (dims, ((), ())), preferred_element_type=jnp.float32)


NT = ((1,), (1,))
TN = ((0,), (0,))


def allowed_mask(row_ref, col_ref, seg):
    row, col = row_ref[seg], col_ref[seg]
    return (row == col) | (row < 0) | (col < 0)


def forward_kernel(
    w_hbm, tok_ref, row_ref, col_ref, reset_ref, vec_ref, ext_ref, pos_ref,
    x_o, hc_o, proj_o, p_o, one_o, mid_o, gp_o, act_o, two_o, chosen_o,
    w, x, hc, proj, probs, one, mid, gp, act, two, mask, hid, final, sem_w, sem_o,
):
    bf, f32 = jnp.bfloat16, jnp.float32
    loads = [pltpu.make_async_copy(w_hbm.at[:, b], w.at[b], sem_w.at[b]) for b in range(12)]
    for load in loads:
        load.start()
    waited = set()

    def weight(b):
        if b not in waited:
            loads[b].wait()
            waited.add(b)
        return w[b].reshape(D, D)

    stores = []

    def store(src, dst):
        copy = pltpu.make_async_copy(src, dst, sem_o.at[len(stores)])
        copy.start()
        stores.append(copy)

    vec = [vec_ref[k : k + 1, :] for k in range(12)]
    b_q, b_v, b_o, g_one, b_one = vec[:5]
    b_up, b_down, g_two, b_two = vec[5:9], vec[9], vec[10], vec[11]
    gain_e, bias_e = ext_ref[404:405, :], ext_ref[405:406, :]
    lane = lax.broadcasted_iota(jnp.int32, (1, 2 * HD), 1)
    low_half = lane < HD
    for seg in range(SEGS):
        rows = pl.ds(seg * ROWS, ROWS)
        x[seg] = tok_ref[rows, :].astype(f32) + ext_ref[:ROWS, :]
        x[seg, ROWS - MEM :, :] += ext_ref[ROWS + MEM : ROWS + 2 * MEM, :]
        first = ext_ref[ROWS : ROWS + MEM, :]
        if seg == 0:
            x[seg, :MEM, :] += first
        else:
            x[seg, :MEM, :] += jnp.where(reset_ref[seg - 1] > 0, first, hid[ROWS - MEM :, :])
        store(x.at[seg], x_o.at[seg])
        mask[...] = allowed_mask(row_ref, col_ref, seg).astype(f32)
        unit, _ = norm_parts(x[seg])
        h = unit * gain_e + bias_e
        hid[...] = h
        h_low = h.astype(bf)
        hc[0, rows, :] = h_low
        for k, bias in ((0, b_q), (1, None), (2, b_v)):
            made = dot(h_low, weight(k))
            proj[k, rows, :] = (made if bias is None else made + bias).astype(bf)
        store(hc.at[0, rows], hc_o.at[0, rows])
        store(proj.at[:, rows], proj_o.at[:, rows])
        for pair in range(HEADS // 2):
            cols = pl.ds(pair * 2 * HD, 2 * HD)
            query, keyed, value = (proj[k, rows, cols] for k in range(3))
            query = query * jnp.asarray(HD ** (-0.5), bf)
            parts = []
            for side in range(2):
                keep = low_half if side == 0 else ~low_half
                scores = dot(jnp.where(keep, query, jnp.zeros_like(query)), keyed, NT)
                scores = jnp.where(mask[...] > 0, scores, MASKED)
                expd = jnp.exp(scores - jnp.max(scores, axis=-1, keepdims=True))
                p_low = (expd * (1.0 / jnp.sum(expd, axis=-1, keepdims=True))).astype(bf)
                probs[seg, pair * 2 + side] = p_low
                parts.append(dot(p_low, value))
            hc[1, rows, cols] = jnp.where(low_half, parts[0], parts[1]).astype(bf)
        store(probs.at[seg], p_o.at[seg])
        store(hc.at[1, rows], hc_o.at[1, rows])
        sum_one = hid[...] + (dot(hc[1, rows, :], weight(3)) + b_o)
        one[seg] = sum_one
        store(one.at[seg], one_o.at[seg])
        unit, _ = norm_parts(sum_one)
        mid_now = unit * g_one + b_one
        mid_low = mid_now.astype(bf)
        mid[rows, :] = mid_low
        store(mid.at[rows], mid_o.at[rows])
        for j in range(4):
            up = dot(mid_low, weight(4 + j)) + b_up[j]
            half = 0.5 * (1.0 + lax.erf(up * 0.7071067811865476))
            gp[j, rows, :] = (half + up * jnp.exp(-0.5 * up * up) * 0.3989422804014327).astype(bf)
            act[j, rows, :] = (up * half).astype(bf)
        store(gp.at[:, rows], gp_o.at[:, rows])
        store(act.at[:, rows], act_o.at[:, rows])
        total = mid_now + b_down
        for j in range(4):
            total = total + dot(act[j, rows, :], weight(8 + j))
        two[seg] = total
        store(two.at[seg], two_o.at[seg])
        unit, _ = norm_parts(total)
        h = unit * g_two + b_two
        hid[...] = h
        final[rows, :] = h.astype(bf)
    at = lax.broadcasted_iota(jnp.int32, (MLM_PAD, SEGS * ROWS), 1)
    chosen_o[...] = dot((at == pos_ref[...]).astype(bf), final[...]).astype(bf)
    for copy in stores:
        copy.wait()


def run_forward(w_all, tok, marks, reset, vec, ext, pos):
    f32, bf = jnp.float32, jnp.bfloat16
    n = SEGS * ROWS
    saved = [
        ((SEGS, ROWS, D), f32),
        ((2, n, D), bf),
        ((3, n, D), bf),
        ((SEGS, HEADS, ROWS, ROWS), bf),
        ((SEGS, ROWS, D), f32),
        ((n, D), bf),
        ((4, n, D), bf),
        ((4, n, D), bf),
        ((SEGS, ROWS, D), f32),
    ]
    hbm = pl.BlockSpec(memory_space=pl.ANY)
    vmem = pl.BlockSpec(memory_space=pltpu.VMEM)
    return pl.pallas_call(
        forward_kernel,
        out_shape=[jax.ShapeDtypeStruct(s, k) for s, k in saved]
        + [jax.ShapeDtypeStruct((MLM_PAD, D), bf)],
        in_specs=[hbm, vmem, vmem, vmem, pl.BlockSpec(memory_space=pltpu.SMEM), vmem, vmem, vmem],
        out_specs=[hbm] * len(saved) + [vmem],
        scratch_shapes=[pltpu.VMEM((12, w_all.shape[0]) + w_all.shape[2:], bf)]
        + [pltpu.VMEM(s, k) for s, k in saved]
        + [
            pltpu.VMEM((ROWS, ROWS), f32),
            pltpu.VMEM((ROWS, D), f32),
            pltpu.VMEM((n, D), bf),
            pltpu.SemaphoreType.DMA((12,)),
            pltpu.SemaphoreType.DMA((SEGS * 10,)),
        ],
        compiler_params=pltpu.CompilerParams(vmem_limit_bytes=60 << 20),
    )(w_all, tok, marks[:, None, :], marks[:, :, None], reset, vec, ext, pos[:, None])


def backward_kernel(
    cuts,
    w_hbm, x_i, hc_i, proj_i, p_i, one_i, mid_i, gp_i, act_i, two_i,
    dch_ref, reset_ref, vec_ref, ext_ref, pos_ref, give_ref, slot_ref, v_ref,
    share_o, small_o, dpack_o, dtok,
    w, x, hc, right, probs, one, mid, rup, act, two, rdown, grad, dmem, sem_w, sem_i,
):
    bf, f32 = jnp.bfloat16, jnp.float32
    small_o[...] = jnp.zeros_like(small_o)
    loads = {}
    state = {"n": 0}

    def load(name, src, dst):
        copy = pltpu.make_async_copy(src, dst, sem_i.at[state["n"]])
        state["n"] += 1
        copy.start()
        loads[name] = copy

    def need(name):
        if name in loads:
            loads.pop(name).wait()

    wl = [pltpu.make_async_copy(w_hbm.at[:, b], w.at[b], sem_w.at[b]) for b in range(12)]
    waited = set()

    def weight(b):
        if b not in waited:
            wl[b].wait()
            waited.add(b)
        return w[b].reshape(D, D)

    order = list(reversed(range(SEGS)))
    for i, seg in enumerate(order):
        rows = pl.ds(seg * ROWS, ROWS)
        load(("two", seg), two_i.at[seg], two.at[seg])
        if i == 0:
            for b in range(8, 12):
                wl[b].start()
        load(("gp", seg), gp_i.at[:, rows], rup.at[:, rows])
        if i == 0:
            for b in range(4, 8):
                wl[b].start()
        load(("one", seg), one_i.at[seg], one.at[seg])
        if i == 0:
            wl[3].start()
            load(("p", seg), p_i.at[seg], probs)
        load(("proj", seg), proj_i.at[:, rows], right.at[pl.ds(0, 3), rows])
        if i == 0:
            for b in range(3):
                wl[b].start()
        load(("x", seg), x_i.at[seg], x.at[seg])
    load("hc", hc_i, hc)
    load("mid", mid_i, mid)
    load("act", act_i, act)

    vec = [vec_ref[k : k + 1, :] for k in range(12)]
    g_one, g_two, gain_e = vec[3], vec[10], ext_ref[404:405, :]
    lane = lax.broadcasted_iota(jnp.int32, (1, 2 * HD), 1)
    low_half = lane < HD
    at = lax.broadcasted_iota(jnp.int32, (MLM_PAD, SEGS * ROWS), 1)
    at_pos = (at == pos_ref[...]).astype(bf)
    v0 = EXT

    def add_row(k, value):
        small_o[v0 + k : v0 + k + 1, :] += value

    def sums(values):
        return jnp.sum(values.astype(f32), axis=0, keepdims=True)

    for i, seg in enumerate(order):
        rows = pl.ds(seg * ROWS, ROWS)
        grad[...] = dot(at_pos[:, seg * ROWS : (seg + 1) * ROWS], dch_ref[...], TN)
        if i > 0:
            grad[ROWS - MEM :, :] += dmem[...]
        need(("two", seg))
        d_two, d_gain, d_shift = norm_back(two[seg], grad[...], g_two)
        add_row(10, d_gain)
        add_row(11, d_shift)
        r_down = d_two.astype(bf)
        rdown[rows, :] = r_down
        add_row(9, sums(r_down))
        need(("gp", seg))
        for j in range(4):
            r_up = (rup[j, rows, :].astype(f32) * dot(r_down, weight(8 + j), NT)).astype(bf)
            rup[j, rows, :] = r_up
            add_row(5 + j, sums(r_up))
        for j in range(4):
            d_two = d_two + dot(rup[j, rows, :], weight(4 + j), NT)
        need(("one", seg))
        d_one, d_gain, d_shift = norm_back(one[seg], d_two, g_one)
        add_row(3, d_gain)
        add_row(4, d_shift)
        grad[...] = d_one
        r_att = d_one.astype(bf)
        right[3, rows, :] = r_att
        add_row(2, sums(r_att))
        d_ctx = dot(r_att, weight(3), NT).astype(bf)
        need(("p", seg))
        need(("proj", seg))
        for pair in range(HEADS // 2):
            cols = pl.ds(pair * 2 * HD, 2 * HD)
            query, keyed, value = (right[k, rows, cols] for k in range(3))
            d_out = d_ctx[:, pair * 2 * HD : (pair + 1) * 2 * HD]
            made = []
            for side in range(2):
                keep = low_half if side == 0 else ~low_half
                p_low = probs[pair * 2 + side]
                p_now = p_low.astype(f32)
                d_p = dot(jnp.where(keep, d_out, jnp.zeros_like(d_out)), value, NT)
                weighted = p_now * d_p
                d_s = weighted - p_now * jnp.sum(weighted, axis=-1, keepdims=True)
                d_s = d_s.astype(bf)
                made.append((dot(d_s, keyed), dot(d_s, query, TN), dot(p_low, d_out, TN)))
            for k, scale in ((0, HD ** (-0.5)), (1, HD ** (-0.5)), (2, 1.0)):
                both = jnp.where(low_half, made[0][k], made[1][k]) * scale
                right[k, rows, cols] = both.astype(bf)
        if i + 1 < SEGS:
            load(("p", order[i + 1]), p_i.at[order[i + 1]], probs)
        d_h = grad[...]
        for k in range(3):
            d_h = d_h + dot(right[k, rows, :], weight(k), NT)
        add_row(0, sums(right[0, rows, :]))
        add_row(1, sums(right[2, rows, :]))
        need(("x", seg))
        d_x, d_gain, d_shift = norm_back(x[seg], d_h, gain_e)
        grad[...] = d_x
        dtok[rows, :] = d_x.astype(bf)
        small_o[:ROWS, :] += d_x
        small_o[ROWS + MEM : ROWS + 2 * MEM, :] += grad[ROWS - MEM :, :]
        small_o[404:405, :] += d_gain
        small_o[405:406, :] += d_shift
        d_read = grad[:MEM, :]
        if seg > 0:
            back = reset_ref[seg - 1] > 0
            small_o[ROWS : ROWS + MEM, :] += jnp.where(back, d_read, 0.0)
            dmem[...] = jnp.where(back, 0.0, d_read)
        else:
            small_o[ROWS : ROWS + MEM, :] += d_read
    dpack_o[...] = dot((give_ref[...] == slot_ref[...]).astype(bf), dtok[...]).astype(bf)
    need("hc")
    need("mid")
    need("act")
    v = v_ref[0]
    width = D // cuts
    block, cut = v // cuts, v % cuts
    cols = pl.ds(pl.multiple_of(cut * width, 128), width)
    share_o[0] = dot(hc[block // 3], right[block, :, cols], TN).astype(bf)
    share_o[1] = dot(mid[...], rup[block, :, cols], TN).astype(bf)
    share_o[2] = dot(act[block], rdown[:, cols], TN).astype(bf)


def run_backward(
    w_all, saved, d_chosen, reset, vec, ext, pos, give, slot, v_idx, cuts, small_rows
):
    f32, bf = jnp.float32, jnp.bfloat16
    n = SEGS * ROWS
    hbm = pl.BlockSpec(memory_space=pl.ANY)
    vmem = pl.BlockSpec(memory_space=pltpu.VMEM)
    smem = pl.BlockSpec(memory_space=pltpu.SMEM)
    return pl.pallas_call(
        functools.partial(backward_kernel, cuts),
        out_shape=[
            jax.ShapeDtypeStruct((3, D, D // cuts), bf),
            jax.ShapeDtypeStruct((small_rows, D), f32),
            jax.ShapeDtypeStruct((give.shape[0], D), bf),
            jax.ShapeDtypeStruct((n, D), bf),
        ],
        in_specs=[hbm] * 10 + [vmem, smem, vmem, vmem, vmem, vmem, vmem, smem],
        out_specs=[vmem] * 4,
        scratch_shapes=[
            pltpu.VMEM((12, w_all.shape[0]) + w_all.shape[2:], bf),
            pltpu.VMEM((SEGS, ROWS, D), f32),
            pltpu.VMEM((2, n, D), bf),
            pltpu.VMEM((4, n, D), bf),
            pltpu.VMEM((HEADS, ROWS, ROWS), bf),
            pltpu.VMEM((SEGS, ROWS, D), f32),
            pltpu.VMEM((n, D), bf),
            pltpu.VMEM((4, n, D), bf),
            pltpu.VMEM((4, n, D), bf),
            pltpu.VMEM((SEGS, ROWS, D), f32),
            pltpu.VMEM((n, D), bf),
            pltpu.VMEM((ROWS, D), f32),
            pltpu.VMEM((MEM, D), f32),
            pltpu.SemaphoreType.DMA((12,)),
            pltpu.SemaphoreType.DMA((SEGS * 6 + 4,)),
        ],
        compiler_params=pltpu.CompilerParams(vmem_limit_bytes=61 << 20),
    )(
        w_all, *saved, d_chosen, reset, vec, ext, pos[:, None],
        give[:, None], slot[None, :], v_idx,
    )


def ceil_to(value, unit):
    return -(-value // unit) * unit


def per_device(
    ids,
    docs,
    resets,
    mlm_pos,
    mlm_label,
    step,
    qkv_master,
    qkv_first,
    qkv_second,
    out_master,
    out_first,
    out_second,
    up_master,
    up_first,
    up_second,
    down_master,
    down_first,
    down_second,
    embed_master,
    embed_first,
    embed_second,
    vectors_master,
    vectors_first,
    vectors_second,
    extras_master,
    extras_first,
    extras_second,
):
    f32, bf = jnp.float32, jnp.bfloat16
    n_dp = lax.axis_size("dp")
    n_v = lax.axis_size("vocab")
    d_idx = lax.axis_index("dp")
    v_idx = lax.axis_index("vocab")
    count = n_dp * MLM
    own_rows = embed_master.shape[0]
    tokens_n = SEGS * SEG
    rb = qkv_master.shape[1]
    cuts = max(1, n_v // 4)
    width = D // cuts
    groups = 12 * cuts // n_v

    def to_blocks(qkv, out, up, down):
        full = jnp.concatenate(
            [
                qkv[0].reshape(rb, 3, D).transpose(1, 0, 2),
                out,
                up[0].reshape(rb, n_dp, 4, rb).transpose(2, 0, 1, 3).reshape(4, rb, D),
                down[0].reshape(4, rb, D),
            ]
        )
        return full.reshape(12, rb, cuts, width).transpose(0, 2, 1, 3).reshape(12 * cuts, rb, width)

    def from_blocks(blocks):
        full = blocks.reshape(12, cuts, rb, width).transpose(0, 2, 1, 3).reshape(12, rb, D)
        return (
            full[:3].transpose(1, 0, 2).reshape(1, rb, 3 * D),
            full[3:4],
            full[4:8].reshape(4, rb, n_dp, rb).transpose(1, 2, 0, 3).reshape(1, rb, FF),
            full[8:].reshape(1, 4 * rb, D),
        )

    ids_all = lax.all_gather(ids, "dp", axis=0, tiled=True)
    labels = jnp.full((n_dp, MLM_PAD - MLM), -1, jnp.int32)
    labels_all = jnp.concatenate([lax.all_gather(mlm_label, "dp", axis=0, tiled=True), labels], axis=1)
    holder = ids_all // own_rows
    local_row = ids_all % own_rows
    order = jnp.arange(tokens_n, dtype=jnp.int32)
    same = (holder[:, :, None] == holder[:, None, :]) & (order[None, :, None] > order[None, None, :])
    rank = jnp.sum(same.astype(jnp.int32), axis=-1)
    cap = ceil_to(2 * tokens_n // (n_dp * n_v) + 2, 16)
    overflow = jnp.max(rank) >= cap
    mine = holder == d_idx * n_v + v_idx
    places = jnp.arange(cap, dtype=jnp.int32)
    hit = mine[:, None, :] & (rank[:, None, :] == places[None, :, None])
    packed_row = jnp.sum(jnp.where(hit, local_row[:, None, :] + 1, 0), axis=-1) - 1
    own_slots = jnp.arange(own_rows, dtype=jnp.int32)
    pick = (packed_row.reshape(n_dp * cap)[:, None] == own_slots[None, :]).astype(bf)
    table = embed_master.astype(bf)
    packed = jnp.dot(pick, table, preferred_element_type=f32).astype(bf).reshape(n_dp, cap, D)

    blocks = to_blocks(
        qkv_master.astype(bf), out_master.astype(bf), up_master.astype(bf), down_master.astype(bf)
    )
    w_all, tok_all = gather_weights(blocks, packed, n_dp, n_v)
    if cuts > 1 or rb % 16:
        w_all = w_all.reshape(n_dp, 12, cuts, rb, width).transpose(1, 0, 3, 2, 4).reshape(1, 12, D, D)

    my_holder = holder[d_idx]
    my_rank = rank[d_idx]
    slot = (my_holder * cap + my_rank).reshape(SEGS, SEG)
    slot = jnp.pad(slot, ((0, 0), (MEM, MEM)), constant_values=-1).reshape(SEGS * ROWS)

    def packed_tokens(_):
        slots = jnp.arange(n_dp * n_v * cap, dtype=jnp.int32)
        onehot = (slot[:, None] == slots[None, :]).astype(bf)
        rows = tok_all.reshape(n_dp * n_v * cap, D)
        return jnp.dot(onehot, rows, preferred_element_type=f32).astype(bf)

    def whole_tokens(_):
        whole = lax.all_gather(table, "dp", axis=0, tiled=True)
        at = jnp.arange(n_dp * own_rows, dtype=jnp.int32)
        row_ids = (at // own_rows * n_v + v_idx) * own_rows + at % own_rows
        onehot = (ids[0][:, None] == row_ids[None, :]).astype(bf)
        rows = lax.psum(jnp.dot(onehot, whole, preferred_element_type=f32).astype(bf), "vocab")
        return jnp.pad(rows.reshape(SEGS, SEG, D), ((0, 0), (MEM, MEM), (0, 0))).reshape(-1, D)

    tokens = lax.cond(overflow, whole_tokens, packed_tokens, 0)
    marks = jnp.pad(docs.reshape(SEGS, SEG), ((0, 0), (MEM, MEM)), constant_values=-1)
    vec = vectors_master[0].reshape(12, D)
    b_up = vec[5:9].reshape(n_dp, 4, rb).transpose(1, 0, 2).reshape(4, D)
    vec = jnp.concatenate([vec[:5], b_up, vec[9:]])
    positions = mlm_pos[0]
    at_rows = positions // SEG * ROWS + MEM + positions % SEG
    at_rows = jnp.concatenate([at_rows, jnp.full((MLM_PAD - MLM,), -1, jnp.int32)])
    *saved, chosen = run_forward(w_all, tokens, marks, resets[0], vec, extras_master, at_rows)
    rows_v = MLM_PAD // n_v
    chosen_all = gather_chosen(chosen.reshape(n_v, rows_v, D), n_dp, n_v).reshape(n_dp * MLM_PAD, D)

    logits = jnp.einsum("md,vd->mv", chosen_all, table, preferred_element_type=f32)
    row_ids = (d_idx * n_v + v_idx) * own_rows + own_slots
    label_flat = labels_all.reshape(n_dp * MLM_PAD)
    hits = label_flat[:, None] == row_ids[None, :]
    top = lax.pmax(jnp.max(logits, axis=-1), ("dp", "vocab"))
    sums, target = lax.psum(
        (
            jnp.sum(jnp.exp(logits - top[:, None]), axis=-1),
            jnp.sum(jnp.where(hits, logits, 0.0), axis=-1),
        ),
        ("dp", "vocab"),
    )
    lse = top + jnp.log(sums)
    real = label_flat >= 0
    loss = jnp.sum(jnp.where(real, lse - target, 0.0)) / count
    d_logits = ((jnp.exp(logits - lse[:, None]) - hits.astype(f32)) / count).astype(bf)
    d_table = jnp.einsum("mv,md->vd", d_logits, chosen_all, preferred_element_type=f32)
    d_part = jnp.dot(d_logits, table, preferred_element_type=f32).astype(bf)
    d_chosen = reduce_d_chosen(
        d_part.reshape(n_dp // 2, 2, n_v // 2, 2, rows_v, D), n_dp, n_v
    ).reshape(MLM_PAD, D)
    small_rows = EXT + 12
    e_rows = ceil_to(-(-small_rows // (n_dp * n_v)), 16)
    at = jnp.arange(n_dp * cap, dtype=jnp.int32)
    give = (at // cap * n_v + v_idx) * cap + at % cap
    shares, small, d_packed, d_tok = run_backward(
        w_all,
        saved,
        d_chosen,
        resets[0],
        vec,
        extras_master,
        at_rows,
        give,
        slot,
        v_idx[None],
        cuts,
        ceil_to(small_rows, 8),
    )
    shares = shares.reshape(groups, n_dp // 2, 2, rb, width)
    small = jnp.pad(small.astype(bf), ((0, e_rows * n_dp * n_v - small.shape[0]), (0, 0)))
    small = small.reshape(n_dp // 2, 2, n_v, e_rows, D)
    small = lax.dynamic_index_in_dim(small, v_idx, axis=2, keepdims=False)
    d_packed = d_packed.reshape(n_dp, cap, D)
    g_blocks, small_all, d_packed_all = reduce_grads(shares, small, d_packed, n_dp, n_v)

    def packed_d_table(_):
        return jnp.einsum(
            "tv,td->vd", pick, d_packed_all.reshape(n_dp * cap, D), preferred_element_type=f32
        )

    def whole_d_table(_):
        d_all = d_tok.reshape(SEGS, ROWS, D)[:, MEM : MEM + SEG].reshape(tokens_n, D)
        d_all = lax.all_gather(d_all, "dp", axis=0, tiled=True)
        onehot = (ids_all.reshape(-1)[:, None] == row_ids[None, :]).astype(bf)
        return jnp.einsum("tv,td->vd", onehot, d_all, preferred_element_type=f32)

    s_table = d_table + lax.cond(overflow, whole_d_table, packed_d_table, 0)
    s_qkv, s_out, s_up, s_down = from_blocks(g_blocks.astype(f32))
    small_all = small_all.astype(f32).reshape(n_dp * n_v * e_rows, D)
    g_ext = small_all[: extras_master.shape[0]]
    g_vec = small_all[EXT:small_rows]
    g_up_bias = g_vec[5:9].reshape(4, n_dp, rb).transpose(1, 0, 2).reshape(4, D)
    g_vec = jnp.concatenate([g_vec[:5], g_up_bias, g_vec[9:]]).reshape(vectors_master.shape)

    layer_sq = jnp.where(v_idx == 0, squares((s_qkv, s_out, s_up, s_down)), 0.0)
    small_sq = jnp.where((v_idx == 0) & (d_idx == 0), squares((g_vec, g_ext)), 0.0)
    norm = jnp.sqrt(lax.psum(layer_sq + squares((s_table,)) + small_sq, ("dp", "vocab")))
    coef = jnp.minimum(1.0, CLIP / (norm + 1e-06))
    step_count = step[0].astype(f32)
    results = [loss, norm]
    for master, first, second, grad, rate in (
        (qkv_master, qkv_first, qkv_second, s_qkv, LR_BIG),
        (out_master, out_first, out_second, s_out, LR_BIG),
        (up_master, up_first, up_second, s_up, LR_BIG),
        (down_master, down_first, down_second, s_down, LR_BIG),
        (embed_master, embed_first, embed_second, s_table, LR_BIG),
        (vectors_master, vectors_first, vectors_second, g_vec, LR_SMALL),
        (extras_master, extras_first, extras_second, g_ext, LR_SMALL),
    ):
        results.extend(adam(master, first, second, grad, coef, step_count, rate))
    return tuple(results)


def solution(mesh):
    in_specs = (
        P("dp", None),
        P("dp", None),
        P("dp", None),
        P("dp", None),
        P("dp", None),
        P(),
        P(None, "dp", None),
        P(None, "dp", None),
        P(None, "dp", None),
        P(None, "dp", None),
        P(None, "dp", None),
        P(None, "dp", None),
        P(None, "dp", None),
        P(None, "dp", None),
        P(None, "dp", None),
        P(None, "dp", None),
        P(None, "dp", None),
        P(None, "dp", None),
        P(("dp", "vocab"), None),
        P(("dp", "vocab"), None),
        P(("dp", "vocab"), None),
        P(),
        P(),
        P(),
        P(),
        P(),
        P(),
    )
    out_specs = (
        P(),
        P(),
        P(None, "dp", None),
        P(None, "dp", None),
        P(None, "dp", None),
        P(None, "dp", None),
        P(None, "dp", None),
        P(None, "dp", None),
        P(None, "dp", None),
        P(None, "dp", None),
        P(None, "dp", None),
        P(None, "dp", None),
        P(None, "dp", None),
        P(None, "dp", None),
        P(("dp", "vocab"), None),
        P(("dp", "vocab"), None),
        P(("dp", "vocab"), None),
        P(),
        P(),
        P(),
        P(),
        P(),
        P(),
    )
    return jax.shard_map(
        per_device, mesh=mesh, in_specs=in_specs, out_specs=out_specs, check_vma=False
    )
```

```python
import functools

import jax
import jax.numpy as jnp
from jax import lax
from jax.experimental import pallas as pl
from jax.experimental.pallas import tpu as pltpu
from jax.sharding import PartitionSpec as P

D = 768
HEADS = 12
HD = 64
FF = 3072
MEM = 10
SEG = 364
SEGS = 2
LAYERS = 1
MLM = 112
ROWS = 384


BETA_ONE = 0.9
BETA_TWO = 0.999
ADAM_EPS = 1e-08
DECAY = 0.01
LN_EPS = 1e-06
CLIP = 0.02
LR_BIG = 0.04
LR_SMALL = 0.5
MASKED = -1000000000.0


MESH = pl.DeviceIdType.MESH
MLM_PAD = 128
EXT = ROWS + 2 * MEM + 2


class Place:
    def __init__(self, n_dp, n_v):
        self.A, self.Y = n_dp // 2, n_v // 2
        self.d, self.v = lax.axis_index("dp"), lax.axis_index("vocab")
        self.a, self.x = self.d // 2, self.d % 2
        self.y, self.c = self.v // 2, self.v % 2
        self.me = (self.d, self.v)
        self.xp = (self.d + 1 - 2 * self.x, self.v)
        self.cp = (self.d, self.v + 1 - 2 * self.c)

    def from_a(self, k):
        return lax.rem(self.a + self.A - k, self.A)

    def to_a(self, k):
        return lax.rem(self.a + k, self.A)

    def from_y(self, k):
        return lax.rem(self.y + self.Y - k, self.Y)

    def zp(self, k):
        return (self.to_a(k) * 2 + self.x, self.v)

    def yp(self, k):
        return (self.d, lax.rem(self.y + k, self.Y) * 2 + self.c)

    def barrier(self, extra=()):
        sem = pltpu.get_barrier_semaphore()
        partners = [self.zp(k) for k in range(1, self.A)] + [self.xp]
        partners += [self.yp(k) for k in range(1, self.Y)] + [self.cp] + list(extra)
        for partner in partners:
            pl.semaphore_signal(sem, 1, device_id=partner, device_id_type=MESH)
        pl.semaphore_wait(sem, len(partners))


class Copies:
    def __init__(self, me, send_sem, recv_sem):
        self.me, self.send_sem, self.recv_sem, self.started = me, send_sem, recv_sem, []

    def send(self, number, src, dst, partner):
        copy = pltpu.make_async_remote_copy(
            src, dst, self.send_sem.at[number], self.recv_sem.at[number], partner, MESH
        )
        copy.start()
        self.started.append(copy)

    def arrived(self, number, dst):
        pltpu.make_async_remote_copy(
            dst, dst, self.send_sem.at[number], self.recv_sem.at[number], self.me, MESH
        ).wait_recv()

    def finish(self):
        for copy in self.started:
            copy.wait_send()


class Gather:
    def __init__(self, place, copies, base, ref, own=None, shared=False):
        self.p, self.q, self.base, self.ref, self.own = place, copies, base, ref, own
        self.least = 1 if shared else 0
        A, Y = place.A, place.Y
        self.x0 = base + A - 1
        self.y0 = self.x0 + A
        self.c0 = self.y0 + 2 * A * (Y - 1)
        self.end = self.c0 + 2 * A * Y

    @staticmethod
    def count(n_dp, n_v):
        A, Y = n_dp // 2, n_v // 2
        return A - 1 + A + 2 * A * (Y - 1) + 2 * A * Y

    def at(self, slot, j=0, c=None):
        p = self.p
        k = slot % p.A
        x = p.x if slot < p.A else 1 - p.x
        c = p.c if c is None else c
        return self.ref(p.from_a(k) * 2 + x, p.from_y(j) * 2 + c)

    def spread(self, slot):
        p = self.p
        src = self.at(slot) if (slot or self.own is None) else self.own
        if slot < p.A:
            self.q.send(self.x0 + slot, src, self.at(slot), p.xp)
        if slot < self.least:
            return
        for k in range(1, p.Y):
            self.q.send(self.y0 + slot * (p.Y - 1) + k - 1, src, self.at(slot), p.yp(k))
        self.q.send(self.c0 + slot * p.Y, src, self.at(slot), p.cp)

    def start(self):
        p = self.p
        src = self.at(0) if self.own is None else self.own
        for k in range(1, p.A):
            self.q.send(self.base + k - 1, src, self.at(0), p.zp(k))
        self.spread(0)

    def step_a(self):
        for k in range(1, self.p.A):
            self.q.arrived(self.base + k - 1, self.at(k))
            self.spread(k)

    def step_x(self):
        A = self.p.A
        for k in range(A):
            self.q.arrived(self.x0 + k, self.at(A + k))
            self.spread(A + k)

    def step_y(self):
        p = self.p
        for slot in range(self.least, 2 * p.A):
            for j in range(1, p.Y):
                self.q.arrived(self.y0 + slot * (p.Y - 1) + j - 1, self.at(slot, j))
                self.q.send(self.c0 + slot * p.Y + j, self.at(slot, j), self.at(slot, j), p.cp)

    def step_c(self):
        p = self.p
        for slot in range(self.least, 2 * p.A):
            for j in range(p.Y):
                self.q.arrived(self.c0 + slot * p.Y + j, self.at(slot, j, 1 - p.c))


def weights_kernel(n_dp, n_v, w_ref, tok_ref, out_ref, tok_out, ss, rs, ls):
    p = Place(n_dp, n_v)
    others = []
    for k in range(1, p.A):
        others.append((p.to_a(k) * 2 + 1 - p.x, p.v))
    p.barrier(others)
    q = Copies(p.me, ss, rs)
    groups = w_ref.shape[0] // n_v
    local = pltpu.make_async_copy(tok_ref.at[p.d], tok_out.at[p.d, p.v], ls.at[0])
    local.start()
    locals_ = [local]
    gathers = []
    base = 0
    own = pltpu.make_async_copy(w_ref, out_ref.at[p.d], ls.at[1])
    own.start()
    locals_.append(own)
    for g in range(groups):
        gather = Gather(
            p,
            q,
            base,
            lambda d, v, g=g: out_ref.at[d, g * n_v + v],
            own=w_ref.at[g * n_v + p.v],
            shared=True,
        )
        base = gather.end
        gathers.append(gather)
    for k in range(1, n_dp):
        to = lax.rem(p.d + k, n_dp)
        q.send(base + k - 1, tok_ref.at[to], tok_out.at[p.d, p.v], (to, p.v))
    for gather in gathers:
        gather.start()
    local.wait()
    first = base
    base = base + n_dp - 1

    def relay(slot, src_d):
        for k in range(1, p.Y):
            number = base + slot * (p.Y - 1) + k - 1
            q.send(number, tok_out.at[src_d, p.v], tok_out.at[src_d, p.v], p.yp(k))
        number = base + n_dp * (p.Y - 1) + slot * p.Y
        q.send(number, tok_out.at[src_d, p.v], tok_out.at[src_d, p.v], p.cp)

    relay(0, p.d)
    for k in range(1, n_dp):
        src_d = lax.rem(p.d + n_dp - k, n_dp)
        q.arrived(first + k - 1, tok_out.at[src_d, p.v])
        relay(k, src_d)
    for gather in gathers:
        gather.step_a()
    for gather in gathers:
        gather.step_x()
    for slot in range(n_dp):
        src_d = lax.rem(p.d + n_dp - slot, n_dp)
        for j in range(1, p.Y):
            v = p.from_y(j) * 2 + p.c
            q.arrived(base + slot * (p.Y - 1) + j - 1, tok_out.at[src_d, v])
            number = base + n_dp * (p.Y - 1) + slot * p.Y + j
            q.send(number, tok_out.at[src_d, v], tok_out.at[src_d, v], p.cp)
    for gather in gathers:
        gather.step_y()
    for slot in range(n_dp):
        src_d = lax.rem(p.d + n_dp - slot, n_dp)
        for j in range(p.Y):
            v = p.from_y(j) * 2 + 1 - p.c
            q.arrived(base + n_dp * (p.Y - 1) + slot * p.Y + j, tok_out.at[src_d, v])
    for gather in gathers:
        gather.step_c()
    q.finish()
    for copy in locals_[1:]:
        copy.wait()


def gather_weights(blocks, packed, n_dp, n_v):
    groups = blocks.shape[0] // n_v
    count = groups * Gather.count(n_dp, n_v) + (n_dp - 1) + n_dp * (n_v // 2 - 1) + n_dp * (n_v // 2)
    return pl.pallas_call(
        functools.partial(weights_kernel, n_dp, n_v),
        out_shape=(
            jax.ShapeDtypeStruct((n_dp,) + blocks.shape, blocks.dtype),
            jax.ShapeDtypeStruct((n_dp, n_v) + packed.shape[1:], packed.dtype),
        ),
        in_specs=[pl.BlockSpec(memory_space=pl.ANY)] * 2,
        out_specs=(pl.BlockSpec(memory_space=pl.ANY),) * 2,
        scratch_shapes=[
            pltpu.SemaphoreType.DMA((count,)),
            pltpu.SemaphoreType.DMA((count,)),
            pltpu.SemaphoreType.DMA((2,)),
        ],
        compiler_params=pltpu.CompilerParams(collective_id=0, has_side_effects=True),
    )(blocks, packed)


def ints_kernel(n_dp, in_ref, out_ref, ss, rs):
    d, v = lax.axis_index("dp"), lax.axis_index("vocab")
    sem = pltpu.get_barrier_semaphore()
    for k in range(1, n_dp):
        partner = (lax.rem(d + k, n_dp), v)
        pl.semaphore_signal(sem, 1, device_id=partner, device_id_type=MESH)
    pl.semaphore_wait(sem, n_dp - 1)
    q = Copies((d, v), ss, rs)
    for k in range(1, n_dp):
        q.send(k - 1, in_ref, out_ref.at[d], (lax.rem(d + k, n_dp), v))
    out_ref[d] = in_ref[...]
    for k in range(1, n_dp):
        q.arrived(k - 1, out_ref.at[lax.rem(d + n_dp - k, n_dp)])
    q.finish()


def gather_ints(values, n_dp):
    return pl.pallas_call(
        functools.partial(ints_kernel, n_dp),
        out_shape=jax.ShapeDtypeStruct((n_dp,) + values.shape, values.dtype),
        in_specs=[pl.BlockSpec(memory_space=pltpu.VMEM)],
        out_specs=pl.BlockSpec(memory_space=pltpu.VMEM),
        scratch_shapes=[pltpu.SemaphoreType.DMA((n_dp - 1,)), pltpu.SemaphoreType.DMA((n_dp - 1,))],
        compiler_params=pltpu.CompilerParams(collective_id=1, has_side_effects=True),
    )(values)


def head_kernel(
    n_dp, n_v, ch_ref, table_ref, label_ref, tags_ref,
    out_ref, dtab_ref, loss_ref,
    al, logits, dlog, st, sd, sv, lse_s, part, bc, by, bx, bz, pc, py, px, ss, rs,
):
    f32, bf = jnp.float32, jnp.bfloat16
    p = Place(n_dp, n_v)
    A, Y = p.A, p.Y
    count = n_dp * MLM
    others = [(lax.rem(p.d + k, n_dp), p.v) for k in range(1, n_dp)]
    partners = [(p.d, lax.rem(p.v + k, n_v)) for k in range(1, n_v)]
    sem = pltpu.get_barrier_semaphore()
    for partner in others + partners:
        pl.semaphore_signal(sem, 1, device_id=partner, device_id_type=MESH)
    pl.semaphore_wait(sem, n_dp - 1 + n_v - 1)
    q = Copies(p.me, ss, rs)
    gather = Gather(p, q, 0, lambda d, v: al.at[d, v], shared=True)
    al[p.d] = ch_ref[...]
    gather.start()
    gather.step_a()
    gather.step_x()
    gather.step_y()
    gather.step_c()
    n = gather.end
    rows_v, total_m = ch_ref.shape[1], n_dp * MLM_PAD
    chosen = al[...].reshape(total_m, D)
    logits[...] = dot(table_ref[...], chosen, NT)
    rows = table_ref.shape[0]
    row_ids = (p.d * n_v + p.v) * rows + lax.broadcasted_iota(jnp.int32, (rows, 1), 0)
    hits = row_ids == label_ref[...]
    top = jnp.max(logits[...], axis=0, keepdims=True)
    stats = (
        top,
        jnp.sum(jnp.exp(logits[...] - top), axis=0, keepdims=True),
        jnp.sum(jnp.where(hits, logits[...], 0.0), axis=0, keepdims=True),
    )
    tall = total_m // 128
    for k, values in enumerate(stats):
        for r in range(tall):
            st[k * tall + r : k * tall + r + 1, :] = values[:, r * 128 : (r + 1) * 128]

    def merged(ref, amount):
        tops = [ref[k, :tall, :] for k in range(amount)]
        best = functools.reduce(jnp.maximum, tops)
        parts = [ref[k, tall : 2 * tall, :] * jnp.exp(tops[k] - best) for k in range(amount)]
        return best, sum(parts[1:], parts[0]), sum(ref[k, 2 * tall :, :] for k in range(amount))

    sd[p.d] = st[...]
    for k in range(1, n_dp):
        q.send(n + k - 1, st, sd.at[p.d], others[k - 1])
    for k in range(1, n_dp):
        q.arrived(n + k - 1, sd.at[lax.rem(p.d + n_dp - k, n_dp)])
    n = n + n_dp - 1
    for k, values in enumerate(merged(sd, n_dp)):
        sv[p.v, k * tall : (k + 1) * tall, :] = values
    for k in range(1, n_v):
        q.send(n + k - 1, sv.at[p.v], sv.at[p.v], partners[k - 1])
    for k in range(1, n_v):
        q.arrived(n + k - 1, sv.at[lax.rem(p.v + n_v - k, n_v)])
    n = n + n_v - 1
    best, total, target = merged(sv, n_v)
    lse = best + jnp.log(total)
    lse_s[...] = lse
    lost = jnp.sum(jnp.where(tags_ref[...] >= 0, lse - target, 0.0), axis=1, keepdims=True)
    lost = jnp.sum(lost, axis=0, keepdims=True) / count
    loss_ref[...] = jnp.broadcast_to(lost, loss_ref.shape)
    lse_row = jnp.concatenate([lse_s[r : r + 1, :] for r in range(tall)], axis=1)
    d_log = (jnp.exp(logits[...] - lse_row) - hits.astype(f32)) * (1.0 / count)
    dlog[...] = d_log.astype(bf)
    made = dot(dlog[...], table_ref[...], TN).astype(bf)
    part[...] = made.reshape(A, 2, Y, 2, rows_v, D)
    q.send(n, part.at[:, :, :, 1 - p.c], bc, p.cp)
    dtab_ref[...] = dot(dlog[...], chosen)
    q.arrived(n, bc)
    pc[...] = (part[:, :, :, p.c].astype(f32) + bc[...].astype(f32)).astype(bf)
    n = n + 1
    for k in range(1, Y):
        q.send(n + k - 1, pc.at[:, :, lax.rem(p.y + k, Y)], by.at[k - 1], p.yp(k))
    total = pc[:, :, p.y].astype(f32)
    for k in range(1, Y):
        q.arrived(n + k - 1, by.at[k - 1])
        total = total + by[k - 1].astype(f32)
    py[...] = total.astype(bf)
    n = n + Y - 1
    q.send(n, py.at[:, 1 - p.x], bx, p.xp)
    q.arrived(n, bx)
    n = n + 1
    px[...] = (py[:, p.x].astype(f32) + bx[...].astype(f32)).astype(bf)
    for k in range(1, A):
        q.send(n + k - 1, px.at[p.to_a(k)], bz.at[k - 1], p.zp(k))
    total = px[p.a].astype(f32)
    for k in range(1, A):
        q.arrived(n + k - 1, bz.at[k - 1])
        total = total + bz[k - 1].astype(f32)
    n = n + A - 1
    out_ref[p.v] = total.astype(bf)
    for k in range(1, n_v):
        q.send(n + k - 1, out_ref.at[p.v], out_ref.at[p.v], partners[k - 1])
    for k in range(1, n_v):
        q.arrived(n + k - 1, out_ref.at[lax.rem(p.v + n_v - k, n_v)])
    q.finish()


def run_head(chosen, table, labels, n_dp, n_v):
    f32, kind = jnp.float32, chosen.dtype
    A, Y = n_dp // 2, n_v // 2
    _, rows_v, width = chosen.shape
    rows, total_m = table.shape[0], n_dp * MLM_PAD
    tall = total_m // 128
    count = Gather.count(n_dp, n_v) + n_dp - 1 + n_v - 1 + 1 + Y - 1 + 1 + A - 1 + n_v - 1
    vmem = pl.BlockSpec(memory_space=pltpu.VMEM)
    return pl.pallas_call(
        functools.partial(head_kernel, n_dp, n_v),
        out_shape=[
            jax.ShapeDtypeStruct(chosen.shape, kind),
            jax.ShapeDtypeStruct(table.shape, f32),
            jax.ShapeDtypeStruct((8, 128), f32),
        ],
        in_specs=[vmem] * 4,
        out_specs=[vmem] * 3,
        scratch_shapes=[
            pltpu.VMEM((n_dp,) + chosen.shape, kind),
            pltpu.VMEM((rows, total_m), f32),
            pltpu.VMEM((rows, total_m), kind),
            pltpu.VMEM((3 * tall, 128), f32),
            pltpu.VMEM((n_dp, 3 * tall, 128), f32),
            pltpu.VMEM((n_v, 3 * tall, 128), f32),
            pltpu.VMEM((tall, 128), f32),
            pltpu.VMEM((A, 2, Y, 2, rows_v, width), kind),
            pltpu.VMEM((A, 2, Y, rows_v, width), kind),
            pltpu.VMEM((Y - 1, A, 2, rows_v, width), kind),
            pltpu.VMEM((A, rows_v, width), kind),
            pltpu.VMEM((A - 1, rows_v, width), kind),
            pltpu.VMEM((A, 2, Y, rows_v, width), kind),
            pltpu.VMEM((A, 2, rows_v, width), kind),
            pltpu.VMEM((A, rows_v, width), kind),
            pltpu.SemaphoreType.DMA((count,)),
            pltpu.SemaphoreType.DMA((count,)),
        ],
        compiler_params=pltpu.CompilerParams(
            collective_id=2, has_side_effects=True, vmem_limit_bytes=56 << 20
        ),
    )(chosen, table, labels.reshape(1, total_m), labels.reshape(tall, 128))


def norm_kernel(n_dp, n_v, layer_ref, small_ref, table_ref, out_ref, sd, sv, ss, rs):
    f32 = jnp.float32
    d, v = lax.axis_index("dp"), lax.axis_index("vocab")
    others = [(lax.rem(d + k, n_dp), v) for k in range(1, n_dp)]
    partners = [(d, lax.rem(v + k, n_v)) for k in range(1, n_v)]
    sem = pltpu.get_barrier_semaphore()
    for partner in others + partners:
        pl.semaphore_signal(sem, 1, device_id=partner, device_id_type=MESH)

    def square(values):
        values = values.astype(f32)
        values = values * values
        while values.ndim > 2:
            values = jnp.sum(values, axis=0)
        return jnp.sum(jnp.sum(values, axis=0, keepdims=True), axis=1, keepdims=True)

    total = square(table_ref[...])
    total = total + jnp.where(v == 0, square(layer_ref[...]), 0.0)
    total = total + jnp.where((v == 0) & (d == 0), square(small_ref[...]), 0.0)
    sd[d] = jnp.broadcast_to(total, sd.shape[1:])
    pl.semaphore_wait(sem, n_dp - 1 + n_v - 1)
    q = Copies((d, v), ss, rs)
    for k in range(1, n_dp):
        q.send(k - 1, sd.at[d], sd.at[d], others[k - 1])
    for k in range(1, n_dp):
        q.arrived(k - 1, sd.at[lax.rem(d + n_dp - k, n_dp)])
    sv[v] = jnp.sum(sd[...], axis=0)
    for k in range(1, n_v):
        q.send(n_dp + k - 2, sv.at[v], sv.at[v], partners[k - 1])
    for k in range(1, n_v):
        q.arrived(n_dp + k - 2, sv.at[lax.rem(v + n_v - k, n_v)])
    out_ref[...] = jnp.sum(sv[...], axis=0)
    q.finish()


def run_norm(layer, small, table, n_dp, n_v):
    f32 = jnp.float32
    vmem = pl.BlockSpec(memory_space=pltpu.VMEM)
    count = n_dp + n_v - 2
    return pl.pallas_call(
        functools.partial(norm_kernel, n_dp, n_v),
        out_shape=jax.ShapeDtypeStruct((8, 128), f32),
        in_specs=[vmem] * 3,
        out_specs=vmem,
        scratch_shapes=[
            pltpu.VMEM((n_dp, 8, 128), f32),
            pltpu.VMEM((n_v, 8, 128), f32),
            pltpu.SemaphoreType.DMA((count,)),
            pltpu.SemaphoreType.DMA((count,)),
        ],
        compiler_params=pltpu.CompilerParams(
            collective_id=4, has_side_effects=True, vmem_limit_bytes=40 << 20
        ),
    )(layer, small, table)


def adam_kernel(rates, scal_ref, *refs):
    n = len(rates)
    grads, ins, outs = refs[:n], refs[n : 4 * n], refs[4 * n : 7 * n]
    bufs, sem_i, sem_o = refs[7 * n : 10 * n], refs[10 * n], refs[10 * n + 1]
    loads = [pltpu.make_async_copy(ins[k], bufs[k], sem_i.at[k]) for k in range(3 * n)]
    for copy in loads:
        copy.start()
    coef, one_hat, two_hat = scal_ref[0], scal_ref[1], scal_ref[2]
    stores = []
    for i, rate in enumerate(rates):
        master, first, second = bufs[3 * i : 3 * i + 3]
        for copy in loads[3 * i : 3 * i + 3]:
            copy.wait()
        rows = master.shape[0]
        chunk = 32 if rows % 32 == 0 else rows

        def update(c, _, i=i, rate=rate, master=master, first=first, second=second, chunk=chunk):
            at = pl.ds(c * chunk if isinstance(c, int) else pl.multiple_of(c * chunk, chunk), chunk)
            g = grads[i][at, :].astype(jnp.float32) * coef
            one = BETA_ONE * first[at, :] + (1.0 - BETA_ONE) * g
            two = BETA_TWO * second[at, :] + (1.0 - BETA_TWO) * g * g
            old = master[at, :]
            move = one * one_hat / (jnp.sqrt(two * two_hat) + ADAM_EPS) + DECAY * old
            first[at, :] = one
            second[at, :] = two
            master[at, :] = old - rate * move
            return 0

        if rows == chunk:
            update(0, 0)
        else:
            lax.fori_loop(0, rows // chunk, update, 0)
        for k in range(3 * i, 3 * i + 3):
            copy = pltpu.make_async_copy(bufs[k], outs[k], sem_o.at[k])
            copy.start()
            stores.append(copy)
    for copy in stores:
        copy.wait()


def run_adam(scalars, grads, states, rates):
    hbm = pl.BlockSpec(memory_space=pl.ANY)
    n = len(rates)
    flat = [array for state in states for array in state]
    return pl.pallas_call(
        functools.partial(adam_kernel, rates),
        out_shape=[jax.ShapeDtypeStruct(a.shape, a.dtype) for a in flat],
        in_specs=[pl.BlockSpec(memory_space=pltpu.SMEM)]
        + [pl.BlockSpec(memory_space=pltpu.VMEM)] * n
        + [hbm] * (3 * n),
        out_specs=[hbm] * (3 * n),
        scratch_shapes=[pltpu.VMEM(a.shape, a.dtype) for a in flat]
        + [pltpu.SemaphoreType.DMA((3 * n,)), pltpu.SemaphoreType.DMA((3 * n,))],
        compiler_params=pltpu.CompilerParams(vmem_limit_bytes=56 << 20),
    )(scalars, *grads, *flat)


def grads_kernel(n_dp, n_v, g_ref, e_ref, t_ref, g_out, e_out, t_out, bx, px, bz, ebx, epx, ebz, ss, rs, ls):
    f32, bf = jnp.float32, jnp.bfloat16
    p = Place(n_dp, n_v)
    A, Y = p.A, p.Y
    p.barrier([(p.to_a(k) * 2 + 1 - p.x, p.v) for k in range(1, A)])
    q = Copies(p.me, ss, rs)
    groups = g_ref.shape[0]
    n = 0
    for g in range(groups):
        q.send(n + g, g_ref.at[g, :, 1 - p.x], bx.at[g], p.xp)
    x0 = n
    n = n + groups
    q.send(n, e_ref.at[:, 1 - p.x], ebx, p.xp)
    ex0 = n
    n = n + 1
    t0 = n
    for k in range(1, n_dp):
        to = lax.rem(p.d + k, n_dp)
        q.send(t0 + k - 1, t_ref.at[to], t_out.at[p.d], (to, p.v))
    n = n + n_dp - 1
    local = pltpu.make_async_copy(t_ref.at[p.d], t_out.at[p.d], ls)
    local.start()
    z0 = n
    n = n + groups * (A - 1)
    ez0 = n
    n = n + A - 1
    for g in range(groups):
        q.arrived(x0 + g, bx.at[g])
        for k in range(1, A + 1):
            to = p.to_a(k)
            px[g, to] = (g_ref[g, to, p.x].astype(f32) + bx[g, to].astype(f32)).astype(bf)
            if k < A:
                q.send(z0 + g * (A - 1) + k - 1, px.at[g, to], bz.at[g, k - 1], p.zp(k))
    q.arrived(ex0, ebx)
    epx[...] = (e_ref[:, p.x].astype(f32) + ebx[...].astype(f32)).astype(bf)
    for k in range(1, A):
        q.send(ez0 + k - 1, epx.at[p.to_a(k)], ebz.at[k - 1], p.zp(k))
    total = epx[p.a].astype(f32)
    for k in range(1, A):
        q.arrived(ez0 + k - 1, ebz.at[k - 1])
        total = total + ebz[k - 1].astype(f32)
    e_out[p.d, p.v] = total.astype(bf)
    small = Gather(p, q, n, lambda d, v: e_out.at[d, v])
    n = small.end
    small.start()
    y0 = n
    n = n + groups * (Y - 1)
    c0 = n
    for g in range(groups):
        total = px[g, p.a].astype(f32)
        for k in range(1, A):
            q.arrived(z0 + g * (A - 1) + k - 1, bz.at[g, k - 1])
            total = total + bz[g, k - 1].astype(f32)
        mine = g_out.at[g * n_v + p.v]
        g_out[g * n_v + p.v] = total.astype(bf)
        for k in range(1, Y):
            q.send(y0 + g * (Y - 1) + k - 1, mine, mine, p.yp(k))
        q.send(c0 + g * Y, mine, mine, p.cp)
    small.step_a()
    small.step_x()
    for g in range(groups):
        for j in range(1, Y):
            piece = g_out.at[g * n_v + p.from_y(j) * 2 + p.c]
            q.arrived(y0 + g * (Y - 1) + j - 1, piece)
            q.send(c0 + g * Y + j, piece, piece, p.cp)
    small.step_y()
    for g in range(groups):
        for j in range(Y):
            q.arrived(c0 + g * Y + j, g_out.at[g * n_v + p.from_y(j) * 2 + 1 - p.c])
    small.step_c()
    for k in range(1, n_dp):
        q.arrived(t0 + k - 1, t_out.at[lax.rem(p.d + n_dp - k, n_dp)])
    q.finish()
    local.wait()


def reduce_grads(grads, extras, tokens, n_dp, n_v):
    A, Y = n_dp // 2, n_v // 2
    groups, _, _, rows, width = grads.shape
    e_rows, e_width = extras.shape[2:]
    kind = grads.dtype
    count = groups * (1 + A - 1 + Y - 1 + Y) + 1 + (n_dp - 1) + (A - 1) + Gather.count(n_dp, n_v)
    vmem = pl.BlockSpec(memory_space=pltpu.VMEM)
    return pl.pallas_call(
        functools.partial(grads_kernel, n_dp, n_v),
        out_shape=(
            jax.ShapeDtypeStruct((groups * n_v, rows, width), kind),
            jax.ShapeDtypeStruct((n_dp, n_v, e_rows, e_width), kind),
            jax.ShapeDtypeStruct(tokens.shape, tokens.dtype),
        ),
        in_specs=[vmem, vmem, vmem],
        out_specs=(vmem, vmem, vmem),
        scratch_shapes=[
            pltpu.VMEM((groups, A, rows, width), kind),
            pltpu.VMEM((groups, A, rows, width), kind),
            pltpu.VMEM((groups, A - 1, rows, width), kind),
            pltpu.VMEM((A, e_rows, e_width), kind),
            pltpu.VMEM((A, e_rows, e_width), kind),
            pltpu.VMEM((A - 1, e_rows, e_width), kind),
            pltpu.SemaphoreType.DMA((count,)),
            pltpu.SemaphoreType.DMA((count,)),
            pltpu.SemaphoreType.DMA,
        ],
        compiler_params=pltpu.CompilerParams(
            collective_id=3, has_side_effects=True, vmem_limit_bytes=56 << 20
        ),
    )(grads, extras, tokens)


def lane_mean(values):
    return jnp.sum(values, axis=-1, keepdims=True) * (1.0 / D)


def norm_parts(values):
    centered = values - lane_mean(values)
    rate = lax.rsqrt(lane_mean(centered * centered) + LN_EPS)
    return centered * rate, rate


def norm_back(values, grad, gain):
    unit, rate = norm_parts(values)
    scaled = grad * gain
    d_values = rate * (scaled - lane_mean(scaled) - unit * lane_mean(scaled * unit))
    return (
        d_values,
        jnp.sum(grad * unit, axis=0, keepdims=True),
        jnp.sum(grad, axis=0, keepdims=True),
    )


def dot(left, right, dims=((1,), (0,))):
    return lax.dot_general(left, right, (dims, ((), ())), preferred_element_type=jnp.float32)


NT = ((1,), (1,))
TN = ((0,), (0,))


def allowed_mask(row_ref, col_ref, seg):
    row, col = row_ref[seg], col_ref[seg]
    return (row == col) | (row < 0) | (col < 0)


def forward_kernel(
    w_hbm, tok_ref, row_ref, col_ref, reset_ref, vec_ref, ext_ref, pos_ref,
    x_o, hc_o, proj_o, p_o, one_o, mid_o, gp_o, act_o, two_o, chosen_o,
    w, x, hc, proj, probs, one, mid, gp, act, two, mask, hid, final, sem_w, sem_o,
):
    bf, f32 = jnp.bfloat16, jnp.float32
    loads = [pltpu.make_async_copy(w_hbm.at[:, b], w.at[b], sem_w.at[b]) for b in range(12)]
    for load in loads:
        load.start()
    waited = set()

    def weight(b):
        if b not in waited:
            loads[b].wait()
            waited.add(b)
        return w[b].reshape(D, D)

    stores = []

    def store(src, dst):
        copy = pltpu.make_async_copy(src, dst, sem_o.at[len(stores)])
        copy.start()
        stores.append(copy)

    vec = [vec_ref[k : k + 1, :] for k in range(12)]
    b_q, b_v, b_o, g_one, b_one = vec[:5]
    b_up, b_down, g_two, b_two = vec[5:9], vec[9], vec[10], vec[11]
    gain_e, bias_e = ext_ref[404:405, :], ext_ref[405:406, :]
    lane = lax.broadcasted_iota(jnp.int32, (1, 2 * HD), 1)
    low_half = lane < HD
    for seg in range(SEGS):
        rows = pl.ds(seg * ROWS, ROWS)
        x[seg] = tok_ref[rows, :].astype(f32) + ext_ref[:ROWS, :]
        x[seg, ROWS - MEM :, :] += ext_ref[ROWS + MEM : ROWS + 2 * MEM, :]
        first = ext_ref[ROWS : ROWS + MEM, :]
        if seg == 0:
            x[seg, :MEM, :] += first
        else:
            x[seg, :MEM, :] += jnp.where(reset_ref[seg - 1] > 0, first, hid[ROWS - MEM :, :])
        store(x.at[seg], x_o.at[seg])
        mask[...] = allowed_mask(row_ref, col_ref, seg).astype(f32)
        unit, _ = norm_parts(x[seg])
        h = unit * gain_e + bias_e
        hid[...] = h
        h_low = h.astype(bf)
        hc[0, rows, :] = h_low
        for k, bias in ((0, b_q), (1, None), (2, b_v)):
            made = dot(h_low, weight(k))
            proj[k, rows, :] = (made if bias is None else made + bias).astype(bf)
        store(hc.at[0, rows], hc_o.at[0, rows])
        store(proj.at[:, rows], proj_o.at[:, rows])
        for pair in range(HEADS // 2):
            cols = pl.ds(pair * 2 * HD, 2 * HD)
            query, keyed, value = (proj[k, rows, cols] for k in range(3))
            query = query * jnp.asarray(HD ** (-0.5), bf)
            parts = []
            for side in range(2):
                keep = low_half if side == 0 else ~low_half
                scores = dot(jnp.where(keep, query, jnp.zeros_like(query)), keyed, NT)
                scores = jnp.where(mask[...] > 0, scores, MASKED)
                expd = jnp.exp(scores - jnp.max(scores, axis=-1, keepdims=True))
                p_low = (expd * (1.0 / jnp.sum(expd, axis=-1, keepdims=True))).astype(bf)
                probs[seg, pair * 2 + side] = p_low
                parts.append(dot(p_low, value))
            hc[1, rows, cols] = jnp.where(low_half, parts[0], parts[1]).astype(bf)
        store(probs.at[seg], p_o.at[seg])
        store(hc.at[1, rows], hc_o.at[1, rows])
        sum_one = hid[...] + (dot(hc[1, rows, :], weight(3)) + b_o)
        one[seg] = sum_one
        store(one.at[seg], one_o.at[seg])
        unit, _ = norm_parts(sum_one)
        mid_now = unit * g_one + b_one
        mid_low = mid_now.astype(bf)
        mid[rows, :] = mid_low
        store(mid.at[rows], mid_o.at[rows])
        for j in range(4):
            up = dot(mid_low, weight(4 + j)) + b_up[j]
            half = 0.5 * (1.0 + lax.erf(up * 0.7071067811865476))
            gp[j, rows, :] = (half + up * jnp.exp(-0.5 * up * up) * 0.3989422804014327).astype(bf)
            act[j, rows, :] = (up * half).astype(bf)
        store(gp.at[:, rows], gp_o.at[:, rows])
        store(act.at[:, rows], act_o.at[:, rows])
        total = mid_now + b_down
        for j in range(4):
            total = total + dot(act[j, rows, :], weight(8 + j))
        two[seg] = total
        store(two.at[seg], two_o.at[seg])
        unit, _ = norm_parts(total)
        h = unit * g_two + b_two
        hid[...] = h
        final[rows, :] = h.astype(bf)
    at = lax.broadcasted_iota(jnp.int32, (MLM_PAD, SEGS * ROWS), 1)
    chosen_o[...] = dot((at == pos_ref[...]).astype(bf), final[...]).astype(bf)
    for copy in stores:
        copy.wait()


def run_forward(w_all, tok, marks, reset, vec, ext, pos):
    f32, bf = jnp.float32, jnp.bfloat16
    n = SEGS * ROWS
    saved = [
        ((SEGS, ROWS, D), f32),
        ((2, n, D), bf),
        ((3, n, D), bf),
        ((SEGS, HEADS, ROWS, ROWS), bf),
        ((SEGS, ROWS, D), f32),
        ((n, D), bf),
        ((4, n, D), bf),
        ((4, n, D), bf),
        ((SEGS, ROWS, D), f32),
    ]
    hbm = pl.BlockSpec(memory_space=pl.ANY)
    vmem = pl.BlockSpec(memory_space=pltpu.VMEM)
    return pl.pallas_call(
        forward_kernel,
        out_shape=[jax.ShapeDtypeStruct(s, k) for s, k in saved]
        + [jax.ShapeDtypeStruct((MLM_PAD, D), bf)],
        in_specs=[hbm, vmem, vmem, vmem, pl.BlockSpec(memory_space=pltpu.SMEM), vmem, vmem, vmem],
        out_specs=[hbm] * len(saved) + [vmem],
        scratch_shapes=[pltpu.VMEM((12, w_all.shape[0]) + w_all.shape[2:], bf)]
        + [pltpu.VMEM(s, k) for s, k in saved]
        + [
            pltpu.VMEM((ROWS, ROWS), f32),
            pltpu.VMEM((ROWS, D), f32),
            pltpu.VMEM((n, D), bf),
            pltpu.SemaphoreType.DMA((12,)),
            pltpu.SemaphoreType.DMA((SEGS * 10,)),
        ],
        compiler_params=pltpu.CompilerParams(vmem_limit_bytes=60 << 20),
    )(w_all, tok, marks[:, None, :], marks[:, :, None], reset, vec, ext, pos[:, None])


def backward_kernel(
    cuts,
    w_hbm, x_i, hc_i, proj_i, p_i, one_i, mid_i, gp_i, act_i, two_i,
    dch_ref, reset_ref, vec_ref, ext_ref, pos_ref, give_ref, slot_ref, v_ref,
    share_o, small_o, dpack_o, dtok,
    w, x, hc, right, probs, one, mid, rup, act, two, rdown, grad, dmem, sem_w, sem_i,
):
    bf, f32 = jnp.bfloat16, jnp.float32
    small_o[...] = jnp.zeros_like(small_o)
    loads = {}
    state = {"n": 0}

    def load(name, src, dst):
        copy = pltpu.make_async_copy(src, dst, sem_i.at[state["n"]])
        state["n"] += 1
        copy.start()
        loads[name] = copy

    def need(name):
        if name in loads:
            loads.pop(name).wait()

    wl = [pltpu.make_async_copy(w_hbm.at[:, b], w.at[b], sem_w.at[b]) for b in range(12)]
    waited = set()

    def weight(b):
        if b not in waited:
            wl[b].wait()
            waited.add(b)
        return w[b].reshape(D, D)

    order = list(reversed(range(SEGS)))
    for i, seg in enumerate(order):
        rows = pl.ds(seg * ROWS, ROWS)
        load(("two", seg), two_i.at[seg], two.at[seg])
        if i == 0:
            for b in range(8, 12):
                wl[b].start()
        load(("gp", seg), gp_i.at[:, rows], rup.at[:, rows])
        if i == 0:
            for b in range(4, 8):
                wl[b].start()
        load(("one", seg), one_i.at[seg], one.at[seg])
        if i == 0:
            wl[3].start()
            load(("p", seg), p_i.at[seg], probs)
        load(("proj", seg), proj_i.at[:, rows], right.at[pl.ds(0, 3), rows])
        if i == 0:
            for b in range(3):
                wl[b].start()
        load(("x", seg), x_i.at[seg], x.at[seg])
    load("hc", hc_i, hc)
    load("mid", mid_i, mid)
    load("act", act_i, act)

    vec = [vec_ref[k : k + 1, :] for k in range(12)]
    g_one, g_two, gain_e = vec[3], vec[10], ext_ref[404:405, :]
    lane = lax.broadcasted_iota(jnp.int32, (1, 2 * HD), 1)
    low_half = lane < HD
    at = lax.broadcasted_iota(jnp.int32, (MLM_PAD, SEGS * ROWS), 1)
    at_pos = (at == pos_ref[...]).astype(bf)
    v0 = EXT

    def add_row(k, value):
        small_o[v0 + k : v0 + k + 1, :] += value

    def sums(values):
        return jnp.sum(values.astype(f32), axis=0, keepdims=True)

    for i, seg in enumerate(order):
        rows = pl.ds(seg * ROWS, ROWS)
        grad[...] = dot(at_pos[:, seg * ROWS : (seg + 1) * ROWS], dch_ref[...], TN)
        if i > 0:
            grad[ROWS - MEM :, :] += dmem[...]
        need(("two", seg))
        d_two, d_gain, d_shift = norm_back(two[seg], grad[...], g_two)
        add_row(10, d_gain)
        add_row(11, d_shift)
        r_down = d_two.astype(bf)
        rdown[rows, :] = r_down
        add_row(9, sums(r_down))
        need(("gp", seg))
        for j in range(4):
            r_up = (rup[j, rows, :].astype(f32) * dot(r_down, weight(8 + j), NT)).astype(bf)
            rup[j, rows, :] = r_up
            add_row(5 + j, sums(r_up))
        for j in range(4):
            d_two = d_two + dot(rup[j, rows, :], weight(4 + j), NT)
        need(("one", seg))
        d_one, d_gain, d_shift = norm_back(one[seg], d_two, g_one)
        add_row(3, d_gain)
        add_row(4, d_shift)
        grad[...] = d_one
        r_att = d_one.astype(bf)
        right[3, rows, :] = r_att
        add_row(2, sums(r_att))
        d_ctx = dot(r_att, weight(3), NT).astype(bf)
        need(("p", seg))
        need(("proj", seg))
        for pair in range(HEADS // 2):
            cols = pl.ds(pair * 2 * HD, 2 * HD)
            query, keyed, value = (right[k, rows, cols] for k in range(3))
            d_out = d_ctx[:, pair * 2 * HD : (pair + 1) * 2 * HD]
            made = []
            for side in range(2):
                keep = low_half if side == 0 else ~low_half
                p_low = probs[pair * 2 + side]
                p_now = p_low.astype(f32)
                d_p = dot(jnp.where(keep, d_out, jnp.zeros_like(d_out)), value, NT)
                weighted = p_now * d_p
                d_s = weighted - p_now * jnp.sum(weighted, axis=-1, keepdims=True)
                d_s = d_s.astype(bf)
                made.append((dot(d_s, keyed), dot(d_s, query, TN), dot(p_low, d_out, TN)))
            for k, scale in ((0, HD ** (-0.5)), (1, HD ** (-0.5)), (2, 1.0)):
                both = jnp.where(low_half, made[0][k], made[1][k]) * scale
                right[k, rows, cols] = both.astype(bf)
        if i + 1 < SEGS:
            load(("p", order[i + 1]), p_i.at[order[i + 1]], probs)
        d_h = grad[...]
        for k in range(3):
            d_h = d_h + dot(right[k, rows, :], weight(k), NT)
        add_row(0, sums(right[0, rows, :]))
        add_row(1, sums(right[2, rows, :]))
        need(("x", seg))
        d_x, d_gain, d_shift = norm_back(x[seg], d_h, gain_e)
        grad[...] = d_x
        dtok[rows, :] = d_x.astype(bf)
        small_o[:ROWS, :] += d_x
        small_o[ROWS + MEM : ROWS + 2 * MEM, :] += grad[ROWS - MEM :, :]
        small_o[404:405, :] += d_gain
        small_o[405:406, :] += d_shift
        d_read = grad[:MEM, :]
        if seg > 0:
            back = reset_ref[seg - 1] > 0
            small_o[ROWS : ROWS + MEM, :] += jnp.where(back, d_read, 0.0)
            dmem[...] = jnp.where(back, 0.0, d_read)
        else:
            small_o[ROWS : ROWS + MEM, :] += d_read
    dpack_o[...] = dot((give_ref[...] == slot_ref[...]).astype(bf), dtok[...]).astype(bf)
    need("hc")
    need("mid")
    need("act")
    v = v_ref[0]
    width = D // cuts
    block, cut = v // cuts, v % cuts
    cols = pl.ds(pl.multiple_of(cut * width, 128), width)
    share_o[0] = dot(hc[block // 3], right[block, :, cols], TN).astype(bf)
    share_o[1] = dot(mid[...], rup[block, :, cols], TN).astype(bf)
    share_o[2] = dot(act[block], rdown[:, cols], TN).astype(bf)


def run_backward(
    w_all, saved, d_chosen, reset, vec, ext, pos, give, slot, v_idx, cuts, small_rows
):
    f32, bf = jnp.float32, jnp.bfloat16
    n = SEGS * ROWS
    hbm = pl.BlockSpec(memory_space=pl.ANY)
    vmem = pl.BlockSpec(memory_space=pltpu.VMEM)
    smem = pl.BlockSpec(memory_space=pltpu.SMEM)
    return pl.pallas_call(
        functools.partial(backward_kernel, cuts),
        out_shape=[
            jax.ShapeDtypeStruct((3, D, D // cuts), bf),
            jax.ShapeDtypeStruct((small_rows, D), f32),
            jax.ShapeDtypeStruct((give.shape[0], D), bf),
            jax.ShapeDtypeStruct((n, D), bf),
        ],
        in_specs=[hbm] * 10 + [vmem, smem, vmem, vmem, vmem, vmem, vmem, smem],
        out_specs=[vmem] * 4,
        scratch_shapes=[
            pltpu.VMEM((12, w_all.shape[0]) + w_all.shape[2:], bf),
            pltpu.VMEM((SEGS, ROWS, D), f32),
            pltpu.VMEM((2, n, D), bf),
            pltpu.VMEM((4, n, D), bf),
            pltpu.VMEM((HEADS, ROWS, ROWS), bf),
            pltpu.VMEM((SEGS, ROWS, D), f32),
            pltpu.VMEM((n, D), bf),
            pltpu.VMEM((4, n, D), bf),
            pltpu.VMEM((4, n, D), bf),
            pltpu.VMEM((SEGS, ROWS, D), f32),
            pltpu.VMEM((n, D), bf),
            pltpu.VMEM((ROWS, D), f32),
            pltpu.VMEM((MEM, D), f32),
            pltpu.SemaphoreType.DMA((12,)),
            pltpu.SemaphoreType.DMA((SEGS * 6 + 4,)),
        ],
        compiler_params=pltpu.CompilerParams(vmem_limit_bytes=61 << 20),
    )(
        w_all, *saved, d_chosen, reset, vec, ext, pos[:, None],
        give[:, None], slot[None, :], v_idx,
    )


def ceil_to(value, unit):
    return -(-value // unit) * unit


def per_device(
    ids,
    docs,
    resets,
    mlm_pos,
    mlm_label,
    step,
    qkv_master,
    qkv_first,
    qkv_second,
    out_master,
    out_first,
    out_second,
    up_master,
    up_first,
    up_second,
    down_master,
    down_first,
    down_second,
    embed_master,
    embed_first,
    embed_second,
    vectors_master,
    vectors_first,
    vectors_second,
    extras_master,
    extras_first,
    extras_second,
):
    f32, bf = jnp.float32, jnp.bfloat16
    n_dp = lax.axis_size("dp")
    n_v = lax.axis_size("vocab")
    d_idx = lax.axis_index("dp")
    v_idx = lax.axis_index("vocab")
    own_rows = embed_master.shape[0]
    tokens_n = SEGS * SEG
    rb = qkv_master.shape[1]
    cuts = max(1, n_v // 4)
    width = D // cuts
    groups = 12 * cuts // n_v

    def to_blocks(qkv, out, up, down):
        full = jnp.concatenate(
            [
                qkv[0].reshape(rb, 3, D).transpose(1, 0, 2),
                out,
                up[0].reshape(rb, n_dp, 4, rb).transpose(2, 0, 1, 3).reshape(4, rb, D),
                down[0].reshape(4, rb, D),
            ]
        )
        return full.reshape(12, rb, cuts, width).transpose(0, 2, 1, 3).reshape(12 * cuts, rb, width)

    def from_blocks(blocks):
        full = blocks.reshape(12, cuts, rb, width).transpose(0, 2, 1, 3).reshape(12, rb, D)
        return (
            full[:3].transpose(1, 0, 2).reshape(1, rb, 3 * D),
            full[3:4],
            full[4:8].reshape(4, rb, n_dp, rb).transpose(1, 2, 0, 3).reshape(1, rb, FF),
            full[8:].reshape(1, 4 * rb, D),
        )

    ints = jnp.concatenate([ids[0], mlm_label[0]])[None]
    ints = jnp.pad(ints, ((0, 0), (0, ceil_to(ints.shape[1], 128) - ints.shape[1])), constant_values=-1)
    ints_all = gather_ints(ints, n_dp)[:, 0]
    ids_all = ints_all[:, :tokens_n]
    labels_all = ints_all[:, tokens_n : tokens_n + MLM]
    labels_all = jnp.pad(labels_all, ((0, 0), (0, MLM_PAD - MLM)), constant_values=-1)
    holder = ids_all // own_rows
    local_row = ids_all % own_rows
    order = jnp.arange(tokens_n, dtype=jnp.int32)
    same = (holder[:, :, None] == holder[:, None, :]) & (order[None, :, None] > order[None, None, :])
    rank = jnp.sum(same.astype(jnp.int32), axis=-1)
    cap = ceil_to(2 * tokens_n // (n_dp * n_v) + 2, 16)
    overflow = jnp.max(rank) >= cap
    mine = holder == d_idx * n_v + v_idx
    places = jnp.arange(cap, dtype=jnp.int32)
    hit = mine[:, None, :] & (rank[:, None, :] == places[None, :, None])
    packed_row = jnp.sum(jnp.where(hit, local_row[:, None, :] + 1, 0), axis=-1) - 1
    own_slots = jnp.arange(own_rows, dtype=jnp.int32)
    pick = (packed_row.reshape(n_dp * cap)[:, None] == own_slots[None, :]).astype(bf)
    table = embed_master.astype(bf)
    packed = jnp.dot(pick, table, preferred_element_type=f32).astype(bf).reshape(n_dp, cap, D)

    blocks = to_blocks(
        qkv_master.astype(bf), out_master.astype(bf), up_master.astype(bf), down_master.astype(bf)
    )
    w_all, tok_all = gather_weights(blocks, packed, n_dp, n_v)
    if cuts > 1 or rb % 16:
        w_all = w_all.reshape(n_dp, 12, cuts, rb, width).transpose(1, 0, 3, 2, 4).reshape(1, 12, D, D)

    my_holder = holder[d_idx]
    my_rank = rank[d_idx]
    slot = (my_holder * cap + my_rank).reshape(SEGS, SEG)
    slot = jnp.pad(slot, ((0, 0), (MEM, MEM)), constant_values=-1).reshape(SEGS * ROWS)

    def packed_tokens(_):
        slots = jnp.arange(n_dp * n_v * cap, dtype=jnp.int32)
        onehot = (slot[:, None] == slots[None, :]).astype(bf)
        rows = tok_all.reshape(n_dp * n_v * cap, D)
        return jnp.dot(onehot, rows, preferred_element_type=f32).astype(bf)

    def whole_tokens(_):
        whole = lax.all_gather(table, "dp", axis=0, tiled=True)
        at = jnp.arange(n_dp * own_rows, dtype=jnp.int32)
        row_ids = (at // own_rows * n_v + v_idx) * own_rows + at % own_rows
        onehot = (ids[0][:, None] == row_ids[None, :]).astype(bf)
        rows = lax.psum(jnp.dot(onehot, whole, preferred_element_type=f32).astype(bf), "vocab")
        return jnp.pad(rows.reshape(SEGS, SEG, D), ((0, 0), (MEM, MEM), (0, 0))).reshape(-1, D)

    tokens = lax.cond(overflow, whole_tokens, packed_tokens, 0)
    marks = jnp.pad(docs.reshape(SEGS, SEG), ((0, 0), (MEM, MEM)), constant_values=-1)
    vec = vectors_master[0].reshape(12, D)
    b_up = vec[5:9].reshape(n_dp, 4, rb).transpose(1, 0, 2).reshape(4, D)
    vec = jnp.concatenate([vec[:5], b_up, vec[9:]])
    positions = mlm_pos[0]
    at_rows = positions // SEG * ROWS + MEM + positions % SEG
    at_rows = jnp.concatenate([at_rows, jnp.full((MLM_PAD - MLM,), -1, jnp.int32)])
    *saved, chosen = run_forward(w_all, tokens, marks, resets[0], vec, extras_master, at_rows)
    rows_v = MLM_PAD // n_v
    d_chosen, d_table, loss = run_head(chosen.reshape(n_v, rows_v, D), table, labels_all, n_dp, n_v)
    loss = loss[0, 0]
    d_chosen = d_chosen.reshape(MLM_PAD, D)
    small_rows = EXT + 12
    e_rows = ceil_to(-(-small_rows // (n_dp * n_v)), 16)
    at = jnp.arange(n_dp * cap, dtype=jnp.int32)
    give = (at // cap * n_v + v_idx) * cap + at % cap
    shares, small, d_packed, d_tok = run_backward(
        w_all,
        saved,
        d_chosen,
        resets[0],
        vec,
        extras_master,
        at_rows,
        give,
        slot,
        v_idx[None],
        cuts,
        ceil_to(small_rows, 8),
    )
    shares = shares.reshape(groups, n_dp // 2, 2, rb, width)
    small = jnp.pad(small.astype(bf), ((0, e_rows * n_dp * n_v - small.shape[0]), (0, 0)))
    small = small.reshape(n_dp // 2, 2, n_v, e_rows, D)
    small = lax.dynamic_index_in_dim(small, v_idx, axis=2, keepdims=False)
    d_packed = d_packed.reshape(n_dp, cap, D)
    g_blocks, small_all, d_packed_all = reduce_grads(shares, small, d_packed, n_dp, n_v)

    def packed_d_table(_):
        return jnp.einsum(
            "tv,td->vd", pick, d_packed_all.reshape(n_dp * cap, D), preferred_element_type=f32
        )

    def whole_d_table(_):
        d_all = d_tok.reshape(SEGS, ROWS, D)[:, MEM : MEM + SEG].reshape(tokens_n, D)
        d_all = lax.all_gather(d_all, "dp", axis=0, tiled=True)
        row_ids = (d_idx * n_v + v_idx) * own_rows + own_slots
        onehot = (ids_all.reshape(-1)[:, None] == row_ids[None, :]).astype(bf)
        return jnp.einsum("tv,td->vd", onehot, d_all, preferred_element_type=f32)

    s_table = d_table + lax.cond(overflow, whole_d_table, packed_d_table, 0)
    small_all = small_all.reshape(n_dp * n_v * e_rows, D)
    norm = jnp.sqrt(run_norm(g_blocks, small_all[:small_rows], s_table, n_dp, n_v)[0, 0])
    s_qkv, s_out, s_up, s_down = (grad[0] for grad in from_blocks(g_blocks))
    g_ext = small_all[:EXT].astype(f32)
    g_vec = small_all[EXT:small_rows].astype(f32)
    g_up_bias = g_vec[5:9].reshape(4, n_dp, rb).transpose(1, 0, 2).reshape(4, D)
    g_vec = jnp.concatenate([g_vec[:5], g_up_bias, g_vec[9:]])
    coef = jnp.minimum(1.0, CLIP / (norm + 1e-06))
    t = step[0].astype(f32)
    scalars = jnp.stack([coef, 1.0 / (1.0 - BETA_ONE**t), 1.0 / (1.0 - BETA_TWO**t)])
    wide = (12, D)
    states = (
        (embed_master, embed_first, embed_second),
        (qkv_master[0], qkv_first[0], qkv_second[0]),
        (out_master[0], out_first[0], out_second[0]),
        (up_master[0], up_first[0], up_second[0]),
        (down_master[0], down_first[0], down_second[0]),
        (extras_master, extras_first, extras_second),
        (vectors_master.reshape(wide), vectors_first.reshape(wide), vectors_second.reshape(wide)),
    )
    new = run_adam(
        scalars,
        (s_table, s_qkv, s_out, s_up, s_down, g_ext, g_vec),
        states,
        (LR_BIG, LR_BIG, LR_BIG, LR_BIG, LR_BIG, LR_SMALL, LR_SMALL),
    )
    layer = [value[None] for value in new[3:15]]
    vectors = [value.reshape(vectors_master.shape) for value in new[18:]]
    return (loss, norm, *layer, *new[:3], *vectors, *new[15:18])


def solution(mesh):
    in_specs = (
        P("dp", None),
        P("dp", None),
        P("dp", None),
        P("dp", None),
        P("dp", None),
        P(),
        P(None, "dp", None),
        P(None, "dp", None),
        P(None, "dp", None),
        P(None, "dp", None),
        P(None, "dp", None),
        P(None, "dp", None),
        P(None, "dp", None),
        P(None, "dp", None),
        P(None, "dp", None),
        P(None, "dp", None),
        P(None, "dp", None),
        P(None, "dp", None),
        P(("dp", "vocab"), None),
        P(("dp", "vocab"), None),
        P(("dp", "vocab"), None),
        P(),
        P(),
        P(),
        P(),
        P(),
        P(),
    )
    out_specs = (
        P(),
        P(),
        P(None, "dp", None),
        P(None, "dp", None),
        P(None, "dp", None),
        P(None, "dp", None),
        P(None, "dp", None),
        P(None, "dp", None),
        P(None, "dp", None),
        P(None, "dp", None),
        P(None, "dp", None),
        P(None, "dp", None),
        P(None, "dp", None),
        P(None, "dp", None),
        P(("dp", "vocab"), None),
        P(("dp", "vocab"), None),
        P(("dp", "vocab"), None),
        P(),
        P(),
        P(),
        P(),
        P(),
        P(),
    )
    return jax.shard_map(
        per_device, mesh=mesh, in_specs=in_specs, out_specs=out_specs, check_vma=False
    )
```

```python
import functools

import jax
import jax.numpy as jnp
from jax import lax
from jax.experimental import pallas as pl
from jax.experimental.pallas import tpu as pltpu
from jax.sharding import PartitionSpec as P

D = 768
HEADS = 12
HD = 64
FF = 3072
MEM = 10
SEG = 364
SEGS = 2
LAYERS = 1
MLM = 112
ROWS = 384


BETA_ONE = 0.9
BETA_TWO = 0.999
ADAM_EPS = 1e-08
DECAY = 0.01
LN_EPS = 1e-06
CLIP = 0.02
LR_BIG = 0.04
LR_SMALL = 0.5
MASKED = -1000000000.0


MESH = pl.DeviceIdType.MESH
MLM_PAD = 128
EXT = ROWS + 2 * MEM + 2


class Place:
    def __init__(self, n_dp, n_v):
        self.A, self.Y = n_dp // 2, n_v // 2
        self.d, self.v = lax.axis_index("dp"), lax.axis_index("vocab")
        self.a, self.x = self.d // 2, self.d % 2
        self.y, self.c = self.v // 2, self.v % 2
        self.me = (self.d, self.v)
        self.xp = (self.d + 1 - 2 * self.x, self.v)
        self.cp = (self.d, self.v + 1 - 2 * self.c)

    def from_a(self, k):
        return lax.rem(self.a + self.A - k, self.A)

    def to_a(self, k):
        return lax.rem(self.a + k, self.A)

    def from_y(self, k):
        return lax.rem(self.y + self.Y - k, self.Y)

    def zp(self, k):
        return (self.to_a(k) * 2 + self.x, self.v)

    def yp(self, k):
        return (self.d, lax.rem(self.y + k, self.Y) * 2 + self.c)

    def barrier(self, extra=()):
        sem = pltpu.get_barrier_semaphore()
        partners = [self.zp(k) for k in range(1, self.A)] + [self.xp]
        partners += [self.yp(k) for k in range(1, self.Y)] + [self.cp] + list(extra)
        for partner in partners:
            pl.semaphore_signal(sem, 1, device_id=partner, device_id_type=MESH)
        pl.semaphore_wait(sem, len(partners))


class Copies:
    def __init__(self, me, send_sem, recv_sem):
        self.me, self.send_sem, self.recv_sem, self.started = me, send_sem, recv_sem, []

    def send(self, number, src, dst, partner):
        copy = pltpu.make_async_remote_copy(
            src, dst, self.send_sem.at[number], self.recv_sem.at[number], partner, MESH
        )
        copy.start()
        self.started.append(copy)

    def arrived(self, number, dst):
        pltpu.make_async_remote_copy(
            dst, dst, self.send_sem.at[number], self.recv_sem.at[number], self.me, MESH
        ).wait_recv()

    def finish(self):
        for copy in self.started:
            copy.wait_send()


class Gather:
    def __init__(self, place, copies, base, ref, own=None, shared=False, flat=False):
        self.flat = flat
        self.p, self.q, self.base, self.ref, self.own = place, copies, base, ref, own
        self.least = 1 if shared else 0
        A, Y = place.A, place.Y
        self.x0 = base + A - 1
        self.y0 = self.x0 + A
        self.c0 = self.y0 + 2 * A * (Y - 1)
        self.end = self.c0 + 2 * A * Y

    @staticmethod
    def count(n_dp, n_v):
        A, Y = n_dp // 2, n_v // 2
        return A - 1 + A + 2 * A * (Y - 1) + 2 * A * Y

    def at(self, slot, j=0, c=None):
        p = self.p
        k = slot % p.A
        x = p.x if slot < p.A else 1 - p.x
        c = p.c if c is None else c
        return self.ref(p.from_a(k) * 2 + x, p.from_y(j) * 2 + c)

    def spread(self, slot):
        p = self.p
        src = self.at(slot) if (slot or self.own is None) else self.own
        if slot < p.A:
            self.q.send(self.x0 + slot, src, self.at(slot), p.xp)
        if slot < self.least:
            return
        if not self.flat:
            for k in range(1, p.Y):
                self.q.send(self.y0 + slot * (p.Y - 1) + k - 1, src, self.at(slot), p.yp(k))
        self.q.send(self.c0 + slot * p.Y, src, self.at(slot), p.cp)

    def start(self):
        p = self.p
        src = self.at(0) if self.own is None else self.own
        for k in range(1, p.A):
            self.q.send(self.base + k - 1, src, self.at(0), p.zp(k))
        self.spread(0)

    def step_a(self):
        for k in range(1, self.p.A):
            self.q.arrived(self.base + k - 1, self.at(k))
            self.spread(k)

    def step_x(self):
        A = self.p.A
        for k in range(A):
            self.q.arrived(self.x0 + k, self.at(A + k))
            self.spread(A + k)

    def step_y(self):
        p = self.p
        if self.flat:
            return
        for slot in range(self.least, 2 * p.A):
            for j in range(1, p.Y):
                self.q.arrived(self.y0 + slot * (p.Y - 1) + j - 1, self.at(slot, j))
                self.q.send(self.c0 + slot * p.Y + j, self.at(slot, j), self.at(slot, j), p.cp)

    def step_c(self):
        p = self.p
        for slot in range(self.least, 2 * p.A):
            for j in range(1 if self.flat else p.Y):
                self.q.arrived(self.c0 + slot * p.Y + j, self.at(slot, j, 1 - p.c))


def front_kernel(
    n_dp, n_v, cap, w_ref, table_ref, ints_ref,
    out_ref, tok_out, ints_out, pick_out, slot_out, rank_out,
    packed, hold, upper, ss, rs, ls,
):
    f32, bf = jnp.float32, jnp.bfloat16
    p = Place(n_dp, n_v)
    q = Copies(p.me, ss, rs)
    others = [(lax.rem(p.d + k, n_dp), p.v) for k in range(1, n_dp)]
    partners = [(p.d, lax.rem(p.v + k, n_v)) for k in range(1, n_v)]
    sem = pltpu.get_barrier_semaphore()
    for partner in others + partners:
        pl.semaphore_signal(sem, 1, device_id=partner, device_id_type=MESH)
    own = pltpu.make_async_copy(w_ref, out_ref.at[p.d], ls.at[0])
    own.start()
    ints_out[p.d] = ints_ref[...]
    pl.semaphore_wait(sem, n_dp - 1 + n_v - 1)
    base = 0
    for k in range(1, n_dp):
        q.send(base + k - 1, ints_ref, ints_out.at[p.d], others[k - 1])
    i0 = base
    base = base + n_dp - 1
    gathers = []
    for g in range(3):
        if g < 2:
            gather = Gather(
                p,
                q,
                base,
                lambda d, v, g=g: out_ref.at[d, g * n_v + v],
                own=w_ref.at[g * n_v + p.v],
                shared=True,
            )
        else:
            half = n_v // 2
            gather = Gather(
                p,
                q,
                base,
                lambda d, v: out_ref.at[d, pl.ds(2 * n_v + (v % 2) * half, half)],
                own=w_ref.at[pl.ds(2 * n_v + p.c * half, half)],
                shared=True,
                flat=True,
            )
        base = gather.end
        gathers.append(gather)
        gather.start()

    tokens_n, wide = SEGS * SEG, ceil_to(SEGS * SEG, 128)
    n_dev = n_dp * n_v
    rows = table_ref.shape[0]
    lane = lax.broadcasted_iota(jnp.int32, (1, wide), 1)
    valid = lane < tokens_n
    device = lax.broadcasted_iota(jnp.int32, (n_dev, 1), 0)
    least = device * rows
    upper[...] = (lax.broadcasted_iota(jnp.int32, (wide, 1), 0) < lane).astype(bf)
    place = lax.broadcasted_iota(jnp.int32, (cap, 1), 0).astype(f32)
    row_at = lax.broadcasted_iota(jnp.int32, (1, rows), 1).astype(f32) + 1.0
    low = (p.d * n_v + p.v) * rows
    for k in range(1, n_dp):
        q.arrived(i0 + k - 1, ints_out.at[lax.rem(p.d + n_dp - k, n_dp)])
    most = jnp.zeros((1, 1), f32)
    batch = hold.shape[0] // n_dev
    for start in range(0, n_dp, batch):
        for i in range(batch):
            ids = ints_out[start + i, :, :wide]
            held = (ids >= least) & (ids < least + rows) & valid
            hold[i * n_dev : (i + 1) * n_dev, :] = held.astype(f32).astype(bf)
        before = dot(hold[...], upper[...])
        for i in range(batch):
            ids = ints_out[start + i, :, :wide]
            held = hold[i * n_dev : (i + 1) * n_dev, :].astype(f32)
            rank = jnp.sum(held * before[i * n_dev : (i + 1) * n_dev, :], axis=0, keepdims=True)
            holder = jnp.sum(held * device.astype(f32), axis=0, keepdims=True)
            most = jnp.maximum(most, jnp.max(rank, axis=1, keepdims=True))
            slot_out[start + i : start + i + 1, :] = jnp.where(valid, holder * cap + rank, -1.0)
            mine = (ids >= low) & (ids < low + rows) & valid
            row = jnp.where(mine, (ids - low).astype(f32) + 1.0, 0.0)
            taken = jnp.sum(jnp.where(rank == place, row, 0.0), axis=1, keepdims=True)
            pick = (taken == row_at).astype(f32).astype(bf)
            pick_out[(start + i) * cap : (start + i + 1) * cap, :] = pick
    rank_out[...] = jnp.broadcast_to(most, rank_out.shape)
    packed[...] = dot(pick_out[...], table_ref[...]).astype(bf).reshape(packed.shape)
    first = base
    for k in range(1, n_dp):
        to = lax.rem(p.d + k, n_dp)
        q.send(first + k - 1, packed.at[to], tok_out.at[p.d, p.v], others[k - 1])
    local = pltpu.make_async_copy(packed.at[p.d], tok_out.at[p.d, p.v], ls.at[1])
    local.start()
    base = base + n_dp - 1
    y0, c0 = base, base + n_dp * (p.Y - 1)

    def relay(slot, src, src_d):
        for k in range(1, p.Y):
            q.send(y0 + slot * (p.Y - 1) + k - 1, src, tok_out.at[src_d, p.v], p.yp(k))
        q.send(c0 + slot * p.Y, src, tok_out.at[src_d, p.v], p.cp)

    relay(0, packed.at[p.d], p.d)
    g0, g1, g2 = gathers
    g0.step_a()
    g0.step_x()
    g1.step_a()
    for k in range(1, n_dp):
        src_d = lax.rem(p.d + n_dp - k, n_dp)
        q.arrived(first + k - 1, tok_out.at[src_d, p.v])
        relay(k, tok_out.at[src_d, p.v], src_d)
    g0.step_y()
    g1.step_x()
    g2.step_a()
    g1.step_y()
    for slot in range(n_dp):
        src_d = lax.rem(p.d + n_dp - slot, n_dp)
        for j in range(1, p.Y):
            piece = tok_out.at[src_d, p.from_y(j) * 2 + p.c]
            q.arrived(y0 + slot * (p.Y - 1) + j - 1, piece)
            q.send(c0 + slot * p.Y + j, piece, piece, p.cp)
    g2.step_x()
    for gather in gathers:
        gather.step_c()
    for slot in range(n_dp):
        src_d = lax.rem(p.d + n_dp - slot, n_dp)
        for j in range(p.Y):
            q.arrived(c0 + slot * p.Y + j, tok_out.at[src_d, p.from_y(j) * 2 + 1 - p.c])
    q.finish()
    own.wait()
    local.wait()


def run_front(blocks, table, ints, cap, n_dp, n_v):
    f32, bf = jnp.float32, jnp.bfloat16
    count = 3 * Gather.count(n_dp, n_v) + 2 * (n_dp - 1) + n_dp * (n_v - 1)
    hbm = pl.BlockSpec(memory_space=pl.ANY)
    vmem = pl.BlockSpec(memory_space=pltpu.VMEM)
    wide = ceil_to(SEGS * SEG, 128)
    rows = table.shape[0]
    return pl.pallas_call(
        functools.partial(front_kernel, n_dp, n_v, cap),
        out_shape=(
            jax.ShapeDtypeStruct((n_dp,) + blocks.shape, bf),
            jax.ShapeDtypeStruct((n_dp, n_v, cap, D), bf),
            jax.ShapeDtypeStruct((n_dp,) + ints.shape, ints.dtype),
            jax.ShapeDtypeStruct((n_dp * cap, rows), bf),
            jax.ShapeDtypeStruct((n_dp, wide), f32),
            jax.ShapeDtypeStruct((8, 128), f32),
        ),
        in_specs=[hbm, vmem, vmem],
        out_specs=(hbm, hbm, vmem, vmem, vmem, vmem),
        scratch_shapes=[
            pltpu.VMEM((n_dp, cap, D), bf),
            pltpu.VMEM((8 * n_dp * n_v, wide), bf),
            pltpu.VMEM((wide, wide), bf),
            pltpu.SemaphoreType.DMA((count,)),
            pltpu.SemaphoreType.DMA((count,)),
            pltpu.SemaphoreType.DMA((2,)),
        ],
        compiler_params=pltpu.CompilerParams(
            collective_id=0, has_side_effects=True, vmem_limit_bytes=48 << 20
        ),
    )(blocks, table, ints)


def head_kernel(
    n_dp, n_v, ch_ref, table_ref, label_ref, tags_ref,
    out_ref, dtab_ref, loss_ref,
    al, logits, dlog, st, sd, sv, lse_s, part, bc, by, bx, bz, pc, py, px, ss, rs,
):
    f32, bf = jnp.float32, jnp.bfloat16
    p = Place(n_dp, n_v)
    A, Y = p.A, p.Y
    count = n_dp * MLM
    others = [(lax.rem(p.d + k, n_dp), p.v) for k in range(1, n_dp)]
    partners = [(p.d, lax.rem(p.v + k, n_v)) for k in range(1, n_v)]
    sem = pltpu.get_barrier_semaphore()
    for partner in others + partners:
        pl.semaphore_signal(sem, 1, device_id=partner, device_id_type=MESH)
    pl.semaphore_wait(sem, n_dp - 1 + n_v - 1)
    q = Copies(p.me, ss, rs)
    gather = Gather(p, q, 0, lambda d, v: al.at[d, v], shared=True)
    al[p.d] = ch_ref[...]
    gather.start()
    gather.step_a()
    gather.step_x()
    gather.step_y()
    gather.step_c()
    n = gather.end
    rows_v, total_m = ch_ref.shape[1], n_dp * MLM_PAD
    chosen = al[...].reshape(total_m, D)
    logits[...] = dot(table_ref[...], chosen, NT)
    rows = table_ref.shape[0]
    row_ids = (p.d * n_v + p.v) * rows + lax.broadcasted_iota(jnp.int32, (rows, 1), 0)
    hits = row_ids == label_ref[...]
    top = jnp.max(logits[...], axis=0, keepdims=True)
    stats = (
        top,
        jnp.sum(jnp.exp(logits[...] - top), axis=0, keepdims=True),
        jnp.sum(jnp.where(hits, logits[...], 0.0), axis=0, keepdims=True),
    )
    tall = total_m // 128
    for k, values in enumerate(stats):
        for r in range(tall):
            st[k * tall + r : k * tall + r + 1, :] = values[:, r * 128 : (r + 1) * 128]

    def merged(ref, amount):
        tops = [ref[k, :tall, :] for k in range(amount)]
        best = functools.reduce(jnp.maximum, tops)
        parts = [ref[k, tall : 2 * tall, :] * jnp.exp(tops[k] - best) for k in range(amount)]
        return best, sum(parts[1:], parts[0]), sum(ref[k, 2 * tall :, :] for k in range(amount))

    sd[p.d] = st[...]
    for k in range(1, n_dp):
        q.send(n + k - 1, st, sd.at[p.d], others[k - 1])
    for k in range(1, n_dp):
        q.arrived(n + k - 1, sd.at[lax.rem(p.d + n_dp - k, n_dp)])
    n = n + n_dp - 1
    for k, values in enumerate(merged(sd, n_dp)):
        sv[p.v, k * tall : (k + 1) * tall, :] = values
    for k in range(1, n_v):
        q.send(n + k - 1, sv.at[p.v], sv.at[p.v], partners[k - 1])
    for k in range(1, n_v):
        q.arrived(n + k - 1, sv.at[lax.rem(p.v + n_v - k, n_v)])
    n = n + n_v - 1
    best, total, target = merged(sv, n_v)
    lse = best + jnp.log(total)
    lse_s[...] = lse
    lost = jnp.sum(jnp.where(tags_ref[...] >= 0, lse - target, 0.0), axis=1, keepdims=True)
    lost = jnp.sum(lost, axis=0, keepdims=True) / count
    loss_ref[...] = jnp.broadcast_to(lost, loss_ref.shape)
    lse_row = jnp.concatenate([lse_s[r : r + 1, :] for r in range(tall)], axis=1)
    d_log = (jnp.exp(logits[...] - lse_row) - hits.astype(f32)) * (1.0 / count)
    dlog[...] = d_log.astype(bf)
    made = dot(dlog[...], table_ref[...], TN).astype(bf)
    part[...] = made.reshape(A, 2, Y, 2, rows_v, D)
    q.send(n, part.at[:, :, :, 1 - p.c], bc, p.cp)
    dtab_ref[...] = dot(dlog[...], chosen)
    q.arrived(n, bc)
    pc[...] = (part[:, :, :, p.c].astype(f32) + bc[...].astype(f32)).astype(bf)
    n = n + 1
    for k in range(1, Y):
        q.send(n + k - 1, pc.at[:, :, lax.rem(p.y + k, Y)], by.at[k - 1], p.yp(k))
    total = pc[:, :, p.y].astype(f32)
    for k in range(1, Y):
        q.arrived(n + k - 1, by.at[k - 1])
        total = total + by[k - 1].astype(f32)
    py[...] = total.astype(bf)
    n = n + Y - 1
    q.send(n, py.at[:, 1 - p.x], bx, p.xp)
    q.arrived(n, bx)
    n = n + 1
    px[...] = (py[:, p.x].astype(f32) + bx[...].astype(f32)).astype(bf)
    for k in range(1, A):
        q.send(n + k - 1, px.at[p.to_a(k)], bz.at[k - 1], p.zp(k))
    total = px[p.a].astype(f32)
    for k in range(1, A):
        q.arrived(n + k - 1, bz.at[k - 1])
        total = total + bz[k - 1].astype(f32)
    n = n + A - 1
    out_ref[p.v] = total.astype(bf)
    for k in range(1, n_v):
        q.send(n + k - 1, out_ref.at[p.v], out_ref.at[p.v], partners[k - 1])
    for k in range(1, n_v):
        q.arrived(n + k - 1, out_ref.at[lax.rem(p.v + n_v - k, n_v)])
    q.finish()


def run_head(chosen, table, labels, n_dp, n_v):
    f32, kind = jnp.float32, chosen.dtype
    A, Y = n_dp // 2, n_v // 2
    _, rows_v, width = chosen.shape
    rows, total_m = table.shape[0], n_dp * MLM_PAD
    tall = total_m // 128
    count = Gather.count(n_dp, n_v) + n_dp - 1 + n_v - 1 + 1 + Y - 1 + 1 + A - 1 + n_v - 1
    vmem = pl.BlockSpec(memory_space=pltpu.VMEM)
    return pl.pallas_call(
        functools.partial(head_kernel, n_dp, n_v),
        out_shape=[
            jax.ShapeDtypeStruct(chosen.shape, kind),
            jax.ShapeDtypeStruct(table.shape, f32),
            jax.ShapeDtypeStruct((8, 128), f32),
        ],
        in_specs=[vmem] * 4,
        out_specs=[vmem] * 3,
        scratch_shapes=[
            pltpu.VMEM((n_dp,) + chosen.shape, kind),
            pltpu.VMEM((rows, total_m), f32),
            pltpu.VMEM((rows, total_m), kind),
            pltpu.VMEM((3 * tall, 128), f32),
            pltpu.VMEM((n_dp, 3 * tall, 128), f32),
            pltpu.VMEM((n_v, 3 * tall, 128), f32),
            pltpu.VMEM((tall, 128), f32),
            pltpu.VMEM((A, 2, Y, 2, rows_v, width), kind),
            pltpu.VMEM((A, 2, Y, rows_v, width), kind),
            pltpu.VMEM((Y - 1, A, 2, rows_v, width), kind),
            pltpu.VMEM((A, rows_v, width), kind),
            pltpu.VMEM((A - 1, rows_v, width), kind),
            pltpu.VMEM((A, 2, Y, rows_v, width), kind),
            pltpu.VMEM((A, 2, rows_v, width), kind),
            pltpu.VMEM((A, rows_v, width), kind),
            pltpu.SemaphoreType.DMA((count,)),
            pltpu.SemaphoreType.DMA((count,)),
        ],
        compiler_params=pltpu.CompilerParams(
            collective_id=2, has_side_effects=True, vmem_limit_bytes=56 << 20
        ),
    )(chosen, table, labels.reshape(1, total_m), labels.reshape(tall, 128))


def norm_kernel(n_dp, n_v, layer_ref, small_ref, table_ref, out_ref, sd, sv, ss, rs):
    f32 = jnp.float32
    d, v = lax.axis_index("dp"), lax.axis_index("vocab")
    others = [(lax.rem(d + k, n_dp), v) for k in range(1, n_dp)]
    partners = [(d, lax.rem(v + k, n_v)) for k in range(1, n_v)]
    sem = pltpu.get_barrier_semaphore()
    for partner in others + partners:
        pl.semaphore_signal(sem, 1, device_id=partner, device_id_type=MESH)

    def square(values):
        values = values.astype(f32)
        values = values * values
        while values.ndim > 2:
            values = jnp.sum(values, axis=0)
        return jnp.sum(jnp.sum(values, axis=0, keepdims=True), axis=1, keepdims=True)

    total = square(table_ref[...])
    total = total + jnp.where(v == 0, square(layer_ref[...]), 0.0)
    total = total + jnp.where((v == 0) & (d == 0), square(small_ref[...]), 0.0)
    sd[d] = jnp.broadcast_to(total, sd.shape[1:])
    pl.semaphore_wait(sem, n_dp - 1 + n_v - 1)
    q = Copies((d, v), ss, rs)
    for k in range(1, n_dp):
        q.send(k - 1, sd.at[d], sd.at[d], others[k - 1])
    for k in range(1, n_dp):
        q.arrived(k - 1, sd.at[lax.rem(d + n_dp - k, n_dp)])
    sv[v] = jnp.sum(sd[...], axis=0)
    for k in range(1, n_v):
        q.send(n_dp + k - 2, sv.at[v], sv.at[v], partners[k - 1])
    for k in range(1, n_v):
        q.arrived(n_dp + k - 2, sv.at[lax.rem(v + n_v - k, n_v)])
    out_ref[...] = jnp.sum(sv[...], axis=0)
    q.finish()


def run_norm(layer, small, table, n_dp, n_v):
    f32 = jnp.float32
    vmem = pl.BlockSpec(memory_space=pltpu.VMEM)
    count = n_dp + n_v - 2
    return pl.pallas_call(
        functools.partial(norm_kernel, n_dp, n_v),
        out_shape=jax.ShapeDtypeStruct((8, 128), f32),
        in_specs=[vmem] * 3,
        out_specs=vmem,
        scratch_shapes=[
            pltpu.VMEM((n_dp, 8, 128), f32),
            pltpu.VMEM((n_v, 8, 128), f32),
            pltpu.SemaphoreType.DMA((count,)),
            pltpu.SemaphoreType.DMA((count,)),
        ],
        compiler_params=pltpu.CompilerParams(
            collective_id=4, has_side_effects=True, vmem_limit_bytes=40 << 20
        ),
    )(layer, small, table)


def adam_kernel(n_dp, cuts, scal_ref, table_g, block_g, small_g, *refs):
    f32 = jnp.float32
    n = 7
    ins, outs, bufs = refs[: 3 * n], refs[3 * n : 6 * n], refs[6 * n : 9 * n]
    up_g, ext_g, bias_g, sem_i, sem_o = refs[9 * n :]
    loads = [pltpu.make_async_copy(ins[k], bufs[k], sem_i.at[k]) for k in range(3 * n)]
    for copy in loads:
        copy.start()
    coef, one_hat, two_hat = scal_ref[0], scal_ref[1], scal_ref[2]
    rb, width = block_g.shape[1:]
    stores = []

    def change(i, at, cols, grad, rate=LR_BIG):
        master, first, second = bufs[3 * i : 3 * i + 3]
        g = grad.astype(f32) * coef
        one = BETA_ONE * first[at, cols] + (1.0 - BETA_ONE) * g
        two = BETA_TWO * second[at, cols] + (1.0 - BETA_TWO) * g * g
        old = master[at, cols]
        first[at, cols] = one
        second[at, cols] = two
        move = one * one_hat / (jnp.sqrt(two * two_hat) + ADAM_EPS) + DECAY * old
        master[at, cols] = old - rate * move

    def begin(i):
        for copy in loads[3 * i : 3 * i + 3]:
            copy.wait()

    def end(i):
        for k in range(3 * i, 3 * i + 3):
            copy = pltpu.make_async_copy(bufs[k], outs[k], sem_o.at[k])
            copy.start()
            stores.append(copy)

    def chunks(rows, act):
        size = 32 if rows % 32 == 0 else rows
        if size == rows:
            act(pl.ds(0, rows))
        else:

            def body(c, _):
                act(pl.ds(pl.multiple_of(c * size, size), size))
                return 0

            lax.fori_loop(0, rows // size, body, 0)

    every = slice(None)
    begin(0)
    chunks(bufs[0].shape[0], lambda at: change(0, at, every, table_g[at, :]))
    end(0)
    for i, blocks in ((1, range(3)), (2, range(3, 4))):
        begin(i)
        for j in blocks:
            for s in range(cuts):
                cols = pl.ds((j - blocks[0]) * D + s * width, width)
                chunks(rb, lambda at: change(i, at, cols, block_g[j * cuts + s, at, :]))
        end(i)
    begin(3)
    for j in range(4):
        for s in range(cuts):
            block = block_g[(4 + j) * cuts + s].astype(f32)
            for d in range(n_dp // cuts):
                to = (s * (n_dp // cuts) + d) * 4 * rb + j * rb
                up_g[:, to : to + rb] = block[:, d * rb : (d + 1) * rb]
    chunks(rb, lambda at: change(3, at, every, up_g[at, :]))
    end(3)
    begin(4)
    for j in range(4):
        for s in range(cuts):
            cols = pl.ds(s * width, width)

            def down(at, j=j, s=s, cols=cols):
                change(4, pl.ds(j * rb + at.start, at.size), cols, block_g[(8 + j) * cuts + s, at, :])

            chunks(rb, down)
    end(4)
    ext_g[...] = small_g[: ext_g.shape[0], :].astype(f32)
    begin(5)
    done = EXT // 8 * 8
    for at in (pl.ds(0, done // 2), pl.ds(done // 2, done // 2), pl.ds(done, EXT - done)):
        change(5, at, every, ext_g[at, :], LR_SMALL)
    end(5)
    begin(6)
    for j in range(4):
        for d in range(n_dp):
            piece = ext_g[EXT + 5 + j : EXT + 6 + j, d * rb : (d + 1) * rb]
            bias_g[:, d * 4 * rb + j * rb : d * 4 * rb + (j + 1) * rb] = piece
    for k in range(12):
        if 5 <= k < 9:
            grad = bias_g[:, (k - 5) * D : (k - 4) * D]
        else:
            grad = ext_g[EXT + k : EXT + k + 1, :]
        change(6, every, pl.ds(k * D, D), grad, LR_SMALL)
    end(6)
    for copy in stores:
        copy.wait()


def run_adam(scalars, table_g, block_g, small_g, states, n_dp, cuts):
    hbm = pl.BlockSpec(memory_space=pl.ANY)
    vmem = pl.BlockSpec(memory_space=pltpu.VMEM)
    flat = [array for state in states for array in state]
    n = len(flat)
    rb = block_g.shape[1]
    return pl.pallas_call(
        functools.partial(adam_kernel, n_dp, cuts),
        out_shape=[jax.ShapeDtypeStruct(a.shape, a.dtype) for a in flat],
        in_specs=[pl.BlockSpec(memory_space=pltpu.SMEM), vmem, vmem, vmem] + [hbm] * n,
        out_specs=[hbm] * n,
        scratch_shapes=[pltpu.VMEM(a.shape, a.dtype) for a in flat]
        + [
            pltpu.VMEM((rb, FF), jnp.float32),
            pltpu.VMEM((ceil_to(EXT + 12, 16), D), jnp.float32),
            pltpu.VMEM((1, FF), jnp.float32),
            pltpu.SemaphoreType.DMA((n,)),
            pltpu.SemaphoreType.DMA((n,)),
        ],
        compiler_params=pltpu.CompilerParams(vmem_limit_bytes=56 << 20),
    )(scalars, table_g, block_g, small_g, *flat)


def grads_kernel(n_dp, n_v, g_ref, e_ref, t_ref, g_out, e_out, t_out, bx, px, bz, ebx, epx, ebz, ss, rs, ls):
    f32, bf = jnp.float32, jnp.bfloat16
    p = Place(n_dp, n_v)
    A, Y = p.A, p.Y
    p.barrier([(p.to_a(k) * 2 + 1 - p.x, p.v) for k in range(1, A)])
    q = Copies(p.me, ss, rs)
    groups = g_ref.shape[0]
    n = 0
    for g in range(groups):
        q.send(n + g, g_ref.at[g, :, 1 - p.x], bx.at[g], p.xp)
    x0 = n
    n = n + groups
    q.send(n, e_ref.at[:, 1 - p.x], ebx, p.xp)
    ex0 = n
    n = n + 1
    t0 = n
    for k in range(1, n_dp):
        to = lax.rem(p.d + k, n_dp)
        q.send(t0 + k - 1, t_ref.at[to], t_out.at[p.d], (to, p.v))
    n = n + n_dp - 1
    local = pltpu.make_async_copy(t_ref.at[p.d], t_out.at[p.d], ls)
    local.start()
    z0 = n
    n = n + groups * (A - 1)
    ez0 = n
    n = n + A - 1
    for g in range(groups):
        q.arrived(x0 + g, bx.at[g])
        for k in range(1, A + 1):
            to = p.to_a(k)
            px[g, to] = (g_ref[g, to, p.x].astype(f32) + bx[g, to].astype(f32)).astype(bf)
            if k < A:
                q.send(z0 + g * (A - 1) + k - 1, px.at[g, to], bz.at[g, k - 1], p.zp(k))
    q.arrived(ex0, ebx)
    epx[...] = (e_ref[:, p.x].astype(f32) + ebx[...].astype(f32)).astype(bf)
    for k in range(1, A):
        q.send(ez0 + k - 1, epx.at[p.to_a(k)], ebz.at[k - 1], p.zp(k))
    total = epx[p.a].astype(f32)
    for k in range(1, A):
        q.arrived(ez0 + k - 1, ebz.at[k - 1])
        total = total + ebz[k - 1].astype(f32)
    e_out[p.d, p.v] = total.astype(bf)
    small = Gather(p, q, n, lambda d, v: e_out.at[d, v])
    n = small.end
    small.start()
    y0 = n
    n = n + groups * (Y - 1)
    c0 = n
    for g in range(groups):
        total = px[g, p.a].astype(f32)
        for k in range(1, A):
            q.arrived(z0 + g * (A - 1) + k - 1, bz.at[g, k - 1])
            total = total + bz[g, k - 1].astype(f32)
        mine = g_out.at[g * n_v + p.v]
        g_out[g * n_v + p.v] = total.astype(bf)
        for k in range(1, Y):
            q.send(y0 + g * (Y - 1) + k - 1, mine, mine, p.yp(k))
        q.send(c0 + g * Y, mine, mine, p.cp)
    small.step_a()
    small.step_x()
    for g in range(groups):
        for j in range(1, Y):
            piece = g_out.at[g * n_v + p.from_y(j) * 2 + p.c]
            q.arrived(y0 + g * (Y - 1) + j - 1, piece)
            q.send(c0 + g * Y + j, piece, piece, p.cp)
    small.step_y()
    for g in range(groups):
        for j in range(Y):
            q.arrived(c0 + g * Y + j, g_out.at[g * n_v + p.from_y(j) * 2 + 1 - p.c])
    small.step_c()
    for k in range(1, n_dp):
        q.arrived(t0 + k - 1, t_out.at[lax.rem(p.d + n_dp - k, n_dp)])
    q.finish()
    local.wait()


def reduce_grads(grads, extras, tokens, n_dp, n_v):
    A, Y = n_dp // 2, n_v // 2
    groups, _, _, rows, width = grads.shape
    e_rows, e_width = extras.shape[2:]
    kind = grads.dtype
    count = groups * (1 + A - 1 + Y - 1 + Y) + 1 + (n_dp - 1) + (A - 1) + Gather.count(n_dp, n_v)
    vmem = pl.BlockSpec(memory_space=pltpu.VMEM)
    return pl.pallas_call(
        functools.partial(grads_kernel, n_dp, n_v),
        out_shape=(
            jax.ShapeDtypeStruct((groups * n_v, rows, width), kind),
            jax.ShapeDtypeStruct((n_dp, n_v, e_rows, e_width), kind),
            jax.ShapeDtypeStruct(tokens.shape, tokens.dtype),
        ),
        in_specs=[vmem, vmem, vmem],
        out_specs=(vmem, vmem, vmem),
        scratch_shapes=[
            pltpu.VMEM((groups, A, rows, width), kind),
            pltpu.VMEM((groups, A, rows, width), kind),
            pltpu.VMEM((groups, A - 1, rows, width), kind),
            pltpu.VMEM((A, e_rows, e_width), kind),
            pltpu.VMEM((A, e_rows, e_width), kind),
            pltpu.VMEM((A - 1, e_rows, e_width), kind),
            pltpu.SemaphoreType.DMA((count,)),
            pltpu.SemaphoreType.DMA((count,)),
            pltpu.SemaphoreType.DMA,
        ],
        compiler_params=pltpu.CompilerParams(
            collective_id=3, has_side_effects=True, vmem_limit_bytes=56 << 20
        ),
    )(grads, extras, tokens)


def lane_mean(values):
    return jnp.sum(values, axis=-1, keepdims=True) * (1.0 / D)


def norm_parts(values):
    centered = values - lane_mean(values)
    rate = lax.rsqrt(lane_mean(centered * centered) + LN_EPS)
    return centered * rate, rate


def norm_back(values, grad, gain):
    unit, rate = norm_parts(values)
    scaled = grad * gain
    d_values = rate * (scaled - lane_mean(scaled) - unit * lane_mean(scaled * unit))
    return (
        d_values,
        jnp.sum(grad * unit, axis=0, keepdims=True),
        jnp.sum(grad, axis=0, keepdims=True),
    )


def dot(left, right, dims=((1,), (0,))):
    return lax.dot_general(left, right, (dims, ((), ())), preferred_element_type=jnp.float32)


NT = ((1,), (1,))
TN = ((0,), (0,))


def allowed_mask(row_ref, col_ref, seg):
    row, col = row_ref[seg], col_ref[seg]
    return (row == col) | (row < 0) | (col < 0)


def forward_kernel(
    w_hbm, tok_ref, slot_ref, row_ref, col_ref, reset_ref, vec_ref, ext_ref, pos_ref,
    x_o, hc_o, proj_o, p_o, one_o, mid_o, gp_o, act_o, two_o, chosen_o,
    w, x, hc, proj, probs, one, mid, gp, act, two, mask, hid, final, sem_w, sem_o,
):
    bf, f32 = jnp.bfloat16, jnp.float32
    loads = [pltpu.make_async_copy(w_hbm.at[:, b], w.at[b], sem_w.at[b]) for b in range(12)]
    for load in loads:
        load.start()
    waited = set()

    def weight(b):
        if b not in waited:
            loads[b].wait()
            waited.add(b)
        return w[b].reshape(D, D)

    stores = []

    def store(src, dst):
        copy = pltpu.make_async_copy(src, dst, sem_o.at[len(stores)])
        copy.start()
        stores.append(copy)

    vec = [vec_ref[k : k + 1, :] for k in range(12)]
    b_q, b_v, b_o, g_one, b_one = vec[:5]
    b_up, b_down, g_two, b_two = vec[5:9], vec[9], vec[10], vec[11]
    gain_e, bias_e = ext_ref[404:405, :], ext_ref[405:406, :]
    lane = lax.broadcasted_iota(jnp.int32, (1, 2 * HD), 1)
    low_half = lane < HD
    for seg in range(SEGS):
        rows = pl.ds(seg * ROWS, ROWS)
        held = lax.broadcasted_iota(jnp.int32, (1, tok_ref.shape[0]), 1).astype(f32)
        onehot = (slot_ref[rows, :] == held).astype(f32).astype(bf)
        x[seg] = dot(onehot, tok_ref[...]) + ext_ref[:ROWS, :]
        x[seg, ROWS - MEM :, :] += ext_ref[ROWS + MEM : ROWS + 2 * MEM, :]
        first = ext_ref[ROWS : ROWS + MEM, :]
        if seg == 0:
            x[seg, :MEM, :] += first
        else:
            x[seg, :MEM, :] += jnp.where(reset_ref[seg - 1] > 0, first, hid[ROWS - MEM :, :])
        store(x.at[seg], x_o.at[seg])
        mask[...] = allowed_mask(row_ref, col_ref, seg).astype(f32)
        unit, _ = norm_parts(x[seg])
        h = unit * gain_e + bias_e
        hid[...] = h
        h_low = h.astype(bf)
        hc[0, rows, :] = h_low
        for k, bias in ((0, b_q), (1, None), (2, b_v)):
            made = dot(h_low, weight(k))
            proj[k, rows, :] = (made if bias is None else made + bias).astype(bf)
        store(hc.at[0, rows], hc_o.at[0, rows])
        store(proj.at[:, rows], proj_o.at[:, rows])
        for pair in range(HEADS // 2):
            cols = pl.ds(pair * 2 * HD, 2 * HD)
            query, keyed, value = (proj[k, rows, cols] for k in range(3))
            query = query * jnp.asarray(HD ** (-0.5), bf)
            parts = []
            for side in range(2):
                keep = low_half if side == 0 else ~low_half
                scores = dot(jnp.where(keep, query, jnp.zeros_like(query)), keyed, NT)
                scores = jnp.where(mask[...] > 0, scores, MASKED)
                expd = jnp.exp(scores - jnp.max(scores, axis=-1, keepdims=True))
                p_low = (expd * (1.0 / jnp.sum(expd, axis=-1, keepdims=True))).astype(bf)
                probs[seg, pair * 2 + side] = p_low
                parts.append(dot(p_low, value))
            hc[1, rows, cols] = jnp.where(low_half, parts[0], parts[1]).astype(bf)
        store(probs.at[seg], p_o.at[seg])
        store(hc.at[1, rows], hc_o.at[1, rows])
        sum_one = hid[...] + (dot(hc[1, rows, :], weight(3)) + b_o)
        one[seg] = sum_one
        store(one.at[seg], one_o.at[seg])
        unit, _ = norm_parts(sum_one)
        mid_now = unit * g_one + b_one
        mid_low = mid_now.astype(bf)
        mid[rows, :] = mid_low
        store(mid.at[rows], mid_o.at[rows])
        for j in range(4):
            up = dot(mid_low, weight(4 + j)) + b_up[j]
            half = 0.5 * (1.0 + lax.erf(up * 0.7071067811865476))
            gp[j, rows, :] = (half + up * jnp.exp(-0.5 * up * up) * 0.3989422804014327).astype(bf)
            act[j, rows, :] = (up * half).astype(bf)
        store(gp.at[:, rows], gp_o.at[:, rows])
        store(act.at[:, rows], act_o.at[:, rows])
        total = mid_now + b_down
        for j in range(4):
            total = total + dot(act[j, rows, :], weight(8 + j))
        two[seg] = total
        store(two.at[seg], two_o.at[seg])
        unit, _ = norm_parts(total)
        h = unit * g_two + b_two
        hid[...] = h
        final[rows, :] = h.astype(bf)
    at = lax.broadcasted_iota(jnp.int32, (MLM_PAD, SEGS * ROWS), 1)
    chosen_o[...] = dot((at == pos_ref[...]).astype(bf), final[...]).astype(bf)
    for copy in stores:
        copy.wait()


def run_forward(w_all, tok, slot, marks, reset, vec, ext, pos):
    f32, bf = jnp.float32, jnp.bfloat16
    n = SEGS * ROWS
    saved = [
        ((SEGS, ROWS, D), f32),
        ((2, n, D), bf),
        ((3, n, D), bf),
        ((SEGS, HEADS, ROWS, ROWS), bf),
        ((SEGS, ROWS, D), f32),
        ((n, D), bf),
        ((4, n, D), bf),
        ((4, n, D), bf),
        ((SEGS, ROWS, D), f32),
    ]
    hbm = pl.BlockSpec(memory_space=pl.ANY)
    vmem = pl.BlockSpec(memory_space=pltpu.VMEM)
    return pl.pallas_call(
        forward_kernel,
        out_shape=[jax.ShapeDtypeStruct(s, k) for s, k in saved]
        + [jax.ShapeDtypeStruct((MLM_PAD, D), bf)],
        in_specs=[hbm] + [vmem] * 4 + [pl.BlockSpec(memory_space=pltpu.SMEM), vmem, vmem, vmem],
        out_specs=[hbm] * len(saved) + [vmem],
        scratch_shapes=[pltpu.VMEM((12, w_all.shape[0]) + w_all.shape[2:], bf)]
        + [pltpu.VMEM(s, k) for s, k in saved]
        + [
            pltpu.VMEM((ROWS, ROWS), f32),
            pltpu.VMEM((ROWS, D), f32),
            pltpu.VMEM((n, D), bf),
            pltpu.SemaphoreType.DMA((12,)),
            pltpu.SemaphoreType.DMA((SEGS * 10,)),
        ],
        compiler_params=pltpu.CompilerParams(vmem_limit_bytes=60 << 20),
    )(w_all, tok, slot[:, None], marks[:, None, :], marks[:, :, None], reset, vec, ext, pos[:, None])


def backward_kernel(
    cuts,
    w_hbm, x_i, hc_i, proj_i, p_i, one_i, mid_i, gp_i, act_i, two_i,
    dch_ref, reset_ref, vec_ref, ext_ref, pos_ref, give_ref, slot_ref, v_ref,
    share_o, small_o, dpack_o, dtok,
    w, x, hc, right, probs, one, mid, rup, act, two, rdown, grad, dmem, sem_w, sem_i,
):
    bf, f32 = jnp.bfloat16, jnp.float32
    small_o[...] = jnp.zeros_like(small_o)
    loads = {}
    state = {"n": 0}

    def load(name, src, dst):
        copy = pltpu.make_async_copy(src, dst, sem_i.at[state["n"]])
        state["n"] += 1
        copy.start()
        loads[name] = copy

    def need(name):
        if name in loads:
            loads.pop(name).wait()

    wl = [pltpu.make_async_copy(w_hbm.at[:, b], w.at[b], sem_w.at[b]) for b in range(12)]
    waited = set()

    def weight(b):
        if b not in waited:
            wl[b].wait()
            waited.add(b)
        return w[b].reshape(D, D)

    order = list(reversed(range(SEGS)))
    for i, seg in enumerate(order):
        rows = pl.ds(seg * ROWS, ROWS)
        load(("two", seg), two_i.at[seg], two.at[seg])
        if i == 0:
            for b in range(8, 12):
                wl[b].start()
        load(("gp", seg), gp_i.at[:, rows], rup.at[:, rows])
        if i == 0:
            for b in range(4, 8):
                wl[b].start()
        load(("one", seg), one_i.at[seg], one.at[seg])
        if i == 0:
            wl[3].start()
            load(("p", seg), p_i.at[seg], probs)
        load(("proj", seg), proj_i.at[:, rows], right.at[pl.ds(0, 3), rows])
        if i == 0:
            for b in range(3):
                wl[b].start()
        load(("x", seg), x_i.at[seg], x.at[seg])
    load("hc", hc_i, hc)
    load("mid", mid_i, mid)
    load("act", act_i, act)

    vec = [vec_ref[k : k + 1, :] for k in range(12)]
    g_one, g_two, gain_e = vec[3], vec[10], ext_ref[404:405, :]
    lane = lax.broadcasted_iota(jnp.int32, (1, 2 * HD), 1)
    low_half = lane < HD
    at = lax.broadcasted_iota(jnp.int32, (MLM_PAD, SEGS * ROWS), 1)
    at_pos = (at == pos_ref[...]).astype(bf)
    v0 = EXT

    def add_row(k, value):
        small_o[v0 + k : v0 + k + 1, :] += value

    def sums(values):
        return jnp.sum(values.astype(f32), axis=0, keepdims=True)

    for i, seg in enumerate(order):
        rows = pl.ds(seg * ROWS, ROWS)
        grad[...] = dot(at_pos[:, seg * ROWS : (seg + 1) * ROWS], dch_ref[...], TN)
        if i > 0:
            grad[ROWS - MEM :, :] += dmem[...]
        need(("two", seg))
        d_two, d_gain, d_shift = norm_back(two[seg], grad[...], g_two)
        add_row(10, d_gain)
        add_row(11, d_shift)
        r_down = d_two.astype(bf)
        rdown[rows, :] = r_down
        add_row(9, sums(r_down))
        need(("gp", seg))
        for j in range(4):
            r_up = (rup[j, rows, :].astype(f32) * dot(r_down, weight(8 + j), NT)).astype(bf)
            rup[j, rows, :] = r_up
            add_row(5 + j, sums(r_up))
        for j in range(4):
            d_two = d_two + dot(rup[j, rows, :], weight(4 + j), NT)
        need(("one", seg))
        d_one, d_gain, d_shift = norm_back(one[seg], d_two, g_one)
        add_row(3, d_gain)
        add_row(4, d_shift)
        grad[...] = d_one
        r_att = d_one.astype(bf)
        right[3, rows, :] = r_att
        add_row(2, sums(r_att))
        d_ctx = dot(r_att, weight(3), NT).astype(bf)
        need(("p", seg))
        need(("proj", seg))
        for pair in range(HEADS // 2):
            cols = pl.ds(pair * 2 * HD, 2 * HD)
            query, keyed, value = (right[k, rows, cols] for k in range(3))
            d_out = d_ctx[:, pair * 2 * HD : (pair + 1) * 2 * HD]
            made = []
            for side in range(2):
                keep = low_half if side == 0 else ~low_half
                p_low = probs[pair * 2 + side]
                p_now = p_low.astype(f32)
                d_p = dot(jnp.where(keep, d_out, jnp.zeros_like(d_out)), value, NT)
                weighted = p_now * d_p
                d_s = weighted - p_now * jnp.sum(weighted, axis=-1, keepdims=True)
                d_s = d_s.astype(bf)
                made.append((dot(d_s, keyed), dot(d_s, query, TN), dot(p_low, d_out, TN)))
            for k, scale in ((0, HD ** (-0.5)), (1, HD ** (-0.5)), (2, 1.0)):
                both = jnp.where(low_half, made[0][k], made[1][k]) * scale
                right[k, rows, cols] = both.astype(bf)
        if i + 1 < SEGS:
            load(("p", order[i + 1]), p_i.at[order[i + 1]], probs)
        d_h = grad[...]
        for k in range(3):
            d_h = d_h + dot(right[k, rows, :], weight(k), NT)
        add_row(0, sums(right[0, rows, :]))
        add_row(1, sums(right[2, rows, :]))
        need(("x", seg))
        d_x, d_gain, d_shift = norm_back(x[seg], d_h, gain_e)
        grad[...] = d_x
        dtok[rows, :] = d_x.astype(bf)
        small_o[:ROWS, :] += d_x
        small_o[ROWS + MEM : ROWS + 2 * MEM, :] += grad[ROWS - MEM :, :]
        small_o[404:405, :] += d_gain
        small_o[405:406, :] += d_shift
        d_read = grad[:MEM, :]
        if seg > 0:
            back = reset_ref[seg - 1] > 0
            small_o[ROWS : ROWS + MEM, :] += jnp.where(back, d_read, 0.0)
            dmem[...] = jnp.where(back, 0.0, d_read)
        else:
            small_o[ROWS : ROWS + MEM, :] += d_read
    dpack_o[...] = dot((give_ref[...] == slot_ref[...]).astype(bf), dtok[...]).astype(bf)
    need("hc")
    need("mid")
    need("act")
    v = v_ref[0]
    width = D // cuts
    block, cut = v // cuts, v % cuts
    cols = pl.ds(pl.multiple_of(cut * width, 128), width)
    share_o[0] = dot(hc[block // 3], right[block, :, cols], TN).astype(bf)
    share_o[1] = dot(mid[...], rup[block, :, cols], TN).astype(bf)
    share_o[2] = dot(act[block], rdown[:, cols], TN).astype(bf)


def run_backward(
    w_all, saved, d_chosen, reset, vec, ext, pos, give, slot, v_idx, cuts, small_rows
):
    f32, bf = jnp.float32, jnp.bfloat16
    n = SEGS * ROWS
    hbm = pl.BlockSpec(memory_space=pl.ANY)
    vmem = pl.BlockSpec(memory_space=pltpu.VMEM)
    smem = pl.BlockSpec(memory_space=pltpu.SMEM)
    return pl.pallas_call(
        functools.partial(backward_kernel, cuts),
        out_shape=[
            jax.ShapeDtypeStruct((3, D, D // cuts), bf),
            jax.ShapeDtypeStruct((small_rows, D), f32),
            jax.ShapeDtypeStruct((give.shape[0], D), bf),
            jax.ShapeDtypeStruct((n, D), bf),
        ],
        in_specs=[hbm] * 10 + [vmem, smem, vmem, vmem, vmem, vmem, vmem, smem],
        out_specs=[vmem] * 4,
        scratch_shapes=[
            pltpu.VMEM((12, w_all.shape[0]) + w_all.shape[2:], bf),
            pltpu.VMEM((SEGS, ROWS, D), f32),
            pltpu.VMEM((2, n, D), bf),
            pltpu.VMEM((4, n, D), bf),
            pltpu.VMEM((HEADS, ROWS, ROWS), bf),
            pltpu.VMEM((SEGS, ROWS, D), f32),
            pltpu.VMEM((n, D), bf),
            pltpu.VMEM((4, n, D), bf),
            pltpu.VMEM((4, n, D), bf),
            pltpu.VMEM((SEGS, ROWS, D), f32),
            pltpu.VMEM((n, D), bf),
            pltpu.VMEM((ROWS, D), f32),
            pltpu.VMEM((MEM, D), f32),
            pltpu.SemaphoreType.DMA((12,)),
            pltpu.SemaphoreType.DMA((SEGS * 6 + 4,)),
        ],
        compiler_params=pltpu.CompilerParams(vmem_limit_bytes=61 << 20),
    )(
        w_all, *saved, d_chosen, reset, vec, ext, pos[:, None],
        give[:, None], slot[None, :], v_idx,
    )


def ceil_to(value, unit):
    return -(-value // unit) * unit


def per_device(
    ids,
    docs,
    resets,
    mlm_pos,
    mlm_label,
    step,
    qkv_master,
    qkv_first,
    qkv_second,
    out_master,
    out_first,
    out_second,
    up_master,
    up_first,
    up_second,
    down_master,
    down_first,
    down_second,
    embed_master,
    embed_first,
    embed_second,
    vectors_master,
    vectors_first,
    vectors_second,
    extras_master,
    extras_first,
    extras_second,
):
    f32, bf = jnp.float32, jnp.bfloat16
    n_dp = lax.axis_size("dp")
    n_v = lax.axis_size("vocab")
    d_idx = lax.axis_index("dp")
    v_idx = lax.axis_index("vocab")
    own_rows = embed_master.shape[0]
    tokens_n = SEGS * SEG
    rb = qkv_master.shape[1]
    cuts = max(1, n_v // 4)
    width = D // cuts
    groups = 12 * cuts // n_v

    def to_blocks(qkv, out, up, down):
        full = jnp.concatenate(
            [
                qkv[0].reshape(rb, 3, D).transpose(1, 0, 2),
                out,
                up[0].reshape(rb, n_dp, 4, rb).transpose(2, 0, 1, 3).reshape(4, rb, D),
                down[0].reshape(4, rb, D),
            ]
        )
        return full.reshape(12, rb, cuts, width).transpose(0, 2, 1, 3).reshape(12 * cuts, rb, width)

    ints = jnp.concatenate([ids[0], mlm_label[0]])[None]
    ints = jnp.pad(ints, ((0, 0), (0, ceil_to(ints.shape[1], 128) - ints.shape[1])), constant_values=-1)
    cap = ceil_to(2 * tokens_n // (n_dp * n_v) + 2, 16)
    table = embed_master.astype(bf)
    blocks = to_blocks(
        qkv_master.astype(bf), out_master.astype(bf), up_master.astype(bf), down_master.astype(bf)
    )
    w_all, tok_all, ints_all, pick, slots, most = run_front(blocks, table, ints, cap, n_dp, n_v)
    if cuts > 1 or rb % 16:
        w_all = w_all.reshape(n_dp, 12, cuts, rb, width).transpose(1, 0, 3, 2, 4).reshape(1, 12, D, D)
    ids_all = ints_all[:, 0, :tokens_n]
    labels_all = ints_all[:, 0, tokens_n : tokens_n + MLM]
    labels_all = jnp.pad(labels_all, ((0, 0), (0, MLM_PAD - MLM)), constant_values=-1)
    overflow = most[0, 0] >= cap

    def padded(values):
        values = values.reshape((SEGS, SEG) + values.shape[1:])
        edges = ((0, 0), (MEM, MEM)) + ((0, 0),) * (values.ndim - 2)
        values = jnp.pad(values, edges, constant_values=-1)
        return values.reshape((SEGS * ROWS,) + values.shape[2:])

    slot = padded(lax.dynamic_index_in_dim(slots, d_idx, keepdims=False)[:tokens_n])

    def packed_tokens(_):
        return tok_all.reshape(n_dp * n_v * cap, D), slot

    def whole_tokens(_):
        whole = lax.all_gather(table, "dp", axis=0, tiled=True)
        at = jnp.arange(n_dp * own_rows, dtype=jnp.int32)
        row_ids = (at // own_rows * n_v + v_idx) * own_rows + at % own_rows
        onehot = (ids[0][:, None] == row_ids[None, :]).astype(bf)
        rows = lax.psum(jnp.dot(onehot, whole, preferred_element_type=f32).astype(bf), "vocab")
        rows = jnp.pad(rows, ((0, n_dp * n_v * cap - tokens_n), (0, 0)))
        return rows, padded(jnp.arange(tokens_n, dtype=jnp.int32).astype(f32))

    token_rows, token_slot = lax.cond(overflow, whole_tokens, packed_tokens, 0)
    marks = jnp.pad(docs.reshape(SEGS, SEG), ((0, 0), (MEM, MEM)), constant_values=-1)
    vec = vectors_master[0].reshape(12, D)
    b_up = vec[5:9].reshape(n_dp, 4, rb).transpose(1, 0, 2).reshape(4, D)
    vec = jnp.concatenate([vec[:5], b_up, vec[9:]])
    positions = mlm_pos[0]
    at_rows = positions // SEG * ROWS + MEM + positions % SEG
    at_rows = jnp.concatenate([at_rows, jnp.full((MLM_PAD - MLM,), -1, jnp.int32)])
    *saved, chosen = run_forward(w_all, token_rows, token_slot, marks, resets[0], vec, extras_master, at_rows)
    rows_v = MLM_PAD // n_v
    d_chosen, d_table, loss = run_head(chosen.reshape(n_v, rows_v, D), table, labels_all, n_dp, n_v)
    loss = loss[0, 0]
    d_chosen = d_chosen.reshape(MLM_PAD, D)
    small_rows = EXT + 12
    e_rows = ceil_to(-(-small_rows // (n_dp * n_v)), 16)
    at = jnp.arange(n_dp * cap, dtype=jnp.int32)
    give = ((at // cap * n_v + v_idx) * cap + at % cap).astype(f32)
    shares, small, d_packed, d_tok = run_backward(
        w_all,
        saved,
        d_chosen,
        resets[0],
        vec,
        extras_master,
        at_rows,
        give,
        slot,
        v_idx[None],
        cuts,
        ceil_to(small_rows, 8),
    )
    shares = shares.reshape(groups, n_dp // 2, 2, rb, width)
    small = jnp.pad(small.astype(bf), ((0, e_rows * n_dp * n_v - small.shape[0]), (0, 0)))
    small = small.reshape(n_dp // 2, 2, n_v, e_rows, D)
    small = lax.dynamic_index_in_dim(small, v_idx, axis=2, keepdims=False)
    d_packed = d_packed.reshape(n_dp, cap, D)
    g_blocks, small_all, d_packed_all = reduce_grads(shares, small, d_packed, n_dp, n_v)

    def packed_d_table(_):
        return jnp.einsum(
            "tv,td->vd", pick, d_packed_all.reshape(n_dp * cap, D), preferred_element_type=f32
        )

    def whole_d_table(_):
        d_all = d_tok.reshape(SEGS, ROWS, D)[:, MEM : MEM + SEG].reshape(tokens_n, D)
        d_all = lax.all_gather(d_all, "dp", axis=0, tiled=True)
        row_ids = (d_idx * n_v + v_idx) * own_rows + jnp.arange(own_rows, dtype=jnp.int32)
        onehot = (ids_all.reshape(-1)[:, None] == row_ids[None, :]).astype(bf)
        return jnp.einsum("tv,td->vd", onehot, d_all, preferred_element_type=f32)

    s_table = d_table + lax.cond(overflow, whole_d_table, packed_d_table, 0)
    small_all = small_all.reshape(n_dp * n_v * e_rows, D)
    norm = jnp.sqrt(run_norm(g_blocks, small_all, s_table, n_dp, n_v)[0, 0])
    coef = jnp.minimum(1.0, CLIP / (norm + 1e-06))
    t = step[0].astype(f32)
    scalars = jnp.stack([coef, 1.0 / (1.0 - BETA_ONE**t), 1.0 / (1.0 - BETA_TWO**t)])
    states = (
        (embed_master, embed_first, embed_second),
        (qkv_master[0], qkv_first[0], qkv_second[0]),
        (out_master[0], out_first[0], out_second[0]),
        (up_master[0], up_first[0], up_second[0]),
        (down_master[0], down_first[0], down_second[0]),
        (extras_master, extras_first, extras_second),
        (vectors_master, vectors_first, vectors_second),
    )
    new = run_adam(scalars, s_table, g_blocks, small_all, states, n_dp, cuts)
    layer = [value[None] for value in new[3:15]]
    return (loss, norm, *layer, *new[:3], *new[18:], *new[15:18])


def solution(mesh):
    in_specs = (
        P("dp", None),
        P("dp", None),
        P("dp", None),
        P("dp", None),
        P("dp", None),
        P(),
        P(None, "dp", None),
        P(None, "dp", None),
        P(None, "dp", None),
        P(None, "dp", None),
        P(None, "dp", None),
        P(None, "dp", None),
        P(None, "dp", None),
        P(None, "dp", None),
        P(None, "dp", None),
        P(None, "dp", None),
        P(None, "dp", None),
        P(None, "dp", None),
        P(("dp", "vocab"), None),
        P(("dp", "vocab"), None),
        P(("dp", "vocab"), None),
        P(),
        P(),
        P(),
        P(),
        P(),
        P(),
    )
    out_specs = (
        P(),
        P(),
        P(None, "dp", None),
        P(None, "dp", None),
        P(None, "dp", None),
        P(None, "dp", None),
        P(None, "dp", None),
        P(None, "dp", None),
        P(None, "dp", None),
        P(None, "dp", None),
        P(None, "dp", None),
        P(None, "dp", None),
        P(None, "dp", None),
        P(None, "dp", None),
        P(("dp", "vocab"), None),
        P(("dp", "vocab"), None),
        P(("dp", "vocab"), None),
        P(),
        P(),
        P(),
        P(),
        P(),
        P(),
    )
    return jax.shard_map(
        per_device, mesh=mesh, in_specs=in_specs, out_specs=out_specs, check_vma=False
    )
```

```python
import functools

import jax
import jax.numpy as jnp
from jax import lax
from jax.experimental import pallas as pl
from jax.experimental.pallas import tpu as pltpu
from jax.sharding import PartitionSpec as P

D = 768
HEADS = 12
HD = 64
FF = 3072
MEM = 10
SEG = 364
SEGS = 2
LAYERS = 1
MLM = 112
ROWS = 384


BETA_ONE = 0.9
BETA_TWO = 0.999
ADAM_EPS = 1e-08
DECAY = 0.01
LN_EPS = 1e-06
CLIP = 0.02
LR_BIG = 0.04
LR_SMALL = 0.5
MASKED = -1000000000.0


MESH = pl.DeviceIdType.MESH
MLM_PAD = 128
EXT = ROWS + 2 * MEM + 2


class Place:
    def __init__(self, n_dp, n_v):
        self.A, self.Y = n_dp // 2, n_v // 2
        self.d, self.v = lax.axis_index("dp"), lax.axis_index("vocab")
        self.a, self.x = self.d // 2, self.d % 2
        self.y, self.c = self.v // 2, self.v % 2
        self.me = (self.d, self.v)
        self.xp = (self.d + 1 - 2 * self.x, self.v)
        self.cp = (self.d, self.v + 1 - 2 * self.c)

    def from_a(self, k):
        return lax.rem(self.a + self.A - k, self.A)

    def to_a(self, k):
        return lax.rem(self.a + k, self.A)

    def from_y(self, k):
        return lax.rem(self.y + self.Y - k, self.Y)

    def zp(self, k):
        return (self.to_a(k) * 2 + self.x, self.v)

    def yp(self, k):
        return (self.d, lax.rem(self.y + k, self.Y) * 2 + self.c)

    def barrier(self, extra=()):
        sem = pltpu.get_barrier_semaphore()
        partners = [self.zp(k) for k in range(1, self.A)] + [self.xp]
        partners += [self.yp(k) for k in range(1, self.Y)] + [self.cp] + list(extra)
        for partner in partners:
            pl.semaphore_signal(sem, 1, device_id=partner, device_id_type=MESH)
        pl.semaphore_wait(sem, len(partners))


class Copies:
    def __init__(self, me, send_sem, recv_sem):
        self.me, self.send_sem, self.recv_sem, self.started = me, send_sem, recv_sem, []

    def send(self, number, src, dst, partner):
        copy = pltpu.make_async_remote_copy(
            src, dst, self.send_sem.at[number], self.recv_sem.at[number], partner, MESH
        )
        copy.start()
        self.started.append(copy)

    def arrived(self, number, dst):
        pltpu.make_async_remote_copy(
            dst, dst, self.send_sem.at[number], self.recv_sem.at[number], self.me, MESH
        ).wait_recv()

    def finish(self):
        for copy in self.started:
            copy.wait_send()


class Gather:
    def __init__(self, place, copies, base, ref, own=None, shared=False, flat=False):
        self.flat = flat
        self.p, self.q, self.base, self.ref, self.own = place, copies, base, ref, own
        self.least = 1 if shared else 0
        A, Y = place.A, place.Y
        self.x0 = base + A - 1
        self.y0 = self.x0 + A
        self.c0 = self.y0 + 2 * A * (Y - 1)
        self.end = self.c0 + 2 * A * Y

    @staticmethod
    def count(n_dp, n_v):
        A, Y = n_dp // 2, n_v // 2
        return A - 1 + A + 2 * A * (Y - 1) + 2 * A * Y

    def at(self, slot, j=0, c=None):
        p = self.p
        k = slot % p.A
        x = p.x if slot < p.A else 1 - p.x
        c = p.c if c is None else c
        return self.ref(p.from_a(k) * 2 + x, p.from_y(j) * 2 + c)

    def spread(self, slot):
        p = self.p
        src = self.at(slot) if (slot or self.own is None) else self.own
        if slot < p.A:
            self.q.send(self.x0 + slot, src, self.at(slot), p.xp)
        if slot < self.least:
            return
        if not self.flat:
            for k in range(1, p.Y):
                self.q.send(self.y0 + slot * (p.Y - 1) + k - 1, src, self.at(slot), p.yp(k))
        self.q.send(self.c0 + slot * p.Y, src, self.at(slot), p.cp)

    def start(self):
        p = self.p
        src = self.at(0) if self.own is None else self.own
        for k in range(1, p.A):
            self.q.send(self.base + k - 1, src, self.at(0), p.zp(k))
        self.spread(0)

    def step_a(self):
        for k in range(1, self.p.A):
            self.q.arrived(self.base + k - 1, self.at(k))
            self.spread(k)

    def step_x(self):
        A = self.p.A
        for k in range(A):
            self.q.arrived(self.x0 + k, self.at(A + k))
            self.spread(A + k)

    def step_y(self):
        p = self.p
        if self.flat:
            return
        for slot in range(self.least, 2 * p.A):
            for j in range(1, p.Y):
                self.q.arrived(self.y0 + slot * (p.Y - 1) + j - 1, self.at(slot, j))
                self.q.send(self.c0 + slot * p.Y + j, self.at(slot, j), self.at(slot, j), p.cp)

    def step_c(self):
        p = self.p
        for slot in range(self.least, 2 * p.A):
            for j in range(1 if self.flat else p.Y):
                self.q.arrived(self.c0 + slot * p.Y + j, self.at(slot, j, 1 - p.c))


def front_kernel(
    n_dp, n_v, cap, w_ref, table_ref, ints_ref,
    out_ref, tok_out, ints_out, pick_out, slot_out, rank_out,
    packed, hold, upper, ss, rs, ls,
):
    f32, bf = jnp.float32, jnp.bfloat16
    p = Place(n_dp, n_v)
    q = Copies(p.me, ss, rs)
    others = [(lax.rem(p.d + k, n_dp), p.v) for k in range(1, n_dp)]
    partners = [(p.d, lax.rem(p.v + k, n_v)) for k in range(1, n_v)]
    sem = pltpu.get_barrier_semaphore()
    for partner in others + partners:
        pl.semaphore_signal(sem, 1, device_id=partner, device_id_type=MESH)
    own = pltpu.make_async_copy(w_ref, out_ref.at[p.d], ls.at[0])
    own.start()
    ints_out[p.d] = ints_ref[...]
    pl.semaphore_wait(sem, n_dp - 1 + n_v - 1)
    base = 0
    for k in range(1, n_dp):
        q.send(base + k - 1, ints_ref, ints_out.at[p.d], others[k - 1])
    i0 = base
    base = base + n_dp - 1
    gathers = []
    for g in range(3):
        if g < 2:
            gather = Gather(
                p,
                q,
                base,
                lambda d, v, g=g: out_ref.at[d, g * n_v + v],
                own=w_ref.at[g * n_v + p.v],
                shared=True,
            )
        else:
            half = n_v // 2
            gather = Gather(
                p,
                q,
                base,
                lambda d, v: out_ref.at[d, pl.ds(2 * n_v + (v % 2) * half, half)],
                own=w_ref.at[pl.ds(2 * n_v + p.c * half, half)],
                shared=True,
                flat=True,
            )
        base = gather.end
        gathers.append(gather)
        gather.start()

    tokens_n, wide = SEGS * SEG, ceil_to(SEGS * SEG, 128)
    n_dev = n_dp * n_v
    rows = table_ref.shape[0]
    lane = lax.broadcasted_iota(jnp.int32, (1, wide), 1)
    valid = lane < tokens_n
    device = lax.broadcasted_iota(jnp.int32, (n_dev, 1), 0)
    least = device * rows
    upper[...] = (lax.broadcasted_iota(jnp.int32, (wide, 1), 0) < lane).astype(bf)
    place = lax.broadcasted_iota(jnp.int32, (cap, 1), 0).astype(f32)
    row_at = lax.broadcasted_iota(jnp.int32, (1, rows), 1).astype(f32) + 1.0
    low = (p.d * n_v + p.v) * rows
    for k in range(1, n_dp):
        q.arrived(i0 + k - 1, ints_out.at[lax.rem(p.d + n_dp - k, n_dp)])
    most = jnp.zeros((1, 1), f32)
    batch = hold.shape[0] // n_dev
    for start in range(0, n_dp, batch):
        for i in range(batch):
            ids = ints_out[start + i, :, :wide]
            held = (ids >= least) & (ids < least + rows) & valid
            hold[i * n_dev : (i + 1) * n_dev, :] = held.astype(f32).astype(bf)
        before = dot(hold[...], upper[...])
        for i in range(batch):
            ids = ints_out[start + i, :, :wide]
            held = hold[i * n_dev : (i + 1) * n_dev, :].astype(f32)
            rank = jnp.sum(held * before[i * n_dev : (i + 1) * n_dev, :], axis=0, keepdims=True)
            holder = jnp.sum(held * device.astype(f32), axis=0, keepdims=True)
            most = jnp.maximum(most, jnp.max(rank, axis=1, keepdims=True))
            slot_out[start + i : start + i + 1, :] = jnp.where(valid, holder * cap + rank, -1.0)
            mine = (ids >= low) & (ids < low + rows) & valid
            row = jnp.where(mine, (ids - low).astype(f32) + 1.0, 0.0)
            taken = jnp.sum(jnp.where(rank == place, row, 0.0), axis=1, keepdims=True)
            pick = (taken == row_at).astype(f32).astype(bf)
            pick_out[(start + i) * cap : (start + i + 1) * cap, :] = pick
    rank_out[...] = jnp.broadcast_to(most, rank_out.shape)
    packed[...] = dot(pick_out[...], table_ref[...]).astype(bf).reshape(packed.shape)
    first = base
    for k in range(1, n_dp):
        to = lax.rem(p.d + k, n_dp)
        q.send(first + k - 1, packed.at[to], tok_out.at[p.d, p.v], others[k - 1])
    local = pltpu.make_async_copy(packed.at[p.d], tok_out.at[p.d, p.v], ls.at[1])
    local.start()
    base = base + n_dp - 1
    y0, c0 = base, base + n_dp * (p.Y - 1)

    def relay(slot, src, src_d):
        for k in range(1, p.Y):
            q.send(y0 + slot * (p.Y - 1) + k - 1, src, tok_out.at[src_d, p.v], p.yp(k))
        q.send(c0 + slot * p.Y, src, tok_out.at[src_d, p.v], p.cp)

    relay(0, packed.at[p.d], p.d)
    g0, g1, g2 = gathers
    g0.step_a()
    g0.step_x()
    g1.step_a()
    for k in range(1, n_dp):
        src_d = lax.rem(p.d + n_dp - k, n_dp)
        q.arrived(first + k - 1, tok_out.at[src_d, p.v])
        relay(k, tok_out.at[src_d, p.v], src_d)
    g0.step_y()
    g1.step_x()
    g2.step_a()
    g1.step_y()
    for slot in range(n_dp):
        src_d = lax.rem(p.d + n_dp - slot, n_dp)
        for j in range(1, p.Y):
            piece = tok_out.at[src_d, p.from_y(j) * 2 + p.c]
            q.arrived(y0 + slot * (p.Y - 1) + j - 1, piece)
            q.send(c0 + slot * p.Y + j, piece, piece, p.cp)
    g2.step_x()
    for gather in gathers:
        gather.step_c()
    for slot in range(n_dp):
        src_d = lax.rem(p.d + n_dp - slot, n_dp)
        for j in range(p.Y):
            q.arrived(c0 + slot * p.Y + j, tok_out.at[src_d, p.from_y(j) * 2 + 1 - p.c])
    q.finish()
    own.wait()
    local.wait()


def run_front(blocks, table, ints, cap, n_dp, n_v):
    f32, bf = jnp.float32, jnp.bfloat16
    count = 3 * Gather.count(n_dp, n_v) + 2 * (n_dp - 1) + n_dp * (n_v - 1)
    hbm = pl.BlockSpec(memory_space=pl.ANY)
    vmem = pl.BlockSpec(memory_space=pltpu.VMEM)
    wide = ceil_to(SEGS * SEG, 128)
    rows = table.shape[0]
    return pl.pallas_call(
        functools.partial(front_kernel, n_dp, n_v, cap),
        out_shape=(
            jax.ShapeDtypeStruct((n_dp,) + blocks.shape, bf),
            jax.ShapeDtypeStruct((n_dp, n_v, cap, D), bf),
            jax.ShapeDtypeStruct((n_dp,) + ints.shape, ints.dtype),
            jax.ShapeDtypeStruct((n_dp * cap, rows), bf),
            jax.ShapeDtypeStruct((n_dp, wide), f32),
            jax.ShapeDtypeStruct((8, 128), f32),
        ),
        in_specs=[hbm, vmem, vmem],
        out_specs=(hbm, hbm, vmem, vmem, vmem, vmem),
        scratch_shapes=[
            pltpu.VMEM((n_dp, cap, D), bf),
            pltpu.VMEM((8 * n_dp * n_v, wide), bf),
            pltpu.VMEM((wide, wide), bf),
            pltpu.SemaphoreType.DMA((count,)),
            pltpu.SemaphoreType.DMA((count,)),
            pltpu.SemaphoreType.DMA((2,)),
        ],
        compiler_params=pltpu.CompilerParams(
            collective_id=0, has_side_effects=True, vmem_limit_bytes=48 << 20
        ),
    )(blocks, table, ints)


def head_kernel(
    n_dp, n_v, ch_ref, table_ref, label_ref, tags_ref,
    out_ref, dtab_ref, loss_ref,
    al, logits, dlog, st, sd, sv, lse_s, part, bc, by, bx, bz, pc, py, px, ss, rs,
):
    f32, bf = jnp.float32, jnp.bfloat16
    p = Place(n_dp, n_v)
    A, Y = p.A, p.Y
    count = n_dp * MLM
    others = [(lax.rem(p.d + k, n_dp), p.v) for k in range(1, n_dp)]
    partners = [(p.d, lax.rem(p.v + k, n_v)) for k in range(1, n_v)]
    sem = pltpu.get_barrier_semaphore()
    for partner in others + partners:
        pl.semaphore_signal(sem, 1, device_id=partner, device_id_type=MESH)
    pl.semaphore_wait(sem, n_dp - 1 + n_v - 1)
    q = Copies(p.me, ss, rs)
    gather = Gather(p, q, 0, lambda d, v: al.at[d, v], shared=True)
    al[p.d] = ch_ref[...]
    gather.start()
    gather.step_a()
    gather.step_x()
    gather.step_y()
    gather.step_c()
    n = gather.end
    rows_v, total_m = ch_ref.shape[1], n_dp * MLM_PAD
    chosen = al[...].reshape(total_m, D)
    logits[...] = dot(table_ref[...], chosen, NT)
    rows = table_ref.shape[0]
    row_ids = (p.d * n_v + p.v) * rows + lax.broadcasted_iota(jnp.int32, (rows, 1), 0)
    hits = row_ids == label_ref[...]
    top = jnp.max(logits[...], axis=0, keepdims=True)
    stats = (
        top,
        jnp.sum(jnp.exp(logits[...] - top), axis=0, keepdims=True),
        jnp.sum(jnp.where(hits, logits[...], 0.0), axis=0, keepdims=True),
    )
    tall = total_m // 128
    for k, values in enumerate(stats):
        for r in range(tall):
            st[k * tall + r : k * tall + r + 1, :] = values[:, r * 128 : (r + 1) * 128]

    def merged(ref, amount):
        tops = [ref[k, :tall, :] for k in range(amount)]
        best = functools.reduce(jnp.maximum, tops)
        parts = [ref[k, tall : 2 * tall, :] * jnp.exp(tops[k] - best) for k in range(amount)]
        return best, sum(parts[1:], parts[0]), sum(ref[k, 2 * tall :, :] for k in range(amount))

    sd[p.d] = st[...]
    for k in range(1, n_dp):
        q.send(n + k - 1, st, sd.at[p.d], others[k - 1])
    for k in range(1, n_dp):
        q.arrived(n + k - 1, sd.at[lax.rem(p.d + n_dp - k, n_dp)])
    n = n + n_dp - 1
    for k, values in enumerate(merged(sd, n_dp)):
        sv[p.v, k * tall : (k + 1) * tall, :] = values
    for k in range(1, n_v):
        q.send(n + k - 1, sv.at[p.v], sv.at[p.v], partners[k - 1])
    for k in range(1, n_v):
        q.arrived(n + k - 1, sv.at[lax.rem(p.v + n_v - k, n_v)])
    n = n + n_v - 1
    best, total, target = merged(sv, n_v)
    lse = best + jnp.log(total)
    lse_s[...] = lse
    lost = jnp.sum(jnp.where(tags_ref[...] >= 0, lse - target, 0.0), axis=1, keepdims=True)
    lost = jnp.sum(lost, axis=0, keepdims=True) / count
    loss_ref[...] = jnp.broadcast_to(lost, loss_ref.shape)
    lse_row = jnp.concatenate([lse_s[r : r + 1, :] for r in range(tall)], axis=1)
    d_log = (jnp.exp(logits[...] - lse_row) - hits.astype(f32)) * (1.0 / count)
    dlog[...] = d_log.astype(bf)
    made = dot(dlog[...], table_ref[...], TN).astype(bf)
    part[...] = made.reshape(A, 2, Y, 2, rows_v, D)
    q.send(n, part.at[:, :, :, 1 - p.c], bc, p.cp)
    dtab_ref[...] = dot(dlog[...], chosen)
    q.arrived(n, bc)
    pc[...] = (part[:, :, :, p.c].astype(f32) + bc[...].astype(f32)).astype(bf)
    n = n + 1
    for k in range(1, Y):
        q.send(n + k - 1, pc.at[:, :, lax.rem(p.y + k, Y)], by.at[k - 1], p.yp(k))
    total = pc[:, :, p.y].astype(f32)
    for k in range(1, Y):
        q.arrived(n + k - 1, by.at[k - 1])
        total = total + by[k - 1].astype(f32)
    py[...] = total.astype(bf)
    n = n + Y - 1
    q.send(n, py.at[:, 1 - p.x], bx, p.xp)
    q.arrived(n, bx)
    n = n + 1
    px[...] = (py[:, p.x].astype(f32) + bx[...].astype(f32)).astype(bf)
    for k in range(1, A):
        q.send(n + k - 1, px.at[p.to_a(k)], bz.at[k - 1], p.zp(k))
    total = px[p.a].astype(f32)
    for k in range(1, A):
        q.arrived(n + k - 1, bz.at[k - 1])
        total = total + bz[k - 1].astype(f32)
    n = n + A - 1
    out_ref[p.v] = total.astype(bf)
    for k in range(1, n_v):
        q.send(n + k - 1, out_ref.at[p.v], out_ref.at[p.v], partners[k - 1])
    for k in range(1, n_v):
        q.arrived(n + k - 1, out_ref.at[lax.rem(p.v + n_v - k, n_v)])
    q.finish()


def run_head(chosen, table, labels, n_dp, n_v):
    f32, kind = jnp.float32, chosen.dtype
    A, Y = n_dp // 2, n_v // 2
    _, rows_v, width = chosen.shape
    rows, total_m = table.shape[0], n_dp * MLM_PAD
    tall = total_m // 128
    count = Gather.count(n_dp, n_v) + n_dp - 1 + n_v - 1 + 1 + Y - 1 + 1 + A - 1 + n_v - 1
    vmem = pl.BlockSpec(memory_space=pltpu.VMEM)
    return pl.pallas_call(
        functools.partial(head_kernel, n_dp, n_v),
        out_shape=[
            jax.ShapeDtypeStruct(chosen.shape, kind),
            jax.ShapeDtypeStruct(table.shape, f32),
            jax.ShapeDtypeStruct((8, 128), f32),
        ],
        in_specs=[vmem] * 4,
        out_specs=[vmem] * 3,
        scratch_shapes=[
            pltpu.VMEM((n_dp,) + chosen.shape, kind),
            pltpu.VMEM((rows, total_m), f32),
            pltpu.VMEM((rows, total_m), kind),
            pltpu.VMEM((3 * tall, 128), f32),
            pltpu.VMEM((n_dp, 3 * tall, 128), f32),
            pltpu.VMEM((n_v, 3 * tall, 128), f32),
            pltpu.VMEM((tall, 128), f32),
            pltpu.VMEM((A, 2, Y, 2, rows_v, width), kind),
            pltpu.VMEM((A, 2, Y, rows_v, width), kind),
            pltpu.VMEM((Y - 1, A, 2, rows_v, width), kind),
            pltpu.VMEM((A, rows_v, width), kind),
            pltpu.VMEM((A - 1, rows_v, width), kind),
            pltpu.VMEM((A, 2, Y, rows_v, width), kind),
            pltpu.VMEM((A, 2, rows_v, width), kind),
            pltpu.VMEM((A, rows_v, width), kind),
            pltpu.SemaphoreType.DMA((count,)),
            pltpu.SemaphoreType.DMA((count,)),
        ],
        compiler_params=pltpu.CompilerParams(
            collective_id=2, has_side_effects=True, vmem_limit_bytes=56 << 20
        ),
    )(chosen, table, labels.reshape(1, total_m), labels.reshape(tall, 128))


def norm_kernel(n_dp, n_v, layer_ref, small_ref, table_ref, out_ref, sd, sv, ss, rs):
    f32 = jnp.float32
    d, v = lax.axis_index("dp"), lax.axis_index("vocab")
    others = [(lax.rem(d + k, n_dp), v) for k in range(1, n_dp)]
    partners = [(d, lax.rem(v + k, n_v)) for k in range(1, n_v)]
    sem = pltpu.get_barrier_semaphore()
    for partner in others + partners:
        pl.semaphore_signal(sem, 1, device_id=partner, device_id_type=MESH)

    def square(values):
        values = values.astype(f32)
        values = values * values
        while values.ndim > 2:
            values = jnp.sum(values, axis=0)
        return jnp.sum(jnp.sum(values, axis=0, keepdims=True), axis=1, keepdims=True)

    total = square(table_ref[...])
    total = total + jnp.where(v == 0, square(layer_ref[...]), 0.0)
    total = total + jnp.where((v == 0) & (d == 0), square(small_ref[...]), 0.0)
    sd[d] = jnp.broadcast_to(total, sd.shape[1:])
    pl.semaphore_wait(sem, n_dp - 1 + n_v - 1)
    q = Copies((d, v), ss, rs)
    for k in range(1, n_dp):
        q.send(k - 1, sd.at[d], sd.at[d], others[k - 1])
    for k in range(1, n_dp):
        q.arrived(k - 1, sd.at[lax.rem(d + n_dp - k, n_dp)])
    sv[v] = jnp.sum(sd[...], axis=0)
    for k in range(1, n_v):
        q.send(n_dp + k - 2, sv.at[v], sv.at[v], partners[k - 1])
    for k in range(1, n_v):
        q.arrived(n_dp + k - 2, sv.at[lax.rem(v + n_v - k, n_v)])
    out_ref[...] = jnp.sum(sv[...], axis=0)
    q.finish()


def run_norm(layer, small, table, n_dp, n_v):
    f32 = jnp.float32
    vmem = pl.BlockSpec(memory_space=pltpu.VMEM)
    count = n_dp + n_v - 2
    return pl.pallas_call(
        functools.partial(norm_kernel, n_dp, n_v),
        out_shape=jax.ShapeDtypeStruct((8, 128), f32),
        in_specs=[vmem] * 3,
        out_specs=vmem,
        scratch_shapes=[
            pltpu.VMEM((n_dp, 8, 128), f32),
            pltpu.VMEM((n_v, 8, 128), f32),
            pltpu.SemaphoreType.DMA((count,)),
            pltpu.SemaphoreType.DMA((count,)),
        ],
        compiler_params=pltpu.CompilerParams(
            collective_id=4, has_side_effects=True, vmem_limit_bytes=40 << 20
        ),
    )(layer, small, table)


def adam_kernel(n_dp, cuts, scal_ref, table_g, block_g, small_g, *refs):
    f32 = jnp.float32
    n = 7
    ins, outs, bufs = refs[: 3 * n], refs[3 * n : 6 * n], refs[6 * n : 9 * n]
    up_g, ext_g, bias_g, sem_i, sem_o = refs[9 * n :]
    loads = [pltpu.make_async_copy(ins[k], bufs[k], sem_i.at[k]) for k in range(3 * n)]
    for copy in loads:
        copy.start()
    coef, one_hat, two_hat = scal_ref[0], scal_ref[1], scal_ref[2]
    rb, width = block_g.shape[1:]
    stores = []

    def change(i, at, cols, grad, rate=LR_BIG):
        master, first, second = bufs[3 * i : 3 * i + 3]
        g = grad.astype(f32) * coef
        one = BETA_ONE * first[at, cols] + (1.0 - BETA_ONE) * g
        two = BETA_TWO * second[at, cols] + (1.0 - BETA_TWO) * g * g
        old = master[at, cols]
        first[at, cols] = one
        second[at, cols] = two
        move = one * one_hat / (jnp.sqrt(two * two_hat) + ADAM_EPS) + DECAY * old
        master[at, cols] = old - rate * move

    def begin(i):
        for copy in loads[3 * i : 3 * i + 3]:
            copy.wait()

    def end(i):
        for k in range(3 * i, 3 * i + 3):
            copy = pltpu.make_async_copy(bufs[k], outs[k], sem_o.at[k])
            copy.start()
            stores.append(copy)

    def chunks(rows, act):
        size = 32 if rows % 32 == 0 else rows
        if size == rows:
            act(pl.ds(0, rows))
        else:

            def body(c, _):
                act(pl.ds(pl.multiple_of(c * size, size), size))
                return 0

            lax.fori_loop(0, rows // size, body, 0)

    every = slice(None)
    begin(0)
    chunks(bufs[0].shape[0], lambda at: change(0, at, every, table_g[at, :]))
    end(0)
    for i, blocks in ((1, range(3)), (2, range(3, 4))):
        begin(i)
        for j in blocks:
            for s in range(cuts):
                cols = pl.ds((j - blocks[0]) * D + s * width, width)
                chunks(rb, lambda at: change(i, at, cols, block_g[j * cuts + s, at, :]))
        end(i)
    begin(3)
    for j in range(4):
        for s in range(cuts):
            block = block_g[(4 + j) * cuts + s].astype(f32)
            for d in range(n_dp // cuts):
                to = (s * (n_dp // cuts) + d) * 4 * rb + j * rb
                up_g[:, to : to + rb] = block[:, d * rb : (d + 1) * rb]
    chunks(rb, lambda at: change(3, at, every, up_g[at, :]))
    end(3)
    begin(4)
    for j in range(4):
        for s in range(cuts):
            cols = pl.ds(s * width, width)

            def down(at, j=j, s=s, cols=cols):
                change(4, pl.ds(j * rb + at.start, at.size), cols, block_g[(8 + j) * cuts + s, at, :])

            chunks(rb, down)
    end(4)
    ext_g[...] = small_g[: ext_g.shape[0], :].astype(f32)
    begin(5)
    done = EXT // 8 * 8
    for at in (pl.ds(0, done // 2), pl.ds(done // 2, done // 2), pl.ds(done, EXT - done)):
        change(5, at, every, ext_g[at, :], LR_SMALL)
    end(5)
    begin(6)
    for j in range(4):
        for d in range(n_dp):
            piece = ext_g[EXT + 5 + j : EXT + 6 + j, d * rb : (d + 1) * rb]
            bias_g[:, d * 4 * rb + j * rb : d * 4 * rb + (j + 1) * rb] = piece
    for k in range(12):
        if 5 <= k < 9:
            grad = bias_g[:, (k - 5) * D : (k - 4) * D]
        else:
            grad = ext_g[EXT + k : EXT + k + 1, :]
        change(6, every, pl.ds(k * D, D), grad, LR_SMALL)
    end(6)
    for copy in stores:
        copy.wait()


def run_adam(scalars, table_g, block_g, small_g, states, n_dp, cuts):
    hbm = pl.BlockSpec(memory_space=pl.ANY)
    vmem = pl.BlockSpec(memory_space=pltpu.VMEM)
    flat = [array for state in states for array in state]
    n = len(flat)
    rb = block_g.shape[1]
    return pl.pallas_call(
        functools.partial(adam_kernel, n_dp, cuts),
        out_shape=[jax.ShapeDtypeStruct(a.shape, a.dtype) for a in flat],
        in_specs=[pl.BlockSpec(memory_space=pltpu.SMEM), vmem, vmem, vmem] + [hbm] * n,
        out_specs=[hbm] * n,
        scratch_shapes=[pltpu.VMEM(a.shape, a.dtype) for a in flat]
        + [
            pltpu.VMEM((rb, FF), jnp.float32),
            pltpu.VMEM((ceil_to(EXT + 12, 16), D), jnp.float32),
            pltpu.VMEM((1, FF), jnp.float32),
            pltpu.SemaphoreType.DMA((n,)),
            pltpu.SemaphoreType.DMA((n,)),
        ],
        compiler_params=pltpu.CompilerParams(vmem_limit_bytes=56 << 20),
    )(scalars, table_g, block_g, small_g, *flat)


def lane_mean(values):
    return jnp.sum(values, axis=-1, keepdims=True) * (1.0 / D)


def norm_parts(values):
    centered = values - lane_mean(values)
    rate = lax.rsqrt(lane_mean(centered * centered) + LN_EPS)
    return centered * rate, rate


def norm_back(values, grad, gain):
    unit, rate = norm_parts(values)
    scaled = grad * gain
    d_values = rate * (scaled - lane_mean(scaled) - unit * lane_mean(scaled * unit))
    return (
        d_values,
        jnp.sum(grad * unit, axis=0, keepdims=True),
        jnp.sum(grad, axis=0, keepdims=True),
    )


def dot(left, right, dims=((1,), (0,))):
    return lax.dot_general(left, right, (dims, ((), ())), preferred_element_type=jnp.float32)


NT = ((1,), (1,))
TN = ((0,), (0,))


def allowed_mask(row_ref, col_ref, seg):
    row, col = row_ref[seg], col_ref[seg]
    return (row == col) | (row < 0) | (col < 0)


def forward_kernel(
    w_hbm, tok_ref, slot_ref, row_ref, col_ref, reset_ref, vec_ref, ext_ref, pos_ref,
    x_o, hc_o, proj_o, p_o, one_o, mid_o, gp_o, act_o, two_o, chosen_o,
    w, x, hc, proj, probs, one, mid, gp, act, two, mask, hid, final, sem_w, sem_o,
):
    bf, f32 = jnp.bfloat16, jnp.float32
    loads = [pltpu.make_async_copy(w_hbm.at[:, b], w.at[b], sem_w.at[b]) for b in range(12)]
    for load in loads:
        load.start()
    waited = set()

    def weight(b):
        if b not in waited:
            loads[b].wait()
            waited.add(b)
        return w[b].reshape(D, D)

    stores = []

    def store(src, dst):
        copy = pltpu.make_async_copy(src, dst, sem_o.at[len(stores)])
        copy.start()
        stores.append(copy)

    vec = [vec_ref[k : k + 1, :] for k in range(12)]
    b_q, b_v, b_o, g_one, b_one = vec[:5]
    b_up, b_down, g_two, b_two = vec[5:9], vec[9], vec[10], vec[11]
    gain_e, bias_e = ext_ref[404:405, :], ext_ref[405:406, :]
    lane = lax.broadcasted_iota(jnp.int32, (1, 2 * HD), 1)
    low_half = lane < HD
    for seg in range(SEGS):
        rows = pl.ds(seg * ROWS, ROWS)
        held = lax.broadcasted_iota(jnp.int32, (1, tok_ref.shape[0]), 1).astype(f32)
        onehot = (slot_ref[rows, :] == held).astype(f32).astype(bf)
        x[seg] = dot(onehot, tok_ref[...]) + ext_ref[:ROWS, :]
        x[seg, ROWS - MEM :, :] += ext_ref[ROWS + MEM : ROWS + 2 * MEM, :]
        first = ext_ref[ROWS : ROWS + MEM, :]
        if seg == 0:
            x[seg, :MEM, :] += first
        else:
            x[seg, :MEM, :] += jnp.where(reset_ref[seg - 1] > 0, first, hid[ROWS - MEM :, :])
        store(x.at[seg], x_o.at[seg])
        mask[...] = allowed_mask(row_ref, col_ref, seg).astype(f32)
        unit, _ = norm_parts(x[seg])
        h = unit * gain_e + bias_e
        hid[...] = h
        h_low = h.astype(bf)
        hc[0, rows, :] = h_low
        for k, bias in ((0, b_q), (1, None), (2, b_v)):
            made = dot(h_low, weight(k))
            proj[k, rows, :] = (made if bias is None else made + bias).astype(bf)
        store(hc.at[0, rows], hc_o.at[0, rows])
        store(proj.at[:, rows], proj_o.at[:, rows])
        for pair in range(HEADS // 2):
            cols = pl.ds(pair * 2 * HD, 2 * HD)
            query, keyed, value = (proj[k, rows, cols] for k in range(3))
            query = query * jnp.asarray(HD ** (-0.5), bf)
            parts = []
            for side in range(2):
                keep = low_half if side == 0 else ~low_half
                scores = dot(jnp.where(keep, query, jnp.zeros_like(query)), keyed, NT)
                scores = jnp.where(mask[...] > 0, scores, MASKED)
                expd = jnp.exp(scores - jnp.max(scores, axis=-1, keepdims=True))
                p_low = (expd * (1.0 / jnp.sum(expd, axis=-1, keepdims=True))).astype(bf)
                probs[seg, pair * 2 + side] = p_low
                parts.append(dot(p_low, value))
            hc[1, rows, cols] = jnp.where(low_half, parts[0], parts[1]).astype(bf)
        store(probs.at[seg], p_o.at[seg])
        store(hc.at[1, rows], hc_o.at[1, rows])
        sum_one = hid[...] + (dot(hc[1, rows, :], weight(3)) + b_o)
        one[seg] = sum_one
        store(one.at[seg], one_o.at[seg])
        unit, _ = norm_parts(sum_one)
        mid_now = unit * g_one + b_one
        mid_low = mid_now.astype(bf)
        mid[rows, :] = mid_low
        store(mid.at[rows], mid_o.at[rows])
        for j in range(4):
            up = dot(mid_low, weight(4 + j)) + b_up[j]
            half = 0.5 * (1.0 + lax.erf(up * 0.7071067811865476))
            gp[j, rows, :] = (half + up * jnp.exp(-0.5 * up * up) * 0.3989422804014327).astype(bf)
            act[j, rows, :] = (up * half).astype(bf)
        store(gp.at[:, rows], gp_o.at[:, rows])
        store(act.at[:, rows], act_o.at[:, rows])
        total = mid_now + b_down
        for j in range(4):
            total = total + dot(act[j, rows, :], weight(8 + j))
        two[seg] = total
        store(two.at[seg], two_o.at[seg])
        unit, _ = norm_parts(total)
        h = unit * g_two + b_two
        hid[...] = h
        final[rows, :] = h.astype(bf)
    at = lax.broadcasted_iota(jnp.int32, (MLM_PAD, SEGS * ROWS), 1)
    chosen_o[...] = dot((at == pos_ref[...]).astype(bf), final[...]).astype(bf)
    for copy in stores:
        copy.wait()


def run_forward(w_all, tok, slot, marks, reset, vec, ext, pos):
    f32, bf = jnp.float32, jnp.bfloat16
    n = SEGS * ROWS
    saved = [
        ((SEGS, ROWS, D), f32),
        ((2, n, D), bf),
        ((3, n, D), bf),
        ((SEGS, HEADS, ROWS, ROWS), bf),
        ((SEGS, ROWS, D), f32),
        ((n, D), bf),
        ((4, n, D), bf),
        ((4, n, D), bf),
        ((SEGS, ROWS, D), f32),
    ]
    hbm = pl.BlockSpec(memory_space=pl.ANY)
    vmem = pl.BlockSpec(memory_space=pltpu.VMEM)
    return pl.pallas_call(
        forward_kernel,
        out_shape=[jax.ShapeDtypeStruct(s, k) for s, k in saved]
        + [jax.ShapeDtypeStruct((MLM_PAD, D), bf)],
        in_specs=[hbm] + [vmem] * 4 + [pl.BlockSpec(memory_space=pltpu.SMEM), vmem, vmem, vmem],
        out_specs=[hbm] * len(saved) + [vmem],
        scratch_shapes=[pltpu.VMEM((12, w_all.shape[0]) + w_all.shape[2:], bf)]
        + [pltpu.VMEM(s, k) for s, k in saved]
        + [
            pltpu.VMEM((ROWS, ROWS), f32),
            pltpu.VMEM((ROWS, D), f32),
            pltpu.VMEM((n, D), bf),
            pltpu.SemaphoreType.DMA((12,)),
            pltpu.SemaphoreType.DMA((SEGS * 10,)),
        ],
        compiler_params=pltpu.CompilerParams(vmem_limit_bytes=60 << 20),
    )(w_all, tok, slot[:, None], marks[:, None, :], marks[:, :, None], reset, vec, ext, pos[:, None])


def backward_kernel(
    n_dp, n_v,
    w_hbm, x_i, hc_i, proj_i, p_i, one_i, mid_i, gp_i, act_i, two_i,
    dch_ref, reset_ref, vec_ref, ext_ref, pos_ref, give_ref, slot_ref,
    g_out, e_out, t_out, dtok,
    w, x, hc, right, probs, one, mid, rup, act, two, rdown, grad, dmem,
    small_o, dpack, share, bx, px, bz, own_g, e_in, eb, own_e, sem_w, sem_i, ss, rs, ls,
):
    bf, f32 = jnp.bfloat16, jnp.float32
    p = Place(n_dp, n_v)
    A, Y = p.A, p.Y
    others = [(lax.rem(p.d + k, n_dp), p.v) for k in range(1, n_dp)]
    partners = [(p.d, lax.rem(p.v + k, n_v)) for k in range(1, n_v)]
    barrier = pltpu.get_barrier_semaphore()
    for partner in others + partners:
        pl.semaphore_signal(barrier, 1, device_id=partner, device_id_type=MESH)
    q = Copies(p.me, ss, rs)
    groups = share.shape[0]
    x0 = 0
    t0 = x0 + groups
    z0 = t0 + n_dp - 1
    e0 = z0 + groups * (A - 1)
    y0 = e0 + 2 * (n_dp - 1) + n_v - 1
    c0 = y0 + groups * (Y - 1)
    cuts = n_v // 4
    width = D // cuts
    block, cut = p.v // cuts, p.v % cuts
    cols_v = pl.ds(pl.multiple_of(cut * width, 128), width)

    def p_to(k):
        return lax.rem(p.d + k, n_dp)

    def p_from(k):
        return lax.rem(p.d + n_dp - k, n_dp)

    def make_share(g, left, right_cols):
        made = dot(left, right_cols, TN)
        share[g] = made.reshape(share.shape[1:]).astype(bf)
        q.send(x0 + g, share.at[g, :, 1 - p.x], bx.at[g], p.xp)

    def half_sums(g):
        q.arrived(x0 + g, bx.at[g])
        for k in range(1, A + 1):
            to = p.to_a(k)
            px[g, to] = (share[g, to, p.x].astype(f32) + bx[g, to].astype(f32)).astype(bf)
            if k < A:
                q.send(z0 + g * (A - 1) + k - 1, px.at[g, to], bz.at[g, k - 1], p.zp(k))

    small_o[...] = jnp.zeros_like(small_o)
    loads = {}
    state = {"n": 0}

    def load(name, src, dst):
        copy = pltpu.make_async_copy(src, dst, sem_i.at[state["n"]])
        state["n"] += 1
        copy.start()
        loads[name] = copy

    def need(name):
        if name in loads:
            loads.pop(name).wait()

    wl = [pltpu.make_async_copy(w_hbm.at[:, b], w.at[b], sem_w.at[b]) for b in range(12)]
    waited = set()

    def weight(b):
        if b not in waited:
            wl[b].wait()
            waited.add(b)
        return w[b].reshape(D, D)

    order = list(reversed(range(SEGS)))
    for i, seg in enumerate(order):
        rows = pl.ds(seg * ROWS, ROWS)
        load(("two", seg), two_i.at[seg], two.at[seg])
        if i == 0:
            for b in range(8, 12):
                wl[b].start()
        load(("gp", seg), gp_i.at[:, rows], rup.at[:, rows])
        if i == 0:
            for b in range(4, 8):
                wl[b].start()
        load(("one", seg), one_i.at[seg], one.at[seg])
        if i == 0:
            wl[3].start()
            load(("p", seg), p_i.at[seg], probs)
        load(("proj", seg), proj_i.at[:, rows], right.at[pl.ds(0, 3), rows])
        if i == 0:
            for b in range(3):
                wl[b].start()
        load(("x", seg), x_i.at[seg], x.at[seg])
    load("hc", hc_i, hc)
    load("mid", mid_i, mid)
    load("act", act_i, act)

    vec = [vec_ref[k : k + 1, :] for k in range(12)]
    g_one, g_two, gain_e = vec[3], vec[10], ext_ref[404:405, :]
    lane = lax.broadcasted_iota(jnp.int32, (1, 2 * HD), 1)
    low_half = lane < HD
    at = lax.broadcasted_iota(jnp.int32, (MLM_PAD, SEGS * ROWS), 1)
    at_pos = (at == pos_ref[...]).astype(bf)
    v0 = EXT

    def add_row(k, value):
        small_o[v0 + k : v0 + k + 1, :] += value

    def sums(values):
        return jnp.sum(values.astype(f32), axis=0, keepdims=True)

    for i, seg in enumerate(order):
        rows = pl.ds(seg * ROWS, ROWS)
        grad[...] = dot(at_pos[:, seg * ROWS : (seg + 1) * ROWS], dch_ref[...], TN)
        if i > 0:
            grad[ROWS - MEM :, :] += dmem[...]
        need(("two", seg))
        d_two, d_gain, d_shift = norm_back(two[seg], grad[...], g_two)
        add_row(10, d_gain)
        add_row(11, d_shift)
        r_down = d_two.astype(bf)
        rdown[rows, :] = r_down
        add_row(9, sums(r_down))
        if i == SEGS - 1:
            need("act")
            pl.semaphore_wait(barrier, n_dp - 1 + n_v - 1)
            make_share(2, act[block], rdown[:, cols_v])
        need(("gp", seg))
        for j in range(4):
            r_up = (rup[j, rows, :].astype(f32) * dot(r_down, weight(8 + j), NT)).astype(bf)
            rup[j, rows, :] = r_up
            add_row(5 + j, sums(r_up))
        if i == SEGS - 1:
            need("mid")
            make_share(1, mid[...], rup[block, :, cols_v])
        for j in range(4):
            d_two = d_two + dot(rup[j, rows, :], weight(4 + j), NT)
        need(("one", seg))
        d_one, d_gain, d_shift = norm_back(one[seg], d_two, g_one)
        add_row(3, d_gain)
        add_row(4, d_shift)
        grad[...] = d_one
        r_att = d_one.astype(bf)
        right[3, rows, :] = r_att
        add_row(2, sums(r_att))
        d_ctx = dot(r_att, weight(3), NT).astype(bf)
        need(("p", seg))
        need(("proj", seg))
        for pair in range(HEADS // 2):
            if i == SEGS - 1 and pair == HEADS // 3:
                half_sums(2)
            cols = pl.ds(pair * 2 * HD, 2 * HD)
            query, keyed, value = (right[k, rows, cols] for k in range(3))
            d_out = d_ctx[:, pair * 2 * HD : (pair + 1) * 2 * HD]
            made = []
            for side in range(2):
                keep = low_half if side == 0 else ~low_half
                p_low = probs[pair * 2 + side]
                p_now = p_low.astype(f32)
                d_p = dot(jnp.where(keep, d_out, jnp.zeros_like(d_out)), value, NT)
                weighted = p_now * d_p
                d_s = weighted - p_now * jnp.sum(weighted, axis=-1, keepdims=True)
                d_s = d_s.astype(bf)
                made.append((dot(d_s, keyed), dot(d_s, query, TN), dot(p_low, d_out, TN)))
            for k, scale in ((0, HD ** (-0.5)), (1, HD ** (-0.5)), (2, 1.0)):
                both = jnp.where(low_half, made[0][k], made[1][k]) * scale
                right[k, rows, cols] = both.astype(bf)
        if i + 1 < SEGS:
            load(("p", order[i + 1]), p_i.at[order[i + 1]], probs)
        if i == SEGS - 1:
            need("hc")
            make_share(0, hc[block // 3], right[block, :, cols_v])
        d_h = grad[...]
        for k in range(3):
            d_h = d_h + dot(right[k, rows, :], weight(k), NT)
        add_row(0, sums(right[0, rows, :]))
        add_row(1, sums(right[2, rows, :]))
        need(("x", seg))
        d_x, d_gain, d_shift = norm_back(x[seg], d_h, gain_e)
        grad[...] = d_x
        dtok[rows, :] = d_x.astype(bf)
        small_o[:ROWS, :] += d_x
        small_o[ROWS + MEM : ROWS + 2 * MEM, :] += grad[ROWS - MEM :, :]
        small_o[404:405, :] += d_gain
        small_o[405:406, :] += d_shift
        d_read = grad[:MEM, :]
        if seg > 0:
            back = reset_ref[seg - 1] > 0
            small_o[ROWS : ROWS + MEM, :] += jnp.where(back, d_read, 0.0)
            dmem[...] = jnp.where(back, 0.0, d_read)
        else:
            small_o[ROWS : ROWS + MEM, :] += d_read
    held = (give_ref[...] == slot_ref[...]).astype(f32).astype(bf)
    dpack[...] = dot(held, dtok[...]).astype(bf).reshape(dpack.shape)
    e_rows = e_in.shape[1]
    for d in range(n_dp):
        at = (d * n_v + p.v) * e_rows
        fits = at < small_o.shape[0]

        @pl.when(fits)
        def _(d=d, at=at):
            e_in[d] = small_o[pl.ds(pl.multiple_of(at, e_rows), e_rows), :].astype(bf)

        @pl.when(jnp.logical_not(fits))
        def _(d=d):
            e_in[d] = jnp.zeros(e_in.shape[1:], bf)

    for k in range(1, n_dp):
        q.send(e0 + k - 1, e_in.at[p_to(k)], eb.at[p.d], others[k - 1])
    eb[p.d] = e_in[p.d]
    half_sums(1)
    for k in range(1, n_dp):
        q.arrived(e0 + k - 1, eb.at[p_from(k)])
    own_e[...] = jnp.sum(eb[...].astype(f32), axis=0).astype(bf)
    e1 = e0 + n_dp - 1
    locals_ = []

    def keep(src, dst):
        copy = pltpu.make_async_copy(src, dst, ls.at[len(locals_)])
        copy.start()
        locals_.append(copy)

    keep(own_e, e_out.at[p.d, p.v])
    for k in range(1, n_dp):
        q.send(e1 + k - 1, own_e, e_out.at[p.d, p.v], others[k - 1])

    def whole_sums(g):
        total = px[g, p.a].astype(f32)
        for k in range(1, A):
            q.arrived(z0 + g * (A - 1) + k - 1, bz.at[g, k - 1])
            total = total + bz[g, k - 1].astype(f32)
        own_g[g] = total.astype(bf)
        mine = g_out.at[g * n_v + p.v]
        for k in range(1, Y):
            q.send(y0 + g * (Y - 1) + k - 1, own_g.at[g], mine, p.yp(k))
        q.send(c0 + g * Y, own_g.at[g], mine, p.cp)
        keep(own_g.at[g], mine)

    def hand_on(g):
        for j in range(1, Y):
            piece = g_out.at[g * n_v + p.from_y(j) * 2 + p.c]
            q.arrived(y0 + g * (Y - 1) + j - 1, piece)
            q.send(c0 + g * Y + j, piece, piece, p.cp)

    whole_sums(2)
    half_sums(0)
    for k in range(1, n_dp):
        q.send(t0 + k - 1, dpack.at[p_to(k)], t_out.at[p.d], others[k - 1])
    keep(dpack.at[p.d], t_out.at[p.d])
    e2 = e1 + n_dp - 1
    for k in range(1, n_dp):
        q.arrived(e1 + k - 1, e_out.at[p_from(k), p.v])
    locals_[0].wait()
    for k in range(1, n_v):
        q.send(e2 + k - 1, e_out.at[:, p.v], e_out.at[:, p.v], partners[k - 1])
    hand_on(2)
    whole_sums(1)
    hand_on(1)
    whole_sums(0)
    hand_on(0)
    for k in range(1, n_v):
        q.arrived(e2 + k - 1, e_out.at[:, lax.rem(p.v + n_v - k, n_v)])
    for g in range(groups):
        for j in range(Y):
            q.arrived(c0 + g * Y + j, g_out.at[g * n_v + p.from_y(j) * 2 + 1 - p.c])
    for k in range(1, n_dp):
        q.arrived(t0 + k - 1, t_out.at[p_from(k)])
    q.finish()
    for copy in locals_[1:]:
        copy.wait()


def run_backward(w_all, saved, d_chosen, reset, vec, ext, pos, give, slot, rb, n_dp, n_v):
    f32, bf = jnp.float32, jnp.bfloat16
    n = SEGS * ROWS
    A, Y, groups = n_dp // 2, n_v // 2, 3
    width = D // (n_v // 4)
    e_rows = ceil_to(-(-(EXT + 12) // (n_dp * n_v)), 16)
    cap = give.shape[0] // n_dp
    hbm = pl.BlockSpec(memory_space=pl.ANY)
    vmem = pl.BlockSpec(memory_space=pltpu.VMEM)
    smem = pl.BlockSpec(memory_space=pltpu.SMEM)
    count = groups * (1 + A - 1 + Y - 1 + Y) + 3 * (n_dp - 1) + n_v - 1
    return pl.pallas_call(
        functools.partial(backward_kernel, n_dp, n_v),
        out_shape=[
            jax.ShapeDtypeStruct((groups * n_v, rb, width), bf),
            jax.ShapeDtypeStruct((n_dp, n_v, e_rows, D), bf),
            jax.ShapeDtypeStruct((n_dp, cap, D), bf),
            jax.ShapeDtypeStruct((n, D), bf),
        ],
        in_specs=[hbm] * 10 + [vmem, smem] + [vmem] * 5,
        out_specs=[hbm, hbm, hbm, vmem],
        scratch_shapes=[
            pltpu.VMEM((12, w_all.shape[0]) + w_all.shape[2:], bf),
            pltpu.VMEM((SEGS, ROWS, D), f32),
            pltpu.VMEM((2, n, D), bf),
            pltpu.VMEM((4, n, D), bf),
            pltpu.VMEM((HEADS, ROWS, ROWS), bf),
            pltpu.VMEM((SEGS, ROWS, D), f32),
            pltpu.VMEM((n, D), bf),
            pltpu.VMEM((4, n, D), bf),
            pltpu.VMEM((4, n, D), bf),
            pltpu.VMEM((SEGS, ROWS, D), f32),
            pltpu.VMEM((n, D), bf),
            pltpu.VMEM((ROWS, D), f32),
            pltpu.VMEM((MEM, D), f32),
            pltpu.VMEM((ceil_to(EXT + 12, e_rows), D), f32),
            pltpu.VMEM((n_dp, cap, D), bf),
            pltpu.VMEM((groups, A, 2, rb, width), bf),
            pltpu.VMEM((groups, A, rb, width), bf),
            pltpu.VMEM((groups, A, rb, width), bf),
            pltpu.VMEM((groups, A - 1, rb, width), bf),
            pltpu.VMEM((groups, rb, width), bf),
            pltpu.VMEM((n_dp, e_rows, D), bf),
            pltpu.VMEM((n_dp, e_rows, D), bf),
            pltpu.VMEM((e_rows, D), bf),
            pltpu.SemaphoreType.DMA((12,)),
            pltpu.SemaphoreType.DMA((SEGS * 6 + 4,)),
            pltpu.SemaphoreType.DMA((count,)),
            pltpu.SemaphoreType.DMA((count,)),
            pltpu.SemaphoreType.DMA((2 + groups,)),
        ],
        compiler_params=pltpu.CompilerParams(
            collective_id=3, has_side_effects=True, vmem_limit_bytes=63 << 20
        ),
    )(
        w_all, *saved, d_chosen, reset, vec, ext, pos[:, None], give[:, None], slot[None, :],
    )


def ceil_to(value, unit):
    return -(-value // unit) * unit


def per_device(
    ids,
    docs,
    resets,
    mlm_pos,
    mlm_label,
    step,
    qkv_master,
    qkv_first,
    qkv_second,
    out_master,
    out_first,
    out_second,
    up_master,
    up_first,
    up_second,
    down_master,
    down_first,
    down_second,
    embed_master,
    embed_first,
    embed_second,
    vectors_master,
    vectors_first,
    vectors_second,
    extras_master,
    extras_first,
    extras_second,
):
    f32, bf = jnp.float32, jnp.bfloat16
    n_dp = lax.axis_size("dp")
    n_v = lax.axis_size("vocab")
    d_idx = lax.axis_index("dp")
    v_idx = lax.axis_index("vocab")
    own_rows = embed_master.shape[0]
    tokens_n = SEGS * SEG
    rb = qkv_master.shape[1]
    cuts = max(1, n_v // 4)
    width = D // cuts
    groups = 12 * cuts // n_v

    def to_blocks(qkv, out, up, down):
        full = jnp.concatenate(
            [
                qkv[0].reshape(rb, 3, D).transpose(1, 0, 2),
                out,
                up[0].reshape(rb, n_dp, 4, rb).transpose(2, 0, 1, 3).reshape(4, rb, D),
                down[0].reshape(4, rb, D),
            ]
        )
        return full.reshape(12, rb, cuts, width).transpose(0, 2, 1, 3).reshape(12 * cuts, rb, width)

    ints = jnp.concatenate([ids[0], mlm_label[0]])[None]
    ints = jnp.pad(ints, ((0, 0), (0, ceil_to(ints.shape[1], 128) - ints.shape[1])), constant_values=-1)
    cap = ceil_to(2 * tokens_n // (n_dp * n_v) + 2, 16)
    table = embed_master.astype(bf)
    blocks = to_blocks(
        qkv_master.astype(bf), out_master.astype(bf), up_master.astype(bf), down_master.astype(bf)
    )
    w_all, tok_all, ints_all, pick, slots, most = run_front(blocks, table, ints, cap, n_dp, n_v)
    if cuts > 1 or rb % 16:
        w_all = w_all.reshape(n_dp, 12, cuts, rb, width).transpose(1, 0, 3, 2, 4).reshape(1, 12, D, D)
    ids_all = ints_all[:, 0, :tokens_n]
    labels_all = ints_all[:, 0, tokens_n : tokens_n + MLM]
    labels_all = jnp.pad(labels_all, ((0, 0), (0, MLM_PAD - MLM)), constant_values=-1)
    overflow = most[0, 0] >= cap

    def padded(values):
        values = values.reshape((SEGS, SEG) + values.shape[1:])
        edges = ((0, 0), (MEM, MEM)) + ((0, 0),) * (values.ndim - 2)
        values = jnp.pad(values, edges, constant_values=-1)
        return values.reshape((SEGS * ROWS,) + values.shape[2:])

    slot = padded(lax.dynamic_index_in_dim(slots, d_idx, keepdims=False)[:tokens_n])

    def packed_tokens(_):
        return tok_all.reshape(n_dp * n_v * cap, D), slot

    def whole_tokens(_):
        whole = lax.all_gather(table, "dp", axis=0, tiled=True)
        at = jnp.arange(n_dp * own_rows, dtype=jnp.int32)
        row_ids = (at // own_rows * n_v + v_idx) * own_rows + at % own_rows
        onehot = (ids[0][:, None] == row_ids[None, :]).astype(bf)
        rows = lax.psum(jnp.dot(onehot, whole, preferred_element_type=f32).astype(bf), "vocab")
        rows = jnp.pad(rows, ((0, n_dp * n_v * cap - tokens_n), (0, 0)))
        return rows, padded(jnp.arange(tokens_n, dtype=jnp.int32).astype(f32))

    token_rows, token_slot = lax.cond(overflow, whole_tokens, packed_tokens, 0)
    marks = jnp.pad(docs.reshape(SEGS, SEG), ((0, 0), (MEM, MEM)), constant_values=-1)
    vec = vectors_master[0].reshape(12, D)
    b_up = vec[5:9].reshape(n_dp, 4, rb).transpose(1, 0, 2).reshape(4, D)
    vec = jnp.concatenate([vec[:5], b_up, vec[9:]])
    positions = mlm_pos[0]
    at_rows = positions // SEG * ROWS + MEM + positions % SEG
    at_rows = jnp.concatenate([at_rows, jnp.full((MLM_PAD - MLM,), -1, jnp.int32)])
    *saved, chosen = run_forward(w_all, token_rows, token_slot, marks, resets[0], vec, extras_master, at_rows)
    rows_v = MLM_PAD // n_v
    d_chosen, d_table, loss = run_head(chosen.reshape(n_v, rows_v, D), table, labels_all, n_dp, n_v)
    loss = loss[0, 0]
    d_chosen = d_chosen.reshape(MLM_PAD, D)
    at = jnp.arange(n_dp * cap, dtype=jnp.int32)
    give = ((at // cap * n_v + v_idx) * cap + at % cap).astype(f32)
    g_blocks, small_all, d_packed_all, d_tok = run_backward(
        w_all, saved, d_chosen, resets[0], vec, extras_master, at_rows, give, slot, rb, n_dp, n_v
    )

    def packed_d_table(_):
        return jnp.einsum(
            "tv,td->vd", pick, d_packed_all.reshape(n_dp * cap, D), preferred_element_type=f32
        )

    def whole_d_table(_):
        d_all = d_tok.reshape(SEGS, ROWS, D)[:, MEM : MEM + SEG].reshape(tokens_n, D)
        d_all = lax.all_gather(d_all, "dp", axis=0, tiled=True)
        row_ids = (d_idx * n_v + v_idx) * own_rows + jnp.arange(own_rows, dtype=jnp.int32)
        onehot = (ids_all.reshape(-1)[:, None] == row_ids[None, :]).astype(bf)
        return jnp.einsum("tv,td->vd", onehot, d_all, preferred_element_type=f32)

    s_table = d_table + lax.cond(overflow, whole_d_table, packed_d_table, 0)
    small_all = small_all.reshape(-1, D)
    norm = jnp.sqrt(run_norm(g_blocks, small_all, s_table, n_dp, n_v)[0, 0])
    coef = jnp.minimum(1.0, CLIP / (norm + 1e-06))
    t = step[0].astype(f32)
    scalars = jnp.stack([coef, 1.0 / (1.0 - BETA_ONE**t), 1.0 / (1.0 - BETA_TWO**t)])
    states = (
        (embed_master, embed_first, embed_second),
        (qkv_master[0], qkv_first[0], qkv_second[0]),
        (out_master[0], out_first[0], out_second[0]),
        (up_master[0], up_first[0], up_second[0]),
        (down_master[0], down_first[0], down_second[0]),
        (extras_master, extras_first, extras_second),
        (vectors_master, vectors_first, vectors_second),
    )
    new = run_adam(scalars, s_table, g_blocks, small_all, states, n_dp, cuts)
    layer = [value[None] for value in new[3:15]]
    return (loss, norm, *layer, *new[:3], *new[18:], *new[15:18])


def solution(mesh):
    in_specs = (
        P("dp", None),
        P("dp", None),
        P("dp", None),
        P("dp", None),
        P("dp", None),
        P(),
        P(None, "dp", None),
        P(None, "dp", None),
        P(None, "dp", None),
        P(None, "dp", None),
        P(None, "dp", None),
        P(None, "dp", None),
        P(None, "dp", None),
        P(None, "dp", None),
        P(None, "dp", None),
        P(None, "dp", None),
        P(None, "dp", None),
        P(None, "dp", None),
        P(("dp", "vocab"), None),
        P(("dp", "vocab"), None),
        P(("dp", "vocab"), None),
        P(),
        P(),
        P(),
        P(),
        P(),
        P(),
    )
    out_specs = (
        P(),
        P(),
        P(None, "dp", None),
        P(None, "dp", None),
        P(None, "dp", None),
        P(None, "dp", None),
        P(None, "dp", None),
        P(None, "dp", None),
        P(None, "dp", None),
        P(None, "dp", None),
        P(None, "dp", None),
        P(None, "dp", None),
        P(None, "dp", None),
        P(None, "dp", None),
        P(("dp", "vocab"), None),
        P(("dp", "vocab"), None),
        P(("dp", "vocab"), None),
        P(),
        P(),
        P(),
        P(),
        P(),
        P(),
    )
    return jax.shard_map(
        per_device, mesh=mesh, in_specs=in_specs, out_specs=out_specs, check_vma=False
    )
```

```python
import functools

import jax
import jax.numpy as jnp
from jax import lax
from jax.experimental import pallas as pl
from jax.experimental.pallas import tpu as pltpu
from jax.sharding import PartitionSpec as P

D = 768
HEADS = 12
HD = 64
FF = 3072
MEM = 10
SEG = 364
SEGS = 2
LAYERS = 1
MLM = 112
ROWS = 384


BETA_ONE = 0.9
BETA_TWO = 0.999
ADAM_EPS = 1e-08
DECAY = 0.01
LN_EPS = 1e-06
CLIP = 0.02
LR_BIG = 0.04
LR_SMALL = 0.5
MASKED = -1000000000.0


MESH = pl.DeviceIdType.MESH
MLM_PAD = 128
EXT = ROWS + 2 * MEM + 2


class Place:
    def __init__(self, n_dp, n_v):
        self.A, self.Y = n_dp // 2, n_v // 2
        self.d, self.v = lax.axis_index("dp"), lax.axis_index("vocab")
        self.a, self.x = self.d // 2, self.d % 2
        self.y, self.c = self.v // 2, self.v % 2
        self.me = (self.d, self.v)
        self.xp = (self.d + 1 - 2 * self.x, self.v)
        self.cp = (self.d, self.v + 1 - 2 * self.c)

    def from_a(self, k):
        return lax.rem(self.a + self.A - k, self.A)

    def to_a(self, k):
        return lax.rem(self.a + k, self.A)

    def from_y(self, k):
        return lax.rem(self.y + self.Y - k, self.Y)

    def zp(self, k):
        return (self.to_a(k) * 2 + self.x, self.v)

    def yp(self, k):
        return (self.d, lax.rem(self.y + k, self.Y) * 2 + self.c)

    def barrier(self, extra=()):
        sem = pltpu.get_barrier_semaphore()
        partners = [self.zp(k) for k in range(1, self.A)] + [self.xp]
        partners += [self.yp(k) for k in range(1, self.Y)] + [self.cp] + list(extra)
        for partner in partners:
            pl.semaphore_signal(sem, 1, device_id=partner, device_id_type=MESH)
        pl.semaphore_wait(sem, len(partners))


class Copies:
    def __init__(self, me, send_sem, recv_sem):
        self.me, self.send_sem, self.recv_sem, self.started = me, send_sem, recv_sem, []

    def send(self, number, src, dst, partner):
        copy = pltpu.make_async_remote_copy(
            src, dst, self.send_sem.at[number], self.recv_sem.at[number], partner, MESH
        )
        copy.start()
        self.started.append(copy)

    def arrived(self, number, dst):
        pltpu.make_async_remote_copy(
            dst, dst, self.send_sem.at[number], self.recv_sem.at[number], self.me, MESH
        ).wait_recv()

    def finish(self):
        for copy in self.started:
            copy.wait_send()


class Gather:
    def __init__(self, place, copies, base, ref, own=None, shared=False, flat=False):
        self.flat = flat
        self.p, self.q, self.base, self.ref, self.own = place, copies, base, ref, own
        self.least = 1 if shared else 0
        A, Y = place.A, place.Y
        self.x0 = base + A - 1
        self.y0 = self.x0 + A
        self.c0 = self.y0 + 2 * A * (Y - 1)
        self.end = self.c0 + 2 * A * Y

    @staticmethod
    def count(n_dp, n_v):
        A, Y = n_dp // 2, n_v // 2
        return A - 1 + A + 2 * A * (Y - 1) + 2 * A * Y

    def at(self, slot, j=0, c=None):
        p = self.p
        k = slot % p.A
        x = p.x if slot < p.A else 1 - p.x
        c = p.c if c is None else c
        return self.ref(p.from_a(k) * 2 + x, p.from_y(j) * 2 + c)

    def spread(self, slot):
        p = self.p
        src = self.at(slot) if (slot or self.own is None) else self.own
        if slot < p.A:
            self.q.send(self.x0 + slot, src, self.at(slot), p.xp)
        if slot < self.least:
            return
        if not self.flat:
            for k in range(1, p.Y):
                self.q.send(self.y0 + slot * (p.Y - 1) + k - 1, src, self.at(slot), p.yp(k))
        self.q.send(self.c0 + slot * p.Y, src, self.at(slot), p.cp)

    def start(self):
        p = self.p
        src = self.at(0) if self.own is None else self.own
        for k in range(1, p.A):
            self.q.send(self.base + k - 1, src, self.at(0), p.zp(k))
        self.spread(0)

    def step_a(self):
        for k in range(1, self.p.A):
            self.q.arrived(self.base + k - 1, self.at(k))
            self.spread(k)

    def step_x(self):
        A = self.p.A
        for k in range(A):
            self.q.arrived(self.x0 + k, self.at(A + k))
            self.spread(A + k)

    def step_y(self):
        p = self.p
        if self.flat:
            return
        for slot in range(self.least, 2 * p.A):
            for j in range(1, p.Y):
                self.q.arrived(self.y0 + slot * (p.Y - 1) + j - 1, self.at(slot, j))
                self.q.send(self.c0 + slot * p.Y + j, self.at(slot, j), self.at(slot, j), p.cp)

    def step_c(self):
        p = self.p
        for slot in range(self.least, 2 * p.A):
            for j in range(1 if self.flat else p.Y):
                self.q.arrived(self.c0 + slot * p.Y + j, self.at(slot, j, 1 - p.c))


def front_kernel(
    n_dp, n_v, cap, qkv_ref, o_ref, up_ref, down_ref, master_ref, ints_ref,
    out_ref, tok_out, ints_out, pick_out, slot_out, rank_out, table_ref,
    w_ref, upped, packed, hold, upper, ss, rs, ls,
):
    f32, bf = jnp.float32, jnp.bfloat16
    p = Place(n_dp, n_v)
    q = Copies(p.me, ss, rs)
    others = [(lax.rem(p.d + k, n_dp), p.v) for k in range(1, n_dp)]
    partners = [(p.d, lax.rem(p.v + k, n_v)) for k in range(1, n_v)]
    sem = pltpu.get_barrier_semaphore()
    for partner in others + partners:
        pl.semaphore_signal(sem, 1, device_id=partner, device_id_type=MESH)
    ints_out[p.d] = ints_ref[...]
    rb, width = w_ref.shape[1:]
    cuts = D // width

    def put(block, ref, row, col):
        for s in range(cuts):
            values = ref[row : row + rb, col + s * width : col + (s + 1) * width]
            w_ref[block * cuts + s] = values.astype(bf)

    for j in range(3):
        put(j, qkv_ref, 0, j * D)
    put(3, o_ref, 0, 0)
    pl.semaphore_wait(sem, n_dp - 1 + n_v - 1)
    base = 0
    for k in range(1, n_dp):
        q.send(base + k - 1, ints_ref, ints_out.at[p.d], others[k - 1])
    i0 = base
    base = base + n_dp - 1
    gathers = []
    for g in range(3):
        if g < 2:
            gather = Gather(
                p,
                q,
                base,
                lambda d, v, g=g: out_ref.at[d, g * n_v + v],
                own=w_ref.at[g * n_v + p.v],
                shared=True,
            )
        else:
            half = n_v // 2
            gather = Gather(
                p,
                q,
                base,
                lambda d, v: out_ref.at[d, pl.ds(2 * n_v + (v % 2) * half, half)],
                own=w_ref.at[pl.ds(2 * n_v + p.c * half, half)],
                shared=True,
                flat=True,
            )
        base = gather.end
        gathers.append(gather)
    g0, g1, g2 = gathers
    g0.start()
    for j in range(4):
        for d in range(n_dp):
            at = (d * 4 + j) * rb
            upped[:, d * rb : (d + 1) * rb] = up_ref[:, at : at + rb]
        put(4 + j, upped, 0, 0)
        put(8 + j, down_ref, j * rb, 0)
    own = pltpu.make_async_copy(w_ref, out_ref.at[p.d], ls.at[0])
    own.start()
    table_ref[...] = master_ref[...].astype(bf)

    tokens_n, wide = SEGS * SEG, ceil_to(SEGS * SEG, 128)
    n_dev = n_dp * n_v
    rows = table_ref.shape[0]
    lane = lax.broadcasted_iota(jnp.int32, (1, wide), 1)
    valid = lane < tokens_n
    device = lax.broadcasted_iota(jnp.int32, (n_dev, 1), 0)
    least = device * rows
    upper[...] = (lax.broadcasted_iota(jnp.int32, (wide, 1), 0) < lane).astype(bf)
    place = lax.broadcasted_iota(jnp.int32, (cap, 1), 0).astype(f32)
    row_at = lax.broadcasted_iota(jnp.int32, (1, rows), 1).astype(f32) + 1.0
    low = (p.d * n_v + p.v) * rows
    for k in range(1, n_dp):
        q.arrived(i0 + k - 1, ints_out.at[lax.rem(p.d + n_dp - k, n_dp)])
    most = jnp.zeros((1, 1), f32)
    batch = hold.shape[0] // n_dev
    for start in range(0, n_dp, batch):
        for i in range(batch):
            ids = ints_out[start + i, :, :wide]
            held = (ids >= least) & (ids < least + rows) & valid
            hold[i * n_dev : (i + 1) * n_dev, :] = held.astype(f32).astype(bf)
        before = dot(hold[...], upper[...])
        for i in range(batch):
            ids = ints_out[start + i, :, :wide]
            held = hold[i * n_dev : (i + 1) * n_dev, :].astype(f32)
            rank = jnp.sum(held * before[i * n_dev : (i + 1) * n_dev, :], axis=0, keepdims=True)
            holder = jnp.sum(held * device.astype(f32), axis=0, keepdims=True)
            most = jnp.maximum(most, jnp.max(rank, axis=1, keepdims=True))
            slot_out[start + i : start + i + 1, :] = jnp.where(valid, holder * cap + rank, -1.0)
            mine = (ids >= low) & (ids < low + rows) & valid
            row = jnp.where(mine, (ids - low).astype(f32) + 1.0, 0.0)
            taken = jnp.sum(jnp.where(rank == place, row, 0.0), axis=1, keepdims=True)
            pick = (taken == row_at).astype(f32).astype(bf)
            pick_out[(start + i) * cap : (start + i + 1) * cap, :] = pick
    rank_out[...] = jnp.broadcast_to(most, rank_out.shape)
    packed[...] = dot(pick_out[...], table_ref[...]).astype(bf).reshape(packed.shape)
    first = base
    for k in range(1, n_dp):
        to = lax.rem(p.d + k, n_dp)
        q.send(first + k - 1, packed.at[to], tok_out.at[p.d, p.v], others[k - 1])
    local = pltpu.make_async_copy(packed.at[p.d], tok_out.at[p.d, p.v], ls.at[1])
    local.start()
    base = base + n_dp - 1
    y0, c0 = base, base + n_dp * (p.Y - 1)

    def relay(slot, src, src_d):
        for k in range(1, p.Y):
            q.send(y0 + slot * (p.Y - 1) + k - 1, src, tok_out.at[src_d, p.v], p.yp(k))
        q.send(c0 + slot * p.Y, src, tok_out.at[src_d, p.v], p.cp)

    relay(0, packed.at[p.d], p.d)
    g1.start()
    g2.start()
    g0.step_a()
    g0.step_x()
    for k in range(1, n_dp):
        src_d = lax.rem(p.d + n_dp - k, n_dp)
        q.arrived(first + k - 1, tok_out.at[src_d, p.v])
        relay(k, tok_out.at[src_d, p.v], src_d)
    g1.step_a()
    g0.step_y()
    g1.step_x()
    g2.step_a()
    for slot in range(n_dp):
        src_d = lax.rem(p.d + n_dp - slot, n_dp)
        for j in range(1, p.Y):
            piece = tok_out.at[src_d, p.from_y(j) * 2 + p.c]
            q.arrived(y0 + slot * (p.Y - 1) + j - 1, piece)
            q.send(c0 + slot * p.Y + j, piece, piece, p.cp)
    g1.step_y()
    g2.step_x()
    for gather in gathers:
        gather.step_c()
    for slot in range(n_dp):
        src_d = lax.rem(p.d + n_dp - slot, n_dp)
        for j in range(p.Y):
            q.arrived(c0 + slot * p.Y + j, tok_out.at[src_d, p.from_y(j) * 2 + 1 - p.c])
    q.finish()
    own.wait()
    local.wait()


def run_front(masters, table, ints, cap, n_dp, n_v):
    f32, bf = jnp.float32, jnp.bfloat16
    count = 3 * Gather.count(n_dp, n_v) + 2 * (n_dp - 1) + n_dp * (n_v - 1)
    hbm = pl.BlockSpec(memory_space=pl.ANY)
    vmem = pl.BlockSpec(memory_space=pltpu.VMEM)
    wide = ceil_to(SEGS * SEG, 128)
    rows, rb = table.shape[0], masters[0].shape[0]
    cuts = max(1, n_v // 4)
    shape = (12 * cuts, rb, D // cuts)
    return pl.pallas_call(
        functools.partial(front_kernel, n_dp, n_v, cap),
        out_shape=(
            jax.ShapeDtypeStruct((n_dp,) + shape, bf),
            jax.ShapeDtypeStruct((n_dp, n_v, cap, D), bf),
            jax.ShapeDtypeStruct((n_dp,) + ints.shape, ints.dtype),
            jax.ShapeDtypeStruct((n_dp * cap, rows), bf),
            jax.ShapeDtypeStruct((n_dp, wide), f32),
            jax.ShapeDtypeStruct((8, 128), f32),
            jax.ShapeDtypeStruct(table.shape, bf),
        ),
        in_specs=[vmem] * 6,
        out_specs=(hbm, hbm, vmem, vmem, vmem, vmem, vmem),
        scratch_shapes=[
            pltpu.VMEM(shape, bf),
            pltpu.VMEM((rb, D), f32),
            pltpu.VMEM((n_dp, cap, D), bf),
            pltpu.VMEM((8 * n_dp * n_v, wide), bf),
            pltpu.VMEM((wide, wide), bf),
            pltpu.SemaphoreType.DMA((count,)),
            pltpu.SemaphoreType.DMA((count,)),
            pltpu.SemaphoreType.DMA((2,)),
        ],
        compiler_params=pltpu.CompilerParams(
            collective_id=0, has_side_effects=True, vmem_limit_bytes=48 << 20
        ),
    )(*masters, table, ints)


def head_kernel(
    n_dp, n_v, ch_ref, table_ref, label_ref, tags_ref,
    out_ref, dtab_ref, loss_ref,
    al, logits, dlog, st, sd, sv, lse_s, part, bc, by, bx, bz, pc, py, px, pr, br, ss, rs,
):
    f32, bf = jnp.float32, jnp.bfloat16
    p = Place(n_dp, n_v)
    A, Y = p.A, p.Y
    count = n_dp * MLM
    others = [(lax.rem(p.d + k, n_dp), p.v) for k in range(1, n_dp)]
    partners = [(p.d, lax.rem(p.v + k, n_v)) for k in range(1, n_v)]
    sem = pltpu.get_barrier_semaphore()
    for partner in others + partners:
        pl.semaphore_signal(sem, 1, device_id=partner, device_id_type=MESH)
    pl.semaphore_wait(sem, n_dp - 1 + n_v - 1)
    q = Copies(p.me, ss, rs)
    gather = Gather(p, q, 0, lambda d, v: al.at[d, v], shared=True)
    al[p.d] = ch_ref[...]
    gather.start()
    gather.step_a()
    gather.step_x()
    gather.step_y()
    gather.step_c()
    n = gather.end
    rows_v, total_m = ch_ref.shape[1], n_dp * MLM_PAD
    chosen = al[...].reshape(total_m, D)
    logits[...] = dot(table_ref[...], chosen, NT)
    rows = table_ref.shape[0]
    row_ids = (p.d * n_v + p.v) * rows + lax.broadcasted_iota(jnp.int32, (rows, 1), 0)
    hits = row_ids == label_ref[...]
    top = jnp.max(logits[...], axis=0, keepdims=True)
    stats = (
        top,
        jnp.sum(jnp.exp(logits[...] - top), axis=0, keepdims=True),
        jnp.sum(jnp.where(hits, logits[...], 0.0), axis=0, keepdims=True),
    )
    tall = total_m // 128
    for k, values in enumerate(stats):
        for r in range(tall):
            st[k * tall + r : k * tall + r + 1, :] = values[:, r * 128 : (r + 1) * 128]

    def merged(ref, amount):
        tops = [ref[k, :tall, :] for k in range(amount)]
        best = functools.reduce(jnp.maximum, tops)
        parts = [ref[k, tall : 2 * tall, :] * jnp.exp(tops[k] - best) for k in range(amount)]
        return best, sum(parts[1:], parts[0]), sum(ref[k, 2 * tall :, :] for k in range(amount))

    sd[p.d] = st[...]
    for k in range(1, n_dp):
        q.send(n + k - 1, st, sd.at[p.d], others[k - 1])
    for k in range(1, n_dp):
        q.arrived(n + k - 1, sd.at[lax.rem(p.d + n_dp - k, n_dp)])
    n = n + n_dp - 1
    for k, values in enumerate(merged(sd, n_dp)):
        sv[p.v, k * tall : (k + 1) * tall, :] = values
    for k in range(1, n_v):
        q.send(n + k - 1, sv.at[p.v], sv.at[p.v], partners[k - 1])
    for k in range(1, n_v):
        q.arrived(n + k - 1, sv.at[lax.rem(p.v + n_v - k, n_v)])
    n = n + n_v - 1
    best, total, target = merged(sv, n_v)
    lse = best + jnp.log(total)
    lse_s[...] = lse
    lost = jnp.sum(jnp.where(tags_ref[...] >= 0, lse - target, 0.0), axis=1, keepdims=True)
    lost = jnp.sum(lost, axis=0, keepdims=True) / count
    loss_ref[...] = jnp.broadcast_to(lost, loss_ref.shape)
    lse_row = jnp.concatenate([lse_s[r : r + 1, :] for r in range(tall)], axis=1)
    d_log = (jnp.exp(logits[...] - lse_row) - hits.astype(f32)) * (1.0 / count)
    dlog[...] = d_log.astype(bf)
    made = dot(dlog[...], table_ref[...], TN).astype(bf)
    part[...] = made.reshape(A, 2, Y, 2, rows_v, D)
    q.send(n, part.at[:, :, :, 1 - p.c], bc, p.cp)
    dtab_ref[...] = dot(dlog[...], chosen)
    q.arrived(n, bc)
    pc[...] = (part[:, :, :, p.c].astype(f32) + bc[...].astype(f32)).astype(bf)
    n = n + 1
    left, right = pl.ds(0, D // 2), pl.ds(D // 2, D // 2)
    y1, x1, x2, y2 = n, n + Y - 1, n + Y, n + Y + 1
    for k in range(1, Y):
        q.send(y1 + k - 1, pc.at[:, :, lax.rem(p.y + k, Y), :, left], by.at[k - 1], p.yp(k))
    q.send(x1, pc.at[:, 1 - p.x, :, :, right], bx.at[1], p.xp)
    total = pc[:, :, p.y, :, left].astype(f32)
    for k in range(1, Y):
        q.arrived(y1 + k - 1, by.at[k - 1])
        total = total + by[k - 1].astype(f32)
    py[...] = total.astype(bf)
    q.send(x2, py.at[:, 1 - p.x], bx.at[0, :, 0], p.xp)
    q.arrived(x1, bx.at[1])
    pr[...] = (pc[:, p.x, :, :, right].astype(f32) + bx[1].astype(f32)).astype(bf)
    for k in range(1, Y):
        q.send(y2 + k - 1, pr.at[:, lax.rem(p.y + k, Y)], br.at[k - 1], p.yp(k))
    q.arrived(x2, bx.at[0, :, 0])
    px[:, :, left] = (py[:, p.x].astype(f32) + bx[0, :, 0].astype(f32)).astype(bf)
    total = pr[:, p.y].astype(f32)
    for k in range(1, Y):
        q.arrived(y2 + k - 1, br.at[k - 1])
        total = total + br[k - 1].astype(f32)
    px[:, :, right] = total.astype(bf)
    n = n + 2 * Y
    for k in range(1, A):
        q.send(n + k - 1, px.at[p.to_a(k)], bz.at[k - 1], p.zp(k))
    total = px[p.a].astype(f32)
    for k in range(1, A):
        q.arrived(n + k - 1, bz.at[k - 1])
        total = total + bz[k - 1].astype(f32)
    n = n + A - 1
    out_ref[p.v] = total.astype(bf)
    for k in range(1, n_v):
        q.send(n + k - 1, out_ref.at[p.v], out_ref.at[p.v], partners[k - 1])
    for k in range(1, n_v):
        q.arrived(n + k - 1, out_ref.at[lax.rem(p.v + n_v - k, n_v)])
    q.finish()


def run_head(chosen, table, labels, n_dp, n_v):
    f32, kind = jnp.float32, chosen.dtype
    A, Y = n_dp // 2, n_v // 2
    _, rows_v, width = chosen.shape
    rows, total_m = table.shape[0], n_dp * MLM_PAD
    tall = total_m // 128
    count = Gather.count(n_dp, n_v) + n_dp - 1 + n_v - 1 + 1 + 2 * Y + A - 1 + n_v - 1
    vmem = pl.BlockSpec(memory_space=pltpu.VMEM)
    return pl.pallas_call(
        functools.partial(head_kernel, n_dp, n_v),
        out_shape=[
            jax.ShapeDtypeStruct(chosen.shape, kind),
            jax.ShapeDtypeStruct(table.shape, f32),
            jax.ShapeDtypeStruct((8, 128), f32),
        ],
        in_specs=[vmem] * 4,
        out_specs=[vmem] * 3,
        scratch_shapes=[
            pltpu.VMEM((n_dp,) + chosen.shape, kind),
            pltpu.VMEM((rows, total_m), f32),
            pltpu.VMEM((rows, total_m), kind),
            pltpu.VMEM((3 * tall, 128), f32),
            pltpu.VMEM((n_dp, 3 * tall, 128), f32),
            pltpu.VMEM((n_v, 3 * tall, 128), f32),
            pltpu.VMEM((tall, 128), f32),
            pltpu.VMEM((A, 2, Y, 2, rows_v, width), kind),
            pltpu.VMEM((A, 2, Y, rows_v, width), kind),
            pltpu.VMEM((Y - 1, A, 2, rows_v, width // 2), kind),
            pltpu.VMEM((2, A, Y, rows_v, width // 2), kind),
            pltpu.VMEM((A - 1, rows_v, width), kind),
            pltpu.VMEM((A, 2, Y, rows_v, width), kind),
            pltpu.VMEM((A, 2, rows_v, width // 2), kind),
            pltpu.VMEM((A, rows_v, width), kind),
            pltpu.VMEM((A, Y, rows_v, width // 2), kind),
            pltpu.VMEM((Y - 1, A, rows_v, width // 2), kind),
            pltpu.SemaphoreType.DMA((count,)),
            pltpu.SemaphoreType.DMA((count,)),
        ],
        compiler_params=pltpu.CompilerParams(
            collective_id=2, has_side_effects=True, vmem_limit_bytes=56 << 20
        ),
    )(chosen, table, labels.reshape(1, total_m), labels.reshape(tall, 128))


def norm_kernel(n_dp, n_v, layer_ref, small_ref, table_ref, out_ref, sd, sv, ss, rs):
    f32 = jnp.float32
    d, v = lax.axis_index("dp"), lax.axis_index("vocab")
    others = [(lax.rem(d + k, n_dp), v) for k in range(1, n_dp)]
    partners = [(d, lax.rem(v + k, n_v)) for k in range(1, n_v)]
    sem = pltpu.get_barrier_semaphore()
    for partner in others + partners:
        pl.semaphore_signal(sem, 1, device_id=partner, device_id_type=MESH)

    def square(values):
        values = values.astype(f32)
        values = values * values
        while values.ndim > 2:
            values = jnp.sum(values, axis=0)
        return jnp.sum(jnp.sum(values, axis=0, keepdims=True), axis=1, keepdims=True)

    total = square(table_ref[...])
    total = total + jnp.where(v == 0, square(layer_ref[...]), 0.0)
    total = total + jnp.where((v == 0) & (d == 0), square(small_ref[...]), 0.0)
    sd[d] = jnp.broadcast_to(total, sd.shape[1:])
    pl.semaphore_wait(sem, n_dp - 1 + n_v - 1)
    q = Copies((d, v), ss, rs)
    for k in range(1, n_dp):
        q.send(k - 1, sd.at[d], sd.at[d], others[k - 1])
    for k in range(1, n_dp):
        q.arrived(k - 1, sd.at[lax.rem(d + n_dp - k, n_dp)])
    sv[v] = jnp.sum(sd[...], axis=0)
    for k in range(1, n_v):
        q.send(n_dp + k - 2, sv.at[v], sv.at[v], partners[k - 1])
    for k in range(1, n_v):
        q.arrived(n_dp + k - 2, sv.at[lax.rem(v + n_v - k, n_v)])
    out_ref[...] = jnp.sum(sv[...], axis=0)
    q.finish()


def run_norm(layer, small, table, n_dp, n_v):
    f32 = jnp.float32
    vmem = pl.BlockSpec(memory_space=pltpu.VMEM)
    count = n_dp + n_v - 2
    return pl.pallas_call(
        functools.partial(norm_kernel, n_dp, n_v),
        out_shape=jax.ShapeDtypeStruct((8, 128), f32),
        in_specs=[vmem] * 3,
        out_specs=vmem,
        scratch_shapes=[
            pltpu.VMEM((n_dp, 8, 128), f32),
            pltpu.VMEM((n_v, 8, 128), f32),
            pltpu.SemaphoreType.DMA((count,)),
            pltpu.SemaphoreType.DMA((count,)),
        ],
        compiler_params=pltpu.CompilerParams(
            collective_id=4, has_side_effects=True, vmem_limit_bytes=40 << 20
        ),
    )(layer, small, table)


def adam_kernel(n_dp, cuts, scal_ref, table_g, block_g, small_g, *refs):
    f32 = jnp.float32
    n = 7
    ins, outs, bufs = refs[: 3 * n], refs[3 * n : 6 * n], refs[6 * n : 9 * n]
    up_g, ext_g, bias_g, sem_i, sem_o = refs[9 * n :]
    loads = [pltpu.make_async_copy(ins[k], bufs[k], sem_i.at[k]) for k in range(3 * n)]
    for copy in loads:
        copy.start()
    coef, one_hat, two_hat = scal_ref[0], scal_ref[1], scal_ref[2]
    rb, width = block_g.shape[1:]
    stores = []

    def change(i, at, cols, grad, rate=LR_BIG):
        master, first, second = bufs[3 * i : 3 * i + 3]
        g = grad.astype(f32) * coef
        one = BETA_ONE * first[at, cols] + (1.0 - BETA_ONE) * g
        two = BETA_TWO * second[at, cols] + (1.0 - BETA_TWO) * g * g
        old = master[at, cols]
        first[at, cols] = one
        second[at, cols] = two
        move = one * one_hat / (jnp.sqrt(two * two_hat) + ADAM_EPS) + DECAY * old
        master[at, cols] = old - rate * move

    def begin(i):
        for copy in loads[3 * i : 3 * i + 3]:
            copy.wait()

    def end(i):
        for k in range(3 * i, 3 * i + 3):
            copy = pltpu.make_async_copy(bufs[k], outs[k], sem_o.at[k])
            copy.start()
            stores.append(copy)

    def chunks(rows, act):
        size = 32 if rows % 32 == 0 else rows
        if size == rows:
            act(pl.ds(0, rows))
        else:

            def body(c, _):
                act(pl.ds(pl.multiple_of(c * size, size), size))
                return 0

            lax.fori_loop(0, rows // size, body, 0)

    every = slice(None)
    begin(0)
    chunks(bufs[0].shape[0], lambda at: change(0, at, every, table_g[at, :]))
    end(0)
    for i, blocks in ((1, range(3)), (2, range(3, 4))):
        begin(i)
        for j in blocks:
            for s in range(cuts):
                cols = pl.ds((j - blocks[0]) * D + s * width, width)
                chunks(rb, lambda at: change(i, at, cols, block_g[j * cuts + s, at, :]))
        end(i)
    begin(3)
    for j in range(4):
        for s in range(cuts):
            block = block_g[(4 + j) * cuts + s].astype(f32)
            for d in range(n_dp // cuts):
                to = (s * (n_dp // cuts) + d) * 4 * rb + j * rb
                up_g[:, to : to + rb] = block[:, d * rb : (d + 1) * rb]
    chunks(rb, lambda at: change(3, at, every, up_g[at, :]))
    end(3)
    begin(4)
    for j in range(4):
        for s in range(cuts):
            cols = pl.ds(s * width, width)

            def down(at, j=j, s=s, cols=cols):
                change(4, pl.ds(j * rb + at.start, at.size), cols, block_g[(8 + j) * cuts + s, at, :])

            chunks(rb, down)
    end(4)
    ext_g[...] = small_g[: ext_g.shape[0], :].astype(f32)
    begin(5)
    done = EXT // 8 * 8
    for at in (pl.ds(0, done // 2), pl.ds(done // 2, done // 2), pl.ds(done, EXT - done)):
        change(5, at, every, ext_g[at, :], LR_SMALL)
    end(5)
    begin(6)
    for j in range(4):
        for d in range(n_dp):
            piece = ext_g[EXT + 5 + j : EXT + 6 + j, d * rb : (d + 1) * rb]
            bias_g[:, d * 4 * rb + j * rb : d * 4 * rb + (j + 1) * rb] = piece
    for k in range(12):
        if 5 <= k < 9:
            grad = bias_g[:, (k - 5) * D : (k - 4) * D]
        else:
            grad = ext_g[EXT + k : EXT + k + 1, :]
        change(6, every, pl.ds(k * D, D), grad, LR_SMALL)
    end(6)
    for copy in stores:
        copy.wait()


def run_adam(scalars, table_g, block_g, small_g, states, n_dp, cuts):
    hbm = pl.BlockSpec(memory_space=pl.ANY)
    vmem = pl.BlockSpec(memory_space=pltpu.VMEM)
    flat = [array for state in states for array in state]
    n = len(flat)
    rb = block_g.shape[1]
    return pl.pallas_call(
        functools.partial(adam_kernel, n_dp, cuts),
        out_shape=[jax.ShapeDtypeStruct(a.shape, a.dtype) for a in flat],
        in_specs=[pl.BlockSpec(memory_space=pltpu.SMEM), vmem, vmem, vmem] + [hbm] * n,
        out_specs=[hbm] * n,
        scratch_shapes=[pltpu.VMEM(a.shape, a.dtype) for a in flat]
        + [
            pltpu.VMEM((rb, FF), jnp.float32),
            pltpu.VMEM((ceil_to(EXT + 12, 16), D), jnp.float32),
            pltpu.VMEM((1, FF), jnp.float32),
            pltpu.SemaphoreType.DMA((n,)),
            pltpu.SemaphoreType.DMA((n,)),
        ],
        compiler_params=pltpu.CompilerParams(vmem_limit_bytes=56 << 20),
    )(scalars, table_g, block_g, small_g, *flat)


def lane_mean(values):
    return jnp.sum(values, axis=-1, keepdims=True) * (1.0 / D)


def norm_parts(values):
    centered = values - lane_mean(values)
    rate = lax.rsqrt(lane_mean(centered * centered) + LN_EPS)
    return centered * rate, rate


def norm_back(values, grad, gain):
    unit, rate = norm_parts(values)
    scaled = grad * gain
    d_values = rate * (scaled - lane_mean(scaled) - unit * lane_mean(scaled * unit))
    return (
        d_values,
        jnp.sum(grad * unit, axis=0, keepdims=True),
        jnp.sum(grad, axis=0, keepdims=True),
    )


def dot(left, right, dims=((1,), (0,))):
    return lax.dot_general(left, right, (dims, ((), ())), preferred_element_type=jnp.float32)


NT = ((1,), (1,))
TN = ((0,), (0,))


def allowed_mask(row_ref, col_ref, seg):
    row, col = row_ref[seg], col_ref[seg]
    return (row == col) | (row < 0) | (col < 0)


def forward_kernel(
    w_hbm, tok_ref, slot_ref, row_ref, col_ref, reset_ref, vec_ref, ext_ref, pos_ref,
    x_o, hc_o, proj_o, p_o, one_o, mid_o, gp_o, act_o, two_o, chosen_o,
    w, x, hc, proj, probs, one, mid, gp, act, two, mask, hid, final, sem_w, sem_o,
):
    bf, f32 = jnp.bfloat16, jnp.float32
    loads = [pltpu.make_async_copy(w_hbm.at[:, b], w.at[b], sem_w.at[b]) for b in range(12)]
    for load in loads:
        load.start()
    waited = set()

    def weight(b):
        if b not in waited:
            loads[b].wait()
            waited.add(b)
        return w[b].reshape(D, D)

    stores = []

    def store(src, dst):
        copy = pltpu.make_async_copy(src, dst, sem_o.at[len(stores)])
        copy.start()
        stores.append(copy)

    vec = [vec_ref[k : k + 1, :] for k in range(12)]
    b_q, b_v, b_o, g_one, b_one = vec[:5]
    b_up, b_down, g_two, b_two = vec[5:9], vec[9], vec[10], vec[11]
    gain_e, bias_e = ext_ref[404:405, :], ext_ref[405:406, :]
    lane = lax.broadcasted_iota(jnp.int32, (1, 2 * HD), 1)
    low_half = lane < HD
    for seg in range(SEGS):
        rows = pl.ds(seg * ROWS, ROWS)
        held = lax.broadcasted_iota(jnp.int32, (1, tok_ref.shape[0]), 1).astype(f32)
        onehot = (slot_ref[rows, :] == held).astype(f32).astype(bf)
        x[seg] = dot(onehot, tok_ref[...]) + ext_ref[:ROWS, :]
        x[seg, ROWS - MEM :, :] += ext_ref[ROWS + MEM : ROWS + 2 * MEM, :]
        first = ext_ref[ROWS : ROWS + MEM, :]
        if seg == 0:
            x[seg, :MEM, :] += first
        else:
            x[seg, :MEM, :] += jnp.where(reset_ref[seg - 1] > 0, first, hid[ROWS - MEM :, :])
        store(x.at[seg], x_o.at[seg])
        mask[...] = allowed_mask(row_ref, col_ref, seg).astype(f32)
        unit, _ = norm_parts(x[seg])
        h = unit * gain_e + bias_e
        hid[...] = h
        h_low = h.astype(bf)
        hc[0, rows, :] = h_low
        for k, bias in ((0, b_q), (1, None), (2, b_v)):
            made = dot(h_low, weight(k))
            proj[k, rows, :] = (made if bias is None else made + bias).astype(bf)
        store(hc.at[0, rows], hc_o.at[0, rows])
        store(proj.at[:, rows], proj_o.at[:, rows])
        for pair in range(HEADS // 2):
            cols = pl.ds(pair * 2 * HD, 2 * HD)
            query, keyed, value = (proj[k, rows, cols] for k in range(3))
            query = query * jnp.asarray(HD ** (-0.5), bf)
            parts = []
            for side in range(2):
                keep = low_half if side == 0 else ~low_half
                scores = dot(jnp.where(keep, query, jnp.zeros_like(query)), keyed, NT)
                scores = jnp.where(mask[...] > 0, scores, MASKED)
                expd = jnp.exp(scores - jnp.max(scores, axis=-1, keepdims=True))
                p_low = (expd * (1.0 / jnp.sum(expd, axis=-1, keepdims=True))).astype(bf)
                probs[seg, pair * 2 + side] = p_low
                parts.append(dot(p_low, value))
            hc[1, rows, cols] = jnp.where(low_half, parts[0], parts[1]).astype(bf)
        store(probs.at[seg], p_o.at[seg])
        store(hc.at[1, rows], hc_o.at[1, rows])
        sum_one = hid[...] + (dot(hc[1, rows, :], weight(3)) + b_o)
        one[seg] = sum_one
        store(one.at[seg], one_o.at[seg])
        unit, _ = norm_parts(sum_one)
        mid_now = unit * g_one + b_one
        mid_low = mid_now.astype(bf)
        mid[rows, :] = mid_low
        store(mid.at[rows], mid_o.at[rows])
        for j in range(4):
            up = dot(mid_low, weight(4 + j)) + b_up[j]
            half = 0.5 * (1.0 + lax.erf(up * 0.7071067811865476))
            gp[j, rows, :] = (half + up * jnp.exp(-0.5 * up * up) * 0.3989422804014327).astype(bf)
            act[j, rows, :] = (up * half).astype(bf)
        store(gp.at[:, rows], gp_o.at[:, rows])
        store(act.at[:, rows], act_o.at[:, rows])
        total = mid_now + b_down
        for j in range(4):
            total = total + dot(act[j, rows, :], weight(8 + j))
        two[seg] = total
        store(two.at[seg], two_o.at[seg])
        unit, _ = norm_parts(total)
        h = unit * g_two + b_two
        hid[...] = h
        final[rows, :] = h.astype(bf)
    at = lax.broadcasted_iota(jnp.int32, (MLM_PAD, SEGS * ROWS), 1)
    chosen_o[...] = dot((at == pos_ref[...]).astype(bf), final[...]).astype(bf)
    for copy in stores:
        copy.wait()


def run_forward(w_all, tok, slot, marks, reset, vec, ext, pos):
    f32, bf = jnp.float32, jnp.bfloat16
    n = SEGS * ROWS
    saved = [
        ((SEGS, ROWS, D), f32),
        ((2, n, D), bf),
        ((3, n, D), bf),
        ((SEGS, HEADS, ROWS, ROWS), bf),
        ((SEGS, ROWS, D), f32),
        ((n, D), bf),
        ((4, n, D), bf),
        ((4, n, D), bf),
        ((SEGS, ROWS, D), f32),
    ]
    hbm = pl.BlockSpec(memory_space=pl.ANY)
    vmem = pl.BlockSpec(memory_space=pltpu.VMEM)
    return pl.pallas_call(
        forward_kernel,
        out_shape=[jax.ShapeDtypeStruct(s, k) for s, k in saved]
        + [jax.ShapeDtypeStruct((MLM_PAD, D), bf)],
        in_specs=[hbm] + [vmem] * 4 + [pl.BlockSpec(memory_space=pltpu.SMEM), vmem, vmem, vmem],
        out_specs=[hbm] * len(saved) + [vmem],
        scratch_shapes=[pltpu.VMEM((12, w_all.shape[0]) + w_all.shape[2:], bf)]
        + [pltpu.VMEM(s, k) for s, k in saved]
        + [
            pltpu.VMEM((ROWS, ROWS), f32),
            pltpu.VMEM((ROWS, D), f32),
            pltpu.VMEM((n, D), bf),
            pltpu.SemaphoreType.DMA((12,)),
            pltpu.SemaphoreType.DMA((SEGS * 10,)),
        ],
        compiler_params=pltpu.CompilerParams(vmem_limit_bytes=60 << 20),
    )(w_all, tok, slot[:, None], marks[:, None, :], marks[:, :, None], reset, vec, ext, pos[:, None])


def backward_kernel(
    n_dp, n_v,
    w_hbm, x_i, hc_i, proj_i, p_i, one_i, mid_i, gp_i, act_i, two_i,
    dch_ref, reset_ref, vec_ref, ext_ref, pos_ref, give_ref, slot_ref,
    g_out, e_out, t_out, dtok,
    w, x, hc, right, probs, one, mid, rup, act, two, rdown, grad, dmem,
    small_o, dpack, share, bx, px, bz, own_g, e_in, eb, own_e, sem_w, sem_i, ss, rs, ls,
):
    bf, f32 = jnp.bfloat16, jnp.float32
    p = Place(n_dp, n_v)
    A, Y = p.A, p.Y
    others = [(lax.rem(p.d + k, n_dp), p.v) for k in range(1, n_dp)]
    partners = [(p.d, lax.rem(p.v + k, n_v)) for k in range(1, n_v)]
    barrier = pltpu.get_barrier_semaphore()
    for partner in others + partners:
        pl.semaphore_signal(barrier, 1, device_id=partner, device_id_type=MESH)
    q = Copies(p.me, ss, rs)
    groups = share.shape[0]
    x0 = 0
    t0 = x0 + groups
    z0 = t0 + n_dp - 1
    e0 = z0 + groups * (A - 1)
    y0 = e0 + 2 * (n_dp - 1) + n_v - 1
    c0 = y0 + groups * (Y - 1)
    cuts = n_v // 4
    width = D // cuts
    block, cut = p.v // cuts, p.v % cuts
    cols_v = pl.ds(pl.multiple_of(cut * width, 128), width)

    def p_to(k):
        return lax.rem(p.d + k, n_dp)

    def p_from(k):
        return lax.rem(p.d + n_dp - k, n_dp)

    def make_share(g, left, right_cols):
        made = dot(left, right_cols, TN)
        share[g] = made.reshape(share.shape[1:]).astype(bf)
        q.send(x0 + g, share.at[g, :, 1 - p.x], bx.at[g], p.xp)

    def half_sums(g):
        q.arrived(x0 + g, bx.at[g])
        for k in range(1, A + 1):
            to = p.to_a(k)
            px[g, to] = (share[g, to, p.x].astype(f32) + bx[g, to].astype(f32)).astype(bf)
            if k < A:
                q.send(z0 + g * (A - 1) + k - 1, px.at[g, to], bz.at[g, k - 1], p.zp(k))

    small_o[...] = jnp.zeros_like(small_o)
    loads = {}
    state = {"n": 0}

    def load(name, src, dst):
        copy = pltpu.make_async_copy(src, dst, sem_i.at[state["n"]])
        state["n"] += 1
        copy.start()
        loads[name] = copy

    def need(name):
        if name in loads:
            loads.pop(name).wait()

    wl = [pltpu.make_async_copy(w_hbm.at[:, b], w.at[b], sem_w.at[b]) for b in range(12)]
    waited = set()

    def weight(b):
        if b not in waited:
            wl[b].wait()
            waited.add(b)
        return w[b].reshape(D, D)

    order = list(reversed(range(SEGS)))
    for i, seg in enumerate(order):
        rows = pl.ds(seg * ROWS, ROWS)
        load(("two", seg), two_i.at[seg], two.at[seg])
        if i == 0:
            for b in range(8, 12):
                wl[b].start()
        load(("gp", seg), gp_i.at[:, rows], rup.at[:, rows])
        if i == 0:
            for b in range(4, 8):
                wl[b].start()
        load(("one", seg), one_i.at[seg], one.at[seg])
        if i == 0:
            wl[3].start()
            load(("p", seg), p_i.at[seg], probs)
        load(("proj", seg), proj_i.at[:, rows], right.at[pl.ds(0, 3), rows])
        if i == 0:
            for b in range(3):
                wl[b].start()
        load(("x", seg), x_i.at[seg], x.at[seg])
    load("hc", hc_i, hc)
    load("mid", mid_i, mid)
    load("act", act_i, act)

    vec = [vec_ref[k : k + 1, :] for k in range(12)]
    g_one, g_two, gain_e = vec[3], vec[10], ext_ref[404:405, :]
    lane = lax.broadcasted_iota(jnp.int32, (1, 2 * HD), 1)
    low_half = lane < HD
    at = lax.broadcasted_iota(jnp.int32, (MLM_PAD, SEGS * ROWS), 1)
    at_pos = (at == pos_ref[...]).astype(bf)
    v0 = EXT

    def add_row(k, value):
        small_o[v0 + k : v0 + k + 1, :] += value

    def sums(values):
        return jnp.sum(values.astype(f32), axis=0, keepdims=True)

    for i, seg in enumerate(order):
        rows = pl.ds(seg * ROWS, ROWS)
        grad[...] = dot(at_pos[:, seg * ROWS : (seg + 1) * ROWS], dch_ref[...], TN)
        if i > 0:
            grad[ROWS - MEM :, :] += dmem[...]
        need(("two", seg))
        d_two, d_gain, d_shift = norm_back(two[seg], grad[...], g_two)
        add_row(10, d_gain)
        add_row(11, d_shift)
        r_down = d_two.astype(bf)
        rdown[rows, :] = r_down
        add_row(9, sums(r_down))
        if i == SEGS - 1:
            need("act")
            pl.semaphore_wait(barrier, n_dp - 1 + n_v - 1)
            make_share(2, act[block], rdown[:, cols_v])
        need(("gp", seg))
        for j in range(4):
            r_up = (rup[j, rows, :].astype(f32) * dot(r_down, weight(8 + j), NT)).astype(bf)
            rup[j, rows, :] = r_up
            add_row(5 + j, sums(r_up))
        if i == SEGS - 1:
            need("mid")
            make_share(1, mid[...], rup[block, :, cols_v])
        for j in range(4):
            d_two = d_two + dot(rup[j, rows, :], weight(4 + j), NT)
        need(("one", seg))
        d_one, d_gain, d_shift = norm_back(one[seg], d_two, g_one)
        add_row(3, d_gain)
        add_row(4, d_shift)
        grad[...] = d_one
        r_att = d_one.astype(bf)
        right[3, rows, :] = r_att
        add_row(2, sums(r_att))
        d_ctx = dot(r_att, weight(3), NT).astype(bf)
        need(("p", seg))
        need(("proj", seg))
        for pair in range(HEADS // 2):
            if i == SEGS - 1 and pair == HEADS // 3:
                half_sums(2)
            cols = pl.ds(pair * 2 * HD, 2 * HD)
            query, keyed, value = (right[k, rows, cols] for k in range(3))
            d_out = d_ctx[:, pair * 2 * HD : (pair + 1) * 2 * HD]
            made = []
            for side in range(2):
                keep = low_half if side == 0 else ~low_half
                p_low = probs[pair * 2 + side]
                p_now = p_low.astype(f32)
                d_p = dot(jnp.where(keep, d_out, jnp.zeros_like(d_out)), value, NT)
                weighted = p_now * d_p
                d_s = weighted - p_now * jnp.sum(weighted, axis=-1, keepdims=True)
                d_s = d_s.astype(bf)
                made.append((dot(d_s, keyed), dot(d_s, query, TN), dot(p_low, d_out, TN)))
            for k, scale in ((0, HD ** (-0.5)), (1, HD ** (-0.5)), (2, 1.0)):
                both = jnp.where(low_half, made[0][k], made[1][k]) * scale
                right[k, rows, cols] = both.astype(bf)
        if i + 1 < SEGS:
            load(("p", order[i + 1]), p_i.at[order[i + 1]], probs)
        if i == SEGS - 1:
            need("hc")
            make_share(0, hc[block // 3], right[block, :, cols_v])
        d_h = grad[...]
        for k in range(3):
            d_h = d_h + dot(right[k, rows, :], weight(k), NT)
        add_row(0, sums(right[0, rows, :]))
        add_row(1, sums(right[2, rows, :]))
        need(("x", seg))
        d_x, d_gain, d_shift = norm_back(x[seg], d_h, gain_e)
        grad[...] = d_x
        dtok[rows, :] = d_x.astype(bf)
        small_o[:ROWS, :] += d_x
        small_o[ROWS + MEM : ROWS + 2 * MEM, :] += grad[ROWS - MEM :, :]
        small_o[404:405, :] += d_gain
        small_o[405:406, :] += d_shift
        d_read = grad[:MEM, :]
        if seg > 0:
            back = reset_ref[seg - 1] > 0
            small_o[ROWS : ROWS + MEM, :] += jnp.where(back, d_read, 0.0)
            dmem[...] = jnp.where(back, 0.0, d_read)
        else:
            small_o[ROWS : ROWS + MEM, :] += d_read
    held = (give_ref[...] == slot_ref[...]).astype(f32).astype(bf)
    dpack[...] = dot(held, dtok[...]).astype(bf).reshape(dpack.shape)
    e_rows = e_in.shape[1]
    for d in range(n_dp):
        at = (d * n_v + p.v) * e_rows
        fits = at < small_o.shape[0]

        @pl.when(fits)
        def _(d=d, at=at):
            e_in[d] = small_o[pl.ds(pl.multiple_of(at, e_rows), e_rows), :].astype(bf)

        @pl.when(jnp.logical_not(fits))
        def _(d=d):
            e_in[d] = jnp.zeros(e_in.shape[1:], bf)

    for k in range(1, n_dp):
        q.send(e0 + k - 1, e_in.at[p_to(k)], eb.at[p.d], others[k - 1])
    eb[p.d] = e_in[p.d]
    locals_ = []

    def keep(src, dst):
        copy = pltpu.make_async_copy(src, dst, ls.at[len(locals_)])
        copy.start()
        locals_.append(copy)

    e1 = e0 + n_dp - 1
    e2 = e1 + n_dp - 1
    def whole_sums(g):
        total = px[g, p.a].astype(f32)
        for k in range(1, A):
            q.arrived(z0 + g * (A - 1) + k - 1, bz.at[g, k - 1])
            total = total + bz[g, k - 1].astype(f32)
        own_g[g] = total.astype(bf)
        mine = g_out.at[g * n_v + p.v]
        for k in range(1, Y):
            q.send(y0 + g * (Y - 1) + k - 1, own_g.at[g], mine, p.yp(k))
        q.send(c0 + g * Y, own_g.at[g], mine, p.cp)
        keep(own_g.at[g], mine)

    def hand_on(g):
        for j in range(1, Y):
            piece = g_out.at[g * n_v + p.from_y(j) * 2 + p.c]
            q.arrived(y0 + g * (Y - 1) + j - 1, piece)
            q.send(c0 + g * Y + j, piece, piece, p.cp)

    half_sums(1)
    for k in range(1, n_dp):
        q.arrived(e0 + k - 1, eb.at[p_from(k)])
    own_e[...] = jnp.sum(eb[...].astype(f32), axis=0).astype(bf)
    keep(own_e, e_out.at[p.d, p.v])
    for k in range(1, n_dp):
        q.send(e1 + k - 1, own_e, e_out.at[p.d, p.v], others[k - 1])
    half_sums(0)
    for k in range(1, n_dp):
        q.send(t0 + k - 1, dpack.at[p_to(k)], t_out.at[p.d], others[k - 1])
    keep(dpack.at[p.d], t_out.at[p.d])
    whole_sums(2)
    hand_on(2)
    for k in range(1, n_dp):
        q.arrived(e1 + k - 1, e_out.at[p_from(k), p.v])
    locals_[0].wait()
    for k in range(1, n_v):
        q.send(e2 + k - 1, e_out.at[:, p.v], e_out.at[:, p.v], partners[k - 1])
    whole_sums(1)
    hand_on(1)
    whole_sums(0)
    hand_on(0)
    for k in range(1, n_v):
        q.arrived(e2 + k - 1, e_out.at[:, lax.rem(p.v + n_v - k, n_v)])
    for g in range(groups):
        for j in range(Y):
            q.arrived(c0 + g * Y + j, g_out.at[g * n_v + p.from_y(j) * 2 + 1 - p.c])
    for k in range(1, n_dp):
        q.arrived(t0 + k - 1, t_out.at[p_from(k)])
    q.finish()
    for copy in locals_[1:]:
        copy.wait()


def run_backward(w_all, saved, d_chosen, reset, vec, ext, pos, give, slot, rb, n_dp, n_v):
    f32, bf = jnp.float32, jnp.bfloat16
    n = SEGS * ROWS
    A, Y, groups = n_dp // 2, n_v // 2, 3
    width = D // (n_v // 4)
    e_rows = ceil_to(-(-(EXT + 12) // (n_dp * n_v)), 16)
    cap = give.shape[0] // n_dp
    hbm = pl.BlockSpec(memory_space=pl.ANY)
    vmem = pl.BlockSpec(memory_space=pltpu.VMEM)
    smem = pl.BlockSpec(memory_space=pltpu.SMEM)
    count = groups * (1 + A - 1 + Y - 1 + Y) + 3 * (n_dp - 1) + n_v - 1
    return pl.pallas_call(
        functools.partial(backward_kernel, n_dp, n_v),
        out_shape=[
            jax.ShapeDtypeStruct((groups * n_v, rb, width), bf),
            jax.ShapeDtypeStruct((n_dp, n_v, e_rows, D), bf),
            jax.ShapeDtypeStruct((n_dp, cap, D), bf),
            jax.ShapeDtypeStruct((n, D), bf),
        ],
        in_specs=[hbm] * 10 + [vmem, smem] + [vmem] * 5,
        out_specs=[hbm, hbm, hbm, vmem],
        scratch_shapes=[
            pltpu.VMEM((12, w_all.shape[0]) + w_all.shape[2:], bf),
            pltpu.VMEM((SEGS, ROWS, D), f32),
            pltpu.VMEM((2, n, D), bf),
            pltpu.VMEM((4, n, D), bf),
            pltpu.VMEM((HEADS, ROWS, ROWS), bf),
            pltpu.VMEM((SEGS, ROWS, D), f32),
            pltpu.VMEM((n, D), bf),
            pltpu.VMEM((4, n, D), bf),
            pltpu.VMEM((4, n, D), bf),
            pltpu.VMEM((SEGS, ROWS, D), f32),
            pltpu.VMEM((n, D), bf),
            pltpu.VMEM((ROWS, D), f32),
            pltpu.VMEM((MEM, D), f32),
            pltpu.VMEM((ceil_to(EXT + 12, e_rows), D), f32),
            pltpu.VMEM((n_dp, cap, D), bf),
            pltpu.VMEM((groups, A, 2, rb, width), bf),
            pltpu.VMEM((groups, A, rb, width), bf),
            pltpu.VMEM((groups, A, rb, width), bf),
            pltpu.VMEM((groups, A - 1, rb, width), bf),
            pltpu.VMEM((groups, rb, width), bf),
            pltpu.VMEM((n_dp, e_rows, D), bf),
            pltpu.VMEM((n_dp, e_rows, D), bf),
            pltpu.VMEM((e_rows, D), bf),
            pltpu.SemaphoreType.DMA((12,)),
            pltpu.SemaphoreType.DMA((SEGS * 6 + 4,)),
            pltpu.SemaphoreType.DMA((count,)),
            pltpu.SemaphoreType.DMA((count,)),
            pltpu.SemaphoreType.DMA((2 + groups,)),
        ],
        compiler_params=pltpu.CompilerParams(
            collective_id=3, has_side_effects=True, vmem_limit_bytes=63 << 20
        ),
    )(
        w_all, *saved, d_chosen, reset, vec, ext, pos[:, None], give[:, None], slot[None, :],
    )


def ceil_to(value, unit):
    return -(-value // unit) * unit


def per_device(
    ids,
    docs,
    resets,
    mlm_pos,
    mlm_label,
    step,
    qkv_master,
    qkv_first,
    qkv_second,
    out_master,
    out_first,
    out_second,
    up_master,
    up_first,
    up_second,
    down_master,
    down_first,
    down_second,
    embed_master,
    embed_first,
    embed_second,
    vectors_master,
    vectors_first,
    vectors_second,
    extras_master,
    extras_first,
    extras_second,
):
    f32, bf = jnp.float32, jnp.bfloat16
    n_dp = lax.axis_size("dp")
    n_v = lax.axis_size("vocab")
    d_idx = lax.axis_index("dp")
    v_idx = lax.axis_index("vocab")
    own_rows = embed_master.shape[0]
    tokens_n = SEGS * SEG
    rb = qkv_master.shape[1]
    cuts = max(1, n_v // 4)
    width = D // cuts

    ints = jnp.concatenate([ids[0], mlm_label[0]])[None]
    ints = jnp.pad(ints, ((0, 0), (0, ceil_to(ints.shape[1], 128) - ints.shape[1])), constant_values=-1)
    cap = ceil_to(2 * tokens_n // (n_dp * n_v) + 2, 16)
    masters = (qkv_master[0], out_master[0], up_master[0], down_master[0])
    w_all, tok_all, ints_all, pick, slots, most, table = run_front(
        masters, embed_master, ints, cap, n_dp, n_v
    )
    if cuts > 1 or rb % 16:
        w_all = w_all.reshape(n_dp, 12, cuts, rb, width).transpose(1, 0, 3, 2, 4).reshape(1, 12, D, D)
    ids_all = ints_all[:, 0, :tokens_n]
    labels_all = ints_all[:, 0, tokens_n : tokens_n + MLM]
    labels_all = jnp.pad(labels_all, ((0, 0), (0, MLM_PAD - MLM)), constant_values=-1)
    overflow = most[0, 0] >= cap

    def padded(values):
        values = values.reshape((SEGS, SEG) + values.shape[1:])
        edges = ((0, 0), (MEM, MEM)) + ((0, 0),) * (values.ndim - 2)
        values = jnp.pad(values, edges, constant_values=-1)
        return values.reshape((SEGS * ROWS,) + values.shape[2:])

    slot = padded(lax.dynamic_index_in_dim(slots, d_idx, keepdims=False)[:tokens_n])

    def packed_tokens(_):
        return tok_all.reshape(n_dp * n_v * cap, D), slot

    def whole_tokens(_):
        whole = lax.all_gather(table, "dp", axis=0, tiled=True)
        at = jnp.arange(n_dp * own_rows, dtype=jnp.int32)
        row_ids = (at // own_rows * n_v + v_idx) * own_rows + at % own_rows
        onehot = (ids[0][:, None] == row_ids[None, :]).astype(bf)
        rows = lax.psum(jnp.dot(onehot, whole, preferred_element_type=f32).astype(bf), "vocab")
        rows = jnp.pad(rows, ((0, n_dp * n_v * cap - tokens_n), (0, 0)))
        return rows, padded(jnp.arange(tokens_n, dtype=jnp.int32).astype(f32))

    token_rows, token_slot = lax.cond(overflow, whole_tokens, packed_tokens, 0)
    marks = jnp.pad(docs.reshape(SEGS, SEG), ((0, 0), (MEM, MEM)), constant_values=-1)
    vec = vectors_master[0].reshape(12, D)
    b_up = vec[5:9].reshape(n_dp, 4, rb).transpose(1, 0, 2).reshape(4, D)
    vec = jnp.concatenate([vec[:5], b_up, vec[9:]])
    positions = mlm_pos[0]
    at_rows = positions // SEG * ROWS + MEM + positions % SEG
    at_rows = jnp.concatenate([at_rows, jnp.full((MLM_PAD - MLM,), -1, jnp.int32)])
    *saved, chosen = run_forward(w_all, token_rows, token_slot, marks, resets[0], vec, extras_master, at_rows)
    rows_v = MLM_PAD // n_v
    d_chosen, d_table, loss = run_head(chosen.reshape(n_v, rows_v, D), table, labels_all, n_dp, n_v)
    loss = loss[0, 0]
    d_chosen = d_chosen.reshape(MLM_PAD, D)
    at = jnp.arange(n_dp * cap, dtype=jnp.int32)
    give = ((at // cap * n_v + v_idx) * cap + at % cap).astype(f32)
    g_blocks, small_all, d_packed_all, d_tok = run_backward(
        w_all, saved, d_chosen, resets[0], vec, extras_master, at_rows, give, slot, rb, n_dp, n_v
    )

    def packed_d_table(_):
        return jnp.einsum(
            "tv,td->vd", pick, d_packed_all.reshape(n_dp * cap, D), preferred_element_type=f32
        )

    def whole_d_table(_):
        d_all = d_tok.reshape(SEGS, ROWS, D)[:, MEM : MEM + SEG].reshape(tokens_n, D)
        d_all = lax.all_gather(d_all, "dp", axis=0, tiled=True)
        row_ids = (d_idx * n_v + v_idx) * own_rows + jnp.arange(own_rows, dtype=jnp.int32)
        onehot = (ids_all.reshape(-1)[:, None] == row_ids[None, :]).astype(bf)
        return jnp.einsum("tv,td->vd", onehot, d_all, preferred_element_type=f32)

    s_table = d_table + lax.cond(overflow, whole_d_table, packed_d_table, 0)
    small_all = small_all.reshape(-1, D)
    norm = jnp.sqrt(run_norm(g_blocks, small_all, s_table, n_dp, n_v)[0, 0])
    coef = jnp.minimum(1.0, CLIP / (norm + 1e-06))
    t = step[0].astype(f32)
    scalars = jnp.stack([coef, 1.0 / (1.0 - BETA_ONE**t), 1.0 / (1.0 - BETA_TWO**t)])
    states = (
        (embed_master, embed_first, embed_second),
        (qkv_master[0], qkv_first[0], qkv_second[0]),
        (out_master[0], out_first[0], out_second[0]),
        (up_master[0], up_first[0], up_second[0]),
        (down_master[0], down_first[0], down_second[0]),
        (extras_master, extras_first, extras_second),
        (vectors_master, vectors_first, vectors_second),
    )
    new = run_adam(scalars, s_table, g_blocks, small_all, states, n_dp, cuts)
    layer = [value[None] for value in new[3:15]]
    return (loss, norm, *layer, *new[:3], *new[18:], *new[15:18])


def solution(mesh):
    in_specs = (
        P("dp", None),
        P("dp", None),
        P("dp", None),
        P("dp", None),
        P("dp", None),
        P(),
        P(None, "dp", None),
        P(None, "dp", None),
        P(None, "dp", None),
        P(None, "dp", None),
        P(None, "dp", None),
        P(None, "dp", None),
        P(None, "dp", None),
        P(None, "dp", None),
        P(None, "dp", None),
        P(None, "dp", None),
        P(None, "dp", None),
        P(None, "dp", None),
        P(("dp", "vocab"), None),
        P(("dp", "vocab"), None),
        P(("dp", "vocab"), None),
        P(),
        P(),
        P(),
        P(),
        P(),
        P(),
    )
    out_specs = (
        P(),
        P(),
        P(None, "dp", None),
        P(None, "dp", None),
        P(None, "dp", None),
        P(None, "dp", None),
        P(None, "dp", None),
        P(None, "dp", None),
        P(None, "dp", None),
        P(None, "dp", None),
        P(None, "dp", None),
        P(None, "dp", None),
        P(None, "dp", None),
        P(None, "dp", None),
        P(("dp", "vocab"), None),
        P(("dp", "vocab"), None),
        P(("dp", "vocab"), None),
        P(),
        P(),
        P(),
        P(),
        P(),
        P(),
    )
    return jax.shard_map(
        per_device, mesh=mesh, in_specs=in_specs, out_specs=out_specs, check_vma=False
    )
```

```python
import functools

import jax
import jax.numpy as jnp
from jax import lax
from jax.experimental import pallas as pl
from jax.experimental.pallas import tpu as pltpu
from jax.sharding import PartitionSpec as P

D = 768
HEADS = 12
HD = 64
FF = 3072
MEM = 10
SEG = 364
SEGS = 2
LAYERS = 1
MLM = 112
ROWS = 384


BETA_ONE = 0.9
BETA_TWO = 0.999
ADAM_EPS = 1e-08
DECAY = 0.01
LN_EPS = 1e-06
CLIP = 0.02
LR_BIG = 0.04
LR_SMALL = 0.5
MASKED = -1000000000.0


MESH = pl.DeviceIdType.MESH
MLM_PAD = 128
EXT = ROWS + 2 * MEM + 2


class Place:
    def __init__(self, n_dp, n_v):
        self.A, self.Y = n_dp // 2, n_v // 2
        self.d, self.v = lax.axis_index("dp"), lax.axis_index("vocab")
        self.a, self.x = self.d // 2, self.d % 2
        self.y, self.c = self.v // 2, self.v % 2
        self.me = (self.d, self.v)
        self.xp = (self.d + 1 - 2 * self.x, self.v)
        self.cp = (self.d, self.v + 1 - 2 * self.c)

    def from_a(self, k):
        return lax.rem(self.a + self.A - k, self.A)

    def to_a(self, k):
        return lax.rem(self.a + k, self.A)

    def from_y(self, k):
        return lax.rem(self.y + self.Y - k, self.Y)

    def zp(self, k):
        return (self.to_a(k) * 2 + self.x, self.v)

    def yp(self, k):
        return (self.d, lax.rem(self.y + k, self.Y) * 2 + self.c)

    def barrier(self, extra=()):
        sem = pltpu.get_barrier_semaphore()
        partners = [self.zp(k) for k in range(1, self.A)] + [self.xp]
        partners += [self.yp(k) for k in range(1, self.Y)] + [self.cp] + list(extra)
        for partner in partners:
            pl.semaphore_signal(sem, 1, device_id=partner, device_id_type=MESH)
        pl.semaphore_wait(sem, len(partners))


class Copies:
    def __init__(self, me, send_sem, recv_sem):
        self.me, self.send_sem, self.recv_sem, self.started = me, send_sem, recv_sem, []

    def send(self, number, src, dst, partner):
        copy = pltpu.make_async_remote_copy(
            src, dst, self.send_sem.at[number], self.recv_sem.at[number], partner, MESH
        )
        copy.start()
        self.started.append(copy)

    def arrived(self, number, dst):
        pltpu.make_async_remote_copy(
            dst, dst, self.send_sem.at[number], self.recv_sem.at[number], self.me, MESH
        ).wait_recv()

    def finish(self):
        for copy in self.started:
            copy.wait_send()


class Gather:
    def __init__(self, place, copies, base, ref, own=None, shared=False, flat=False):
        self.flat = flat
        self.p, self.q, self.base, self.ref, self.own = place, copies, base, ref, own
        self.least = 1 if shared else 0
        A, Y = place.A, place.Y
        self.x0 = base + A - 1
        self.y0 = self.x0 + A
        self.c0 = self.y0 + 2 * A * (Y - 1)
        self.end = self.c0 + 2 * A * Y

    @staticmethod
    def count(n_dp, n_v):
        A, Y = n_dp // 2, n_v // 2
        return A - 1 + A + 2 * A * (Y - 1) + 2 * A * Y

    def at(self, slot, j=0, c=None):
        p = self.p
        k = slot % p.A
        x = p.x if slot < p.A else 1 - p.x
        c = p.c if c is None else c
        return self.ref(p.from_a(k) * 2 + x, p.from_y(j) * 2 + c)

    def spread(self, slot):
        p = self.p
        src = self.at(slot) if (slot or self.own is None) else self.own
        if slot < p.A:
            self.q.send(self.x0 + slot, src, self.at(slot), p.xp)
        if slot < self.least:
            return
        if not self.flat:
            for k in range(1, p.Y):
                self.q.send(self.y0 + slot * (p.Y - 1) + k - 1, src, self.at(slot), p.yp(k))
        self.q.send(self.c0 + slot * p.Y, src, self.at(slot), p.cp)

    def start(self):
        p = self.p
        src = self.at(0) if self.own is None else self.own
        for k in range(1, p.A):
            self.q.send(self.base + k - 1, src, self.at(0), p.zp(k))
        self.spread(0)

    def step_a(self):
        for k in range(1, self.p.A):
            self.q.arrived(self.base + k - 1, self.at(k))
            self.spread(k)

    def step_x(self):
        A = self.p.A
        for k in range(A):
            self.q.arrived(self.x0 + k, self.at(A + k))
            self.spread(A + k)

    def step_y(self):
        p = self.p
        if self.flat:
            return
        for slot in range(self.least, 2 * p.A):
            for j in range(1, p.Y):
                self.q.arrived(self.y0 + slot * (p.Y - 1) + j - 1, self.at(slot, j))
                self.q.send(self.c0 + slot * p.Y + j, self.at(slot, j), self.at(slot, j), p.cp)

    def step_c(self):
        p = self.p
        for slot in range(self.least, 2 * p.A):
            for j in range(1 if self.flat else p.Y):
                self.q.arrived(self.c0 + slot * p.Y + j, self.at(slot, j, 1 - p.c))


def front_kernel(
    n_dp, n_v, cap, qkv_hbm, o_hbm, up_hbm, down_hbm, master_hbm, ints_ref,
    out_ref, tok_out, ints_out, pick_out, slot_out, rank_out, table_ref,
    qkv_ref, o_ref, up_ref, down_ref, master_ref,
    w_ref, upped, packed, hold, upper, ss, rs, ls,
):
    f32, bf = jnp.float32, jnp.bfloat16
    p = Place(n_dp, n_v)
    q = Copies(p.me, ss, rs)
    others = [(lax.rem(p.d + k, n_dp), p.v) for k in range(1, n_dp)]
    partners = [(p.d, lax.rem(p.v + k, n_v)) for k in range(1, n_v)]
    sem = pltpu.get_barrier_semaphore()
    for partner in others + partners:
        pl.semaphore_signal(sem, 1, device_id=partner, device_id_type=MESH)
    pairs = (qkv_hbm, qkv_ref), (o_hbm, o_ref), (up_hbm, up_ref), (down_hbm, down_ref), (master_hbm, master_ref)
    loads = [pltpu.make_async_copy(src, dst, ls.at[2 + k]) for k, (src, dst) in enumerate(pairs)]
    for load in loads:
        load.start()
    ints_out[p.d] = ints_ref[...]
    rb, width = w_ref.shape[1:]
    cuts = D // width

    def put(block, ref, row, col):
        for s in range(cuts):
            values = ref[row : row + rb, col + s * width : col + (s + 1) * width]
            w_ref[block * cuts + s] = values.astype(bf)

    loads[0].wait()
    loads[1].wait()
    for j in range(3):
        put(j, qkv_ref, 0, j * D)
    put(3, o_ref, 0, 0)
    pl.semaphore_wait(sem, n_dp - 1 + n_v - 1)
    base = 0
    for k in range(1, n_dp):
        q.send(base + k - 1, ints_ref, ints_out.at[p.d], others[k - 1])
    i0 = base
    base = base + n_dp - 1
    gathers = []
    for g in range(3):
        if g < 2:
            gather = Gather(
                p,
                q,
                base,
                lambda d, v, g=g: out_ref.at[d, g * n_v + v],
                own=w_ref.at[g * n_v + p.v],
                shared=True,
            )
        else:
            half = n_v // 2
            gather = Gather(
                p,
                q,
                base,
                lambda d, v: out_ref.at[d, pl.ds(2 * n_v + (v % 2) * half, half)],
                own=w_ref.at[pl.ds(2 * n_v + p.c * half, half)],
                shared=True,
                flat=True,
            )
        base = gather.end
        gathers.append(gather)
    g0, g1, g2 = gathers
    g0.start()
    for load in loads[2:]:
        load.wait()
    for j in range(4):
        for d in range(n_dp):
            at = (d * 4 + j) * rb
            upped[:, d * rb : (d + 1) * rb] = up_ref[:, at : at + rb]
        put(4 + j, upped, 0, 0)
        put(8 + j, down_ref, j * rb, 0)
    own = pltpu.make_async_copy(w_ref, out_ref.at[p.d], ls.at[0])
    own.start()
    table_ref[...] = master_ref[...].astype(bf)

    tokens_n, wide = SEGS * SEG, ceil_to(SEGS * SEG, 128)
    n_dev = n_dp * n_v
    rows = table_ref.shape[0]
    lane = lax.broadcasted_iota(jnp.int32, (1, wide), 1)
    valid = lane < tokens_n
    device = lax.broadcasted_iota(jnp.int32, (n_dev, 1), 0)
    least = device * rows
    upper[...] = (lax.broadcasted_iota(jnp.int32, (wide, 1), 0) < lane).astype(bf)
    place = lax.broadcasted_iota(jnp.int32, (cap, 1), 0).astype(f32)
    row_at = lax.broadcasted_iota(jnp.int32, (1, rows), 1).astype(f32) + 1.0
    low = (p.d * n_v + p.v) * rows
    for k in range(1, n_dp):
        q.arrived(i0 + k - 1, ints_out.at[lax.rem(p.d + n_dp - k, n_dp)])
    most = jnp.zeros((1, 1), f32)
    batch = hold.shape[0] // n_dev
    for start in range(0, n_dp, batch):
        for i in range(batch):
            ids = ints_out[start + i, :, :wide]
            held = (ids >= least) & (ids < least + rows) & valid
            hold[i * n_dev : (i + 1) * n_dev, :] = held.astype(f32).astype(bf)
        before = dot(hold[...], upper[...])
        for i in range(batch):
            ids = ints_out[start + i, :, :wide]
            held = hold[i * n_dev : (i + 1) * n_dev, :].astype(f32)
            rank = jnp.sum(held * before[i * n_dev : (i + 1) * n_dev, :], axis=0, keepdims=True)
            holder = jnp.sum(held * device.astype(f32), axis=0, keepdims=True)
            most = jnp.maximum(most, jnp.max(rank, axis=1, keepdims=True))
            slot_out[start + i : start + i + 1, :] = jnp.where(valid, holder * cap + rank, -1.0)
            mine = (ids >= low) & (ids < low + rows) & valid
            row = jnp.where(mine, (ids - low).astype(f32) + 1.0, 0.0)
            taken = jnp.sum(jnp.where(rank == place, row, 0.0), axis=1, keepdims=True)
            pick = (taken == row_at).astype(f32).astype(bf)
            pick_out[(start + i) * cap : (start + i + 1) * cap, :] = pick
    rank_out[...] = jnp.broadcast_to(most, rank_out.shape)
    packed[...] = dot(pick_out[...], table_ref[...]).astype(bf).reshape(packed.shape)
    first = base
    for k in range(1, n_dp):
        to = lax.rem(p.d + k, n_dp)
        q.send(first + k - 1, packed.at[to], tok_out.at[p.d, p.v], others[k - 1])
    local = pltpu.make_async_copy(packed.at[p.d], tok_out.at[p.d, p.v], ls.at[1])
    local.start()
    base = base + n_dp - 1
    y0, c0 = base, base + n_dp * (p.Y - 1)

    def relay(slot, src, src_d):
        for k in range(1, p.Y):
            q.send(y0 + slot * (p.Y - 1) + k - 1, src, tok_out.at[src_d, p.v], p.yp(k))
        q.send(c0 + slot * p.Y, src, tok_out.at[src_d, p.v], p.cp)

    relay(0, packed.at[p.d], p.d)
    g1.start()
    g2.start()
    g0.step_a()
    g0.step_x()
    for k in range(1, n_dp):
        src_d = lax.rem(p.d + n_dp - k, n_dp)
        q.arrived(first + k - 1, tok_out.at[src_d, p.v])
        relay(k, tok_out.at[src_d, p.v], src_d)
    g1.step_a()
    g0.step_y()
    g1.step_x()
    g2.step_a()
    for slot in range(n_dp):
        src_d = lax.rem(p.d + n_dp - slot, n_dp)
        for j in range(1, p.Y):
            piece = tok_out.at[src_d, p.from_y(j) * 2 + p.c]
            q.arrived(y0 + slot * (p.Y - 1) + j - 1, piece)
            q.send(c0 + slot * p.Y + j, piece, piece, p.cp)
    g1.step_y()
    g2.step_x()
    for gather in gathers:
        gather.step_c()
    for slot in range(n_dp):
        src_d = lax.rem(p.d + n_dp - slot, n_dp)
        for j in range(p.Y):
            q.arrived(c0 + slot * p.Y + j, tok_out.at[src_d, p.from_y(j) * 2 + 1 - p.c])
    q.finish()
    own.wait()
    local.wait()


def run_front(masters, table, ints, cap, n_dp, n_v):
    f32, bf = jnp.float32, jnp.bfloat16
    count = 3 * Gather.count(n_dp, n_v) + 2 * (n_dp - 1) + n_dp * (n_v - 1)
    hbm = pl.BlockSpec(memory_space=pl.ANY)
    vmem = pl.BlockSpec(memory_space=pltpu.VMEM)
    wide = ceil_to(SEGS * SEG, 128)
    rows, rb = table.shape[0], masters[0].shape[0]
    cuts = max(1, n_v // 4)
    shape = (12 * cuts, rb, D // cuts)
    return pl.pallas_call(
        functools.partial(front_kernel, n_dp, n_v, cap),
        out_shape=(
            jax.ShapeDtypeStruct((n_dp,) + shape, bf),
            jax.ShapeDtypeStruct((n_dp, n_v, cap, D), bf),
            jax.ShapeDtypeStruct((n_dp,) + ints.shape, ints.dtype),
            jax.ShapeDtypeStruct((n_dp * cap, rows), bf),
            jax.ShapeDtypeStruct((n_dp, wide), f32),
            jax.ShapeDtypeStruct((8, 128), f32),
            jax.ShapeDtypeStruct(table.shape, bf),
        ),
        in_specs=[hbm] * 5 + [vmem],
        out_specs=(hbm, hbm, vmem, vmem, vmem, vmem, vmem),
        scratch_shapes=[pltpu.VMEM(a.shape, f32) for a in (*masters, table)]
        + [
            pltpu.VMEM(shape, bf),
            pltpu.VMEM((rb, D), f32),
            pltpu.VMEM((n_dp, cap, D), bf),
            pltpu.VMEM((8 * n_dp * n_v, wide), bf),
            pltpu.VMEM((wide, wide), bf),
            pltpu.SemaphoreType.DMA((count,)),
            pltpu.SemaphoreType.DMA((count,)),
            pltpu.SemaphoreType.DMA((7,)),
        ],
        compiler_params=pltpu.CompilerParams(
            collective_id=0, has_side_effects=True, vmem_limit_bytes=62 << 20
        ),
    )(*masters, table, ints)


def head_kernel(
    n_dp, n_v, ch_ref, table_ref, label_ref, tags_ref,
    out_ref, dtab_ref, loss_ref,
    al, logits, dlog, st, sd, sv, lse_s, part, bc, by, bx, bz, pc, py, px, pr, br, ss, rs,
):
    f32, bf = jnp.float32, jnp.bfloat16
    p = Place(n_dp, n_v)
    A, Y = p.A, p.Y
    count = n_dp * MLM
    others = [(lax.rem(p.d + k, n_dp), p.v) for k in range(1, n_dp)]
    partners = [(p.d, lax.rem(p.v + k, n_v)) for k in range(1, n_v)]
    sem = pltpu.get_barrier_semaphore()
    for partner in others + partners:
        pl.semaphore_signal(sem, 1, device_id=partner, device_id_type=MESH)
    pl.semaphore_wait(sem, n_dp - 1 + n_v - 1)
    q = Copies(p.me, ss, rs)
    gather = Gather(p, q, 0, lambda d, v: al.at[d, v], shared=True)
    al[p.d] = ch_ref[...]
    gather.start()
    gather.step_a()
    gather.step_x()
    gather.step_y()
    gather.step_c()
    n = gather.end
    rows_v, total_m = ch_ref.shape[1], n_dp * MLM_PAD
    chosen = al[...].reshape(total_m, D)
    logits[...] = dot(table_ref[...], chosen, NT)
    rows = table_ref.shape[0]
    row_ids = (p.d * n_v + p.v) * rows + lax.broadcasted_iota(jnp.int32, (rows, 1), 0)
    hits = row_ids == label_ref[...]
    top = jnp.max(logits[...], axis=0, keepdims=True)
    stats = (
        top,
        jnp.sum(jnp.exp(logits[...] - top), axis=0, keepdims=True),
        jnp.sum(jnp.where(hits, logits[...], 0.0), axis=0, keepdims=True),
    )
    tall = total_m // 128
    for k, values in enumerate(stats):
        for r in range(tall):
            st[k * tall + r : k * tall + r + 1, :] = values[:, r * 128 : (r + 1) * 128]

    def merged(ref, amount):
        tops = [ref[k, :tall, :] for k in range(amount)]
        best = functools.reduce(jnp.maximum, tops)
        parts = [ref[k, tall : 2 * tall, :] * jnp.exp(tops[k] - best) for k in range(amount)]
        return best, sum(parts[1:], parts[0]), sum(ref[k, 2 * tall :, :] for k in range(amount))

    sd[p.d] = st[...]
    for k in range(1, n_dp):
        q.send(n + k - 1, st, sd.at[p.d], others[k - 1])
    for k in range(1, n_dp):
        q.arrived(n + k - 1, sd.at[lax.rem(p.d + n_dp - k, n_dp)])
    n = n + n_dp - 1
    for k, values in enumerate(merged(sd, n_dp)):
        sv[p.v, k * tall : (k + 1) * tall, :] = values
    for k in range(1, n_v):
        q.send(n + k - 1, sv.at[p.v], sv.at[p.v], partners[k - 1])
    for k in range(1, n_v):
        q.arrived(n + k - 1, sv.at[lax.rem(p.v + n_v - k, n_v)])
    n = n + n_v - 1
    best, total, target = merged(sv, n_v)
    lse = best + jnp.log(total)
    lse_s[...] = lse
    lost = jnp.sum(jnp.where(tags_ref[...] >= 0, lse - target, 0.0), axis=1, keepdims=True)
    lost = jnp.sum(lost, axis=0, keepdims=True) / count
    loss_ref[...] = jnp.broadcast_to(lost, loss_ref.shape)
    lse_row = jnp.concatenate([lse_s[r : r + 1, :] for r in range(tall)], axis=1)
    d_log = (jnp.exp(logits[...] - lse_row) - hits.astype(f32)) * (1.0 / count)
    dlog[...] = d_log.astype(bf)
    made = dot(dlog[...], table_ref[...], TN).astype(bf)
    part[...] = made.reshape(A, 2, Y, 2, rows_v, D)
    q.send(n, part.at[:, :, :, 1 - p.c], bc, p.cp)
    dtab_ref[...] = dot(dlog[...], chosen)
    q.arrived(n, bc)
    pc[...] = (part[:, :, :, p.c].astype(f32) + bc[...].astype(f32)).astype(bf)
    n = n + 1
    left, right = pl.ds(0, D // 2), pl.ds(D // 2, D // 2)
    y1, x1, x2, y2 = n, n + Y - 1, n + Y, n + Y + 1
    for k in range(1, Y):
        q.send(y1 + k - 1, pc.at[:, :, lax.rem(p.y + k, Y), :, left], by.at[k - 1], p.yp(k))
    q.send(x1, pc.at[:, 1 - p.x, :, :, right], bx.at[1], p.xp)
    total = pc[:, :, p.y, :, left].astype(f32)
    for k in range(1, Y):
        q.arrived(y1 + k - 1, by.at[k - 1])
        total = total + by[k - 1].astype(f32)
    py[...] = total.astype(bf)
    q.send(x2, py.at[:, 1 - p.x], bx.at[0, :, 0], p.xp)
    q.arrived(x1, bx.at[1])
    pr[...] = (pc[:, p.x, :, :, right].astype(f32) + bx[1].astype(f32)).astype(bf)
    for k in range(1, Y):
        q.send(y2 + k - 1, pr.at[:, lax.rem(p.y + k, Y)], br.at[k - 1], p.yp(k))
    q.arrived(x2, bx.at[0, :, 0])
    px[:, :, left] = (py[:, p.x].astype(f32) + bx[0, :, 0].astype(f32)).astype(bf)
    total = pr[:, p.y].astype(f32)
    for k in range(1, Y):
        q.arrived(y2 + k - 1, br.at[k - 1])
        total = total + br[k - 1].astype(f32)
    px[:, :, right] = total.astype(bf)
    n = n + 2 * Y
    for k in range(1, A):
        q.send(n + k - 1, px.at[p.to_a(k)], bz.at[k - 1], p.zp(k))
    total = px[p.a].astype(f32)
    for k in range(1, A):
        q.arrived(n + k - 1, bz.at[k - 1])
        total = total + bz[k - 1].astype(f32)
    n = n + A - 1
    out_ref[p.v] = total.astype(bf)
    for k in range(1, n_v):
        q.send(n + k - 1, out_ref.at[p.v], out_ref.at[p.v], partners[k - 1])
    for k in range(1, n_v):
        q.arrived(n + k - 1, out_ref.at[lax.rem(p.v + n_v - k, n_v)])
    q.finish()


def run_head(chosen, table, labels, n_dp, n_v):
    f32, kind = jnp.float32, chosen.dtype
    A, Y = n_dp // 2, n_v // 2
    _, rows_v, width = chosen.shape
    rows, total_m = table.shape[0], n_dp * MLM_PAD
    tall = total_m // 128
    count = Gather.count(n_dp, n_v) + n_dp - 1 + n_v - 1 + 1 + 2 * Y + A - 1 + n_v - 1
    vmem = pl.BlockSpec(memory_space=pltpu.VMEM)
    return pl.pallas_call(
        functools.partial(head_kernel, n_dp, n_v),
        out_shape=[
            jax.ShapeDtypeStruct(chosen.shape, kind),
            jax.ShapeDtypeStruct(table.shape, f32),
            jax.ShapeDtypeStruct((8, 128), f32),
        ],
        in_specs=[vmem] * 4,
        out_specs=[vmem] * 3,
        scratch_shapes=[
            pltpu.VMEM((n_dp,) + chosen.shape, kind),
            pltpu.VMEM((rows, total_m), f32),
            pltpu.VMEM((rows, total_m), kind),
            pltpu.VMEM((3 * tall, 128), f32),
            pltpu.VMEM((n_dp, 3 * tall, 128), f32),
            pltpu.VMEM((n_v, 3 * tall, 128), f32),
            pltpu.VMEM((tall, 128), f32),
            pltpu.VMEM((A, 2, Y, 2, rows_v, width), kind),
            pltpu.VMEM((A, 2, Y, rows_v, width), kind),
            pltpu.VMEM((Y - 1, A, 2, rows_v, width // 2), kind),
            pltpu.VMEM((2, A, Y, rows_v, width // 2), kind),
            pltpu.VMEM((A - 1, rows_v, width), kind),
            pltpu.VMEM((A, 2, Y, rows_v, width), kind),
            pltpu.VMEM((A, 2, rows_v, width // 2), kind),
            pltpu.VMEM((A, rows_v, width), kind),
            pltpu.VMEM((A, Y, rows_v, width // 2), kind),
            pltpu.VMEM((Y - 1, A, rows_v, width // 2), kind),
            pltpu.SemaphoreType.DMA((count,)),
            pltpu.SemaphoreType.DMA((count,)),
        ],
        compiler_params=pltpu.CompilerParams(
            collective_id=2, has_side_effects=True, vmem_limit_bytes=56 << 20
        ),
    )(chosen, table, labels.reshape(1, total_m), labels.reshape(tall, 128))


def norm_kernel(n_dp, n_v, layer_ref, small_ref, table_ref, out_ref, sd, sv, ss, rs):
    f32 = jnp.float32
    d, v = lax.axis_index("dp"), lax.axis_index("vocab")
    others = [(lax.rem(d + k, n_dp), v) for k in range(1, n_dp)]
    partners = [(d, lax.rem(v + k, n_v)) for k in range(1, n_v)]
    sem = pltpu.get_barrier_semaphore()
    for partner in others + partners:
        pl.semaphore_signal(sem, 1, device_id=partner, device_id_type=MESH)

    def square(values):
        values = values.astype(f32)
        values = values * values
        while values.ndim > 2:
            values = jnp.sum(values, axis=0)
        return jnp.sum(jnp.sum(values, axis=0, keepdims=True), axis=1, keepdims=True)

    total = square(table_ref[...])
    total = total + jnp.where(v == 0, square(layer_ref[...]), 0.0)
    total = total + jnp.where((v == 0) & (d == 0), square(small_ref[...]), 0.0)
    sd[d] = jnp.broadcast_to(total, sd.shape[1:])
    pl.semaphore_wait(sem, n_dp - 1 + n_v - 1)
    q = Copies((d, v), ss, rs)
    for k in range(1, n_dp):
        q.send(k - 1, sd.at[d], sd.at[d], others[k - 1])
    for k in range(1, n_dp):
        q.arrived(k - 1, sd.at[lax.rem(d + n_dp - k, n_dp)])
    sv[v] = jnp.sum(sd[...], axis=0)
    for k in range(1, n_v):
        q.send(n_dp + k - 2, sv.at[v], sv.at[v], partners[k - 1])
    for k in range(1, n_v):
        q.arrived(n_dp + k - 2, sv.at[lax.rem(v + n_v - k, n_v)])
    out_ref[...] = jnp.sum(sv[...], axis=0)
    q.finish()


def run_norm(layer, small, table, n_dp, n_v):
    f32 = jnp.float32
    vmem = pl.BlockSpec(memory_space=pltpu.VMEM)
    count = n_dp + n_v - 2
    return pl.pallas_call(
        functools.partial(norm_kernel, n_dp, n_v),
        out_shape=jax.ShapeDtypeStruct((8, 128), f32),
        in_specs=[vmem] * 3,
        out_specs=vmem,
        scratch_shapes=[
            pltpu.VMEM((n_dp, 8, 128), f32),
            pltpu.VMEM((n_v, 8, 128), f32),
            pltpu.SemaphoreType.DMA((count,)),
            pltpu.SemaphoreType.DMA((count,)),
        ],
        compiler_params=pltpu.CompilerParams(
            collective_id=4, has_side_effects=True, vmem_limit_bytes=40 << 20
        ),
    )(layer, small, table)


def adam_kernel(n_dp, cuts, scal_ref, table_g, block_g, small_g, *refs):
    f32 = jnp.float32
    n = 7
    ins, outs, bufs = refs[: 3 * n], refs[3 * n : 6 * n], refs[6 * n : 9 * n]
    up_g, ext_g, bias_g, sem_i, sem_o = refs[9 * n :]
    loads = [pltpu.make_async_copy(ins[k], bufs[k], sem_i.at[k]) for k in range(3 * n)]
    for copy in loads:
        copy.start()
    coef, one_hat, two_hat = scal_ref[0], scal_ref[1], scal_ref[2]
    rb, width = block_g.shape[1:]
    stores = []

    def change(i, at, cols, grad, rate=LR_BIG):
        master, first, second = bufs[3 * i : 3 * i + 3]
        g = grad.astype(f32) * coef
        one = BETA_ONE * first[at, cols] + (1.0 - BETA_ONE) * g
        two = BETA_TWO * second[at, cols] + (1.0 - BETA_TWO) * g * g
        old = master[at, cols]
        first[at, cols] = one
        second[at, cols] = two
        move = one * one_hat / (jnp.sqrt(two * two_hat) + ADAM_EPS) + DECAY * old
        master[at, cols] = old - rate * move

    def begin(i):
        for copy in loads[3 * i : 3 * i + 3]:
            copy.wait()

    def end(i):
        for k in range(3 * i, 3 * i + 3):
            copy = pltpu.make_async_copy(bufs[k], outs[k], sem_o.at[k])
            copy.start()
            stores.append(copy)

    def chunks(rows, act):
        size = 32 if rows % 32 == 0 else rows
        if size == rows:
            act(pl.ds(0, rows))
        else:

            def body(c, _):
                act(pl.ds(pl.multiple_of(c * size, size), size))
                return 0

            lax.fori_loop(0, rows // size, body, 0)

    every = slice(None)
    begin(0)
    chunks(bufs[0].shape[0], lambda at: change(0, at, every, table_g[at, :]))
    end(0)
    for i, blocks in ((1, range(3)), (2, range(3, 4))):
        begin(i)
        for j in blocks:
            for s in range(cuts):
                cols = pl.ds((j - blocks[0]) * D + s * width, width)
                chunks(rb, lambda at: change(i, at, cols, block_g[j * cuts + s, at, :]))
        end(i)
    begin(3)
    for j in range(4):
        for s in range(cuts):
            block = block_g[(4 + j) * cuts + s].astype(f32)
            for d in range(n_dp // cuts):
                to = (s * (n_dp // cuts) + d) * 4 * rb + j * rb
                up_g[:, to : to + rb] = block[:, d * rb : (d + 1) * rb]
    chunks(rb, lambda at: change(3, at, every, up_g[at, :]))
    end(3)
    begin(4)
    for j in range(4):
        for s in range(cuts):
            cols = pl.ds(s * width, width)

            def down(at, j=j, s=s, cols=cols):
                change(4, pl.ds(j * rb + at.start, at.size), cols, block_g[(8 + j) * cuts + s, at, :])

            chunks(rb, down)
    end(4)
    ext_g[...] = small_g[: ext_g.shape[0], :].astype(f32)
    begin(5)
    done = EXT // 8 * 8
    for at in (pl.ds(0, done // 2), pl.ds(done // 2, done // 2), pl.ds(done, EXT - done)):
        change(5, at, every, ext_g[at, :], LR_SMALL)
    end(5)
    begin(6)
    for j in range(4):
        for d in range(n_dp):
            piece = ext_g[EXT + 5 + j : EXT + 6 + j, d * rb : (d + 1) * rb]
            bias_g[:, d * 4 * rb + j * rb : d * 4 * rb + (j + 1) * rb] = piece
    for k in range(12):
        if 5 <= k < 9:
            grad = bias_g[:, (k - 5) * D : (k - 4) * D]
        else:
            grad = ext_g[EXT + k : EXT + k + 1, :]
        change(6, every, pl.ds(k * D, D), grad, LR_SMALL)
    end(6)
    for copy in stores:
        copy.wait()


def run_adam(scalars, table_g, block_g, small_g, states, n_dp, cuts):
    hbm = pl.BlockSpec(memory_space=pl.ANY)
    vmem = pl.BlockSpec(memory_space=pltpu.VMEM)
    flat = [array for state in states for array in state]
    n = len(flat)
    rb = block_g.shape[1]
    return pl.pallas_call(
        functools.partial(adam_kernel, n_dp, cuts),
        out_shape=[jax.ShapeDtypeStruct(a.shape, a.dtype) for a in flat],
        in_specs=[pl.BlockSpec(memory_space=pltpu.SMEM), vmem, vmem, vmem] + [hbm] * n,
        out_specs=[hbm] * n,
        scratch_shapes=[pltpu.VMEM(a.shape, a.dtype) for a in flat]
        + [
            pltpu.VMEM((rb, FF), jnp.float32),
            pltpu.VMEM((ceil_to(EXT + 12, 16), D), jnp.float32),
            pltpu.VMEM((1, FF), jnp.float32),
            pltpu.SemaphoreType.DMA((n,)),
            pltpu.SemaphoreType.DMA((n,)),
        ],
        compiler_params=pltpu.CompilerParams(vmem_limit_bytes=56 << 20),
    )(scalars, table_g, block_g, small_g, *flat)


def lane_mean(values):
    return jnp.sum(values, axis=-1, keepdims=True) * (1.0 / D)


def norm_parts(values):
    centered = values - lane_mean(values)
    rate = lax.rsqrt(lane_mean(centered * centered) + LN_EPS)
    return centered * rate, rate


def norm_back(values, grad, gain):
    unit, rate = norm_parts(values)
    scaled = grad * gain
    d_values = rate * (scaled - lane_mean(scaled) - unit * lane_mean(scaled * unit))
    return (
        d_values,
        jnp.sum(grad * unit, axis=0, keepdims=True),
        jnp.sum(grad, axis=0, keepdims=True),
    )


def dot(left, right, dims=((1,), (0,))):
    return lax.dot_general(left, right, (dims, ((), ())), preferred_element_type=jnp.float32)


NT = ((1,), (1,))
TN = ((0,), (0,))


def as_column(row):
    return jnp.broadcast_to(row, (128, row.shape[1])).T[:, :1]


def allowed_mask(row):
    col = as_column(row)
    return (row == col) | (row < 0) | (col < 0)


def forward_kernel(
    w_hbm, tok_ref, slot_ref, row_ref, reset_ref, vec_ref, ext_ref, pos_ref,
    x_o, hc_o, proj_o, p_o, one_o, mid_o, gp_o, act_o, two_o, chosen_o,
    w, x, hc, proj, probs, one, mid, gp, act, two, mask, hid, final, sem_w, sem_o,
):
    bf, f32 = jnp.bfloat16, jnp.float32
    loads = [pltpu.make_async_copy(w_hbm.at[:, b], w.at[b], sem_w.at[b]) for b in range(12)]
    for load in loads:
        load.start()
    waited = set()

    def weight(b):
        if b not in waited:
            loads[b].wait()
            waited.add(b)
        return w[b].reshape(D, D)

    stores = []

    def store(src, dst):
        copy = pltpu.make_async_copy(src, dst, sem_o.at[len(stores)])
        copy.start()
        stores.append(copy)

    vec = [vec_ref[k : k + 1, :] for k in range(12)]
    b_q, b_v, b_o, g_one, b_one = vec[:5]
    b_up, b_down, g_two, b_two = vec[5:9], vec[9], vec[10], vec[11]
    gain_e, bias_e = ext_ref[404:405, :], ext_ref[405:406, :]
    lane = lax.broadcasted_iota(jnp.int32, (1, 2 * HD), 1)
    low_half = lane < HD
    for seg in range(SEGS):
        rows = pl.ds(seg * ROWS, ROWS)
        held = lax.broadcasted_iota(jnp.int32, (1, tok_ref.shape[0]), 1).astype(f32)
        onehot = (as_column(slot_ref[:, seg * ROWS : (seg + 1) * ROWS]) == held).astype(f32).astype(bf)
        x[seg] = dot(onehot, tok_ref[...]) + ext_ref[:ROWS, :]
        x[seg, ROWS - MEM :, :] += ext_ref[ROWS + MEM : ROWS + 2 * MEM, :]
        first = ext_ref[ROWS : ROWS + MEM, :]
        if seg == 0:
            x[seg, :MEM, :] += first
        else:
            x[seg, :MEM, :] += jnp.where(reset_ref[seg - 1] > 0, first, hid[ROWS - MEM :, :])
        store(x.at[seg], x_o.at[seg])
        mask[...] = allowed_mask(row_ref[seg]).astype(f32)
        unit, _ = norm_parts(x[seg])
        h = unit * gain_e + bias_e
        hid[...] = h
        h_low = h.astype(bf)
        hc[0, rows, :] = h_low
        for k, bias in ((0, b_q), (1, None), (2, b_v)):
            made = dot(h_low, weight(k))
            proj[k, rows, :] = (made if bias is None else made + bias).astype(bf)
        store(hc.at[0, rows], hc_o.at[0, rows])
        store(proj.at[:, rows], proj_o.at[:, rows])
        for pair in range(HEADS // 2):
            cols = pl.ds(pair * 2 * HD, 2 * HD)
            query, keyed, value = (proj[k, rows, cols] for k in range(3))
            query = query * jnp.asarray(HD ** (-0.5), bf)
            parts = []
            for side in range(2):
                keep = low_half if side == 0 else ~low_half
                scores = dot(jnp.where(keep, query, jnp.zeros_like(query)), keyed, NT)
                scores = jnp.where(mask[...] > 0, scores, MASKED)
                expd = jnp.exp(scores - jnp.max(scores, axis=-1, keepdims=True))
                p_low = (expd * (1.0 / jnp.sum(expd, axis=-1, keepdims=True))).astype(bf)
                probs[seg, pair * 2 + side] = p_low
                parts.append(dot(p_low, value))
            hc[1, rows, cols] = jnp.where(low_half, parts[0], parts[1]).astype(bf)
        store(probs.at[seg], p_o.at[seg])
        store(hc.at[1, rows], hc_o.at[1, rows])
        sum_one = hid[...] + (dot(hc[1, rows, :], weight(3)) + b_o)
        one[seg] = sum_one
        store(one.at[seg], one_o.at[seg])
        unit, _ = norm_parts(sum_one)
        mid_now = unit * g_one + b_one
        mid_low = mid_now.astype(bf)
        mid[rows, :] = mid_low
        store(mid.at[rows], mid_o.at[rows])
        for j in range(4):
            up = dot(mid_low, weight(4 + j)) + b_up[j]
            half = 0.5 * (1.0 + lax.erf(up * 0.7071067811865476))
            gp[j, rows, :] = (half + up * jnp.exp(-0.5 * up * up) * 0.3989422804014327).astype(bf)
            act[j, rows, :] = (up * half).astype(bf)
        store(gp.at[:, rows], gp_o.at[:, rows])
        store(act.at[:, rows], act_o.at[:, rows])
        total = mid_now + b_down
        for j in range(4):
            total = total + dot(act[j, rows, :], weight(8 + j))
        two[seg] = total
        store(two.at[seg], two_o.at[seg])
        unit, _ = norm_parts(total)
        h = unit * g_two + b_two
        hid[...] = h
        final[rows, :] = h.astype(bf)
    at = lax.broadcasted_iota(jnp.int32, (SEGS * ROWS, 1), 0)
    at_pos = (at == pos_ref[...]).astype(f32).astype(bf)
    chosen_o[...] = dot(at_pos, final[...], TN).astype(bf)
    for copy in stores:
        copy.wait()


def run_forward(w_all, tok, slot, marks, reset, vec, ext, pos):
    f32, bf = jnp.float32, jnp.bfloat16
    n = SEGS * ROWS
    saved = [
        ((SEGS, ROWS, D), f32),
        ((2, n, D), bf),
        ((3, n, D), bf),
        ((SEGS, HEADS, ROWS, ROWS), bf),
        ((SEGS, ROWS, D), f32),
        ((n, D), bf),
        ((4, n, D), bf),
        ((4, n, D), bf),
        ((SEGS, ROWS, D), f32),
    ]
    hbm = pl.BlockSpec(memory_space=pl.ANY)
    vmem = pl.BlockSpec(memory_space=pltpu.VMEM)
    return pl.pallas_call(
        forward_kernel,
        out_shape=[jax.ShapeDtypeStruct(s, k) for s, k in saved]
        + [jax.ShapeDtypeStruct((MLM_PAD, D), bf)],
        in_specs=[hbm] + [vmem] * 3 + [pl.BlockSpec(memory_space=pltpu.SMEM), vmem, vmem, vmem],
        out_specs=[hbm] * len(saved) + [vmem],
        scratch_shapes=[pltpu.VMEM((12, w_all.shape[0]) + w_all.shape[2:], bf)]
        + [pltpu.VMEM(s, k) for s, k in saved]
        + [
            pltpu.VMEM((ROWS, ROWS), f32),
            pltpu.VMEM((ROWS, D), f32),
            pltpu.VMEM((n, D), bf),
            pltpu.SemaphoreType.DMA((12,)),
            pltpu.SemaphoreType.DMA((SEGS * 10,)),
        ],
        compiler_params=pltpu.CompilerParams(vmem_limit_bytes=60 << 20),
    )(w_all, tok, slot[None], marks[:, None, :].astype(f32), reset, vec, ext, pos[None])


def backward_kernel(
    n_dp, n_v,
    w_hbm, x_i, hc_i, proj_i, p_i, one_i, mid_i, gp_i, act_i, two_i,
    dch_ref, reset_ref, vec_ref, ext_ref, pos_ref, slot_ref,
    g_out, e_out, t_out, dtok,
    w, x, hc, right, probs, one, mid, rup, act, two, rdown, grad, dmem,
    small_o, dpack, share, bx, px, bz, own_g, e_in, eb, own_e, held, sem_w, sem_i, ss, rs, ls,
):
    bf, f32 = jnp.bfloat16, jnp.float32
    p = Place(n_dp, n_v)
    A, Y = p.A, p.Y
    others = [(lax.rem(p.d + k, n_dp), p.v) for k in range(1, n_dp)]
    partners = [(p.d, lax.rem(p.v + k, n_v)) for k in range(1, n_v)]
    barrier = pltpu.get_barrier_semaphore()
    for partner in others + partners:
        pl.semaphore_signal(barrier, 1, device_id=partner, device_id_type=MESH)
    q = Copies(p.me, ss, rs)
    groups = share.shape[0]
    x0 = 0
    t0 = x0 + groups * A
    z0 = t0 + n_dp - 1
    e0 = z0 + groups * (A - 1)
    y0 = e0 + 2 * (n_dp - 1) + n_v - 1
    c0 = y0 + groups * (Y - 1)
    cuts = n_v // 4
    width = D // cuts
    block, cut = p.v // cuts, p.v % cuts
    cols_v = pl.ds(pl.multiple_of(cut * width, 128), width)

    def p_to(k):
        return lax.rem(p.d + k, n_dp)

    def p_from(k):
        return lax.rem(p.d + n_dp - k, n_dp)

    def make_share(g, left, right_cols):
        made = dot(left, right_cols, TN)
        share[g] = made.reshape(share.shape[1:]).astype(bf)
        for k in range(1, A + 1):
            to = p.to_a(k)
            q.send(x0 + g * A + k - 1, share.at[g, to, 1 - p.x], bx.at[g, to], p.xp)

    def half_sum(g, k):
        to = p.to_a(k)
        q.arrived(x0 + g * A + k - 1, bx.at[g, to])
        px[g, to] = (share[g, to, p.x].astype(f32) + bx[g, to].astype(f32)).astype(bf)
        if k < A:
            q.send(z0 + g * (A - 1) + k - 1, px.at[g, to], bz.at[g, k - 1], p.zp(k))

    todo = [(g, k) for g in (2, 1, 0) for k in range(1, A + 1)]

    def half_sums(amount):
        for _ in range(amount):
            half_sum(*todo.pop(0))

    small_o[...] = jnp.zeros_like(small_o)
    loads = {}
    state = {"n": 0}

    def load(name, src, dst):
        copy = pltpu.make_async_copy(src, dst, sem_i.at[state["n"]])
        state["n"] += 1
        copy.start()
        loads[name] = copy

    def need(name):
        if name in loads:
            loads.pop(name).wait()

    wl = [pltpu.make_async_copy(w_hbm.at[:, b], w.at[b], sem_w.at[b]) for b in range(12)]
    waited = set()

    def weight(b):
        if b not in waited:
            wl[b].wait()
            waited.add(b)
        return w[b].reshape(D, D)

    order = list(reversed(range(SEGS)))
    for i, seg in enumerate(order):
        rows = pl.ds(seg * ROWS, ROWS)
        load(("two", seg), two_i.at[seg], two.at[seg])
        if i == 0:
            for b in range(8, 12):
                wl[b].start()
        load(("gp", seg), gp_i.at[:, rows], rup.at[:, rows])
        if i == 0:
            for b in range(4, 8):
                wl[b].start()
        load(("one", seg), one_i.at[seg], one.at[seg])
        if i == 0:
            wl[3].start()
            load(("p", seg), p_i.at[seg], probs)
        load(("proj", seg), proj_i.at[:, rows], right.at[pl.ds(0, 3), rows])
        if i == 0:
            for b in range(3):
                wl[b].start()
        load(("x", seg), x_i.at[seg], x.at[seg])
    load("hc", hc_i, hc)
    load("mid", mid_i, mid)
    load("act", act_i, act)

    vec = [vec_ref[k : k + 1, :] for k in range(12)]
    g_one, g_two, gain_e = vec[3], vec[10], ext_ref[404:405, :]
    lane = lax.broadcasted_iota(jnp.int32, (1, 2 * HD), 1)
    low_half = lane < HD
    at = lax.broadcasted_iota(jnp.int32, (SEGS * ROWS, 1), 0)
    at_pos = (at == pos_ref[...]).astype(f32).astype(bf)
    v0 = EXT

    def add_row(k, value):
        small_o[v0 + k : v0 + k + 1, :] += value

    def sums(values):
        return jnp.sum(values.astype(f32), axis=0, keepdims=True)

    for i, seg in enumerate(order):
        rows = pl.ds(seg * ROWS, ROWS)
        grad[...] = dot(at_pos[seg * ROWS : (seg + 1) * ROWS, :], dch_ref[...])
        if i > 0:
            grad[ROWS - MEM :, :] += dmem[...]
        need(("two", seg))
        d_two, d_gain, d_shift = norm_back(two[seg], grad[...], g_two)
        add_row(10, d_gain)
        add_row(11, d_shift)
        r_down = d_two.astype(bf)
        rdown[rows, :] = r_down
        add_row(9, sums(r_down))
        if i == SEGS - 1:
            need("act")
            pl.semaphore_wait(barrier, n_dp - 1 + n_v - 1)
            make_share(2, act[block], rdown[:, cols_v])
        need(("gp", seg))
        for j in range(4):
            r_up = (rup[j, rows, :].astype(f32) * dot(r_down, weight(8 + j), NT)).astype(bf)
            rup[j, rows, :] = r_up
            add_row(5 + j, sums(r_up))
        if i == SEGS - 1:
            need("mid")
            make_share(1, mid[...], rup[block, :, cols_v])
            half_sums(1)
        for j in range(4):
            d_two = d_two + dot(rup[j, rows, :], weight(4 + j), NT)
        need(("one", seg))
        d_one, d_gain, d_shift = norm_back(one[seg], d_two, g_one)
        add_row(3, d_gain)
        add_row(4, d_shift)
        grad[...] = d_one
        r_att = d_one.astype(bf)
        right[3, rows, :] = r_att
        add_row(2, sums(r_att))
        d_ctx = dot(r_att, weight(3), NT).astype(bf)
        need(("p", seg))
        need(("proj", seg))
        for pair in range(HEADS // 2):
            if i == SEGS - 1 and 0 < pair <= 3 and len(todo) > 2 * A:
                half_sums(1)
            cols = pl.ds(pair * 2 * HD, 2 * HD)
            query, keyed, value = (right[k, rows, cols] for k in range(3))
            d_out = d_ctx[:, pair * 2 * HD : (pair + 1) * 2 * HD]
            made = []
            for side in range(2):
                keep = low_half if side == 0 else ~low_half
                p_low = probs[pair * 2 + side]
                p_now = p_low.astype(f32)
                d_p = dot(jnp.where(keep, d_out, jnp.zeros_like(d_out)), value, NT)
                weighted = p_now * d_p
                d_s = weighted - p_now * jnp.sum(weighted, axis=-1, keepdims=True)
                d_s = d_s.astype(bf)
                made.append((dot(d_s, keyed), dot(d_s, query, TN), dot(p_low, d_out, TN)))
            for k, scale in ((0, HD ** (-0.5)), (1, HD ** (-0.5)), (2, 1.0)):
                both = jnp.where(low_half, made[0][k], made[1][k]) * scale
                right[k, rows, cols] = both.astype(bf)
        if i + 1 < SEGS:
            load(("p", order[i + 1]), p_i.at[order[i + 1]], probs)
        if i == SEGS - 1:
            need("hc")
            make_share(0, hc[block // 3], right[block, :, cols_v])
            half_sums(max(0, len(todo) - 2 * A) + 1)
        d_h = grad[...]
        for k in range(3):
            d_h = d_h + dot(right[k, rows, :], weight(k), NT)
        add_row(0, sums(right[0, rows, :]))
        add_row(1, sums(right[2, rows, :]))
        need(("x", seg))
        d_x, d_gain, d_shift = norm_back(x[seg], d_h, gain_e)
        grad[...] = d_x
        dtok[rows, :] = d_x.astype(bf)
        small_o[:ROWS, :] += d_x
        small_o[ROWS + MEM : ROWS + 2 * MEM, :] += grad[ROWS - MEM :, :]
        small_o[404:405, :] += d_gain
        small_o[405:406, :] += d_shift
        d_read = grad[:MEM, :]
        if seg > 0:
            back = reset_ref[seg - 1] > 0
            small_o[ROWS : ROWS + MEM, :] += jnp.where(back, d_read, 0.0)
            dmem[...] = jnp.where(back, 0.0, d_read)
        else:
            small_o[ROWS : ROWS + MEM, :] += d_read
    cap = dpack.shape[1]
    place = lax.broadcasted_iota(jnp.int32, (cap, 1), 0)
    for d in range(n_dp):
        slots = (place + (d * n_v + p.v) * cap).astype(f32)
        held[d * cap : (d + 1) * cap, :] = (slots == slot_ref[...]).astype(f32).astype(bf)
    dpack[...] = dot(held[...], dtok[...]).astype(bf).reshape(dpack.shape)
    e_rows = e_in.shape[1]
    for d in range(n_dp):
        at = (d * n_v + p.v) * e_rows
        fits = at < small_o.shape[0]

        @pl.when(fits)
        def _(d=d, at=at):
            e_in[d] = small_o[pl.ds(pl.multiple_of(at, e_rows), e_rows), :].astype(bf)

        @pl.when(jnp.logical_not(fits))
        def _(d=d):
            e_in[d] = jnp.zeros(e_in.shape[1:], bf)

    for k in range(1, n_dp):
        q.send(e0 + k - 1, e_in.at[p_to(k)], eb.at[p.d], others[k - 1])
    eb[p.d] = e_in[p.d]
    locals_ = []

    def keep(src, dst):
        copy = pltpu.make_async_copy(src, dst, ls.at[len(locals_)])
        copy.start()
        locals_.append(copy)

    e1 = e0 + n_dp - 1
    e2 = e1 + n_dp - 1
    def whole_sums(g):
        total = px[g, p.a].astype(f32)
        for k in range(1, A):
            q.arrived(z0 + g * (A - 1) + k - 1, bz.at[g, k - 1])
            total = total + bz[g, k - 1].astype(f32)
        own_g[g] = total.astype(bf)
        mine = g_out.at[g * n_v + p.v]
        for k in range(1, Y):
            q.send(y0 + g * (Y - 1) + k - 1, own_g.at[g], mine, p.yp(k))
        q.send(c0 + g * Y, own_g.at[g], mine, p.cp)
        keep(own_g.at[g], mine)

    def hand_on(g):
        for j in range(1, Y):
            piece = g_out.at[g * n_v + p.from_y(j) * 2 + p.c]
            q.arrived(y0 + g * (Y - 1) + j - 1, piece)
            q.send(c0 + g * Y + j, piece, piece, p.cp)

    half_sums(len(todo) - A)
    for k in range(1, n_dp):
        q.arrived(e0 + k - 1, eb.at[p_from(k)])
    own_e[...] = jnp.sum(eb[...].astype(f32), axis=0).astype(bf)
    keep(own_e, e_out.at[p.d, p.v])
    for k in range(1, n_dp):
        q.send(e1 + k - 1, own_e, e_out.at[p.d, p.v], others[k - 1])
    half_sums(len(todo))
    for k in range(1, n_dp):
        q.send(t0 + k - 1, dpack.at[p_to(k)], t_out.at[p.d], others[k - 1])
    keep(dpack.at[p.d], t_out.at[p.d])
    whole_sums(2)
    hand_on(2)
    for k in range(1, n_dp):
        q.arrived(e1 + k - 1, e_out.at[p_from(k), p.v])
    locals_[0].wait()
    for k in range(1, n_v):
        q.send(e2 + k - 1, e_out.at[:, p.v], e_out.at[:, p.v], partners[k - 1])
    whole_sums(1)
    hand_on(1)
    whole_sums(0)
    hand_on(0)
    for k in range(1, n_v):
        q.arrived(e2 + k - 1, e_out.at[:, lax.rem(p.v + n_v - k, n_v)])
    for g in range(groups):
        for j in range(Y):
            q.arrived(c0 + g * Y + j, g_out.at[g * n_v + p.from_y(j) * 2 + 1 - p.c])
    for k in range(1, n_dp):
        q.arrived(t0 + k - 1, t_out.at[p_from(k)])
    q.finish()
    for copy in locals_[1:]:
        copy.wait()


def run_backward(w_all, saved, d_chosen, reset, vec, ext, pos, slot, cap, rb, n_dp, n_v):
    f32, bf = jnp.float32, jnp.bfloat16
    n = SEGS * ROWS
    A, Y, groups = n_dp // 2, n_v // 2, 3
    width = D // (n_v // 4)
    e_rows = ceil_to(-(-(EXT + 12) // (n_dp * n_v)), 16)
    hbm = pl.BlockSpec(memory_space=pl.ANY)
    vmem = pl.BlockSpec(memory_space=pltpu.VMEM)
    smem = pl.BlockSpec(memory_space=pltpu.SMEM)
    count = groups * (A + A - 1 + Y - 1 + Y) + 3 * (n_dp - 1) + n_v - 1
    return pl.pallas_call(
        functools.partial(backward_kernel, n_dp, n_v),
        out_shape=[
            jax.ShapeDtypeStruct((groups * n_v, rb, width), bf),
            jax.ShapeDtypeStruct((n_dp, n_v, e_rows, D), bf),
            jax.ShapeDtypeStruct((n_dp, cap, D), bf),
            jax.ShapeDtypeStruct((n, D), bf),
        ],
        in_specs=[hbm] * 10 + [vmem, smem] + [vmem] * 4,
        out_specs=[hbm, hbm, hbm, vmem],
        scratch_shapes=[
            pltpu.VMEM((12, w_all.shape[0]) + w_all.shape[2:], bf),
            pltpu.VMEM((SEGS, ROWS, D), f32),
            pltpu.VMEM((2, n, D), bf),
            pltpu.VMEM((4, n, D), bf),
            pltpu.VMEM((HEADS, ROWS, ROWS), bf),
            pltpu.VMEM((SEGS, ROWS, D), f32),
            pltpu.VMEM((n, D), bf),
            pltpu.VMEM((4, n, D), bf),
            pltpu.VMEM((4, n, D), bf),
            pltpu.VMEM((SEGS, ROWS, D), f32),
            pltpu.VMEM((n, D), bf),
            pltpu.VMEM((ROWS, D), f32),
            pltpu.VMEM((MEM, D), f32),
            pltpu.VMEM((ceil_to(EXT + 12, e_rows), D), f32),
            pltpu.VMEM((n_dp, cap, D), bf),
            pltpu.VMEM((groups, A, 2, rb, width), bf),
            pltpu.VMEM((groups, A, rb, width), bf),
            pltpu.VMEM((groups, A, rb, width), bf),
            pltpu.VMEM((groups, A - 1, rb, width), bf),
            pltpu.VMEM((groups, rb, width), bf),
            pltpu.VMEM((n_dp, e_rows, D), bf),
            pltpu.VMEM((n_dp, e_rows, D), bf),
            pltpu.VMEM((e_rows, D), bf),
            pltpu.VMEM((n_dp * cap, n), bf),
            pltpu.SemaphoreType.DMA((12,)),
            pltpu.SemaphoreType.DMA((SEGS * 6 + 4,)),
            pltpu.SemaphoreType.DMA((count,)),
            pltpu.SemaphoreType.DMA((count,)),
            pltpu.SemaphoreType.DMA((2 + groups,)),
        ],
        compiler_params=pltpu.CompilerParams(
            collective_id=3, has_side_effects=True, vmem_limit_bytes=63 << 20
        ),
    )(
        w_all, *saved, d_chosen, reset, vec, ext, pos[None], slot[None],
    )


def ceil_to(value, unit):
    return -(-value // unit) * unit


def per_device(
    ids,
    docs,
    resets,
    mlm_pos,
    mlm_label,
    step,
    qkv_master,
    qkv_first,
    qkv_second,
    out_master,
    out_first,
    out_second,
    up_master,
    up_first,
    up_second,
    down_master,
    down_first,
    down_second,
    embed_master,
    embed_first,
    embed_second,
    vectors_master,
    vectors_first,
    vectors_second,
    extras_master,
    extras_first,
    extras_second,
):
    f32, bf = jnp.float32, jnp.bfloat16
    n_dp = lax.axis_size("dp")
    n_v = lax.axis_size("vocab")
    d_idx = lax.axis_index("dp")
    v_idx = lax.axis_index("vocab")
    own_rows = embed_master.shape[0]
    tokens_n = SEGS * SEG
    rb = qkv_master.shape[1]
    cuts = max(1, n_v // 4)
    width = D // cuts

    ints = jnp.concatenate([ids[0], mlm_label[0]])[None]
    ints = jnp.pad(ints, ((0, 0), (0, ceil_to(ints.shape[1], 128) - ints.shape[1])), constant_values=-1)
    cap = ceil_to(2 * tokens_n // (n_dp * n_v) + 2, 16)
    masters = (qkv_master[0], out_master[0], up_master[0], down_master[0])
    w_all, tok_all, ints_all, pick, slots, most, table = run_front(
        masters, embed_master, ints, cap, n_dp, n_v
    )
    if cuts > 1 or rb % 16:
        w_all = w_all.reshape(n_dp, 12, cuts, rb, width).transpose(1, 0, 3, 2, 4).reshape(1, 12, D, D)
    ids_all = ints_all[:, 0, :tokens_n]
    labels_all = ints_all[:, 0, tokens_n : tokens_n + MLM]
    labels_all = jnp.pad(labels_all, ((0, 0), (0, MLM_PAD - MLM)), constant_values=-1)
    overflow = most[0, 0] >= cap

    def padded(values):
        values = values.reshape((SEGS, SEG) + values.shape[1:])
        edges = ((0, 0), (MEM, MEM)) + ((0, 0),) * (values.ndim - 2)
        values = jnp.pad(values, edges, constant_values=-1)
        return values.reshape((SEGS * ROWS,) + values.shape[2:])

    slot = padded(lax.dynamic_index_in_dim(slots, d_idx, keepdims=False)[:tokens_n])

    def packed_tokens(_):
        return tok_all.reshape(n_dp * n_v * cap, D), slot

    def whole_tokens(_):
        whole = lax.all_gather(table, "dp", axis=0, tiled=True)
        at = jnp.arange(n_dp * own_rows, dtype=jnp.int32)
        row_ids = (at // own_rows * n_v + v_idx) * own_rows + at % own_rows
        onehot = (ids[0][:, None] == row_ids[None, :]).astype(bf)
        rows = lax.psum(jnp.dot(onehot, whole, preferred_element_type=f32).astype(bf), "vocab")
        rows = jnp.pad(rows, ((0, n_dp * n_v * cap - tokens_n), (0, 0)))
        return rows, padded(jnp.arange(tokens_n, dtype=jnp.int32).astype(f32))

    token_rows, token_slot = lax.cond(overflow, whole_tokens, packed_tokens, 0)
    marks = jnp.pad(docs.reshape(SEGS, SEG), ((0, 0), (MEM, MEM)), constant_values=-1)
    vec = vectors_master[0].reshape(12, D)
    b_up = vec[5:9].reshape(n_dp, 4, rb).transpose(1, 0, 2).reshape(4, D)
    vec = jnp.concatenate([vec[:5], b_up, vec[9:]])
    positions = mlm_pos[0]
    at_rows = positions // SEG * ROWS + MEM + positions % SEG
    at_rows = jnp.concatenate([at_rows, jnp.full((MLM_PAD - MLM,), -1, jnp.int32)])
    *saved, chosen = run_forward(w_all, token_rows, token_slot, marks, resets[0], vec, extras_master, at_rows)
    rows_v = MLM_PAD // n_v
    d_chosen, d_table, loss = run_head(chosen.reshape(n_v, rows_v, D), table, labels_all, n_dp, n_v)
    loss = loss[0, 0]
    d_chosen = d_chosen.reshape(MLM_PAD, D)
    g_blocks, small_all, d_packed_all, d_tok = run_backward(
        w_all, saved, d_chosen, resets[0], vec, extras_master, at_rows, slot, cap, rb, n_dp, n_v
    )

    def packed_d_table(_):
        return jnp.einsum(
            "tv,td->vd", pick, d_packed_all.reshape(n_dp * cap, D), preferred_element_type=f32
        )

    def whole_d_table(_):
        d_all = d_tok.reshape(SEGS, ROWS, D)[:, MEM : MEM + SEG].reshape(tokens_n, D)
        d_all = lax.all_gather(d_all, "dp", axis=0, tiled=True)
        row_ids = (d_idx * n_v + v_idx) * own_rows + jnp.arange(own_rows, dtype=jnp.int32)
        onehot = (ids_all.reshape(-1)[:, None] == row_ids[None, :]).astype(bf)
        return jnp.einsum("tv,td->vd", onehot, d_all, preferred_element_type=f32)

    s_table = d_table + lax.cond(overflow, whole_d_table, packed_d_table, 0)
    small_all = small_all.reshape(-1, D)
    norm = jnp.sqrt(run_norm(g_blocks, small_all, s_table, n_dp, n_v)[0, 0])
    coef = jnp.minimum(1.0, CLIP / (norm + 1e-06))
    t = step[0].astype(f32)
    scalars = jnp.stack([coef, 1.0 / (1.0 - BETA_ONE**t), 1.0 / (1.0 - BETA_TWO**t)])
    states = (
        (embed_master, embed_first, embed_second),
        (qkv_master[0], qkv_first[0], qkv_second[0]),
        (out_master[0], out_first[0], out_second[0]),
        (up_master[0], up_first[0], up_second[0]),
        (down_master[0], down_first[0], down_second[0]),
        (extras_master, extras_first, extras_second),
        (vectors_master, vectors_first, vectors_second),
    )
    new = run_adam(scalars, s_table, g_blocks, small_all, states, n_dp, cuts)
    layer = [value[None] for value in new[3:15]]
    return (loss, norm, *layer, *new[:3], *new[18:], *new[15:18])


def solution(mesh):
    in_specs = (
        P("dp", None),
        P("dp", None),
        P("dp", None),
        P("dp", None),
        P("dp", None),
        P(),
        P(None, "dp", None),
        P(None, "dp", None),
        P(None, "dp", None),
        P(None, "dp", None),
        P(None, "dp", None),
        P(None, "dp", None),
        P(None, "dp", None),
        P(None, "dp", None),
        P(None, "dp", None),
        P(None, "dp", None),
        P(None, "dp", None),
        P(None, "dp", None),
        P(("dp", "vocab"), None),
        P(("dp", "vocab"), None),
        P(("dp", "vocab"), None),
        P(),
        P(),
        P(),
        P(),
        P(),
        P(),
    )
    out_specs = (
        P(),
        P(),
        P(None, "dp", None),
        P(None, "dp", None),
        P(None, "dp", None),
        P(None, "dp", None),
        P(None, "dp", None),
        P(None, "dp", None),
        P(None, "dp", None),
        P(None, "dp", None),
        P(None, "dp", None),
        P(None, "dp", None),
        P(None, "dp", None),
        P(None, "dp", None),
        P(("dp", "vocab"), None),
        P(("dp", "vocab"), None),
        P(("dp", "vocab"), None),
        P(),
        P(),
        P(),
        P(),
        P(),
        P(),
    )
    return jax.shard_map(
        per_device, mesh=mesh, in_specs=in_specs, out_specs=out_specs, check_vma=False
    )
```

```python
import functools

import jax
import jax.numpy as jnp
from jax import lax
from jax.experimental import pallas as pl
from jax.experimental.pallas import tpu as pltpu
from jax.sharding import PartitionSpec as P

D = 768
HEADS = 12
HD = 64
FF = 3072
MEM = 10
SEG = 364
SEGS = 2
LAYERS = 1
MLM = 112
ROWS = 384


BETA_ONE = 0.9
BETA_TWO = 0.999
ADAM_EPS = 1e-08
DECAY = 0.01
LN_EPS = 1e-06
CLIP = 0.02
LR_BIG = 0.04
LR_SMALL = 0.5
MASKED = -1000000000.0


MESH = pl.DeviceIdType.MESH
MLM_PAD = 128
EXT = ROWS + 2 * MEM + 2


class Place:
    def __init__(self, n_dp, n_v):
        self.A, self.Y = n_dp // 2, n_v // 2
        self.d, self.v = lax.axis_index("dp"), lax.axis_index("vocab")
        self.a, self.x = self.d // 2, self.d % 2
        self.y, self.c = self.v // 2, self.v % 2
        self.me = (self.d, self.v)
        self.xp = (self.d + 1 - 2 * self.x, self.v)
        self.cp = (self.d, self.v + 1 - 2 * self.c)

    def from_a(self, k):
        return lax.rem(self.a + self.A - k, self.A)

    def to_a(self, k):
        return lax.rem(self.a + k, self.A)

    def from_y(self, k):
        return lax.rem(self.y + self.Y - k, self.Y)

    def zp(self, k):
        return (self.to_a(k) * 2 + self.x, self.v)

    def yp(self, k):
        return (self.d, lax.rem(self.y + k, self.Y) * 2 + self.c)

    def barrier(self, extra=()):
        sem = pltpu.get_barrier_semaphore()
        partners = [self.zp(k) for k in range(1, self.A)] + [self.xp]
        partners += [self.yp(k) for k in range(1, self.Y)] + [self.cp] + list(extra)
        for partner in partners:
            pl.semaphore_signal(sem, 1, device_id=partner, device_id_type=MESH)
        pl.semaphore_wait(sem, len(partners))


class Copies:
    def __init__(self, me, send_sem, recv_sem):
        self.me, self.send_sem, self.recv_sem, self.started = me, send_sem, recv_sem, []

    def send(self, number, src, dst, partner):
        copy = pltpu.make_async_remote_copy(
            src, dst, self.send_sem.at[number], self.recv_sem.at[number], partner, MESH
        )
        copy.start()
        self.started.append(copy)

    def arrived(self, number, dst):
        pltpu.make_async_remote_copy(
            dst, dst, self.send_sem.at[number], self.recv_sem.at[number], self.me, MESH
        ).wait_recv()

    def finish(self):
        for copy in self.started:
            copy.wait_send()


class Gather:
    def __init__(self, place, copies, base, ref, own=None, shared=False, flat=False):
        self.flat = flat
        self.p, self.q, self.base, self.ref, self.own = place, copies, base, ref, own
        self.least = 1 if shared else 0
        A, Y = place.A, place.Y
        self.x0 = base + A - 1
        self.y0 = self.x0 + A
        self.c0 = self.y0 + 2 * A * (Y - 1)
        self.end = self.c0 + 2 * A * Y

    @staticmethod
    def count(n_dp, n_v):
        A, Y = n_dp // 2, n_v // 2
        return A - 1 + A + 2 * A * (Y - 1) + 2 * A * Y

    def at(self, slot, j=0, c=None):
        p = self.p
        k = slot % p.A
        x = p.x if slot < p.A else 1 - p.x
        c = p.c if c is None else c
        return self.ref(p.from_a(k) * 2 + x, p.from_y(j) * 2 + c)

    def spread(self, slot):
        p = self.p
        src = self.at(slot) if (slot or self.own is None) else self.own
        if slot < p.A:
            self.q.send(self.x0 + slot, src, self.at(slot), p.xp)
        if slot < self.least:
            return
        if not self.flat:
            for k in range(1, p.Y):
                self.q.send(self.y0 + slot * (p.Y - 1) + k - 1, src, self.at(slot), p.yp(k))
        self.q.send(self.c0 + slot * p.Y, src, self.at(slot), p.cp)

    def start(self):
        p = self.p
        src = self.at(0) if self.own is None else self.own
        for k in range(1, p.A):
            self.q.send(self.base + k - 1, src, self.at(0), p.zp(k))
        self.spread(0)

    def step_a(self):
        for k in range(1, self.p.A):
            self.q.arrived(self.base + k - 1, self.at(k))
            self.spread(k)

    def step_x(self):
        A = self.p.A
        for k in range(A):
            self.q.arrived(self.x0 + k, self.at(A + k))
            self.spread(A + k)

    def step_y(self):
        p = self.p
        if self.flat:
            return
        for slot in range(self.least, 2 * p.A):
            for j in range(1, p.Y):
                self.q.arrived(self.y0 + slot * (p.Y - 1) + j - 1, self.at(slot, j))
                self.q.send(self.c0 + slot * p.Y + j, self.at(slot, j), self.at(slot, j), p.cp)

    def step_c(self):
        p = self.p
        for slot in range(self.least, 2 * p.A):
            for j in range(1 if self.flat else p.Y):
                self.q.arrived(self.c0 + slot * p.Y + j, self.at(slot, j, 1 - p.c))


def front_kernel(
    n_dp, n_v, cap, qkv_hbm, o_hbm, up_hbm, down_hbm, master_hbm, ints_ref,
    out_ref, tok_out, ints_out, pick_out, slot_out, rank_out, table_ref,
    qkv_ref, o_ref, up_ref, down_ref, master_ref,
    w_ref, upped, packed, hold, upper, ss, rs, ls,
):
    f32, bf = jnp.float32, jnp.bfloat16
    p = Place(n_dp, n_v)
    q = Copies(p.me, ss, rs)
    others = [(lax.rem(p.d + k, n_dp), p.v) for k in range(1, n_dp)]
    partners = [(p.d, lax.rem(p.v + k, n_v)) for k in range(1, n_v)]
    sem = pltpu.get_barrier_semaphore()
    for partner in others + partners:
        pl.semaphore_signal(sem, 1, device_id=partner, device_id_type=MESH)
    pairs = (qkv_hbm, qkv_ref), (o_hbm, o_ref), (up_hbm, up_ref), (down_hbm, down_ref), (master_hbm, master_ref)
    loads = [pltpu.make_async_copy(src, dst, ls.at[2 + k]) for k, (src, dst) in enumerate(pairs)]
    for load in loads:
        load.start()
    ints_out[p.d] = ints_ref[...]
    rb, width = w_ref.shape[1:]
    cuts = D // width

    def put(block, ref, row, col):
        for s in range(cuts):
            values = ref[row : row + rb, col + s * width : col + (s + 1) * width]
            w_ref[block * cuts + s] = values.astype(bf)

    loads[0].wait()
    loads[1].wait()
    for j in range(3):
        put(j, qkv_ref, 0, j * D)
    put(3, o_ref, 0, 0)
    pl.semaphore_wait(sem, n_dp - 1 + n_v - 1)
    base = 0
    for k in range(1, n_dp):
        q.send(base + k - 1, ints_ref, ints_out.at[p.d], others[k - 1])
    i0 = base
    base = base + n_dp - 1
    gathers = []
    for g in range(3):
        if g < 2:
            gather = Gather(
                p,
                q,
                base,
                lambda d, v, g=g: out_ref.at[d, g * n_v + v],
                own=w_ref.at[g * n_v + p.v],
                shared=True,
            )
        else:
            half = n_v // 2
            gather = Gather(
                p,
                q,
                base,
                lambda d, v: out_ref.at[d, pl.ds(2 * n_v + (v % 2) * half, half)],
                own=w_ref.at[pl.ds(2 * n_v + p.c * half, half)],
                shared=True,
                flat=True,
            )
        base = gather.end
        gathers.append(gather)
    g0, g1, g2 = gathers
    g0.start()
    for load in loads[2:]:
        load.wait()
    for j in range(4):
        for d in range(n_dp):
            at = (d * 4 + j) * rb
            upped[:, d * rb : (d + 1) * rb] = up_ref[:, at : at + rb]
        put(4 + j, upped, 0, 0)
        put(8 + j, down_ref, j * rb, 0)
    own = pltpu.make_async_copy(w_ref, out_ref.at[p.d], ls.at[0])
    own.start()
    table_ref[...] = master_ref[...].astype(bf)

    tokens_n, wide = SEGS * SEG, ceil_to(SEGS * SEG, 128)
    n_dev = n_dp * n_v
    rows = table_ref.shape[0]
    lane = lax.broadcasted_iota(jnp.int32, (1, wide), 1)
    valid = lane < tokens_n
    device = lax.broadcasted_iota(jnp.int32, (n_dev, 1), 0)
    least = device * rows
    upper[...] = (lax.broadcasted_iota(jnp.int32, (wide, 1), 0) < lane).astype(bf)
    place = lax.broadcasted_iota(jnp.int32, (cap, 1), 0).astype(f32)
    row_at = lax.broadcasted_iota(jnp.int32, (1, rows), 1).astype(f32) + 1.0
    low = (p.d * n_v + p.v) * rows
    for k in range(1, n_dp):
        q.arrived(i0 + k - 1, ints_out.at[lax.rem(p.d + n_dp - k, n_dp)])
    most = jnp.zeros((1, 1), f32)
    batch = hold.shape[0] // n_dev
    for start in range(0, n_dp, batch):
        for i in range(batch):
            ids = ints_out[start + i, :, :wide]
            held = (ids >= least) & (ids < least + rows) & valid
            hold[i * n_dev : (i + 1) * n_dev, :] = held.astype(f32).astype(bf)
        before = dot(hold[...], upper[...])
        for i in range(batch):
            ids = ints_out[start + i, :, :wide]
            held = hold[i * n_dev : (i + 1) * n_dev, :].astype(f32)
            rank = jnp.sum(held * before[i * n_dev : (i + 1) * n_dev, :], axis=0, keepdims=True)
            holder = jnp.sum(held * device.astype(f32), axis=0, keepdims=True)
            most = jnp.maximum(most, jnp.max(rank, axis=1, keepdims=True))
            slot_out[start + i : start + i + 1, :] = jnp.where(valid, holder * cap + rank, -1.0)
            mine = (ids >= low) & (ids < low + rows) & valid
            row = jnp.where(mine, (ids - low).astype(f32) + 1.0, 0.0)
            taken = jnp.sum(jnp.where(rank == place, row, 0.0), axis=1, keepdims=True)
            pick = (taken == row_at).astype(f32).astype(bf)
            pick_out[(start + i) * cap : (start + i + 1) * cap, :] = pick
    rank_out[...] = jnp.broadcast_to(most, rank_out.shape)
    packed[...] = dot(pick_out[...], table_ref[...]).astype(bf).reshape(packed.shape)
    first = base
    for k in range(1, n_dp):
        to = lax.rem(p.d + k, n_dp)
        q.send(first + k - 1, packed.at[to], tok_out.at[p.d, p.v], others[k - 1])
    local = pltpu.make_async_copy(packed.at[p.d], tok_out.at[p.d, p.v], ls.at[1])
    local.start()
    base = base + n_dp - 1
    y0, c0 = base, base + n_dp * (p.Y - 1)

    def relay(slot, src, src_d):
        for k in range(1, p.Y):
            q.send(y0 + slot * (p.Y - 1) + k - 1, src, tok_out.at[src_d, p.v], p.yp(k))
        q.send(c0 + slot * p.Y, src, tok_out.at[src_d, p.v], p.cp)

    relay(0, packed.at[p.d], p.d)
    g1.start()
    g2.start()
    g0.step_a()
    g0.step_x()
    for k in range(1, n_dp):
        src_d = lax.rem(p.d + n_dp - k, n_dp)
        q.arrived(first + k - 1, tok_out.at[src_d, p.v])
        relay(k, tok_out.at[src_d, p.v], src_d)
    g1.step_a()
    g0.step_y()
    g1.step_x()
    g2.step_a()
    for slot in range(n_dp):
        src_d = lax.rem(p.d + n_dp - slot, n_dp)
        for j in range(1, p.Y):
            piece = tok_out.at[src_d, p.from_y(j) * 2 + p.c]
            q.arrived(y0 + slot * (p.Y - 1) + j - 1, piece)
            q.send(c0 + slot * p.Y + j, piece, piece, p.cp)
    g1.step_y()
    g2.step_x()
    for gather in gathers:
        gather.step_c()
    for slot in range(n_dp):
        src_d = lax.rem(p.d + n_dp - slot, n_dp)
        for j in range(p.Y):
            q.arrived(c0 + slot * p.Y + j, tok_out.at[src_d, p.from_y(j) * 2 + 1 - p.c])
    q.finish()
    own.wait()
    local.wait()


def run_front(masters, table, ints, cap, n_dp, n_v):
    f32, bf = jnp.float32, jnp.bfloat16
    count = 3 * Gather.count(n_dp, n_v) + 2 * (n_dp - 1) + n_dp * (n_v - 1)
    hbm = pl.BlockSpec(memory_space=pl.ANY)
    vmem = pl.BlockSpec(memory_space=pltpu.VMEM)
    wide = ceil_to(SEGS * SEG, 128)
    rows, rb = table.shape[0], masters[0].shape[0]
    cuts = max(1, n_v // 4)
    shape = (12 * cuts, rb, D // cuts)
    return pl.pallas_call(
        functools.partial(front_kernel, n_dp, n_v, cap),
        out_shape=(
            jax.ShapeDtypeStruct((n_dp,) + shape, bf),
            jax.ShapeDtypeStruct((n_dp, n_v, cap, D), bf),
            jax.ShapeDtypeStruct((n_dp,) + ints.shape, ints.dtype),
            jax.ShapeDtypeStruct((n_dp * cap, rows), bf),
            jax.ShapeDtypeStruct((n_dp, wide), f32),
            jax.ShapeDtypeStruct((8, 128), f32),
            jax.ShapeDtypeStruct(table.shape, bf),
        ),
        in_specs=[hbm] * 5 + [vmem],
        out_specs=(hbm, hbm, vmem, vmem, vmem, vmem, vmem),
        scratch_shapes=[pltpu.VMEM(a.shape, f32) for a in (*masters, table)]
        + [
            pltpu.VMEM(shape, bf),
            pltpu.VMEM((rb, D), f32),
            pltpu.VMEM((n_dp, cap, D), bf),
            pltpu.VMEM((8 * n_dp * n_v, wide), bf),
            pltpu.VMEM((wide, wide), bf),
            pltpu.SemaphoreType.DMA((count,)),
            pltpu.SemaphoreType.DMA((count,)),
            pltpu.SemaphoreType.DMA((7,)),
        ],
        compiler_params=pltpu.CompilerParams(
            collective_id=0, has_side_effects=True, vmem_limit_bytes=62 << 20
        ),
    )(*masters, table, ints)


def head_kernel(
    n_dp, n_v, ch_ref, table_ref, label_ref, tags_ref,
    out_ref, dtab_ref, loss_ref,
    al, logits, dlog, st, sd, sv, lse_s, part, bc, by, bx, bz, pc, py, px, pr, br, ss, rs,
):
    f32, bf = jnp.float32, jnp.bfloat16
    p = Place(n_dp, n_v)
    A, Y = p.A, p.Y
    count = n_dp * MLM
    others = [(lax.rem(p.d + k, n_dp), p.v) for k in range(1, n_dp)]
    partners = [(p.d, lax.rem(p.v + k, n_v)) for k in range(1, n_v)]
    sem = pltpu.get_barrier_semaphore()
    for partner in others + partners:
        pl.semaphore_signal(sem, 1, device_id=partner, device_id_type=MESH)
    pl.semaphore_wait(sem, n_dp - 1 + n_v - 1)
    q = Copies(p.me, ss, rs)
    gather = Gather(p, q, 0, lambda d, v: al.at[d, v], shared=True)
    al[p.d] = ch_ref[...]
    gather.start()
    gather.step_a()
    gather.step_x()
    gather.step_y()
    gather.step_c()
    n = gather.end
    rows_v, total_m = ch_ref.shape[1], n_dp * MLM_PAD
    chosen = al[...].reshape(total_m, D)
    logits[...] = dot(table_ref[...], chosen, NT)
    rows = table_ref.shape[0]
    row_ids = (p.d * n_v + p.v) * rows + lax.broadcasted_iota(jnp.int32, (rows, 1), 0)
    hits = row_ids == label_ref[...]
    top = jnp.max(logits[...], axis=0, keepdims=True)
    stats = (
        top,
        jnp.sum(jnp.exp(logits[...] - top), axis=0, keepdims=True),
        jnp.sum(jnp.where(hits, logits[...], 0.0), axis=0, keepdims=True),
    )
    tall = total_m // 128
    for k, values in enumerate(stats):
        for r in range(tall):
            st[k * tall + r : k * tall + r + 1, :] = values[:, r * 128 : (r + 1) * 128]

    def merged(ref, amount):
        tops = [ref[k, :tall, :] for k in range(amount)]
        best = functools.reduce(jnp.maximum, tops)
        parts = [ref[k, tall : 2 * tall, :] * jnp.exp(tops[k] - best) for k in range(amount)]
        return best, sum(parts[1:], parts[0]), sum(ref[k, 2 * tall :, :] for k in range(amount))

    sd[p.d] = st[...]
    for k in range(1, n_dp):
        q.send(n + k - 1, st, sd.at[p.d], others[k - 1])
    for k in range(1, n_dp):
        q.arrived(n + k - 1, sd.at[lax.rem(p.d + n_dp - k, n_dp)])
    n = n + n_dp - 1
    for k, values in enumerate(merged(sd, n_dp)):
        sv[p.v, k * tall : (k + 1) * tall, :] = values
    for k in range(1, n_v):
        q.send(n + k - 1, sv.at[p.v], sv.at[p.v], partners[k - 1])
    for k in range(1, n_v):
        q.arrived(n + k - 1, sv.at[lax.rem(p.v + n_v - k, n_v)])
    n = n + n_v - 1
    best, total, target = merged(sv, n_v)
    lse = best + jnp.log(total)
    lse_s[...] = lse
    lost = jnp.sum(jnp.where(tags_ref[...] >= 0, lse - target, 0.0), axis=1, keepdims=True)
    lost = jnp.sum(lost, axis=0, keepdims=True) / count
    loss_ref[...] = lost
    lse_row = jnp.concatenate([lse_s[r : r + 1, :] for r in range(tall)], axis=1)
    d_log = (jnp.exp(logits[...] - lse_row) - hits.astype(f32)) * (1.0 / count)
    dlog[...] = d_log.astype(bf)
    made = dot(dlog[...], table_ref[...], TN).astype(bf)
    part[...] = made.reshape(A, 2, Y, 2, rows_v, D)
    q.send(n, part.at[:, :, :, 1 - p.c], bc, p.cp)
    dtab_ref[...] = dot(dlog[...], chosen)
    q.arrived(n, bc)
    pc[...] = (part[:, :, :, p.c].astype(f32) + bc[...].astype(f32)).astype(bf)
    n = n + 1
    left, right = pl.ds(0, D // 2), pl.ds(D // 2, D // 2)
    y1, x1, x2, y2 = n, n + Y - 1, n + Y, n + Y + 1
    for k in range(1, Y):
        q.send(y1 + k - 1, pc.at[:, :, lax.rem(p.y + k, Y), :, left], by.at[k - 1], p.yp(k))
    q.send(x1, pc.at[:, 1 - p.x, :, :, right], bx.at[1], p.xp)
    total = pc[:, :, p.y, :, left].astype(f32)
    for k in range(1, Y):
        q.arrived(y1 + k - 1, by.at[k - 1])
        total = total + by[k - 1].astype(f32)
    py[...] = total.astype(bf)
    q.send(x2, py.at[:, 1 - p.x], bx.at[0, :, 0], p.xp)
    q.arrived(x1, bx.at[1])
    pr[...] = (pc[:, p.x, :, :, right].astype(f32) + bx[1].astype(f32)).astype(bf)
    for k in range(1, Y):
        q.send(y2 + k - 1, pr.at[:, lax.rem(p.y + k, Y)], br.at[k - 1], p.yp(k))
    q.arrived(x2, bx.at[0, :, 0])
    px[:, :, left] = (py[:, p.x].astype(f32) + bx[0, :, 0].astype(f32)).astype(bf)
    total = pr[:, p.y].astype(f32)
    for k in range(1, Y):
        q.arrived(y2 + k - 1, br.at[k - 1])
        total = total + br[k - 1].astype(f32)
    px[:, :, right] = total.astype(bf)
    n = n + 2 * Y
    for k in range(1, A):
        q.send(n + k - 1, px.at[p.to_a(k)], bz.at[k - 1], p.zp(k))
    total = px[p.a].astype(f32)
    for k in range(1, A):
        q.arrived(n + k - 1, bz.at[k - 1])
        total = total + bz[k - 1].astype(f32)
    n = n + A - 1
    out_ref[p.v] = total.astype(bf)
    for k in range(1, n_v):
        q.send(n + k - 1, out_ref.at[p.v], out_ref.at[p.v], partners[k - 1])
    for k in range(1, n_v):
        q.arrived(n + k - 1, out_ref.at[lax.rem(p.v + n_v - k, n_v)])
    q.finish()


def run_head(chosen, table, labels, n_dp, n_v):
    f32, kind = jnp.float32, chosen.dtype
    A, Y = n_dp // 2, n_v // 2
    _, rows_v, width = chosen.shape
    rows, total_m = table.shape[0], n_dp * MLM_PAD
    tall = total_m // 128
    count = Gather.count(n_dp, n_v) + n_dp - 1 + n_v - 1 + 1 + 2 * Y + A - 1 + n_v - 1
    vmem = pl.BlockSpec(memory_space=pltpu.VMEM)
    return pl.pallas_call(
        functools.partial(head_kernel, n_dp, n_v),
        out_shape=[
            jax.ShapeDtypeStruct(chosen.shape, kind),
            jax.ShapeDtypeStruct(table.shape, f32),
            jax.ShapeDtypeStruct((1, 1), f32),
        ],
        in_specs=[vmem] * 4,
        out_specs=[vmem] * 3,
        scratch_shapes=[
            pltpu.VMEM((n_dp,) + chosen.shape, kind),
            pltpu.VMEM((rows, total_m), f32),
            pltpu.VMEM((rows, total_m), kind),
            pltpu.VMEM((3 * tall, 128), f32),
            pltpu.VMEM((n_dp, 3 * tall, 128), f32),
            pltpu.VMEM((n_v, 3 * tall, 128), f32),
            pltpu.VMEM((tall, 128), f32),
            pltpu.VMEM((A, 2, Y, 2, rows_v, width), kind),
            pltpu.VMEM((A, 2, Y, rows_v, width), kind),
            pltpu.VMEM((Y - 1, A, 2, rows_v, width // 2), kind),
            pltpu.VMEM((2, A, Y, rows_v, width // 2), kind),
            pltpu.VMEM((A - 1, rows_v, width), kind),
            pltpu.VMEM((A, 2, Y, rows_v, width), kind),
            pltpu.VMEM((A, 2, rows_v, width // 2), kind),
            pltpu.VMEM((A, rows_v, width), kind),
            pltpu.VMEM((A, Y, rows_v, width // 2), kind),
            pltpu.VMEM((Y - 1, A, rows_v, width // 2), kind),
            pltpu.SemaphoreType.DMA((count,)),
            pltpu.SemaphoreType.DMA((count,)),
        ],
        compiler_params=pltpu.CompilerParams(
            collective_id=2, has_side_effects=True, vmem_limit_bytes=56 << 20
        ),
    )(chosen, table, labels.reshape(1, total_m), labels.reshape(tall, 128))


def norm_kernel(n_dp, n_v, layer_ref, small_ref, table_ref, out_ref, sd, sv, ss, rs):
    f32 = jnp.float32
    d, v = lax.axis_index("dp"), lax.axis_index("vocab")
    others = [(lax.rem(d + k, n_dp), v) for k in range(1, n_dp)]
    partners = [(d, lax.rem(v + k, n_v)) for k in range(1, n_v)]
    sem = pltpu.get_barrier_semaphore()
    for partner in others + partners:
        pl.semaphore_signal(sem, 1, device_id=partner, device_id_type=MESH)

    def square(values):
        values = values.astype(f32)
        values = values * values
        while values.ndim > 2:
            values = jnp.sum(values, axis=0)
        return jnp.sum(jnp.sum(values, axis=0, keepdims=True), axis=1, keepdims=True)

    total = square(table_ref[...])
    total = total + jnp.where(v == 0, square(layer_ref[...]), 0.0)
    total = total + jnp.where((v == 0) & (d == 0), square(small_ref[...]), 0.0)
    sd[d] = jnp.broadcast_to(total, sd.shape[1:])
    pl.semaphore_wait(sem, n_dp - 1 + n_v - 1)
    q = Copies((d, v), ss, rs)
    for k in range(1, n_dp):
        q.send(k - 1, sd.at[d], sd.at[d], others[k - 1])
    for k in range(1, n_dp):
        q.arrived(k - 1, sd.at[lax.rem(d + n_dp - k, n_dp)])
    sv[v] = jnp.sum(sd[...], axis=0)
    for k in range(1, n_v):
        q.send(n_dp + k - 2, sv.at[v], sv.at[v], partners[k - 1])
    for k in range(1, n_v):
        q.arrived(n_dp + k - 2, sv.at[lax.rem(v + n_v - k, n_v)])
    out_ref[...] = jnp.sum(sv[...], axis=0)[:1, :1]
    q.finish()


def run_norm(layer, small, table, n_dp, n_v):
    f32 = jnp.float32
    vmem = pl.BlockSpec(memory_space=pltpu.VMEM)
    count = n_dp + n_v - 2
    return pl.pallas_call(
        functools.partial(norm_kernel, n_dp, n_v),
        out_shape=jax.ShapeDtypeStruct((1, 1), f32),
        in_specs=[vmem] * 3,
        out_specs=vmem,
        scratch_shapes=[
            pltpu.VMEM((n_dp, 8, 128), f32),
            pltpu.VMEM((n_v, 8, 128), f32),
            pltpu.SemaphoreType.DMA((count,)),
            pltpu.SemaphoreType.DMA((count,)),
        ],
        compiler_params=pltpu.CompilerParams(
            collective_id=4, has_side_effects=True, vmem_limit_bytes=40 << 20
        ),
    )(layer, small, table)


def adam_kernel(n_dp, cuts, scal_ref, table_g, block_g, small_g, *refs):
    f32 = jnp.float32
    n = 7
    ins, outs, bufs = refs[: 3 * n], refs[3 * n : 6 * n], refs[6 * n : 9 * n]
    up_g, ext_g, bias_g, sem_i, sem_o = refs[9 * n :]
    loads = [pltpu.make_async_copy(ins[k], bufs[k], sem_i.at[k]) for k in range(3 * n)]
    for copy in loads:
        copy.start()
    coef, one_hat, two_hat = scal_ref[0], scal_ref[1], scal_ref[2]
    rb, width = block_g.shape[1:]
    stores = []

    def change(i, at, cols, grad, rate=LR_BIG):
        master, first, second = bufs[3 * i : 3 * i + 3]
        g = grad.astype(f32) * coef
        one = BETA_ONE * first[at, cols] + (1.0 - BETA_ONE) * g
        two = BETA_TWO * second[at, cols] + (1.0 - BETA_TWO) * g * g
        old = master[at, cols]
        first[at, cols] = one
        second[at, cols] = two
        move = one * one_hat / (jnp.sqrt(two * two_hat) + ADAM_EPS) + DECAY * old
        master[at, cols] = old - rate * move

    def begin(i):
        for copy in loads[3 * i : 3 * i + 3]:
            copy.wait()

    def end(i):
        for k in range(3 * i, 3 * i + 3):
            copy = pltpu.make_async_copy(bufs[k], outs[k], sem_o.at[k])
            copy.start()
            stores.append(copy)

    def chunks(rows, act):
        size = 32 if rows % 32 == 0 else rows
        if size == rows:
            act(pl.ds(0, rows))
        else:

            def body(c, _):
                act(pl.ds(pl.multiple_of(c * size, size), size))
                return 0

            lax.fori_loop(0, rows // size, body, 0)

    every = slice(None)
    begin(0)
    chunks(bufs[0].shape[0], lambda at: change(0, at, every, table_g[at, :]))
    end(0)
    for i, blocks in ((1, range(3)), (2, range(3, 4))):
        begin(i)
        for j in blocks:
            for s in range(cuts):
                cols = pl.ds((j - blocks[0]) * D + s * width, width)
                chunks(rb, lambda at: change(i, at, cols, block_g[j * cuts + s, at, :]))
        end(i)
    begin(3)
    for j in range(4):
        for s in range(cuts):
            block = block_g[(4 + j) * cuts + s].astype(f32)
            for d in range(n_dp // cuts):
                to = (s * (n_dp // cuts) + d) * 4 * rb + j * rb
                up_g[:, to : to + rb] = block[:, d * rb : (d + 1) * rb]
    chunks(rb, lambda at: change(3, at, every, up_g[at, :]))
    end(3)
    begin(4)
    for j in range(4):
        for s in range(cuts):
            cols = pl.ds(s * width, width)

            def down(at, j=j, s=s, cols=cols):
                change(4, pl.ds(j * rb + at.start, at.size), cols, block_g[(8 + j) * cuts + s, at, :])

            chunks(rb, down)
    end(4)
    ext_g[...] = small_g[: ext_g.shape[0], :].astype(f32)
    begin(5)
    done = EXT // 8 * 8
    for at in (pl.ds(0, done // 2), pl.ds(done // 2, done // 2), pl.ds(done, EXT - done)):
        change(5, at, every, ext_g[at, :], LR_SMALL)
    end(5)
    begin(6)
    for j in range(4):
        for d in range(n_dp):
            piece = ext_g[EXT + 5 + j : EXT + 6 + j, d * rb : (d + 1) * rb]
            bias_g[:, d * 4 * rb + j * rb : d * 4 * rb + (j + 1) * rb] = piece
    for k in range(12):
        if 5 <= k < 9:
            grad = bias_g[:, (k - 5) * D : (k - 4) * D]
        else:
            grad = ext_g[EXT + k : EXT + k + 1, :]
        change(6, every, pl.ds(k * D, D), grad, LR_SMALL)
    end(6)
    for copy in stores:
        copy.wait()


def run_adam(scalars, table_g, block_g, small_g, states, n_dp, cuts):
    hbm = pl.BlockSpec(memory_space=pl.ANY)
    vmem = pl.BlockSpec(memory_space=pltpu.VMEM)
    flat = [array for state in states for array in state]
    n = len(flat)
    rb = block_g.shape[1]
    return pl.pallas_call(
        functools.partial(adam_kernel, n_dp, cuts),
        out_shape=[jax.ShapeDtypeStruct(a.shape, a.dtype) for a in flat],
        in_specs=[pl.BlockSpec(memory_space=pltpu.SMEM), vmem, vmem, vmem] + [hbm] * n,
        out_specs=[hbm] * n,
        scratch_shapes=[pltpu.VMEM(a.shape, a.dtype) for a in flat]
        + [
            pltpu.VMEM((rb, FF), jnp.float32),
            pltpu.VMEM((ceil_to(EXT + 12, 16), D), jnp.float32),
            pltpu.VMEM((1, FF), jnp.float32),
            pltpu.SemaphoreType.DMA((n,)),
            pltpu.SemaphoreType.DMA((n,)),
        ],
        compiler_params=pltpu.CompilerParams(vmem_limit_bytes=56 << 20),
    )(scalars, table_g, block_g, small_g, *flat)


def lane_mean(values):
    return jnp.sum(values, axis=-1, keepdims=True) * (1.0 / D)


def norm_parts(values):
    centered = values - lane_mean(values)
    rate = lax.rsqrt(lane_mean(centered * centered) + LN_EPS)
    return centered * rate, rate


def norm_back(values, grad, gain):
    unit, rate = norm_parts(values)
    scaled = grad * gain
    d_values = rate * (scaled - lane_mean(scaled) - unit * lane_mean(scaled * unit))
    return (
        d_values,
        jnp.sum(grad * unit, axis=0, keepdims=True),
        jnp.sum(grad, axis=0, keepdims=True),
    )


def dot(left, right, dims=((1,), (0,))):
    return lax.dot_general(left, right, (dims, ((), ())), preferred_element_type=jnp.float32)


NT = ((1,), (1,))
TN = ((0,), (0,))


def as_column(row):
    return jnp.broadcast_to(row, (128, row.shape[1])).T[:, :1]


def allowed_mask(row):
    col = as_column(row)
    return (row == col) | (row < 0) | (col < 0)


def forward_kernel(
    w_hbm, tok_ref, slot_ref, row_ref, reset_ref, vec_ref, ext_ref, pos_ref,
    x_o, hc_o, proj_o, p_o, one_o, mid_o, gp_o, act_o, two_o, chosen_o,
    w, x, hc, proj, probs, one, mid, gp, act, two, mask, hid, final, sem_w, sem_o,
):
    bf, f32 = jnp.bfloat16, jnp.float32
    loads = [pltpu.make_async_copy(w_hbm.at[:, b], w.at[b], sem_w.at[b]) for b in range(12)]
    for load in loads:
        load.start()
    waited = set()

    def weight(b):
        if b not in waited:
            loads[b].wait()
            waited.add(b)
        return w[b].reshape(D, D)

    stores = []

    def store(src, dst):
        copy = pltpu.make_async_copy(src, dst, sem_o.at[len(stores)])
        copy.start()
        stores.append(copy)

    vec = [vec_ref[k : k + 1, :] for k in range(12)]
    b_q, b_v, b_o, g_one, b_one = vec[:5]
    b_up, b_down, g_two, b_two = vec[5:9], vec[9], vec[10], vec[11]
    gain_e, bias_e = ext_ref[404:405, :], ext_ref[405:406, :]
    lane = lax.broadcasted_iota(jnp.int32, (1, 2 * HD), 1)
    low_half = lane < HD
    for seg in range(SEGS):
        rows = pl.ds(seg * ROWS, ROWS)
        held = lax.broadcasted_iota(jnp.int32, (1, tok_ref.shape[0]), 1).astype(f32)
        onehot = (as_column(slot_ref[:, seg * ROWS : (seg + 1) * ROWS]) == held).astype(f32).astype(bf)
        x[seg] = dot(onehot, tok_ref[...]) + ext_ref[:ROWS, :]
        x[seg, ROWS - MEM :, :] += ext_ref[ROWS + MEM : ROWS + 2 * MEM, :]
        first = ext_ref[ROWS : ROWS + MEM, :]
        if seg == 0:
            x[seg, :MEM, :] += first
        else:
            x[seg, :MEM, :] += jnp.where(reset_ref[seg - 1] > 0, first, hid[ROWS - MEM :, :])
        store(x.at[seg], x_o.at[seg])
        mask[...] = allowed_mask(row_ref[seg]).astype(f32)
        unit, _ = norm_parts(x[seg])
        h = unit * gain_e + bias_e
        hid[...] = h
        h_low = h.astype(bf)
        hc[0, rows, :] = h_low
        for k, bias in ((0, b_q), (1, None), (2, b_v)):
            made = dot(h_low, weight(k))
            proj[k, rows, :] = (made if bias is None else made + bias).astype(bf)
        store(hc.at[0, rows], hc_o.at[0, rows])
        store(proj.at[:, rows], proj_o.at[:, rows])
        for pair in range(HEADS // 2):
            cols = pl.ds(pair * 2 * HD, 2 * HD)
            query, keyed, value = (proj[k, rows, cols] for k in range(3))
            query = query * jnp.asarray(HD ** (-0.5), bf)
            parts = []
            for side in range(2):
                keep = low_half if side == 0 else ~low_half
                scores = dot(jnp.where(keep, query, jnp.zeros_like(query)), keyed, NT)
                scores = jnp.where(mask[...] > 0, scores, MASKED)
                expd = jnp.exp(scores - jnp.max(scores, axis=-1, keepdims=True))
                p_low = (expd * (1.0 / jnp.sum(expd, axis=-1, keepdims=True))).astype(bf)
                probs[seg, pair * 2 + side] = p_low
                parts.append(dot(p_low, value))
            hc[1, rows, cols] = jnp.where(low_half, parts[0], parts[1]).astype(bf)
        store(probs.at[seg], p_o.at[seg])
        store(hc.at[1, rows], hc_o.at[1, rows])
        sum_one = hid[...] + (dot(hc[1, rows, :], weight(3)) + b_o)
        one[seg] = sum_one
        store(one.at[seg], one_o.at[seg])
        unit, _ = norm_parts(sum_one)
        mid_now = unit * g_one + b_one
        mid_low = mid_now.astype(bf)
        mid[rows, :] = mid_low
        store(mid.at[rows], mid_o.at[rows])
        for j in range(4):
            up = dot(mid_low, weight(4 + j)) + b_up[j]
            half = 0.5 * (1.0 + lax.erf(up * 0.7071067811865476))
            gp[j, rows, :] = (half + up * jnp.exp(-0.5 * up * up) * 0.3989422804014327).astype(bf)
            act[j, rows, :] = (up * half).astype(bf)
        store(gp.at[:, rows], gp_o.at[:, rows])
        store(act.at[:, rows], act_o.at[:, rows])
        total = mid_now + b_down
        for j in range(4):
            total = total + dot(act[j, rows, :], weight(8 + j))
        two[seg] = total
        store(two.at[seg], two_o.at[seg])
        unit, _ = norm_parts(total)
        h = unit * g_two + b_two
        hid[...] = h
        final[rows, :] = h.astype(bf)
    at = lax.broadcasted_iota(jnp.int32, (SEGS * ROWS, 1), 0)
    at_pos = (at == pos_ref[...]).astype(f32).astype(bf)
    chosen_o[...] = dot(at_pos, final[...], TN).astype(bf)
    for copy in stores:
        copy.wait()


def run_forward(w_all, tok, slot, marks, reset, vec, ext, pos):
    f32, bf = jnp.float32, jnp.bfloat16
    n = SEGS * ROWS
    saved = [
        ((SEGS, ROWS, D), f32),
        ((2, n, D), bf),
        ((3, n, D), bf),
        ((SEGS, HEADS, ROWS, ROWS), bf),
        ((SEGS, ROWS, D), f32),
        ((n, D), bf),
        ((4, n, D), bf),
        ((4, n, D), bf),
        ((SEGS, ROWS, D), f32),
    ]
    hbm = pl.BlockSpec(memory_space=pl.ANY)
    vmem = pl.BlockSpec(memory_space=pltpu.VMEM)
    return pl.pallas_call(
        forward_kernel,
        out_shape=[jax.ShapeDtypeStruct(s, k) for s, k in saved]
        + [jax.ShapeDtypeStruct((MLM_PAD, D), bf)],
        in_specs=[hbm] + [vmem] * 3 + [pl.BlockSpec(memory_space=pltpu.SMEM), vmem, vmem, vmem],
        out_specs=[hbm] * len(saved) + [vmem],
        scratch_shapes=[pltpu.VMEM((12, w_all.shape[0]) + w_all.shape[2:], bf)]
        + [pltpu.VMEM(s, k) for s, k in saved]
        + [
            pltpu.VMEM((ROWS, ROWS), f32),
            pltpu.VMEM((ROWS, D), f32),
            pltpu.VMEM((n, D), bf),
            pltpu.SemaphoreType.DMA((12,)),
            pltpu.SemaphoreType.DMA((SEGS * 10,)),
        ],
        compiler_params=pltpu.CompilerParams(vmem_limit_bytes=60 << 20),
    )(w_all, tok, slot[None], marks[:, None, :].astype(f32), reset, vec, ext, pos[None])


def backward_kernel(
    n_dp, n_v,
    w_hbm, x_i, hc_i, proj_i, p_i, one_i, mid_i, gp_i, act_i, two_i,
    dch_ref, reset_ref, vec_ref, ext_ref, pos_ref, slot_ref,
    g_out, e_out, t_out, dtok,
    w, x, hc, right, probs, one, mid, rup, act, two, rdown, grad, dmem,
    small_o, dpack, share, bx, px, bz, own_g, e_in, eb, own_e, held, sem_w, sem_i, ss, rs, ls,
):
    bf, f32 = jnp.bfloat16, jnp.float32
    p = Place(n_dp, n_v)
    A, Y = p.A, p.Y
    others = [(lax.rem(p.d + k, n_dp), p.v) for k in range(1, n_dp)]
    partners = [(p.d, lax.rem(p.v + k, n_v)) for k in range(1, n_v)]
    barrier = pltpu.get_barrier_semaphore()
    for partner in others + partners:
        pl.semaphore_signal(barrier, 1, device_id=partner, device_id_type=MESH)
    q = Copies(p.me, ss, rs)
    groups = share.shape[0]
    x0 = 0
    t0 = x0 + groups * A
    z0 = t0 + n_dp - 1
    e0 = z0 + groups * (A - 1)
    y0 = e0 + 2 * (n_dp - 1) + n_v - 1
    c0 = y0 + groups * (Y - 1)
    cuts = n_v // 4
    width = D // cuts
    block, cut = p.v // cuts, p.v % cuts
    cols_v = pl.ds(pl.multiple_of(cut * width, 128), width)

    def p_to(k):
        return lax.rem(p.d + k, n_dp)

    def p_from(k):
        return lax.rem(p.d + n_dp - k, n_dp)

    def make_share(g, left, right_cols):
        made = dot(left, right_cols, TN)
        share[g] = made.reshape(share.shape[1:]).astype(bf)
        for k in range(1, A + 1):
            to = p.to_a(k)
            q.send(x0 + g * A + k - 1, share.at[g, to, 1 - p.x], bx.at[g, to], p.xp)

    def half_sum(g, k):
        to = p.to_a(k)
        q.arrived(x0 + g * A + k - 1, bx.at[g, to])
        px[g, to] = (share[g, to, p.x].astype(f32) + bx[g, to].astype(f32)).astype(bf)
        if k < A:
            q.send(z0 + g * (A - 1) + k - 1, px.at[g, to], bz.at[g, k - 1], p.zp(k))

    todo = [(g, k) for g in (2, 1, 0) for k in range(1, A + 1)]

    def half_sums(amount):
        for _ in range(amount):
            half_sum(*todo.pop(0))

    small_o[...] = jnp.zeros_like(small_o)
    loads = {}
    state = {"n": 0}

    def load(name, src, dst):
        copy = pltpu.make_async_copy(src, dst, sem_i.at[state["n"]])
        state["n"] += 1
        copy.start()
        loads[name] = copy

    def need(name):
        if name in loads:
            loads.pop(name).wait()

    wl = [pltpu.make_async_copy(w_hbm.at[:, b], w.at[b], sem_w.at[b]) for b in range(12)]
    waited = set()

    def weight(b):
        if b not in waited:
            wl[b].wait()
            waited.add(b)
        return w[b].reshape(D, D)

    order = list(reversed(range(SEGS)))
    for i, seg in enumerate(order):
        rows = pl.ds(seg * ROWS, ROWS)
        load(("two", seg), two_i.at[seg], two.at[seg])
        if i == 0:
            for b in range(8, 12):
                wl[b].start()
        load(("gp", seg), gp_i.at[:, rows], rup.at[:, rows])
        if i == 0:
            for b in range(4, 8):
                wl[b].start()
        load(("one", seg), one_i.at[seg], one.at[seg])
        if i == 0:
            wl[3].start()
            load(("p", seg), p_i.at[seg], probs)
        load(("proj", seg), proj_i.at[:, rows], right.at[pl.ds(0, 3), rows])
        if i == 0:
            for b in range(3):
                wl[b].start()
        load(("x", seg), x_i.at[seg], x.at[seg])
    load("hc", hc_i, hc)
    load("mid", mid_i, mid)
    load("act", act_i, act)

    vec = [vec_ref[k : k + 1, :] for k in range(12)]
    g_one, g_two, gain_e = vec[3], vec[10], ext_ref[404:405, :]
    lane = lax.broadcasted_iota(jnp.int32, (1, 2 * HD), 1)
    low_half = lane < HD
    at = lax.broadcasted_iota(jnp.int32, (SEGS * ROWS, 1), 0)
    at_pos = (at == pos_ref[...]).astype(f32).astype(bf)
    v0 = EXT

    def add_row(k, value):
        small_o[v0 + k : v0 + k + 1, :] += value

    def sums(values):
        return jnp.sum(values.astype(f32), axis=0, keepdims=True)

    for i, seg in enumerate(order):
        rows = pl.ds(seg * ROWS, ROWS)
        grad[...] = dot(at_pos[seg * ROWS : (seg + 1) * ROWS, :], dch_ref[...])
        if i > 0:
            grad[ROWS - MEM :, :] += dmem[...]
        need(("two", seg))
        d_two, d_gain, d_shift = norm_back(two[seg], grad[...], g_two)
        add_row(10, d_gain)
        add_row(11, d_shift)
        r_down = d_two.astype(bf)
        rdown[rows, :] = r_down
        add_row(9, sums(r_down))
        if i == SEGS - 1:
            need("act")
            pl.semaphore_wait(barrier, n_dp - 1 + n_v - 1)
            make_share(2, act[block], rdown[:, cols_v])
        need(("gp", seg))
        for j in range(4):
            r_up = (rup[j, rows, :].astype(f32) * dot(r_down, weight(8 + j), NT)).astype(bf)
            rup[j, rows, :] = r_up
            add_row(5 + j, sums(r_up))
        if i == SEGS - 1:
            need("mid")
            make_share(1, mid[...], rup[block, :, cols_v])
            half_sums(1)
        for j in range(4):
            d_two = d_two + dot(rup[j, rows, :], weight(4 + j), NT)
        need(("one", seg))
        d_one, d_gain, d_shift = norm_back(one[seg], d_two, g_one)
        add_row(3, d_gain)
        add_row(4, d_shift)
        grad[...] = d_one
        r_att = d_one.astype(bf)
        right[3, rows, :] = r_att
        add_row(2, sums(r_att))
        d_ctx = dot(r_att, weight(3), NT).astype(bf)
        need(("p", seg))
        need(("proj", seg))
        for pair in range(HEADS // 2):
            if i == SEGS - 1 and 0 < pair <= 3 and len(todo) > 2 * A:
                half_sums(1)
            cols = pl.ds(pair * 2 * HD, 2 * HD)
            query, keyed, value = (right[k, rows, cols] for k in range(3))
            d_out = d_ctx[:, pair * 2 * HD : (pair + 1) * 2 * HD]
            made = []
            for side in range(2):
                keep = low_half if side == 0 else ~low_half
                p_low = probs[pair * 2 + side]
                p_now = p_low.astype(f32)
                d_p = dot(jnp.where(keep, d_out, jnp.zeros_like(d_out)), value, NT)
                weighted = p_now * d_p
                d_s = weighted - p_now * jnp.sum(weighted, axis=-1, keepdims=True)
                d_s = d_s.astype(bf)
                made.append((dot(d_s, keyed), dot(d_s, query, TN), dot(p_low, d_out, TN)))
            for k, scale in ((0, HD ** (-0.5)), (1, HD ** (-0.5)), (2, 1.0)):
                both = jnp.where(low_half, made[0][k], made[1][k]) * scale
                right[k, rows, cols] = both.astype(bf)
        if i + 1 < SEGS:
            load(("p", order[i + 1]), p_i.at[order[i + 1]], probs)
        if i == SEGS - 1:
            need("hc")
            make_share(0, hc[block // 3], right[block, :, cols_v])
            half_sums(max(0, len(todo) - 2 * A) + 1)
        d_h = grad[...]
        for k in range(3):
            d_h = d_h + dot(right[k, rows, :], weight(k), NT)
        add_row(0, sums(right[0, rows, :]))
        add_row(1, sums(right[2, rows, :]))
        need(("x", seg))
        d_x, d_gain, d_shift = norm_back(x[seg], d_h, gain_e)
        grad[...] = d_x
        dtok[rows, :] = d_x.astype(bf)
        small_o[:ROWS, :] += d_x
        small_o[ROWS + MEM : ROWS + 2 * MEM, :] += grad[ROWS - MEM :, :]
        small_o[404:405, :] += d_gain
        small_o[405:406, :] += d_shift
        d_read = grad[:MEM, :]
        if seg > 0:
            back = reset_ref[seg - 1] > 0
            small_o[ROWS : ROWS + MEM, :] += jnp.where(back, d_read, 0.0)
            dmem[...] = jnp.where(back, 0.0, d_read)
        else:
            small_o[ROWS : ROWS + MEM, :] += d_read
    cap = dpack.shape[1]
    place = lax.broadcasted_iota(jnp.int32, (cap, 1), 0)
    for d in range(n_dp):
        slots = (place + (d * n_v + p.v) * cap).astype(f32)
        held[d * cap : (d + 1) * cap, :] = (slots == slot_ref[...]).astype(f32).astype(bf)
    dpack[...] = dot(held[...], dtok[...]).astype(bf).reshape(dpack.shape)
    e_rows = e_in.shape[1]
    for d in range(n_dp):
        at = (d * n_v + p.v) * e_rows
        fits = at < small_o.shape[0]

        @pl.when(fits)
        def _(d=d, at=at):
            e_in[d] = small_o[pl.ds(pl.multiple_of(at, e_rows), e_rows), :].astype(bf)

        @pl.when(jnp.logical_not(fits))
        def _(d=d):
            e_in[d] = jnp.zeros(e_in.shape[1:], bf)

    for k in range(1, n_dp):
        q.send(e0 + k - 1, e_in.at[p_to(k)], eb.at[p.d], others[k - 1])
    eb[p.d] = e_in[p.d]
    locals_ = []

    def keep(src, dst):
        copy = pltpu.make_async_copy(src, dst, ls.at[len(locals_)])
        copy.start()
        locals_.append(copy)

    e1 = e0 + n_dp - 1
    e2 = e1 + n_dp - 1
    def whole_sums(g):
        total = px[g, p.a].astype(f32)
        for k in range(1, A):
            q.arrived(z0 + g * (A - 1) + k - 1, bz.at[g, k - 1])
            total = total + bz[g, k - 1].astype(f32)
        own_g[g] = total.astype(bf)
        mine = g_out.at[g * n_v + p.v]
        for k in range(1, Y):
            q.send(y0 + g * (Y - 1) + k - 1, own_g.at[g], mine, p.yp(k))
        q.send(c0 + g * Y, own_g.at[g], mine, p.cp)
        keep(own_g.at[g], mine)

    def hand_on(g):
        for j in range(1, Y):
            piece = g_out.at[g * n_v + p.from_y(j) * 2 + p.c]
            q.arrived(y0 + g * (Y - 1) + j - 1, piece)
            q.send(c0 + g * Y + j, piece, piece, p.cp)

    half_sums(len(todo) - A)
    for k in range(1, n_dp):
        q.arrived(e0 + k - 1, eb.at[p_from(k)])
    own_e[...] = jnp.sum(eb[...].astype(f32), axis=0).astype(bf)
    keep(own_e, e_out.at[p.d, p.v])
    for k in range(1, n_dp):
        q.send(e1 + k - 1, own_e, e_out.at[p.d, p.v], others[k - 1])
    half_sums(len(todo))
    for k in range(1, n_dp):
        q.send(t0 + k - 1, dpack.at[p_to(k)], t_out.at[p.d], others[k - 1])
    keep(dpack.at[p.d], t_out.at[p.d])
    whole_sums(2)
    hand_on(2)
    for k in range(1, n_dp):
        q.arrived(e1 + k - 1, e_out.at[p_from(k), p.v])
    locals_[0].wait()
    for k in range(1, n_v):
        q.send(e2 + k - 1, e_out.at[:, p.v], e_out.at[:, p.v], partners[k - 1])
    whole_sums(1)
    hand_on(1)
    whole_sums(0)
    hand_on(0)
    for k in range(1, n_v):
        q.arrived(e2 + k - 1, e_out.at[:, lax.rem(p.v + n_v - k, n_v)])
    for g in range(groups):
        for j in range(Y):
            q.arrived(c0 + g * Y + j, g_out.at[g * n_v + p.from_y(j) * 2 + 1 - p.c])
    for k in range(1, n_dp):
        q.arrived(t0 + k - 1, t_out.at[p_from(k)])
    q.finish()
    for copy in locals_[1:]:
        copy.wait()


def run_backward(w_all, saved, d_chosen, reset, vec, ext, pos, slot, cap, rb, n_dp, n_v):
    f32, bf = jnp.float32, jnp.bfloat16
    n = SEGS * ROWS
    A, Y, groups = n_dp // 2, n_v // 2, 3
    width = D // (n_v // 4)
    e_rows = ceil_to(-(-(EXT + 12) // (n_dp * n_v)), 16)
    hbm = pl.BlockSpec(memory_space=pl.ANY)
    vmem = pl.BlockSpec(memory_space=pltpu.VMEM)
    smem = pl.BlockSpec(memory_space=pltpu.SMEM)
    count = groups * (A + A - 1 + Y - 1 + Y) + 3 * (n_dp - 1) + n_v - 1
    return pl.pallas_call(
        functools.partial(backward_kernel, n_dp, n_v),
        out_shape=[
            jax.ShapeDtypeStruct((groups * n_v, rb, width), bf),
            jax.ShapeDtypeStruct((n_dp, n_v, e_rows, D), bf),
            jax.ShapeDtypeStruct((n_dp, cap, D), bf),
            jax.ShapeDtypeStruct((n, D), bf),
        ],
        in_specs=[hbm] * 10 + [vmem, smem] + [vmem] * 4,
        out_specs=[hbm, hbm, hbm, vmem],
        scratch_shapes=[
            pltpu.VMEM((12, w_all.shape[0]) + w_all.shape[2:], bf),
            pltpu.VMEM((SEGS, ROWS, D), f32),
            pltpu.VMEM((2, n, D), bf),
            pltpu.VMEM((4, n, D), bf),
            pltpu.VMEM((HEADS, ROWS, ROWS), bf),
            pltpu.VMEM((SEGS, ROWS, D), f32),
            pltpu.VMEM((n, D), bf),
            pltpu.VMEM((4, n, D), bf),
            pltpu.VMEM((4, n, D), bf),
            pltpu.VMEM((SEGS, ROWS, D), f32),
            pltpu.VMEM((n, D), bf),
            pltpu.VMEM((ROWS, D), f32),
            pltpu.VMEM((MEM, D), f32),
            pltpu.VMEM((ceil_to(EXT + 12, e_rows), D), f32),
            pltpu.VMEM((n_dp, cap, D), bf),
            pltpu.VMEM((groups, A, 2, rb, width), bf),
            pltpu.VMEM((groups, A, rb, width), bf),
            pltpu.VMEM((groups, A, rb, width), bf),
            pltpu.VMEM((groups, A - 1, rb, width), bf),
            pltpu.VMEM((groups, rb, width), bf),
            pltpu.VMEM((n_dp, e_rows, D), bf),
            pltpu.VMEM((n_dp, e_rows, D), bf),
            pltpu.VMEM((e_rows, D), bf),
            pltpu.VMEM((n_dp * cap, n), bf),
            pltpu.SemaphoreType.DMA((12,)),
            pltpu.SemaphoreType.DMA((SEGS * 6 + 4,)),
            pltpu.SemaphoreType.DMA((count,)),
            pltpu.SemaphoreType.DMA((count,)),
            pltpu.SemaphoreType.DMA((2 + groups,)),
        ],
        compiler_params=pltpu.CompilerParams(
            collective_id=3, has_side_effects=True, vmem_limit_bytes=63 << 20
        ),
    )(
        w_all, *saved, d_chosen, reset, vec, ext, pos[None], slot[None],
    )


def ceil_to(value, unit):
    return -(-value // unit) * unit


def per_device(
    ids,
    docs,
    resets,
    mlm_pos,
    mlm_label,
    step,
    qkv_master,
    qkv_first,
    qkv_second,
    out_master,
    out_first,
    out_second,
    up_master,
    up_first,
    up_second,
    down_master,
    down_first,
    down_second,
    embed_master,
    embed_first,
    embed_second,
    vectors_master,
    vectors_first,
    vectors_second,
    extras_master,
    extras_first,
    extras_second,
):
    f32, bf = jnp.float32, jnp.bfloat16
    n_dp = lax.axis_size("dp")
    n_v = lax.axis_size("vocab")
    d_idx = lax.axis_index("dp")
    v_idx = lax.axis_index("vocab")
    own_rows = embed_master.shape[0]
    tokens_n = SEGS * SEG
    rb = qkv_master.shape[1]
    cuts = max(1, n_v // 4)
    width = D // cuts

    ints = jnp.concatenate([ids[0], mlm_label[0]])[None]
    ints = jnp.pad(ints, ((0, 0), (0, ceil_to(ints.shape[1], 128) - ints.shape[1])), constant_values=-1)
    cap = ceil_to(2 * tokens_n // (n_dp * n_v) + 2, 16)
    masters = (qkv_master[0], out_master[0], up_master[0], down_master[0])
    w_all, tok_all, ints_all, pick, slots, most, table = run_front(
        masters, embed_master, ints, cap, n_dp, n_v
    )
    if cuts > 1 or rb % 16:
        w_all = w_all.reshape(n_dp, 12, cuts, rb, width).transpose(1, 0, 3, 2, 4).reshape(1, 12, D, D)
    ids_all = ints_all[:, 0, :tokens_n]
    labels_all = ints_all[:, 0, tokens_n : tokens_n + MLM]
    labels_all = jnp.pad(labels_all, ((0, 0), (0, MLM_PAD - MLM)), constant_values=-1)
    overflow = most[0, 0] >= cap

    def padded(values):
        values = values.reshape((SEGS, SEG) + values.shape[1:])
        edges = ((0, 0), (MEM, MEM)) + ((0, 0),) * (values.ndim - 2)
        values = jnp.pad(values, edges, constant_values=-1)
        return values.reshape((SEGS * ROWS,) + values.shape[2:])

    slot = padded(lax.dynamic_index_in_dim(slots, d_idx, keepdims=False)[:tokens_n])

    def packed_tokens(_):
        return tok_all.reshape(n_dp * n_v * cap, D), slot

    def whole_tokens(_):
        whole = lax.all_gather(table, "dp", axis=0, tiled=True)
        at = jnp.arange(n_dp * own_rows, dtype=jnp.int32)
        row_ids = (at // own_rows * n_v + v_idx) * own_rows + at % own_rows
        onehot = (ids[0][:, None] == row_ids[None, :]).astype(bf)
        rows = lax.psum(jnp.dot(onehot, whole, preferred_element_type=f32).astype(bf), "vocab")
        rows = jnp.pad(rows, ((0, n_dp * n_v * cap - tokens_n), (0, 0)))
        return rows, padded(jnp.arange(tokens_n, dtype=jnp.int32).astype(f32))

    token_rows, token_slot = lax.cond(overflow, whole_tokens, packed_tokens, 0)
    marks = jnp.pad(docs.reshape(SEGS, SEG), ((0, 0), (MEM, MEM)), constant_values=-1)
    vec = vectors_master[0].reshape(12, D)
    b_up = vec[5:9].reshape(n_dp, 4, rb).transpose(1, 0, 2).reshape(4, D)
    vec = jnp.concatenate([vec[:5], b_up, vec[9:]])
    positions = mlm_pos[0]
    at_rows = positions // SEG * ROWS + MEM + positions % SEG
    at_rows = jnp.concatenate([at_rows, jnp.full((MLM_PAD - MLM,), -1, jnp.int32)])
    *saved, chosen = run_forward(w_all, token_rows, token_slot, marks, resets[0], vec, extras_master, at_rows)
    rows_v = MLM_PAD // n_v
    d_chosen, d_table, loss = run_head(chosen.reshape(n_v, rows_v, D), table, labels_all, n_dp, n_v)
    loss = loss[0, 0]
    d_chosen = d_chosen.reshape(MLM_PAD, D)
    g_blocks, small_all, d_packed_all, d_tok = run_backward(
        w_all, saved, d_chosen, resets[0], vec, extras_master, at_rows, slot, cap, rb, n_dp, n_v
    )

    def packed_d_table(_):
        return jnp.einsum(
            "tv,td->vd", pick, d_packed_all.reshape(n_dp * cap, D), preferred_element_type=f32
        )

    def whole_d_table(_):
        d_all = d_tok.reshape(SEGS, ROWS, D)[:, MEM : MEM + SEG].reshape(tokens_n, D)
        d_all = lax.all_gather(d_all, "dp", axis=0, tiled=True)
        row_ids = (d_idx * n_v + v_idx) * own_rows + jnp.arange(own_rows, dtype=jnp.int32)
        onehot = (ids_all.reshape(-1)[:, None] == row_ids[None, :]).astype(bf)
        return jnp.einsum("tv,td->vd", onehot, d_all, preferred_element_type=f32)

    s_table = d_table + lax.cond(overflow, whole_d_table, packed_d_table, 0)
    small_all = small_all.reshape(-1, D)
    norm = jnp.sqrt(run_norm(g_blocks, small_all, s_table, n_dp, n_v)[0, 0])
    coef = jnp.minimum(1.0, CLIP / (norm + 1e-06))
    t = step[0].astype(f32)
    scalars = jnp.stack([coef, 1.0 / (1.0 - BETA_ONE**t), 1.0 / (1.0 - BETA_TWO**t)])
    states = (
        (embed_master, embed_first, embed_second),
        (qkv_master[0], qkv_first[0], qkv_second[0]),
        (out_master[0], out_first[0], out_second[0]),
        (up_master[0], up_first[0], up_second[0]),
        (down_master[0], down_first[0], down_second[0]),
        (extras_master, extras_first, extras_second),
        (vectors_master, vectors_first, vectors_second),
    )
    new = run_adam(scalars, s_table, g_blocks, small_all, states, n_dp, cuts)
    layer = [value[None] for value in new[3:15]]
    return (loss, norm, *layer, *new[:3], *new[18:], *new[15:18])


def solution(mesh):
    in_specs = (
        P("dp", None),
        P("dp", None),
        P("dp", None),
        P("dp", None),
        P("dp", None),
        P(),
        P(None, "dp", None),
        P(None, "dp", None),
        P(None, "dp", None),
        P(None, "dp", None),
        P(None, "dp", None),
        P(None, "dp", None),
        P(None, "dp", None),
        P(None, "dp", None),
        P(None, "dp", None),
        P(None, "dp", None),
        P(None, "dp", None),
        P(None, "dp", None),
        P(("dp", "vocab"), None),
        P(("dp", "vocab"), None),
        P(("dp", "vocab"), None),
        P(),
        P(),
        P(),
        P(),
        P(),
        P(),
    )
    out_specs = (
        P(),
        P(),
        P(None, "dp", None),
        P(None, "dp", None),
        P(None, "dp", None),
        P(None, "dp", None),
        P(None, "dp", None),
        P(None, "dp", None),
        P(None, "dp", None),
        P(None, "dp", None),
        P(None, "dp", None),
        P(None, "dp", None),
        P(None, "dp", None),
        P(None, "dp", None),
        P(("dp", "vocab"), None),
        P(("dp", "vocab"), None),
        P(("dp", "vocab"), None),
        P(),
        P(),
        P(),
        P(),
        P(),
        P(),
    )
    return jax.shard_map(
        per_device, mesh=mesh, in_specs=in_specs, out_specs=out_specs, check_vma=False
    )
```
